32 devices in a mesh: grp: 8 (over z, x), seq: 4 (over y, core).
Axes of the slice: x: 2, y: 2, z: 4, core: 2. Of those that a mesh axis runs over, the one named last changes fastest.
Arguments:
- tokens: bfloat16 [16, 448, 768], P('grp', 'seq'), may hold values from -6 to 6
- encoder_states: bfloat16 [16, 1500, 768], P('grp', 'seq'), may hold values from -6 to 6
- lengths: int32 [16], P('grp'), may hold values from 56 to 448, as said below
- frame_counts: int32 [16], P('grp'), may hold values from 375 to 1500, as said below
- corpus_ids: int32 [16], P('grp'), may hold values from 0 to 8
- corpus_weights: float32 [9], replicated, may hold values from 0.5 to 2
- cotangent: bfloat16 [16, 448, 768], P('grp', 'seq'), may hold values from -6 to 6
- first_gain: bfloat16 [768], P('grp'), may hold values from 0.5 to 1.5
- first_bias: bfloat16 [768], P('grp'), may hold values from -1.5 to 1.5
- query_weight: bfloat16 [768, 768], P('grp', 'seq'), may hold values from -0.3125 to 0.3125
- query_bias: bfloat16 [768], P('grp'), may hold values from -1.5 to 1.5
- key_weight: bfloat16 [768, 768], P('grp', 'seq'), may hold values from -0.3125 to 0.3125
- value_weight: bfloat16 [768, 768], P('grp', 'seq'), may hold values from -0.21875 to 0.21875
- value_bias: bfloat16 [768], P('grp'), may hold values from -1.5 to 1.5
- output_weight: bfloat16 [768, 768], P('grp', 'seq'), may hold values from -1.75 to 1.75
- output_bias: bfloat16 [768], P('grp'), may hold values from -1.5 to 1.5
- second_gain: bfloat16 [768], P('grp'), may hold values from 0.5 to 1.5
- second_bias: bfloat16 [768], P('grp'), may hold values from -1.5 to 1.5
- cross_query_weight: bfloat16 [768, 768], P('grp', 'seq'), may hold values from -0.3125 to 0.3125
- cross_query_bias: bfloat16 [768], P('grp'), may hold values from -1.5 to 1.5
- cross_key_weight: bfloat16 [768, 768], P('grp', 'seq'), may hold values from -0.3125 to 0.3125
- cross_value_weight: bfloat16 [768, 768], P('grp', 'seq'), may hold values from -0.21875 to 0.21875
- cross_value_bias: bfloat16 [768], P('grp'), may hold values from -1.5 to 1.5
- cross_output_weight: bfloat16 [768, 768], P('grp', 'seq'), may hold values from -2.5 to 2.5
- cross_output_bias: bfloat16 [768], P('grp'), may hold values from -1.5 to 1.5
- third_gain: bfloat16 [768], P('grp'), may hold values from 0.5 to 1.5
- third_bias: bfloat16 [768], P('grp'), may hold values from -1.5 to 1.5
- expand_weight: bfloat16 [768, 3072], P('grp', 'seq'), may hold values from -0.21875 to 0.21875
- expand_bias: bfloat16 [3072], P('grp'), may hold values from -1.5 to 1.5
- reduce_weight: bfloat16 [3072, 768], P('grp', 'seq'), may hold values from -0.109375 to 0.109375
- reduce_bias: bfloat16 [768], P('grp'), may hold values from -1.5 to 1.5
Outputs:
- layer_output: bfloat16 [16, 448, 768], P('grp', 'seq')
- tokens_gradient: bfloat16 [16, 448, 768], P('grp', 'seq')
- first_gain_gradient: float32 [768], P('grp')
- first_bias_gradient: float32 [768], P('grp')
- query_weight_gradient: float32 [768, 768], P('grp', 'seq')
- query_bias_gradient: float32 [768], P('grp')
- key_weight_gradient: float32 [768, 768], P('grp', 'seq')
- value_weight_gradient: float32 [768, 768], P('grp', 'seq')
- value_bias_gradient: float32 [768], P('grp')
- output_weight_gradient: float32 [768, 768], P('grp', 'seq')
- output_bias_gradient: float32 [768], P('grp')
- second_gain_gradient: float32 [768], P('grp')
- second_bias_gradient: float32 [768], P('grp')
- cross_query_weight_gradient: float32 [768, 768], P('grp', 'seq')
- cross_query_bias_gradient: float32 [768], P('grp')
- cross_key_weight_gradient: float32 [768, 768], P('grp', 'seq')
- cross_value_weight_gradient: float32 [768, 768], P('grp', 'seq')
- cross_value_bias_gradient: float32 [768], P('grp')
- cross_output_weight_gradient: float32 [768, 768], P('grp', 'seq')
- cross_output_bias_gradient: float32 [768], P('grp')
- third_gain_gradient: float32 [768], P('grp')
- third_bias_gradient: float32 [768], P('grp')
- expand_weight_gradient: float32 [768, 3072], P('grp', 'seq')
- expand_bias_gradient: float32 [3072], P('grp')
- reduce_weight_gradient: float32 [3072, 768], P('grp', 'seq')
- reduce_bias_gradient: float32 [768], P('grp')
The draws below stay inside these ranges and needn't reach their ends.
Inputs may be any that keep to these rules, and one draw needn't show every extreme that they name: `lengths`: in each aligned block of 2 transcripts one has more than 336 valid tokens; some transcript has exactly 448. `frame_counts`: in each aligned block of 2 clips one has more than 1125 valid frames; some clip has exactly 1500.
All inputs are finite; a program needn't handle non-finite values.
Results may differ from the reference program's by a relative error of at most 0.025.
Values may be sent and summed in bfloat16 or wider, within the bound.
A program may use at most 192 MiB of HBM per device.

```python
import math
import jax
import jax.numpy as jnp
from jax import lax

D = 768
HEADS = 12
HEAD_DIM = 64
FF = 3072
SLOTS = 448
FRAMES = 1500
TR = 2
CORPORA = 9
TRANSCRIPTS = 16
STRETCH = 112


def reaching_counts(key, limit, lowest, reach):
    blocks = TRANSCRIPTS // TR
    first_key, second_key, third_key, fourth_key = jax.random.split(key, 4)
    drawn = jax.random.randint(first_key, (blocks, TR), lowest, limit + 1, dtype=jnp.int32)
    longest = jax.random.randint(third_key, (blocks, TR), limit - reach + 1, limit + 1, dtype=jnp.int32)
    picked = jax.random.randint(second_key, (blocks, 1), 0, TR, dtype=jnp.int32)
    place = jnp.arange(TR, dtype=jnp.int32)[None, :]
    values = jnp.where(place == picked, longest, drawn).reshape(-1)
    chosen = jax.random.randint(fourth_key, (), 0, blocks, dtype=jnp.int32)
    slot = chosen * TR + picked.reshape(-1)[chosen]
    index = jnp.arange(TRANSCRIPTS, dtype=jnp.int32)
    return jnp.where(index == slot, limit, values).astype(jnp.int32)


def draw_lengths(key, part):
    key = jax.random.fold_in(key, 11)
    return reaching_counts(key, SLOTS, SLOTS // 8, STRETCH)


def draw_frame_counts(key, part):
    key = jax.random.fold_in(key, 23)
    return reaching_counts(key, FRAMES, FRAMES // 4, FRAMES * STRETCH // SLOTS)


def touch_ends(entries, stream_key, least, largest):
    dims = entries.shape
    spot = [jax.random.randint(jax.random.fold_in(stream_key, axis), (), 0, dims[axis]) for axis in range(len(dims))]
    entries = entries.at[tuple(spot)].set(least)
    longest = dims.index(max(dims))
    spot[longest] = (spot[longest] + 1) % dims[longest]
    return entries.at[tuple(spot)].set(largest)


def levels(stream_key, dims, shards, least, top_value):
    def one(position, parts):
        steps = jax.random.uniform(jax.random.fold_in(jax.random.fold_in(stream_key, 6), position), (parts,), jnp.float32, least / len(shards), top_value / len(shards))
        return jnp.repeat(jnp.exp(steps), dims[position] // parts).reshape((-1,) + (1,) * (len(dims) - position - 1))

    loudness = one(*shards[0])
    for cut in shards[1:]:
        loudness = loudness * one(*cut)
    return loudness


def scatter_about(stream_key, shape, width, most, shards=(), kind=jnp.bfloat16):
    values = jax.random.normal(stream_key, shape, jnp.float32) * width
    if len(shards) > 0:
        values = levels(stream_key, shape, shards, -0.22, 0.18) * values
    return jnp.clip(values, min=-most, max=most).astype(kind)


def setup_inputs(seed: int = 0) -> dict:
    splits = jax.random.split(jax.random.key(seed), 32)
    return {
        "tokens": scatter_about(splits[0], (TRANSCRIPTS, SLOTS, D), 1.0, 6.0, ((0, 8), (1, 4))),
        "encoder_states": scatter_about(splits[1], (TRANSCRIPTS, FRAMES, D), 1.0, 6.0, ((0, 8), (1, 4))),
        "lengths": draw_lengths(jax.random.fold_in(splits[31], 71), 0),
        "frame_counts": draw_frame_counts(jax.random.fold_in(splits[31], 71), 0),
        "corpus_ids": touch_ends(jax.random.randint(splits[4], (TRANSCRIPTS,), 0, CORPORA), jax.random.fold_in(splits[4], 1), 0, CORPORA - 1).astype(jnp.int32),
        "corpus_weights": jnp.clip(jnp.exp(jax.random.uniform(splits[5], (CORPORA,), jnp.float32, math.log(0.5), math.log(2.0))), 0.5, 2.0),
        "cotangent": scatter_about(splits[6], (TRANSCRIPTS, SLOTS, D), 1.0, 6.0, ((0, 8), (1, 4))),
        "first_gain": jnp.clip(1.0 + 0.1 * jax.random.normal(splits[7], (D,), jnp.float32), 0.5, 1.5).astype(jnp.bfloat16),
        "first_bias": scatter_about(splits[8], (D,), 0.3, 1.5, ((0, 8),)),
        "query_weight": scatter_about(splits[9], (D, D), (D // 2) ** -0.5, 0.3125, ((0, 8), (1, 4))),
        "query_bias": scatter_about(splits[10], (D,), 0.3, 1.5, ((0, 8),)),
        "key_weight": scatter_about(splits[11], (D, D), (D // 2) ** -0.5, 0.3125, ((0, 8), (1, 4))),
        "value_weight": scatter_about(splits[12], (D, D), D ** -0.5, 0.21875, ((0, 8), (1, 4))),
        "value_bias": scatter_about(splits[13], (D,), 0.3, 1.5, ((0, 8),)),
        "output_weight": scatter_about(splits[14], (D, D), (max(D // 64, 2)) ** -0.5, 1.75, ((0, 8), (1, 4))),
        "output_bias": scatter_about(splits[15], (D,), 0.3, 1.5, ((0, 8),)),
        "second_gain": jnp.clip(1.0 + 0.1 * jax.random.normal(splits[16], (D,), jnp.float32), 0.5, 1.5).astype(jnp.bfloat16),
        "second_bias": scatter_about(splits[17], (D,), 0.3, 1.5, ((0, 8),)),
        "cross_query_weight": scatter_about(splits[18], (D, D), (D // 2) ** -0.5, 0.3125, ((0, 8), (1, 4))),
        "cross_query_bias": scatter_about(splits[19], (D,), 0.3, 1.5, ((0, 8),)),
        "cross_key_weight": scatter_about(splits[20], (D, D), (D // 2) ** -0.5, 0.3125, ((0, 8), (1, 4))),
        "cross_value_weight": scatter_about(splits[21], (D, D), D ** -0.5, 0.21875, ((0, 8), (1, 4))),
        "cross_value_bias": scatter_about(splits[22], (D,), 0.3, 1.5, ((0, 8),)),
        "cross_output_weight": scatter_about(splits[23], (D, D), (max(D // 128, 2)) ** -0.5, 2.5, ((0, 8), (1, 4))),
        "cross_output_bias": scatter_about(splits[24], (D,), 0.3, 1.5, ((0, 8),)),
        "third_gain": jnp.clip(1.0 + 0.1 * jax.random.normal(splits[25], (D,), jnp.float32), 0.5, 1.5).astype(jnp.bfloat16),
        "third_bias": scatter_about(splits[26], (D,), 0.3, 1.5, ((0, 8),)),
        "expand_weight": scatter_about(splits[27], (D, FF), D ** -0.5, 0.21875, ((0, 8), (1, 4))),
        "expand_bias": scatter_about(splits[28], (FF,), 0.3, 1.5, ((0, 8),)),
        "reduce_weight": scatter_about(splits[29], (FF, D), FF ** -0.5, 0.109375, ((0, 8), (1, 4))),
        "reduce_bias": scatter_about(splits[30], (D,), 0.3, 1.5, ((0, 8),)),
    }


NEG = -1e+30
EPS = 1e-05
HIGH = lax.Precision.HIGHEST

@jax.custom_vjp
def low(v):
    return lax.optimization_barrier(v.astype(jnp.bfloat16)).astype(jnp.float32)

@jax.custom_vjp
def low_back(v):
    return v

def low_keep(v):
    return (low(v), None)

def low_pass(kept, grad):
    return (grad,)

def back_keep(v):
    return (v, None)

def back_low(kept, grad):
    return (low(grad),)
low.defvjp(low_keep, low_pass)
low_back.defvjp(back_keep, back_low)

def norm_rows(values, scaling, offset):
    centre = values - lax.optimization_barrier(jnp.mean(values, axis=-1, keepdims=True))
    spread = lax.optimization_barrier(jnp.mean(centre * centre, axis=-1, keepdims=True))
    return centre * lax.rsqrt(spread + EPS) * scaling + offset

def smooth_gate(values):
    return 0.5 * values * (1.0 + lax.erf(values * 0.7071067811865476))

def mult(inputs, weight):
    return jnp.einsum('bri,ij->brj', inputs, weight, precision=HIGH)

def attend(query, key_rows, values, allowed):
    number, length, breadth = query.shape
    query_heads = query.reshape(number, length, HEADS, HEAD_DIM)
    key_heads = key_rows.reshape(number, key_rows.shape[1], HEADS, HEAD_DIM)
    value_heads = values.reshape(number, key_rows.shape[1], HEADS, HEAD_DIM)
    scores = low_back(jnp.einsum('bqhd,bkhd->bhqk', query_heads, key_heads, precision=HIGH))
    scores = jnp.where(allowed[:, None], scores, NEG)
    maximum = lax.optimization_barrier(jnp.max(scores, axis=-1, keepdims=True))
    raised = jnp.exp(scores - maximum)
    chances = low(raised / lax.optimization_barrier(jnp.sum(raised, axis=-1, keepdims=True)))
    blended = jnp.einsum('bhqk,bkhd->bqhd', chances, value_heads, precision=HIGH)
    return low_back(low(blended.reshape(number, length, breadth)))

def layer(layer_in, frames_in, self_mask, cross_mask, params):
    gain_one, bias_one, w_query, bias_query, w_key, w_value, bias_value, w_mixer, bias_mixer, gain_two, bias_two, x_query, bias_xquery, x_key, x_value, bias_xvalue, x_mixer, bias_xmixer, gain_three, bias_three, w_expand, bias_expand, w_reduce, bias_reduce = params
    factor = 1.0 / math.sqrt(HEAD_DIM)
    normed = low(norm_rows(layer_in, gain_one, bias_one))
    query = low_back(low((mult(normed, w_query) + bias_query) * factor))
    key_rows = low_back(low(mult(normed, w_key)))
    values = low_back(low(mult(normed, w_value) + bias_value))
    mixed = attend(query, key_rows, values, self_mask)
    after_self = layer_in + low_back(mult(mixed, w_mixer) + bias_mixer)
    normed_two = low(norm_rows(after_self, gain_two, bias_two))
    cross_q = low_back(low((mult(normed_two, x_query) + bias_xquery) * factor))
    cross_k = low(mult(frames_in, x_key))
    cross_v = low(mult(frames_in, x_value) + bias_xvalue)
    heard = attend(cross_q, cross_k, cross_v, cross_mask)
    after_cross = after_self + low_back(mult(heard, x_mixer) + bias_xmixer)
    normed_three = low(norm_rows(after_cross, gain_three, bias_three))
    hidden = low_back(mult(normed_three, w_expand) + bias_expand)
    gated = low(smooth_gate(hidden))
    return after_cross + low_back(mult(gated, w_reduce) + bias_reduce)

def reference(tokens, encoder_states, lengths, frame_counts, corpus_ids, corpus_weights, cotangent, first_gain, first_bias, query_weight, query_bias, key_weight, value_weight, value_bias, output_weight, output_bias, second_gain, second_bias, cross_query_weight, cross_query_bias, cross_key_weight, cross_value_weight, cross_value_bias, cross_output_weight, cross_output_bias, third_gain, third_bias, expand_weight, expand_bias, reduce_weight, reduce_bias):
    params = tuple((piece.astype(jnp.float32) for piece in (first_gain, first_bias, query_weight, query_bias, key_weight, value_weight, value_bias, output_weight, output_bias, second_gain, second_bias, cross_query_weight, cross_query_bias, cross_key_weight, cross_value_weight, cross_value_bias, cross_output_weight, cross_output_bias, third_gain, third_bias, expand_weight, expand_bias, reduce_weight, reduce_bias)))
    batch_size = math.gcd(TRANSCRIPTS, 8)
    batches = TRANSCRIPTS // batch_size
    corpus_index = jnp.arange(CORPORA, dtype=jnp.int32)
    row_weight = lax.optimization_barrier(jnp.sum(jnp.where(corpus_ids[:, None] == corpus_index[None, :], corpus_weights[None, :], 0.0), axis=1))
    positions = jnp.arange(SLOTS, dtype=jnp.int32)
    frame_pos = jnp.arange(FRAMES, dtype=jnp.int32)

    def batch_step(totals, step_index):
        first_row = (step_index * batch_size).astype(jnp.int32)
        layer_in = lax.dynamic_slice_in_dim(tokens, first_row, batch_size, 0).astype(jnp.float32)
        frames_in = lax.dynamic_slice_in_dim(encoder_states, first_row, batch_size, 0).astype(jnp.float32)
        lens_here = lax.dynamic_slice_in_dim(lengths, first_row, batch_size, 0)
        counts_here = lax.dynamic_slice_in_dim(frame_counts, first_row, batch_size, 0)
        weight_here = lax.dynamic_slice_in_dim(row_weight, first_row, batch_size, 0)
        grad_in = lax.dynamic_slice_in_dim(cotangent, first_row, batch_size, 0).astype(jnp.float32)
        self_mask = (positions[None, None, :] <= positions[None, :, None]) & (positions[None, None, :] < lens_here[:, None, None])
        cross_mask = frame_pos[None, None, :] < counts_here[:, None, None]

        def forward(inputs, weights):
            return layer(inputs, frames_in, self_mask, cross_mask, weights)
        result, pullback = jax.vjp(forward, layer_in, params)
        present = (positions[None, :] < lens_here[:, None]).astype(jnp.float32) * weight_here[:, None]
        grad_x, grad_w = pullback(grad_in * present[:, :, None])
        summed = tuple((old + new for old, new in zip(totals, grad_w)))
        return (summed, (result.astype(jnp.bfloat16), grad_x.astype(jnp.bfloat16)))
    zeros = tuple((jnp.zeros_like(piece) for piece in params))
    totals, (results, grads) = lax.scan(batch_step, zeros, jnp.arange(batches, dtype=jnp.int32))
    results = results.reshape(TRANSCRIPTS, SLOTS, D)
    grads = grads.reshape(TRANSCRIPTS, SLOTS, D)
    return (results, grads, totals[0], totals[1], totals[2], totals[3], totals[4], totals[5], totals[6], totals[7], totals[8], totals[9], totals[10], totals[11], totals[12], totals[13], totals[14], totals[15], totals[16], totals[17], totals[18], totals[19], totals[20], totals[21], totals[22], totals[23])
```

```python
import math

import jax
import jax.numpy as jnp
from jax import lax
from jax.experimental import pallas as pl
from jax.experimental.pallas import tpu as pltpu
from jax.sharding import PartitionSpec as P

HEADS = 12
HEAD_DIM = 64


NEG = -1e30
EPS = 1e-05


def norm_rows(values, scaling, offset):
    centre = values - jnp.mean(values, axis=-1, keepdims=True)
    spread = jnp.mean(centre * centre, axis=-1, keepdims=True)
    return centre * lax.rsqrt(spread + EPS) * scaling + offset


def smooth_gate(values):
    return 0.5 * values * (1.0 + lax.erf(values * 0.7071067811865476))


def linear(inputs, weight):
    return jnp.einsum("bri,ij->brj", inputs, weight, preferred_element_type=jnp.float32)


def linear_back(gradient, weight):
    return jnp.einsum("brj,ij->bri", gradient, weight, preferred_element_type=jnp.float32)


def outer_sum(inputs, gradient):
    return jnp.einsum("bri,brj->ij", inputs, gradient, preferred_element_type=jnp.float32)


def row_total(gradient):
    return jnp.sum(gradient.astype(jnp.float32), axis=(0, 1))


def split_heads(values):
    return values.reshape(values.shape[0], values.shape[1], HEADS, HEAD_DIM)


def scores_of(query, key_rows, allowed):
    scores = jnp.einsum(
        "bqhd,bkhd->bhqk",
        split_heads(query),
        split_heads(key_rows),
        preferred_element_type=jnp.float32,
    )
    return jnp.where(allowed[:, None], scores, NEG)


def attend(query, key_rows, values, allowed):
    scores = scores_of(query, key_rows, allowed)
    maximum = jnp.max(scores, axis=-1, keepdims=True)
    raised = jnp.exp(scores - maximum)
    summed = jnp.sum(raised, axis=-1, keepdims=True)
    chances = (raised / summed).astype(jnp.bfloat16)
    blended = jnp.einsum(
        "bhqk,bkhd->bqhd", chances, split_heads(values), preferred_element_type=jnp.float32
    )
    return (blended.reshape(query.shape).astype(jnp.bfloat16), maximum + jnp.log(summed))


def attend_back(grad_low, query, key_rows, values, allowed, logsum):
    scores = scores_of(query, key_rows, allowed)
    chances = jnp.exp(scores - logsum)
    grad_heads = split_heads(grad_low)
    grad_chance = jnp.einsum(
        "bqhd,bkhd->bhqk", grad_heads, split_heads(values), preferred_element_type=jnp.float32
    )
    offset = jnp.sum(chances * grad_chance, axis=-1, keepdims=True)
    grad_score = (chances * (grad_chance - offset)).astype(jnp.bfloat16)
    grad_query = jnp.einsum(
        "bhqk,bkhd->bqhd", grad_score, split_heads(key_rows), preferred_element_type=jnp.float32
    )
    grad_keys = jnp.einsum(
        "bhqk,bqhd->bkhd", grad_score, split_heads(query), preferred_element_type=jnp.float32
    )
    grad_values = jnp.einsum(
        "bhqk,bqhd->bkhd",
        chances.astype(jnp.bfloat16),
        grad_heads,
        preferred_element_type=jnp.float32,
    )
    return (
        grad_query.reshape(query.shape),
        grad_keys.reshape(key_rows.shape),
        grad_values.reshape(values.shape),
    )


def on_device_plain(
    tokens,
    encoder_states,
    lengths,
    frame_counts,
    corpus_ids,
    corpus_weights,
    cotangent,
    first_gain,
    first_bias,
    query_weight,
    query_bias,
    key_weight,
    value_weight,
    value_bias,
    output_weight,
    output_bias,
    second_gain,
    second_bias,
    cross_query_weight,
    cross_query_bias,
    cross_key_weight,
    cross_value_weight,
    cross_value_bias,
    cross_output_weight,
    cross_output_bias,
    third_gain,
    third_bias,
    expand_weight,
    expand_bias,
    reduce_weight,
    reduce_bias,
):
    row_parts = (
        lax.all_gather(query_weight, "grp", axis=0, tiled=True),
        lax.all_gather(key_weight, "grp", axis=0, tiled=True),
        lax.all_gather(value_weight, "grp", axis=0, tiled=True),
        lax.all_gather(output_weight, "grp", axis=0, tiled=True),
        lax.all_gather(cross_query_weight, "grp", axis=0, tiled=True),
        lax.all_gather(cross_key_weight, "grp", axis=0, tiled=True),
        lax.all_gather(cross_value_weight, "grp", axis=0, tiled=True),
        lax.all_gather(cross_output_weight, "grp", axis=0, tiled=True),
        lax.all_gather(expand_weight, "grp", axis=0, tiled=True),
        lax.all_gather(reduce_weight, "grp", axis=0, tiled=True),
        lax.all_gather(first_gain, "grp", axis=0, tiled=True),
        lax.all_gather(first_bias, "grp", axis=0, tiled=True),
        lax.all_gather(query_bias, "grp", axis=0, tiled=True),
        lax.all_gather(value_bias, "grp", axis=0, tiled=True),
        lax.all_gather(output_bias, "grp", axis=0, tiled=True),
        lax.all_gather(second_gain, "grp", axis=0, tiled=True),
        lax.all_gather(second_bias, "grp", axis=0, tiled=True),
        lax.all_gather(cross_query_bias, "grp", axis=0, tiled=True),
        lax.all_gather(cross_value_bias, "grp", axis=0, tiled=True),
        lax.all_gather(cross_output_bias, "grp", axis=0, tiled=True),
        lax.all_gather(third_gain, "grp", axis=0, tiled=True),
        lax.all_gather(third_bias, "grp", axis=0, tiled=True),
        lax.all_gather(expand_bias, "grp", axis=0, tiled=True),
        lax.all_gather(reduce_bias, "grp", axis=0, tiled=True),
    )
    gathered = (
        lax.all_gather(row_parts[0], "seq", axis=1, tiled=True),
        lax.all_gather(row_parts[1], "seq", axis=1, tiled=True),
        lax.all_gather(row_parts[2], "seq", axis=1, tiled=True),
        lax.all_gather(row_parts[3], "seq", axis=1, tiled=True),
        lax.all_gather(row_parts[4], "seq", axis=1, tiled=True),
        lax.all_gather(row_parts[5], "seq", axis=1, tiled=True),
        lax.all_gather(row_parts[6], "seq", axis=1, tiled=True),
        lax.all_gather(row_parts[7], "seq", axis=1, tiled=True),
        lax.all_gather(row_parts[8], "seq", axis=1, tiled=True),
        lax.all_gather(row_parts[9], "seq", axis=1, tiled=True),
    )
    w_query, w_key, w_value, w_mixer, x_query, x_key, x_value, x_mixer, w_expand, w_reduce = (
        gathered
    )
    vectors = [piece.astype(jnp.float32) for piece in row_parts[10:]]
    factor = 1.0 / math.sqrt(HEAD_DIM)
    seq_count = lax.axis_size("seq")
    span_rows = tokens.shape[1]
    query_pos = lax.axis_index("seq") * span_rows + jnp.arange(span_rows, dtype=jnp.int32)
    key_pos = jnp.arange(span_rows * seq_count, dtype=jnp.int32)
    self_mask = (key_pos[None, None, :] <= query_pos[None, :, None]) & (
        key_pos[None, None, :] < lengths[:, None, None]
    )
    frame_pos = jnp.arange(encoder_states.shape[1] * seq_count, dtype=jnp.int32)
    cross_mask = frame_pos[None, None, :] < frame_counts[:, None, None]
    layer_in = tokens.astype(jnp.float32)
    normed_one, norm_back_one = jax.vjp(norm_rows, layer_in, vectors[0], vectors[1])
    normed_one = normed_one.astype(jnp.bfloat16)
    query_low = ((linear(normed_one, w_query) + vectors[2]) * factor).astype(jnp.bfloat16)
    key_low = linear(normed_one, w_key).astype(jnp.bfloat16)
    value_low = (linear(normed_one, w_value) + vectors[3]).astype(jnp.bfloat16)
    key_all, value_all = (
        lax.all_gather(key_low, "seq", axis=1, tiled=True),
        lax.all_gather(value_low, "seq", axis=1, tiled=True),
    )
    self_out, self_logsum = attend(query_low, key_all, value_all, self_mask)
    after_self = layer_in + linear(self_out, w_mixer) + vectors[4]
    normed_two, norm_back_two = jax.vjp(norm_rows, after_self, vectors[5], vectors[6])
    normed_two = normed_two.astype(jnp.bfloat16)
    cross_query = ((linear(normed_two, x_query) + vectors[7]) * factor).astype(jnp.bfloat16)
    frames_all = lax.all_gather(encoder_states, "seq", axis=1, tiled=True)
    cross_keys_all = linear(frames_all, x_key).astype(jnp.bfloat16)
    cross_values_all = (linear(frames_all, x_value) + vectors[8]).astype(jnp.bfloat16)
    cross_out, cross_logsum = attend(cross_query, cross_keys_all, cross_values_all, cross_mask)
    after_cross = after_self + linear(cross_out, x_mixer) + vectors[9]
    normed_three, norm_back_three = jax.vjp(norm_rows, after_cross, vectors[10], vectors[11])
    normed_three = normed_three.astype(jnp.bfloat16)
    hidden = linear(normed_three, w_expand) + vectors[12]
    gated, gate_back = jax.vjp(smooth_gate, hidden)
    gated_low = gated.astype(jnp.bfloat16)
    result = after_cross + linear(gated_low, w_reduce) + vectors[13]
    layer_output = result.astype(jnp.bfloat16)
    present = (query_pos[None, :] < lengths[:, None]).astype(jnp.float32)
    corpus_index = jnp.arange(corpus_weights.shape[0], dtype=jnp.int32)
    corpus_scale = jnp.sum(
        jnp.where(corpus_ids[:, None] == corpus_index[None, :], corpus_weights[None, :], 0.0),
        axis=1,
    )
    grad_out = cotangent.astype(jnp.float32) * (present * corpus_scale[:, None])[:, :, None]
    reduce_low = grad_out.astype(jnp.bfloat16)
    slope_reduce_bias = row_total(reduce_low)
    slope_reduce = outer_sum(gated_low, reduce_low)
    grad_hidden = gate_back(linear_back(reduce_low, w_reduce))[0]
    hidden_low = grad_hidden.astype(jnp.bfloat16)
    slope_expand_bias = row_total(hidden_low)
    slope_expand = outer_sum(normed_three, hidden_low)
    grad_norm_in, slope_gain_three, slope_bias_three = norm_back_three(
        linear_back(hidden_low, w_expand)
    )
    grad_cross = grad_out + grad_norm_in
    cross_low = grad_cross.astype(jnp.bfloat16)
    slope_xmixer_bias = row_total(cross_low)
    slope_xmixer = outer_sum(cross_out, cross_low)
    grad_heard = linear_back(cross_low, x_mixer).astype(jnp.bfloat16)
    grad_cq, part_ck, part_cv = attend_back(
        grad_heard, cross_query, cross_keys_all, cross_values_all, cross_mask, cross_logsum
    )
    slope_xkey = outer_sum(frames_all, part_ck)
    slope_xvalue = outer_sum(frames_all, part_cv)
    slope_xvalue_bias = row_total(part_cv)
    low_cq = (grad_cq * factor).astype(jnp.bfloat16)
    slope_xquery_bias = row_total(low_cq)
    slope_xquery = outer_sum(normed_two, low_cq)
    grad_norm_two, slope_gain_two, slope_bias_two = norm_back_two(linear_back(low_cq, x_query))
    grad_self = grad_cross + grad_norm_two
    self_low = grad_self.astype(jnp.bfloat16)
    slope_mixer_bias = row_total(self_low)
    slope_mixer = outer_sum(self_out, self_low)
    grad_mixed = linear_back(self_low, w_mixer).astype(jnp.bfloat16)
    grad_q, part_k, part_v = attend_back(
        grad_mixed, query_low, key_all, value_all, self_mask, self_logsum
    )
    summed_k, summed_v = (
        lax.psum_scatter(
            part_k.astype(jnp.bfloat16), "seq", scatter_dimension=1, tiled=True
        ).astype(jnp.float32),
        lax.psum_scatter(
            part_v.astype(jnp.bfloat16), "seq", scatter_dimension=1, tiled=True
        ).astype(jnp.float32),
    )
    low_k = summed_k.astype(jnp.bfloat16)
    low_v = summed_v.astype(jnp.bfloat16)
    low_q = (grad_q * factor).astype(jnp.bfloat16)
    slope_query = outer_sum(normed_one, low_q)
    slope_query_bias = row_total(low_q)
    slope_key = outer_sum(normed_one, low_k)
    slope_value = outer_sum(normed_one, low_v)
    slope_value_bias = row_total(low_v)
    grad_normed = (
        linear_back(low_q, w_query) + linear_back(low_k, w_key) + linear_back(low_v, w_value)
    )
    grad_norm_one, slope_gain_one, slope_bias_one = norm_back_one(grad_normed)
    tokens_gradient = (grad_self + grad_norm_one).astype(jnp.bfloat16)
    owned = (
        lax.psum_scatter(slope_query, "grp", scatter_dimension=0, tiled=True),
        lax.psum_scatter(slope_key, "grp", scatter_dimension=0, tiled=True),
        lax.psum_scatter(slope_value, "grp", scatter_dimension=0, tiled=True),
        lax.psum_scatter(slope_mixer, "grp", scatter_dimension=0, tiled=True),
        lax.psum_scatter(slope_xquery, "grp", scatter_dimension=0, tiled=True),
        lax.psum_scatter(slope_xkey, "grp", scatter_dimension=0, tiled=True),
        lax.psum_scatter(slope_xvalue, "grp", scatter_dimension=0, tiled=True),
        lax.psum_scatter(slope_xmixer, "grp", scatter_dimension=0, tiled=True),
        lax.psum_scatter(slope_expand, "grp", scatter_dimension=0, tiled=True),
        lax.psum_scatter(slope_reduce, "grp", scatter_dimension=0, tiled=True),
        lax.psum_scatter(slope_gain_one, "grp", scatter_dimension=0, tiled=True),
        lax.psum_scatter(slope_bias_one, "grp", scatter_dimension=0, tiled=True),
        lax.psum_scatter(slope_query_bias, "grp", scatter_dimension=0, tiled=True),
        lax.psum_scatter(slope_value_bias, "grp", scatter_dimension=0, tiled=True),
        lax.psum_scatter(slope_mixer_bias, "grp", scatter_dimension=0, tiled=True),
        lax.psum_scatter(slope_gain_two, "grp", scatter_dimension=0, tiled=True),
        lax.psum_scatter(slope_bias_two, "grp", scatter_dimension=0, tiled=True),
        lax.psum_scatter(slope_xquery_bias, "grp", scatter_dimension=0, tiled=True),
        lax.psum_scatter(slope_xvalue_bias, "grp", scatter_dimension=0, tiled=True),
        lax.psum_scatter(slope_xmixer_bias, "grp", scatter_dimension=0, tiled=True),
        lax.psum_scatter(slope_gain_three, "grp", scatter_dimension=0, tiled=True),
        lax.psum_scatter(slope_bias_three, "grp", scatter_dimension=0, tiled=True),
        lax.psum_scatter(slope_expand_bias, "grp", scatter_dimension=0, tiled=True),
        lax.psum_scatter(slope_reduce_bias, "grp", scatter_dimension=0, tiled=True),
    )
    matrices = (
        lax.psum_scatter(
            owned[0].astype(jnp.bfloat16), "seq", scatter_dimension=1, tiled=True
        ).astype(jnp.float32),
        lax.psum_scatter(
            owned[1].astype(jnp.bfloat16), "seq", scatter_dimension=1, tiled=True
        ).astype(jnp.float32),
        lax.psum_scatter(
            owned[2].astype(jnp.bfloat16), "seq", scatter_dimension=1, tiled=True
        ).astype(jnp.float32),
        lax.psum_scatter(
            owned[3].astype(jnp.bfloat16), "seq", scatter_dimension=1, tiled=True
        ).astype(jnp.float32),
        lax.psum_scatter(
            owned[4].astype(jnp.bfloat16), "seq", scatter_dimension=1, tiled=True
        ).astype(jnp.float32),
        lax.psum_scatter(
            owned[5].astype(jnp.bfloat16), "seq", scatter_dimension=1, tiled=True
        ).astype(jnp.float32),
        lax.psum_scatter(
            owned[6].astype(jnp.bfloat16), "seq", scatter_dimension=1, tiled=True
        ).astype(jnp.float32),
        lax.psum_scatter(
            owned[7].astype(jnp.bfloat16), "seq", scatter_dimension=1, tiled=True
        ).astype(jnp.float32),
        lax.psum_scatter(
            owned[8].astype(jnp.bfloat16), "seq", scatter_dimension=1, tiled=True
        ).astype(jnp.float32),
        lax.psum_scatter(
            owned[9].astype(jnp.bfloat16), "seq", scatter_dimension=1, tiled=True
        ).astype(jnp.float32),
    )
    smaller = lax.psum(
        (
            owned[10],
            owned[11],
            owned[12],
            owned[13],
            owned[14],
            owned[15],
            owned[16],
            owned[17],
            owned[18],
            owned[19],
            owned[20],
            owned[21],
            owned[22],
            owned[23],
        ),
        "seq",
    )
    return (
        layer_output,
        tokens_gradient,
        smaller[0],
        smaller[1],
        matrices[0],
        smaller[2],
        matrices[1],
        matrices[2],
        smaller[3],
        matrices[3],
        smaller[4],
        smaller[5],
        smaller[6],
        matrices[4],
        smaller[7],
        matrices[5],
        matrices[6],
        smaller[8],
        matrices[7],
        smaller[9],
        smaller[10],
        smaller[11],
        matrices[8],
        smaller[12],
        matrices[9],
        smaller[13],
    )


MESH_ID = pl.DeviceIdType.MESH
NZ, NX, NY, NC = 4, 2, 2, 2
GROUPS = 8


def where_am_i():
    grp = lax.axis_index("grp")
    seq = lax.axis_index("seq")
    return grp // NX, lax.rem(grp, NX), seq // NC, lax.rem(seq, NC)


def device_at(z, x, y, c):
    return (z * NX + x, y * NC + c)


def lanes(start, size):
    return pl.ds(pl.multiple_of(start, 128), size)


def pieces_of(bank, group, y, c, x, z_from, z_to):
    pairs, wide, tall = bank
    if group < 4:
        return [pairs.at[group, y, pl.ds(z_from, z_to - z_from), x, :, lanes(c * 384, 384)]]
    if group < 6:
        start = (y * NC + c) * 768 + (group - 4) * 384
        return [wide.at[pl.ds(z_from, z_to - z_from), x, :, lanes(start, 384)]]
    return [
        tall.at[y, c, pl.ds((group - 6) * 96, 96), lanes((z * NX + x) * 384, 384)]
        for z in range(z_from, z_to)
    ]


def piece_at(bank, group, y, c, x, z):
    pairs, wide, tall = bank
    if group < 4:
        return pairs.at[group, y, z, x, :, lanes(c * 384, 384)]
    if group < 6:
        return wide.at[z, x, :, lanes((y * NC + c) * 768 + (group - 4) * 384, 384)]
    return tall.at[y, c, pl.ds((group - 6) * 96, 96), lanes((z * NX + x) * 384, 384)]


def own_piece(bank, group):
    pairs, wide, tall = bank
    if group < 4:
        return pairs.at[group]
    if group < 6:
        return wide.at[:, pl.ds((group - 4) * 384, 384)]
    return tall.at[pl.ds((group - 6) * 96, 96), :]


class Mail:
    def __init__(self, send_sems, recv_sems):
        self.send_sems, self.recv_sems, self.count, self.sent = send_sems, recv_sems, 0, []

    def slots(self, number):
        first = self.count
        self.count += number
        return list(range(first, first + number))

    def post(self, source, target, slot, device):
        copy = pltpu.make_async_remote_copy(
            src_ref=source,
            dst_ref=target,
            send_sem=self.send_sems.at[slot],
            recv_sem=self.recv_sems.at[slot],
            device_id=device,
            device_id_type=MESH_ID,
        )
        copy.start()
        self.sent.append(copy)

    def arrive(self, target, slot, device):
        pltpu.make_async_remote_copy(
            src_ref=target,
            dst_ref=target,
            send_sem=self.send_sems.at[slot],
            recv_sem=self.recv_sems.at[slot],
            device_id=device,
            device_id_type=MESH_ID,
        ).wait_recv()

    def finish(self):
        for copy in self.sent:
            copy.wait_send()


def greet(z, x, y, c):
    barrier = pltpu.get_barrier_semaphore()
    friends = [device_at(lax.rem(z + k, NZ), x, y, c) for k in range(1, NZ)]
    friends += [device_at(lax.rem(z + k, NZ), 1 - x, y, c) for k in range(NZ)]
    friends += [device_at(z, x, 1 - y, c), device_at(z, x, y, 1 - c)]
    for friend in friends:
        pl.semaphore_signal(barrier, inc=1, device_id=friend, device_id_type=MESH_ID)
    pl.semaphore_wait(barrier, len(friends))


def parts_in(group, number):
    return number if group >= 6 else 1


def gather_kernel(
    pairs_in, wide_in, tall_in, small_in, frames_in, tokens_in,
    pairs, wide, tall, small, frames, tokens,
    send_sems, recv_sems, local_sems,
):
    z, x, y, c = where_am_i()
    greet(z, x, y, c)
    mail = Mail(send_sems, recv_sems)
    own = (pairs_in, wide_in, tall_in)
    bank = (pairs, wide, tall)
    x_mate, y_mate = device_at(z, 1 - x, y, c), device_at(z, x, 1 - y, c)
    c_mate = device_at(z, x, y, 1 - c)
    z_mates = [device_at(lax.rem(z + k, NZ), x, y, c) for k in range(1, NZ)]
    grp = z * NX + x
    seq = y * NC + c

    local = []

    def keep(source, target):
        copy = pltpu.make_async_copy(source, target, local_sems.at[len(local)])
        copy.start()
        local.append(copy)

    small_slots = mail.slots(2 * NZ - 1)
    small_to = z_mates + [device_at(lax.rem(z + k, NZ), 1 - x, y, c) for k in range(NZ)]
    for slot, device in zip(small_slots, small_to):
        mail.post(small_in, small.at[grp], slot, device)
    keep(small_in, small.at[grp])
    for group in range(GROUPS):
        keep(own_piece(own, group), piece_at(bank, group, y, c, x, z))
    keep(frames_in, frames.at[seq])
    keep(tokens_in, tokens.at[seq])

    z_slots = [mail.slots(NZ - 1) for _ in range(GROUPS)]

    def to_column(group):
        for k in range(1, NZ):
            mail.post(
                own_piece(own, group), piece_at(bank, group, y, c, x, z), z_slots[group][k - 1], z_mates[k - 1]
            )

    def post_all(group, slots, device, yy, cc, xx, z_from, z_to):
        for slot, ref in zip(slots, pieces_of(bank, group, yy, cc, xx, z_from, z_to)):
            mail.post(ref, ref, slot, device)

    def arrive_all(group, slots, device, yy, cc, xx, z_from, z_to):
        for slot, ref in zip(slots, pieces_of(bank, group, yy, cc, xx, z_from, z_to)):
            mail.arrive(ref, slot, device)

    x_slots = [mail.slots(parts_in(g, 4)) for g in range(GROUPS)]
    y_slots = [mail.slots(parts_in(g, 4)) for g in range(GROUPS)]
    dy_slots = [mail.slots(parts_in(g, 2)) for g in range(GROUPS)]
    dx_slots = [mail.slots(parts_in(g, 2)) for g in range(GROUPS)]
    co_slots = [mail.slots(parts_in(g, 4)) for g in range(GROUPS)]
    cx_slots = [mail.slots(parts_in(g, 4)) for g in range(GROUPS)]
    cy_slots = [mail.slots(parts_in(g, 4)) for g in range(GROUPS)]
    cd_slots = [mail.slots(2 * parts_in(g, 2)) for g in range(GROUPS)]
    token_slots = mail.slots(3)
    frame_slots = mail.slots(3)

    def spread(group):
        for k in range(1, NZ):
            zz = lax.rem(z + NZ - k, NZ)
            mail.arrive(piece_at(bank, group, y, c, x, zz), z_slots[group][k - 1], z_mates[k - 1])
        local[1 + group].wait()
        post_all(group, x_slots[group], x_mate, y, c, x, 0, 4)
        post_all(group, y_slots[group], y_mate, y, c, x, 0, 4)
        post_all(group, co_slots[group], c_mate, y, c, x, 0, 4)

    def turn(group):
        arrive_all(group, x_slots[group], x_mate, y, c, 1 - x, 0, 4)
        post_all(group, dy_slots[group], y_mate, y, c, 1 - x, 0, 2)
        post_all(group, cx_slots[group], c_mate, y, c, 1 - x, 0, 4)
        arrive_all(group, y_slots[group], y_mate, 1 - y, c, x, 0, 4)
        post_all(group, dx_slots[group], x_mate, 1 - y, c, x, 2, 4)
        post_all(group, cy_slots[group], c_mate, 1 - y, c, x, 0, 4)

    def share(group):
        half = parts_in(group, 2)
        arrive_all(group, dy_slots[group], y_mate, 1 - y, c, 1 - x, 0, 2)
        post_all(group, cd_slots[group][:half], c_mate, 1 - y, c, 1 - x, 0, 2)
        arrive_all(group, dx_slots[group], x_mate, 1 - y, c, 1 - x, 2, 4)
        post_all(group, cd_slots[group][half:], c_mate, 1 - y, c, 1 - x, 2, 4)

    def complete(group):
        half = parts_in(group, 2)
        arrive_all(group, co_slots[group], c_mate, y, 1 - c, x, 0, 4)
        arrive_all(group, cx_slots[group], c_mate, y, 1 - c, 1 - x, 0, 4)
        arrive_all(group, cy_slots[group], c_mate, 1 - y, 1 - c, x, 0, 4)
        arrive_all(group, cd_slots[group][:half], c_mate, 1 - y, 1 - c, 1 - x, 0, 2)
        arrive_all(group, cd_slots[group][half:], c_mate, 1 - y, 1 - c, 1 - x, 2, 4)

    def swap_rows(source, bank_rows, slots, first):
        if first:
            mail.post(source, bank_rows.at[seq], slots[0], y_mate)
            mail.post(source, bank_rows.at[seq], slots[1], c_mate)
        else:
            other = (1 - y) * NC + c
            mail.arrive(bank_rows.at[other], slots[0], y_mate)
            mail.post(bank_rows.at[other], bank_rows.at[other], slots[2], c_mate)

    def rows_done(bank_rows, slots):
        mail.arrive(bank_rows.at[y * NC + 1 - c], slots[1], c_mate)
        mail.arrive(bank_rows.at[(1 - y) * NC + 1 - c], slots[2], c_mate)

    to_column(0)
    to_column(1)
    swap_rows(tokens_in, tokens, token_slots, True)
    swap_rows(frames_in, frames, frame_slots, True)
    for step in range(GROUPS + 3):
        if step + 2 < GROUPS:
            to_column(step + 2)
        if step < GROUPS:
            spread(step)
        if 0 <= step - 1 < GROUPS:
            turn(step - 1)
        if 0 <= step - 2 < GROUPS:
            share(step - 2)
        if 0 <= step - 3 < GROUPS:
            complete(step - 3)
        if step == 1:
            swap_rows(tokens_in, tokens, token_slots, False)
        if step == 3:
            swap_rows(frames_in, frames, frame_slots, False)
    rows_done(tokens, token_slots)
    rows_done(frames, frame_slots)
    for k in range(1, NZ):
        zz = lax.rem(z + NZ - k, NZ)
        mail.arrive(small.at[zz * NX + x], small_slots[k - 1], z_mates[k - 1])
    for k in range(NZ):
        zz = lax.rem(z + NZ - k, NZ)
        mail.arrive(small.at[zz * NX + 1 - x], small_slots[NZ - 1 + k], x_mate)
    for number, copy in enumerate(local):
        if not 1 <= number <= GROUPS:
            copy.wait()
    mail.finish()


def slots_needed():
    return (2 * NZ - 1) + 6 + sum(3 + parts_in(g, 4) * 5 + parts_in(g, 2) * 4 for g in range(GROUPS))


def gather_everything(pairs, wide, tall, small, frames, tokens):
    bf16 = jnp.bfloat16
    number = slots_needed()
    anywhere = pl.BlockSpec(memory_space=pl.ANY)
    return pl.pallas_call(
        gather_kernel,
        out_shape=(
            jax.ShapeDtypeStruct((4, NY, NZ, NX, 96, 768), bf16),
            jax.ShapeDtypeStruct((NZ, NX, 96, 3072), bf16),
            jax.ShapeDtypeStruct((NY, NC, 192, 3072), bf16),
            jax.ShapeDtypeStruct((NZ * NX,) + small.shape, bf16),
            jax.ShapeDtypeStruct((NY * NC,) + frames.shape, bf16),
            jax.ShapeDtypeStruct((NY * NC,) + tokens.shape, bf16),
        ),
        in_specs=[anywhere] * 6,
        out_specs=(anywhere,) * 6,
        scratch_shapes=[
            pltpu.SemaphoreType.DMA((number,)),
            pltpu.SemaphoreType.DMA((number,)),
            pltpu.SemaphoreType.DMA((GROUPS + 3,)),
        ],
        compiler_params=pltpu.CompilerParams(collective_id=1, has_side_effects=True),
        name="gather_all",
    )(pairs, wide, tall, small, frames, tokens)


def reduce_kernel(
    pairs, wide, tall, small,
    total, small_total,
    own_acc, core_in, diag_in, x_in, y_in, z_in, small_in, small_sum, small_seq,
    send_sems, recv_sems, local_sems,
):
    z, x, y, c = where_am_i()
    greet(z, x, y, c)
    mail = Mail(send_sems, recv_sems)
    bank = (pairs, wide, tall)
    x_mate, y_mate = device_at(z, 1 - x, y, c), device_at(z, x, 1 - y, c)
    c_mate = device_at(z, x, y, 1 - c)
    z_mates = [device_at(lax.rem(z + k, NZ), x, y, c) for k in range(1, NZ)]
    grp = z * NX + x
    seq = y * NC + c

    small_slots = mail.slots(2 * NZ - 1)
    small_to = [(lax.rem(z + k, NZ), x) for k in range(1, NZ)]
    small_to += [(lax.rem(z + k, NZ), 1 - x) for k in range(NZ)]
    for number, (zz, xx) in enumerate(small_to):
        mail.post(small.at[zz * NX + xx], small_in.at[number], small_slots[number], device_at(zz, xx, y, c))

    core_slots = [mail.slots(4 * parts_in(g, 4)) for g in range(GROUPS)]
    local = []
    count = 0
    columns = [(0, 0), (1, 0), (0, 1), (1, 1)]

    def column(dx, dy):
        return jnp.where(dx, 1 - x, x), jnp.where(dy, 1 - y, y)

    for group in range(GROUPS):
        mine = []
        for place, (dx, dy) in enumerate(columns):
            xx, yy = (1 - x if dx else x), (1 - y if dy else y)
            targets = [core_in.at[group, place]] if group < 6 else [core_in.at[group, place, k] for k in range(4)]
            sources = pieces_of(bank, group, yy, 1 - c, xx, 0, 4)
            many = len(sources)
            for k in range(many):
                mail.post(sources[k], targets[k], core_slots[group][place * many + k], c_mate)
            sources = pieces_of(bank, group, yy, c, xx, 0, 4)
            targets = [own_acc.at[group, place]] if group < 6 else [own_acc.at[group, place, k] for k in range(4)]
            for k in range(many):
                copy = pltpu.make_async_copy(sources[k], targets[k], local_sems.at[count])
                copy.start()
                mine.append(copy)
                count += 1
        local.append(mine)

    dx_slots = [mail.slots(1) for _ in range(GROUPS)]
    dy_slots = [mail.slots(1) for _ in range(GROUPS)]
    x_slots = [mail.slots(1) for _ in range(GROUPS)]
    y_slots = [mail.slots(1) for _ in range(GROUPS)]
    z_slots = [mail.slots(NZ - 1) for _ in range(GROUPS)]

    def core_step(group):
        for copy in local[group]:
            copy.wait()
        many = 4 if group >= 6 else 1
        for place in (3, 1, 2, 0):
            for k in range(many):
                target = core_in.at[group, place] if many == 1 else core_in.at[group, place, k]
                mail.arrive(target, core_slots[group][place * many + k], c_mate)

            def add(k, carry):
                own_acc[group, place, k] = own_acc[group, place, k] + core_in[group, place, k]
                return carry

            lax.fori_loop(0, 4, add, 0)
            if place == 3:
                mail.post(own_acc.at[group, 3, pl.ds(0, 2)], diag_in.at[group, 0], dx_slots[group][0], x_mate)
                mail.post(own_acc.at[group, 3, pl.ds(2, 2)], diag_in.at[group, 1], dy_slots[group][0], y_mate)

    def side_step(group):
        mail.arrive(diag_in.at[group, 0], dx_slots[group][0], x_mate)

        def add_y(k, carry):
            own_acc[group, 2, k] = own_acc[group, 2, k] + diag_in[group, 0, k]
            return carry

        lax.fori_loop(0, 2, add_y, 0)
        mail.post(own_acc.at[group, 2], y_in.at[group], y_slots[group][0], y_mate)
        mail.arrive(diag_in.at[group, 1], dy_slots[group][0], y_mate)

        def add_x(k, carry):
            own_acc[group, 1, k + 2] = own_acc[group, 1, k + 2] + diag_in[group, 1, k]
            return carry

        lax.fori_loop(0, 2, add_x, 0)
        mail.post(own_acc.at[group, 1], x_in.at[group], x_slots[group][0], x_mate)

    def column_step(group):
        mail.arrive(y_in.at[group], y_slots[group][0], y_mate)
        mail.arrive(x_in.at[group], x_slots[group][0], x_mate)

        def add(k, carry):
            own_acc[group, 0, k] = (
                own_acc[group, 0, k].astype(jnp.float32)
                + x_in[group, k].astype(jnp.float32)
                + y_in[group, k].astype(jnp.float32)
            ).astype(jnp.bfloat16)
            return carry

        lax.fori_loop(0, 4, add, 0)
        for k in range(1, NZ):
            zz = lax.rem(z + k, NZ)
            mail.post(own_acc.at[group, 0, zz], z_in.at[group, k - 1], z_slots[group][k - 1], z_mates[k - 1])

    def last_step(group):
        for k in range(1, NZ):
            mail.arrive(z_in.at[group, k - 1], z_slots[group][k - 1], z_mates[k - 1])
        total[group] = own_acc[group, 0, z].astype(jnp.float32) + (
            z_in[group, 0].astype(jnp.float32) + z_in[group, 1].astype(jnp.float32)
        ) + z_in[group, 2].astype(jnp.float32)

    seq_slots = mail.slots(3)
    for step in range(GROUPS + 3):
        if step < GROUPS:
            core_step(step)
        if 0 <= step - 1 < GROUPS:
            side_step(step - 1)
        if 0 <= step - 2 < GROUPS:
            column_step(step - 2)
        if 0 <= step - 3 < GROUPS:
            last_step(step - 3)
        if step == 3:
            for number in range(2 * NZ - 1):
                mail.arrive(small_in.at[number], small_slots[number], x_mate)
            small_sum[...] = (
                (small[grp] + small_in[0]) + (small_in[1] + small_in[2])
                + ((small_in[3] + small_in[4]) + (small_in[5] + small_in[6]))
            )
            mail.post(small_sum, small_seq.at[0], seq_slots[0], c_mate)
        if step == 5:
            mail.arrive(small_seq.at[0], seq_slots[0], c_mate)
            small_seq[1] = small_sum[...] + small_seq[0]
            mail.post(small_seq.at[1], small_seq.at[2], seq_slots[1], y_mate)
        if step == 7:
            mail.arrive(small_seq.at[2], seq_slots[1], y_mate)
            small_total[...] = small_seq[1] + small_seq[2]
    mail.finish()


def reduce_everything(pairs, wide, tall, small):
    bf16 = jnp.bfloat16
    piece = (96, 384)
    number = 7 + 3 + sum(4 * parts_in(g, 4) + 4 + 3 for g in range(GROUPS))
    anywhere = pl.BlockSpec(memory_space=pl.ANY)
    inside = pl.BlockSpec(memory_space=pltpu.VMEM)
    small_piece = small.shape[1:]
    return pl.pallas_call(
        reduce_kernel,
        out_shape=(
            jax.ShapeDtypeStruct((GROUPS,) + piece, jnp.float32),
            jax.ShapeDtypeStruct(small_piece, jnp.float32),
        ),
        in_specs=[anywhere] * 3 + [inside],
        out_specs=(inside, inside),
        scratch_shapes=[
            pltpu.VMEM((GROUPS, 4, NZ) + piece, bf16),
            pltpu.VMEM((GROUPS, 4, NZ) + piece, bf16),
            pltpu.VMEM((GROUPS, 2, 2) + piece, bf16),
            pltpu.VMEM((GROUPS, NZ) + piece, bf16),
            pltpu.VMEM((GROUPS, NZ) + piece, bf16),
            pltpu.VMEM((GROUPS, NZ - 1) + piece, bf16),
            pltpu.VMEM((7,) + small_piece, jnp.float32),
            pltpu.VMEM(small_piece, jnp.float32),
            pltpu.VMEM((3,) + small_piece, jnp.float32),
            pltpu.SemaphoreType.DMA((number,)),
            pltpu.SemaphoreType.DMA((number,)),
            pltpu.SemaphoreType.DMA((4 * sum(parts_in(g, 4) for g in range(GROUPS)),)),
        ],
        compiler_params=pltpu.CompilerParams(
            collective_id=2, has_side_effects=True, vmem_limit_bytes=58 << 20
        ),
        name="reduce_all",
    )(pairs, wide, tall, small)


def joined(first, second):
    return jnp.concatenate([first, second], axis=1)


def on_device_fast(*arguments):
    (
        tokens, encoder_states, lengths, frame_counts, corpus_ids, corpus_weights, cotangent,
        first_gain, first_bias, query_weight, query_bias, key_weight, value_weight, value_bias,
        output_weight, output_bias, second_gain, second_bias, cross_query_weight, cross_query_bias,
        cross_key_weight, cross_value_weight, cross_value_bias, cross_output_weight, cross_output_bias,
        third_gain, third_bias, expand_weight, expand_bias, reduce_weight, reduce_bias,
    ) = arguments
    bf16, f32 = jnp.bfloat16, jnp.float32
    frame_span = encoder_states.shape[1]
    small_vectors = (
        first_gain, first_bias, query_bias, value_bias, output_bias, second_gain, second_bias,
        cross_query_bias, cross_value_bias, cross_output_bias, third_gain, third_bias, expand_bias, reduce_bias,
    )
    sizes = [v.shape[0] for v in small_vectors]
    small = jnp.pad(jnp.concatenate(small_vectors), (0, 2048 - sum(sizes))).reshape(16, 128)
    pairs = jnp.stack([
        joined(query_weight, key_weight),
        joined(value_weight, cross_query_weight),
        joined(cross_key_weight, cross_value_weight),
        joined(output_weight, cross_output_weight),
    ])
    frames_padded = jnp.pad(encoder_states, ((0, 0), (0, 384 - frame_span), (0, 0)))
    pairs_all, wide_all, tall_all, small_all, frames_got, tokens_got = gather_everything(
        pairs, expand_weight, reduce_weight.T, small, frames_padded, tokens
    )
    pairs_all = pairs_all.reshape(4, NY, 768, NC, 2, 192)
    plain = [
        pairs_all[p, :, :, :, h].transpose(1, 0, 2, 3).reshape(768, 768) for p in range(4) for h in range(2)
    ]
    w_query, w_key, w_value, x_query, x_key, x_value, w_mixer, x_mixer = plain
    w_expand = wide_all.reshape(768, 3072)
    w_reduce = tall_all.reshape(768, 3072)
    flat = small_all.reshape(8, 2048)
    vectors, at = [], 0
    for size in sizes:
        vectors.append(flat[:, at:at + size].reshape(-1).astype(f32))
        at += size
    factor = 1.0 / math.sqrt(HEAD_DIM)
    seq_count = lax.axis_size("seq")
    span_rows = tokens.shape[1]
    query_pos = lax.axis_index("seq") * span_rows + jnp.arange(span_rows, dtype=jnp.int32)
    key_pos = jnp.arange(span_rows * seq_count, dtype=jnp.int32)
    self_mask = (key_pos[None, None, :] <= query_pos[None, :, None]) & (
        key_pos[None, None, :] < lengths[:, None, None]
    )
    frame_pos = jnp.arange(384 * seq_count, dtype=jnp.int32)
    inside, block = frame_pos % 384, frame_pos // 384
    cross_mask = (inside < frame_span)[None, None, :] & (
        (block * frame_span + inside)[None, None, :] < frame_counts[:, None, None]
    )
    frames_all = frames_got.transpose(1, 0, 2, 3).reshape(2, 1536, 768)
    tokens_all = tokens_got.transpose(1, 0, 2, 3).reshape(2, span_rows * seq_count, 768).astype(f32)
    layer_in = tokens.astype(f32)
    normed_all = norm_rows(tokens_all, vectors[0], vectors[1]).astype(bf16)
    normed_one, norm_back_one = jax.vjp(norm_rows, layer_in, vectors[0], vectors[1])
    normed_one = normed_one.astype(bf16)
    query_low = ((linear(normed_one, w_query) + vectors[2]) * factor).astype(bf16)
    key_all = linear(normed_all, w_key).astype(bf16)
    value_all = (linear(normed_all, w_value) + vectors[3]).astype(bf16)
    self_out, self_logsum = attend(query_low, key_all, value_all, self_mask)
    after_self = layer_in + linear(self_out, w_mixer) + vectors[4]
    normed_two, norm_back_two = jax.vjp(norm_rows, after_self, vectors[5], vectors[6])
    normed_two = normed_two.astype(bf16)
    cross_query = ((linear(normed_two, x_query) + vectors[7]) * factor).astype(bf16)
    cross_keys_all = linear(frames_all, x_key).astype(bf16)
    cross_values_all = (linear(frames_all, x_value) + vectors[8]).astype(bf16)
    cross_out, cross_logsum = attend(cross_query, cross_keys_all, cross_values_all, cross_mask)
    after_cross = after_self + linear(cross_out, x_mixer) + vectors[9]
    normed_three, norm_back_three = jax.vjp(norm_rows, after_cross, vectors[10], vectors[11])
    normed_three = normed_three.astype(bf16)
    hidden = linear(normed_three, w_expand) + vectors[12]
    gated, gate_back = jax.vjp(smooth_gate, hidden)
    gated_low = gated.astype(bf16)
    result = after_cross + linear_back(gated_low, w_reduce) + vectors[13]
    layer_output = result.astype(bf16)
    present = (query_pos[None, :] < lengths[:, None]).astype(f32)
    corpus_index = jnp.arange(corpus_weights.shape[0], dtype=jnp.int32)
    corpus_scale = jnp.sum(
        jnp.where(corpus_ids[:, None] == corpus_index[None, :], corpus_weights[None, :], 0.0), axis=1
    )
    grad_out = cotangent.astype(f32) * (present * corpus_scale[:, None])[:, :, None]
    reduce_low = grad_out.astype(bf16)
    slope_reduce_bias = row_total(reduce_low)
    slope_reduce = outer_sum(reduce_low, gated_low)
    grad_hidden = gate_back(linear(reduce_low, w_reduce))[0]
    hidden_low = grad_hidden.astype(bf16)
    slope_expand_bias = row_total(hidden_low)
    slope_expand = outer_sum(normed_three, hidden_low)
    grad_norm_in, slope_gain_three, slope_bias_three = norm_back_three(linear_back(hidden_low, w_expand))
    grad_cross = grad_out + grad_norm_in
    cross_low = grad_cross.astype(bf16)
    slope_xmixer_bias = row_total(cross_low)
    slope_xmixer = outer_sum(cross_out, cross_low)
    grad_heard = linear_back(cross_low, x_mixer).astype(bf16)
    grad_cq, part_ck, part_cv = attend_back(
        grad_heard, cross_query, cross_keys_all, cross_values_all, cross_mask, cross_logsum
    )
    slope_xkey = outer_sum(frames_all, part_ck.astype(bf16))
    slope_xvalue = outer_sum(frames_all, part_cv.astype(bf16))
    slope_xvalue_bias = row_total(part_cv)
    low_cq = (grad_cq * factor).astype(bf16)
    slope_xquery_bias = row_total(low_cq)
    slope_xquery = outer_sum(normed_two, low_cq)
    grad_norm_two, slope_gain_two, slope_bias_two = norm_back_two(linear_back(low_cq, x_query))
    grad_self = grad_cross + grad_norm_two
    self_low = grad_self.astype(bf16)
    slope_mixer_bias = row_total(self_low)
    slope_mixer = outer_sum(self_out, self_low)
    grad_mixed = linear_back(self_low, w_mixer).astype(bf16)
    grad_q, part_k, part_v = attend_back(grad_mixed, query_low, key_all, value_all, self_mask, self_logsum)
    low_k, low_v = (
        lax.psum_scatter(part_k.astype(bf16), "seq", scatter_dimension=1, tiled=True),
        lax.psum_scatter(part_v.astype(bf16), "seq", scatter_dimension=1, tiled=True),
    )
    low_q = (grad_q * factor).astype(bf16)
    slope_query = outer_sum(normed_one, low_q)
    slope_query_bias = row_total(low_q)
    slope_key = outer_sum(normed_one, low_k)
    slope_value = outer_sum(normed_one, low_v)
    slope_value_bias = row_total(low_v)
    grad_normed = linear_back(low_q, w_query) + linear_back(low_k, w_key) + linear_back(low_v, w_value)
    grad_norm_one, slope_gain_one, slope_bias_one = norm_back_one(grad_normed)
    tokens_gradient = (grad_self + grad_norm_one).astype(bf16)

    slopes = [
        slope_query, slope_key, slope_value, slope_xquery, slope_xkey, slope_xvalue, slope_mixer, slope_xmixer
    ]
    slopes = [s.astype(bf16).reshape(768, NY, NC, 192) for s in slopes]
    pair_grads = jnp.stack([
        jnp.stack([slopes[2 * p], slopes[2 * p + 1]], axis=3).transpose(1, 0, 2, 3, 4).reshape(NY, NZ, NX, 96, 768)
        for p in range(4)
    ])
    wide_grads = slope_expand.astype(bf16).reshape(NZ, NX, 96, 3072)
    tall_grads = slope_reduce.astype(bf16).reshape(NY, NC, 192, 3072)
    small_grads = [
        slope_gain_one, slope_bias_one, slope_query_bias, slope_value_bias, slope_mixer_bias, slope_gain_two,
        slope_bias_two, slope_xquery_bias, slope_xvalue_bias, slope_xmixer_bias, slope_gain_three,
        slope_bias_three, slope_expand_bias, slope_reduce_bias,
    ]
    small_flat = jnp.concatenate([v.reshape(8, -1) for v in small_grads], axis=1)
    small_flat = jnp.pad(small_flat, ((0, 0), (0, 2048 - sum(sizes)))).reshape(8, 16, 128)
    total, small_total = reduce_everything(pair_grads, wide_grads, tall_grads, small_flat)
    matrices = []
    for p in range(4):
        matrices += [total[p, :, :192], total[p, :, 192:]]
    expand_grad = jnp.concatenate([total[4], total[5]], axis=1)
    reduce_grad = jnp.concatenate([total[6], total[7]], axis=0).T
    flat_total = small_total.reshape(-1)
    smaller, at = [], 0
    for size in sizes:
        smaller.append(flat_total[at:at + size])
        at += size
    m_query, m_key, m_value, m_xquery, m_xkey, m_xvalue, m_mixer, m_xmixer = matrices
    return (
        layer_output, tokens_gradient, smaller[0], smaller[1], m_query, smaller[2], m_key, m_value, smaller[3],
        m_mixer, smaller[4], smaller[5], smaller[6], m_xquery, smaller[7], m_xkey, m_xvalue, smaller[8],
        m_xmixer, smaller[9], smaller[10], smaller[11], expand_grad, smaller[12], reduce_grad, smaller[13],
    )


def solution(mesh):
    placed = (
        P("grp", "seq", None),
        P("grp", "seq", None),
        P("grp"),
        P("grp"),
        P("grp"),
        P(),
        P("grp", "seq", None),
        P("grp"),
        P("grp"),
        P("grp", "seq"),
        P("grp"),
        P("grp", "seq"),
        P("grp", "seq"),
        P("grp"),
        P("grp", "seq"),
        P("grp"),
        P("grp"),
        P("grp"),
        P("grp", "seq"),
        P("grp"),
        P("grp", "seq"),
        P("grp", "seq"),
        P("grp"),
        P("grp", "seq"),
        P("grp"),
        P("grp"),
        P("grp"),
        P("grp", "seq"),
        P("grp"),
        P("grp", "seq"),
        P("grp"),
    )
    small_slice = mesh.shape["grp"] == NZ * NX and mesh.shape["seq"] == NY * NC
    return jax.shard_map(
        on_device_fast if small_slice else on_device_plain,
        mesh=mesh,
        in_specs=placed,
        out_specs=(
            P("grp", "seq", None),
            P("grp", "seq", None),
            P("grp"),
            P("grp"),
            P("grp", "seq"),
            P("grp"),
            P("grp", "seq"),
            P("grp", "seq"),
            P("grp"),
            P("grp", "seq"),
            P("grp"),
            P("grp"),
            P("grp"),
            P("grp", "seq"),
            P("grp"),
            P("grp", "seq"),
            P("grp", "seq"),
            P("grp"),
            P("grp", "seq"),
            P("grp"),
            P("grp"),
            P("grp"),
            P("grp", "seq"),
            P("grp"),
            P("grp", "seq"),
            P("grp"),
        ),
        check_vma=False,
    )
```

```python
import math

import jax
import jax.numpy as jnp
from jax import lax
from jax.experimental import pallas as pl
from jax.experimental.pallas import tpu as pltpu
from jax.sharding import PartitionSpec as P

HEADS = 12
HEAD_DIM = 64


NEG = -1e30
EPS = 1e-05


def norm_rows(values, scaling, offset):
    centre = values - jnp.mean(values, axis=-1, keepdims=True)
    spread = jnp.mean(centre * centre, axis=-1, keepdims=True)
    return centre * lax.rsqrt(spread + EPS) * scaling + offset


def smooth_gate(values):
    return 0.5 * values * (1.0 + lax.erf(values * 0.7071067811865476))


def linear(inputs, weight):
    return jnp.einsum("bri,ij->brj", inputs, weight, preferred_element_type=jnp.float32)


def linear_back(gradient, weight):
    return jnp.einsum("brj,ij->bri", gradient, weight, preferred_element_type=jnp.float32)


def outer_sum(inputs, gradient):
    return jnp.einsum("bri,brj->ij", inputs, gradient, preferred_element_type=jnp.float32)


def row_total(gradient):
    return jnp.sum(gradient.astype(jnp.float32), axis=(0, 1))


def split_heads(values):
    return values.reshape(values.shape[0], values.shape[1], HEADS, HEAD_DIM)


def scores_of(query, key_rows, allowed):
    scores = jnp.einsum(
        "bqhd,bkhd->bhqk",
        split_heads(query),
        split_heads(key_rows),
        preferred_element_type=jnp.float32,
    )
    return jnp.where(allowed[:, None], scores, NEG)


def attend(query, key_rows, values, allowed):
    scores = scores_of(query, key_rows, allowed)
    maximum = jnp.max(scores, axis=-1, keepdims=True)
    raised = jnp.exp(scores - maximum)
    summed = jnp.sum(raised, axis=-1, keepdims=True)
    chances = (raised / summed).astype(jnp.bfloat16)
    blended = jnp.einsum(
        "bhqk,bkhd->bqhd", chances, split_heads(values), preferred_element_type=jnp.float32
    )
    return (blended.reshape(query.shape).astype(jnp.bfloat16), maximum + jnp.log(summed))


def attend_back(grad_low, query, key_rows, values, allowed, logsum):
    scores = scores_of(query, key_rows, allowed)
    chances = jnp.exp(scores - logsum)
    grad_heads = split_heads(grad_low)
    grad_chance = jnp.einsum(
        "bqhd,bkhd->bhqk", grad_heads, split_heads(values), preferred_element_type=jnp.float32
    )
    offset = jnp.sum(chances * grad_chance, axis=-1, keepdims=True)
    grad_score = (chances * (grad_chance - offset)).astype(jnp.bfloat16)
    grad_query = jnp.einsum(
        "bhqk,bkhd->bqhd", grad_score, split_heads(key_rows), preferred_element_type=jnp.float32
    )
    grad_keys = jnp.einsum(
        "bhqk,bqhd->bkhd", grad_score, split_heads(query), preferred_element_type=jnp.float32
    )
    grad_values = jnp.einsum(
        "bhqk,bqhd->bkhd",
        chances.astype(jnp.bfloat16),
        grad_heads,
        preferred_element_type=jnp.float32,
    )
    return (
        grad_query.reshape(query.shape),
        grad_keys.reshape(key_rows.shape),
        grad_values.reshape(values.shape),
    )


def on_device_plain(
    tokens,
    encoder_states,
    lengths,
    frame_counts,
    corpus_ids,
    corpus_weights,
    cotangent,
    first_gain,
    first_bias,
    query_weight,
    query_bias,
    key_weight,
    value_weight,
    value_bias,
    output_weight,
    output_bias,
    second_gain,
    second_bias,
    cross_query_weight,
    cross_query_bias,
    cross_key_weight,
    cross_value_weight,
    cross_value_bias,
    cross_output_weight,
    cross_output_bias,
    third_gain,
    third_bias,
    expand_weight,
    expand_bias,
    reduce_weight,
    reduce_bias,
):
    row_parts = (
        lax.all_gather(query_weight, "grp", axis=0, tiled=True),
        lax.all_gather(key_weight, "grp", axis=0, tiled=True),
        lax.all_gather(value_weight, "grp", axis=0, tiled=True),
        lax.all_gather(output_weight, "grp", axis=0, tiled=True),
        lax.all_gather(cross_query_weight, "grp", axis=0, tiled=True),
        lax.all_gather(cross_key_weight, "grp", axis=0, tiled=True),
        lax.all_gather(cross_value_weight, "grp", axis=0, tiled=True),
        lax.all_gather(cross_output_weight, "grp", axis=0, tiled=True),
        lax.all_gather(expand_weight, "grp", axis=0, tiled=True),
        lax.all_gather(reduce_weight, "grp", axis=0, tiled=True),
        lax.all_gather(first_gain, "grp", axis=0, tiled=True),
        lax.all_gather(first_bias, "grp", axis=0, tiled=True),
        lax.all_gather(query_bias, "grp", axis=0, tiled=True),
        lax.all_gather(value_bias, "grp", axis=0, tiled=True),
        lax.all_gather(output_bias, "grp", axis=0, tiled=True),
        lax.all_gather(second_gain, "grp", axis=0, tiled=True),
        lax.all_gather(second_bias, "grp", axis=0, tiled=True),
        lax.all_gather(cross_query_bias, "grp", axis=0, tiled=True),
        lax.all_gather(cross_value_bias, "grp", axis=0, tiled=True),
        lax.all_gather(cross_output_bias, "grp", axis=0, tiled=True),
        lax.all_gather(third_gain, "grp", axis=0, tiled=True),
        lax.all_gather(third_bias, "grp", axis=0, tiled=True),
        lax.all_gather(expand_bias, "grp", axis=0, tiled=True),
        lax.all_gather(reduce_bias, "grp", axis=0, tiled=True),
    )
    gathered = (
        lax.all_gather(row_parts[0], "seq", axis=1, tiled=True),
        lax.all_gather(row_parts[1], "seq", axis=1, tiled=True),
        lax.all_gather(row_parts[2], "seq", axis=1, tiled=True),
        lax.all_gather(row_parts[3], "seq", axis=1, tiled=True),
        lax.all_gather(row_parts[4], "seq", axis=1, tiled=True),
        lax.all_gather(row_parts[5], "seq", axis=1, tiled=True),
        lax.all_gather(row_parts[6], "seq", axis=1, tiled=True),
        lax.all_gather(row_parts[7], "seq", axis=1, tiled=True),
        lax.all_gather(row_parts[8], "seq", axis=1, tiled=True),
        lax.all_gather(row_parts[9], "seq", axis=1, tiled=True),
    )
    w_query, w_key, w_value, w_mixer, x_query, x_key, x_value, x_mixer, w_expand, w_reduce = (
        gathered
    )
    vectors = [piece.astype(jnp.float32) for piece in row_parts[10:]]
    factor = 1.0 / math.sqrt(HEAD_DIM)
    seq_count = lax.axis_size("seq")
    span_rows = tokens.shape[1]
    query_pos = lax.axis_index("seq") * span_rows + jnp.arange(span_rows, dtype=jnp.int32)
    key_pos = jnp.arange(span_rows * seq_count, dtype=jnp.int32)
    self_mask = (key_pos[None, None, :] <= query_pos[None, :, None]) & (
        key_pos[None, None, :] < lengths[:, None, None]
    )
    frame_pos = jnp.arange(encoder_states.shape[1] * seq_count, dtype=jnp.int32)
    cross_mask = frame_pos[None, None, :] < frame_counts[:, None, None]
    layer_in = tokens.astype(jnp.float32)
    normed_one, norm_back_one = jax.vjp(norm_rows, layer_in, vectors[0], vectors[1])
    normed_one = normed_one.astype(jnp.bfloat16)
    query_low = ((linear(normed_one, w_query) + vectors[2]) * factor).astype(jnp.bfloat16)
    key_low = linear(normed_one, w_key).astype(jnp.bfloat16)
    value_low = (linear(normed_one, w_value) + vectors[3]).astype(jnp.bfloat16)
    key_all, value_all = (
        lax.all_gather(key_low, "seq", axis=1, tiled=True),
        lax.all_gather(value_low, "seq", axis=1, tiled=True),
    )
    self_out, self_logsum = attend(query_low, key_all, value_all, self_mask)
    after_self = layer_in + linear(self_out, w_mixer) + vectors[4]
    normed_two, norm_back_two = jax.vjp(norm_rows, after_self, vectors[5], vectors[6])
    normed_two = normed_two.astype(jnp.bfloat16)
    cross_query = ((linear(normed_two, x_query) + vectors[7]) * factor).astype(jnp.bfloat16)
    frames_all = lax.all_gather(encoder_states, "seq", axis=1, tiled=True)
    cross_keys_all = linear(frames_all, x_key).astype(jnp.bfloat16)
    cross_values_all = (linear(frames_all, x_value) + vectors[8]).astype(jnp.bfloat16)
    cross_out, cross_logsum = attend(cross_query, cross_keys_all, cross_values_all, cross_mask)
    after_cross = after_self + linear(cross_out, x_mixer) + vectors[9]
    normed_three, norm_back_three = jax.vjp(norm_rows, after_cross, vectors[10], vectors[11])
    normed_three = normed_three.astype(jnp.bfloat16)
    hidden = linear(normed_three, w_expand) + vectors[12]
    gated, gate_back = jax.vjp(smooth_gate, hidden)
    gated_low = gated.astype(jnp.bfloat16)
    result = after_cross + linear(gated_low, w_reduce) + vectors[13]
    layer_output = result.astype(jnp.bfloat16)
    present = (query_pos[None, :] < lengths[:, None]).astype(jnp.float32)
    corpus_index = jnp.arange(corpus_weights.shape[0], dtype=jnp.int32)
    corpus_scale = jnp.sum(
        jnp.where(corpus_ids[:, None] == corpus_index[None, :], corpus_weights[None, :], 0.0),
        axis=1,
    )
    grad_out = cotangent.astype(jnp.float32) * (present * corpus_scale[:, None])[:, :, None]
    reduce_low = grad_out.astype(jnp.bfloat16)
    slope_reduce_bias = row_total(reduce_low)
    slope_reduce = outer_sum(gated_low, reduce_low)
    grad_hidden = gate_back(linear_back(reduce_low, w_reduce))[0]
    hidden_low = grad_hidden.astype(jnp.bfloat16)
    slope_expand_bias = row_total(hidden_low)
    slope_expand = outer_sum(normed_three, hidden_low)
    grad_norm_in, slope_gain_three, slope_bias_three = norm_back_three(
        linear_back(hidden_low, w_expand)
    )
    grad_cross = grad_out + grad_norm_in
    cross_low = grad_cross.astype(jnp.bfloat16)
    slope_xmixer_bias = row_total(cross_low)
    slope_xmixer = outer_sum(cross_out, cross_low)
    grad_heard = linear_back(cross_low, x_mixer).astype(jnp.bfloat16)
    grad_cq, part_ck, part_cv = attend_back(
        grad_heard, cross_query, cross_keys_all, cross_values_all, cross_mask, cross_logsum
    )
    slope_xkey = outer_sum(frames_all, part_ck)
    slope_xvalue = outer_sum(frames_all, part_cv)
    slope_xvalue_bias = row_total(part_cv)
    low_cq = (grad_cq * factor).astype(jnp.bfloat16)
    slope_xquery_bias = row_total(low_cq)
    slope_xquery = outer_sum(normed_two, low_cq)
    grad_norm_two, slope_gain_two, slope_bias_two = norm_back_two(linear_back(low_cq, x_query))
    grad_self = grad_cross + grad_norm_two
    self_low = grad_self.astype(jnp.bfloat16)
    slope_mixer_bias = row_total(self_low)
    slope_mixer = outer_sum(self_out, self_low)
    grad_mixed = linear_back(self_low, w_mixer).astype(jnp.bfloat16)
    grad_q, part_k, part_v = attend_back(
        grad_mixed, query_low, key_all, value_all, self_mask, self_logsum
    )
    summed_k, summed_v = (
        lax.psum_scatter(
            part_k.astype(jnp.bfloat16), "seq", scatter_dimension=1, tiled=True
        ).astype(jnp.float32),
        lax.psum_scatter(
            part_v.astype(jnp.bfloat16), "seq", scatter_dimension=1, tiled=True
        ).astype(jnp.float32),
    )
    low_k = summed_k.astype(jnp.bfloat16)
    low_v = summed_v.astype(jnp.bfloat16)
    low_q = (grad_q * factor).astype(jnp.bfloat16)
    slope_query = outer_sum(normed_one, low_q)
    slope_query_bias = row_total(low_q)
    slope_key = outer_sum(normed_one, low_k)
    slope_value = outer_sum(normed_one, low_v)
    slope_value_bias = row_total(low_v)
    grad_normed = (
        linear_back(low_q, w_query) + linear_back(low_k, w_key) + linear_back(low_v, w_value)
    )
    grad_norm_one, slope_gain_one, slope_bias_one = norm_back_one(grad_normed)
    tokens_gradient = (grad_self + grad_norm_one).astype(jnp.bfloat16)
    owned = (
        lax.psum_scatter(slope_query, "grp", scatter_dimension=0, tiled=True),
        lax.psum_scatter(slope_key, "grp", scatter_dimension=0, tiled=True),
        lax.psum_scatter(slope_value, "grp", scatter_dimension=0, tiled=True),
        lax.psum_scatter(slope_mixer, "grp", scatter_dimension=0, tiled=True),
        lax.psum_scatter(slope_xquery, "grp", scatter_dimension=0, tiled=True),
        lax.psum_scatter(slope_xkey, "grp", scatter_dimension=0, tiled=True),
        lax.psum_scatter(slope_xvalue, "grp", scatter_dimension=0, tiled=True),
        lax.psum_scatter(slope_xmixer, "grp", scatter_dimension=0, tiled=True),
        lax.psum_scatter(slope_expand, "grp", scatter_dimension=0, tiled=True),
        lax.psum_scatter(slope_reduce, "grp", scatter_dimension=0, tiled=True),
        lax.psum_scatter(slope_gain_one, "grp", scatter_dimension=0, tiled=True),
        lax.psum_scatter(slope_bias_one, "grp", scatter_dimension=0, tiled=True),
        lax.psum_scatter(slope_query_bias, "grp", scatter_dimension=0, tiled=True),
        lax.psum_scatter(slope_value_bias, "grp", scatter_dimension=0, tiled=True),
        lax.psum_scatter(slope_mixer_bias, "grp", scatter_dimension=0, tiled=True),
        lax.psum_scatter(slope_gain_two, "grp", scatter_dimension=0, tiled=True),
        lax.psum_scatter(slope_bias_two, "grp", scatter_dimension=0, tiled=True),
        lax.psum_scatter(slope_xquery_bias, "grp", scatter_dimension=0, tiled=True),
        lax.psum_scatter(slope_xvalue_bias, "grp", scatter_dimension=0, tiled=True),
        lax.psum_scatter(slope_xmixer_bias, "grp", scatter_dimension=0, tiled=True),
        lax.psum_scatter(slope_gain_three, "grp", scatter_dimension=0, tiled=True),
        lax.psum_scatter(slope_bias_three, "grp", scatter_dimension=0, tiled=True),
        lax.psum_scatter(slope_expand_bias, "grp", scatter_dimension=0, tiled=True),
        lax.psum_scatter(slope_reduce_bias, "grp", scatter_dimension=0, tiled=True),
    )
    matrices = (
        lax.psum_scatter(
            owned[0].astype(jnp.bfloat16), "seq", scatter_dimension=1, tiled=True
        ).astype(jnp.float32),
        lax.psum_scatter(
            owned[1].astype(jnp.bfloat16), "seq", scatter_dimension=1, tiled=True
        ).astype(jnp.float32),
        lax.psum_scatter(
            owned[2].astype(jnp.bfloat16), "seq", scatter_dimension=1, tiled=True
        ).astype(jnp.float32),
        lax.psum_scatter(
            owned[3].astype(jnp.bfloat16), "seq", scatter_dimension=1, tiled=True
        ).astype(jnp.float32),
        lax.psum_scatter(
            owned[4].astype(jnp.bfloat16), "seq", scatter_dimension=1, tiled=True
        ).astype(jnp.float32),
        lax.psum_scatter(
            owned[5].astype(jnp.bfloat16), "seq", scatter_dimension=1, tiled=True
        ).astype(jnp.float32),
        lax.psum_scatter(
            owned[6].astype(jnp.bfloat16), "seq", scatter_dimension=1, tiled=True
        ).astype(jnp.float32),
        lax.psum_scatter(
            owned[7].astype(jnp.bfloat16), "seq", scatter_dimension=1, tiled=True
        ).astype(jnp.float32),
        lax.psum_scatter(
            owned[8].astype(jnp.bfloat16), "seq", scatter_dimension=1, tiled=True
        ).astype(jnp.float32),
        lax.psum_scatter(
            owned[9].astype(jnp.bfloat16), "seq", scatter_dimension=1, tiled=True
        ).astype(jnp.float32),
    )
    smaller = lax.psum(
        (
            owned[10],
            owned[11],
            owned[12],
            owned[13],
            owned[14],
            owned[15],
            owned[16],
            owned[17],
            owned[18],
            owned[19],
            owned[20],
            owned[21],
            owned[22],
            owned[23],
        ),
        "seq",
    )
    return (
        layer_output,
        tokens_gradient,
        smaller[0],
        smaller[1],
        matrices[0],
        smaller[2],
        matrices[1],
        matrices[2],
        smaller[3],
        matrices[3],
        smaller[4],
        smaller[5],
        smaller[6],
        matrices[4],
        smaller[7],
        matrices[5],
        matrices[6],
        smaller[8],
        matrices[7],
        smaller[9],
        smaller[10],
        smaller[11],
        matrices[8],
        smaller[12],
        matrices[9],
        smaller[13],
    )


MESH_ID = pl.DeviceIdType.MESH
NZ, NX, NY, NC = 4, 2, 2, 2
GROUPS = 8


def where_am_i():
    grp = lax.axis_index("grp")
    seq = lax.axis_index("seq")
    return grp // NX, lax.rem(grp, NX), seq // NC, lax.rem(seq, NC)


def device_at(z, x, y, c):
    return (z * NX + x, y * NC + c)


def lanes(start, size):
    return pl.ds(pl.multiple_of(start, 128), size)


def pieces_of(bank, group, y, c, x, z_from, z_to):
    pairs, wide, tall = bank
    if group < 4:
        return [pairs.at[group, y, pl.ds(z_from, z_to - z_from), x, :, lanes(c * 384, 384)]]
    if group < 6:
        start = (y * NC + c) * 768 + (group - 4) * 384
        return [wide.at[pl.ds(z_from, z_to - z_from), x, :, lanes(start, 384)]]
    return [
        tall.at[y, c, pl.ds((group - 6) * 96, 96), lanes((z * NX + x) * 384, 384)]
        for z in range(z_from, z_to)
    ]


def piece_at(bank, group, y, c, x, z):
    pairs, wide, tall = bank
    if group < 4:
        return pairs.at[group, y, z, x, :, lanes(c * 384, 384)]
    if group < 6:
        return wide.at[z, x, :, lanes((y * NC + c) * 768 + (group - 4) * 384, 384)]
    return tall.at[y, c, pl.ds((group - 6) * 96, 96), lanes((z * NX + x) * 384, 384)]


def own_piece(bank, group):
    pairs, wide, tall = bank
    if group < 4:
        return pairs.at[group]
    if group < 6:
        return wide.at[:, pl.ds((group - 4) * 384, 384)]
    return tall.at[pl.ds((group - 6) * 96, 96), :]


class Mail:
    def __init__(self, send_sems, recv_sems):
        self.send_sems, self.recv_sems, self.count, self.sent = send_sems, recv_sems, 0, []

    def slots(self, number):
        first = self.count
        self.count += number
        return list(range(first, first + number))

    def post(self, source, target, slot, device):
        copy = pltpu.make_async_remote_copy(
            src_ref=source,
            dst_ref=target,
            send_sem=self.send_sems.at[slot],
            recv_sem=self.recv_sems.at[slot],
            device_id=device,
            device_id_type=MESH_ID,
        )
        copy.start()
        self.sent.append(copy)

    def arrive(self, target, slot, device):
        pltpu.make_async_remote_copy(
            src_ref=target,
            dst_ref=target,
            send_sem=self.send_sems.at[slot],
            recv_sem=self.recv_sems.at[slot],
            device_id=device,
            device_id_type=MESH_ID,
        ).wait_recv()

    def finish(self):
        for copy in self.sent:
            copy.wait_send()


def greet(z, x, y, c):
    barrier = pltpu.get_barrier_semaphore()
    friends = [device_at(lax.rem(z + k, NZ), x, y, c) for k in range(1, NZ)]
    friends += [device_at(lax.rem(z + k, NZ), 1 - x, y, c) for k in range(NZ)]
    friends += [device_at(z, x, 1 - y, c), device_at(z, x, y, 1 - c)]
    for friend in friends:
        pl.semaphore_signal(barrier, inc=1, device_id=friend, device_id_type=MESH_ID)
    pl.semaphore_wait(barrier, len(friends))


def parts_in(group, number):
    return number if group >= 6 else 1


ORDER = (2, 0, 1, 3, 4, 5, 6, 7)


def forward_kernel(
    frame_span, lengths, counts,
    pairs_in, wide_in, tall_in, small_in, frames_in, tokens_in,
    pairs, wide, tall, frames, vec_out, wide_bias,
    q_to, k_to, v_to, a_to, o_to, h1_to, c_to, p_self_to, ck_to, cv_to, cq_to, o2_to, h2_to, m_to, p_cross_to,
    tokens_got, small, pairs_here, frames_here, q, k, v, a, o, h1, c, p_self, ck, cv, cq, o2, h2, m, p_cross,
    a_all, scores, self_scores, self_bias, cross_bias,
    send_sems, recv_sems, local_sems, load_sems, save_sems,
):
    z, x, y, c_own = where_am_i()
    greet(z, x, y, c_own)
    mail = Mail(send_sems, recv_sems)
    own = (pairs_in, wide_in, tall_in)
    bank = (pairs, wide, tall)
    x_mate, y_mate = device_at(z, 1 - x, y, c_own), device_at(z, x, 1 - y, c_own)
    c_mate = device_at(z, x, y, 1 - c_own)
    z_mates = [device_at(lax.rem(z + n, NZ), x, y, c_own) for n in range(1, NZ)]
    grp = z * NX + x
    seq = y * NC + c_own

    local = []

    def keep(source, target):
        copy = pltpu.make_async_copy(source, target, local_sems.at[len(local)])
        copy.start()
        local.append(copy)

    small_slots = mail.slots(2 * NZ - 1)
    small_to = z_mates + [device_at(lax.rem(z + n, NZ), 1 - x, y, c_own) for n in range(NZ)]
    token_slots = mail.slots(3)
    frame_slots = mail.slots(3)
    z_slots = [mail.slots(NZ - 1) for _ in range(GROUPS)]
    x_slots = [mail.slots(parts_in(g, 4)) for g in range(GROUPS)]
    y_slots = [mail.slots(parts_in(g, 4)) for g in range(GROUPS)]
    dy_slots = [mail.slots(parts_in(g, VIA_X)) for g in range(GROUPS)]
    dx_slots = [mail.slots(parts_in(g, 4 - VIA_X)) for g in range(GROUPS)]
    co_slots = [mail.slots(parts_in(g, 4)) for g in range(GROUPS)]
    cx_slots = [mail.slots(parts_in(g, 4)) for g in range(GROUPS)]
    cy_slots = [mail.slots(parts_in(g, 4)) for g in range(GROUPS)]
    cdy_slots = [mail.slots(parts_in(g, VIA_X)) for g in range(GROUPS)]
    cdx_slots = [mail.slots(parts_in(g, 4 - VIA_X)) for g in range(GROUPS)]

    def to_column(group):
        for n in range(1, NZ):
            mail.post(
                own_piece(own, group), piece_at(bank, group, y, c_own, x, z), z_slots[group][n - 1], z_mates[n - 1]
            )

    def post_all(group, slots, device, yy, cc, xx, z_from, z_to):
        for slot, ref in zip(slots, pieces_of(bank, group, yy, cc, xx, z_from, z_to)):
            mail.post(ref, ref, slot, device)

    def arrive_all(group, slots, device, yy, cc, xx, z_from, z_to):
        for slot, ref in zip(slots, pieces_of(bank, group, yy, cc, xx, z_from, z_to)):
            mail.arrive(ref, slot, device)

    def spread(group):
        for n in range(1, NZ):
            zz = lax.rem(z + NZ - n, NZ)
            mail.arrive(piece_at(bank, group, y, c_own, x, zz), z_slots[group][n - 1], z_mates[n - 1])
        local[group].wait()
        post_all(group, x_slots[group], x_mate, y, c_own, x, 0, 4)
        post_all(group, y_slots[group], y_mate, y, c_own, x, 0, 4)
        post_all(group, co_slots[group], c_mate, y, c_own, x, 0, 4)

    def turn(group):
        arrive_all(group, y_slots[group], y_mate, 1 - y, c_own, x, 0, 4)
        post_all(group, dx_slots[group], x_mate, 1 - y, c_own, x, VIA_X, 4)
        post_all(group, cy_slots[group], c_mate, 1 - y, c_own, x, 0, 4)
        arrive_all(group, x_slots[group], x_mate, y, c_own, 1 - x, 0, 4)
        post_all(group, dy_slots[group], y_mate, y, c_own, 1 - x, 0, VIA_X)
        post_all(group, cx_slots[group], c_mate, y, c_own, 1 - x, 0, 4)

    def share(group):
        arrive_all(group, dy_slots[group], y_mate, 1 - y, c_own, 1 - x, 0, VIA_X)
        post_all(group, cdy_slots[group], c_mate, 1 - y, c_own, 1 - x, 0, VIA_X)
        arrive_all(group, dx_slots[group], x_mate, 1 - y, c_own, 1 - x, VIA_X, 4)
        post_all(group, cdx_slots[group], c_mate, 1 - y, c_own, 1 - x, VIA_X, 4)

    def complete(group):
        arrive_all(group, co_slots[group], c_mate, y, 1 - c_own, x, 0, 4)
        arrive_all(group, cx_slots[group], c_mate, y, 1 - c_own, 1 - x, 0, 4)
        arrive_all(group, cy_slots[group], c_mate, 1 - y, 1 - c_own, x, 0, 4)
        arrive_all(group, cdy_slots[group], c_mate, 1 - y, 1 - c_own, 1 - x, 0, VIA_X)
        arrive_all(group, cdx_slots[group], c_mate, 1 - y, 1 - c_own, 1 - x, VIA_X, 4)

    def frame_rows(number):
        return frames.at[:, number]

    loads = []

    def load(source, target):
        copy = pltpu.make_async_copy(source, target, load_sems.at[len(loads)])
        copy.start()
        loads.append(copy)
        return copy

    def load_pair(group):
        complete(group)
        return load(pairs.at[group], pairs_here.at[group])

    saves = []

    def save(source, target):
        copy = pltpu.make_async_copy(source, target, save_sems.at[len(saves)])
        copy.start()
        saves.append(copy)

    for group in range(GROUPS):
        keep(own_piece(own, group), piece_at(bank, group, y, c_own, x, z))
    keep(small_in, small.at[grp])
    keep(frames_in, frame_rows(seq))
    keep(tokens_in, tokens_got.at[seq])
    to_column(ORDER[0])
    for slot, device in zip(small_slots, small_to):
        mail.post(small_in, small.at[grp], slot, device)
    to_column(ORDER[1])
    mail.post(frames_in, frame_rows(seq), frame_slots[0], y_mate)
    mail.post(frames_in, frame_rows(seq), frame_slots[1], c_mate)
    mail.post(tokens_in, tokens_got.at[seq], token_slots[0], y_mate)
    mail.post(tokens_in, tokens_got.at[seq], token_slots[1], c_mate)
    to_column(ORDER[2])

    pending = []
    for step in range(GROUPS + 2):
        if step + 3 < GROUPS:
            pending.append((to_column, ORDER[step + 3]))
        if step < GROUPS:
            pending.append((spread, ORDER[step]))
        if 0 <= step - 1 < GROUPS:
            pending.append((turn, ORDER[step - 1]))
        if 0 <= step - 2 < GROUPS:
            pending.append((share, ORDER[step - 2]))

    def tick(number=1):
        while number > 0 and pending:
            action, group = pending.pop(0)
            action(group)
            if action is not to_column:
                number -= 1

    def until(action, group):
        while (action, group) in pending:
            tick()

    for n in range(1, NZ):
        zz = lax.rem(z + NZ - n, NZ)
        mail.arrive(small.at[zz * NX + x], small_slots[n - 1], z_mates[n - 1])
    for n in range(NZ):
        zz = lax.rem(z + NZ - n, NZ)
        mail.arrive(small.at[zz * NX + 1 - x], small_slots[NZ - 1 + n], x_mate)
    local[GROUPS].wait()
    vec_out[...] = jnp.concatenate([small[g, 0:16, 0:96].astype(jnp.float32) for g in range(8)], axis=1)
    for g in range(8):
        three = small[g, 16:24, :].astype(jnp.float32)
        for n in range(3):
            at = g * 384 + n * 128
            wide_bias[:, at:at + 128] = three[n:n + 1]

    until(spread, ORDER[1])
    other = (1 - y) * NC + c_own
    mail.arrive(tokens_got.at[other], token_slots[0], y_mate)
    mail.post(tokens_got.at[other], tokens_got.at[other], token_slots[2], c_mate)
    until(turn, ORDER[0])
    mail.arrive(frame_rows(other), frame_slots[0], y_mate)
    mail.post(frame_rows(other), frame_rows(other), frame_slots[2], c_mate)
    until(share, ORDER[0])
    mail.arrive(tokens_got.at[y * NC + 1 - c_own], token_slots[1], c_mate)
    mail.arrive(tokens_got.at[(1 - y) * NC + 1 - c_own], token_slots[2], c_mate)
    mail.arrive(frame_rows(y * NC + 1 - c_own), frame_slots[1], c_mate)
    mail.arrive(frame_rows((1 - y) * NC + 1 - c_own), frame_slots[2], c_mate)
    for copy in local[GROUPS + 1:]:
        copy.wait()
    frames_loaded = load(frames, frames_here)
    kv_loaded = load_pair(2)
    frames_loaded.wait()
    kv_loaded.wait()
    for number, _ in enumerate(cross_keys(frames_here, vec_out, pairs_here.at[2], ck, cv)):
        if number % 2 == 1:
            tick()
    save(ck, ck_to)
    save(cv, cv_to)
    until(share, 1)
    first = load_pair(0)
    second = load_pair(1)
    first.wait()
    second.wait()
    phase = self_forward(
        lengths, tokens_got, vec_out, pairs_here.at[0], pairs_here.at[1], q, k, v, a, o, h1, c, p_self,
        a_all, self_scores, self_bias,
    )
    for number, _ in enumerate(phase):
        if number % 2 == 1:
            tick()
    until(share, 3)
    third = load_pair(3)
    for source, target in (
        (q, q_to), (k, k_to), (v, v_to), (a, a_to), (o, o_to), (h1, h1_to), (c, c_to), (p_self, p_self_to)
    ):
        save(source, target)
    third.wait()
    phase = cross_forward(
        counts, frame_span, c, vec_out, pairs_here.at[3], ck, cv, h1, cq, o2, h2, m, p_cross, scores, cross_bias
    )
    for number, _ in enumerate(phase):
        if 1 <= number <= 12:
            t, pair = (number - 1) // 6, (number - 1) % 6
            save(p_cross.at[t, pair], p_cross_to.at[t, pair])
        if number % 2 == 1:
            tick()
    for source, target in ((cq, cq_to), (o2, o2_to), (h2, h2_to), (m, m_to)):
        save(source, target)
    tick(100)
    for group in (4, 5, 6, 7):
        complete(group)
    for copy in saves:
        copy.wait()
    mail.finish()


VIA_X = 1


def slots_needed():
    return (2 * NZ - 1) + 6 + sum(
        3 + parts_in(g, 4) * 5 + 2 * (parts_in(g, VIA_X) + parts_in(g, 4 - VIA_X)) for g in range(GROUPS)
    )


def run_forward(frame_span, lengths, counts, pairs, wide, tall, small, frames, tokens):
    bf16, f32 = jnp.bfloat16, jnp.float32
    number = slots_needed()
    span = tokens.shape[1]
    anywhere = pl.BlockSpec(memory_space=pl.ANY)
    inside = pl.BlockSpec(memory_space=pltpu.VMEM)
    scalar = pl.BlockSpec(memory_space=pltpu.SMEM)
    rows = (2, span, 768)
    keys = (2, 4, 128, 768)
    kept = [
        (rows, bf16), (keys, bf16), (keys, bf16), (rows, bf16), (rows, bf16), (rows, f32), (rows, bf16),
        ((2, 6, 2 * span, 512), bf16), ((2, 1536, 768), bf16), ((2, 1536, 768), bf16), (rows, bf16), (rows, bf16),
        (rows, f32), (rows, bf16), ((2, 6, 2 * span, 1536), bf16),
    ]
    frames_shape = (2, NY * NC) + frames.shape[1:]
    return pl.pallas_call(
        lambda *refs: forward_kernel(frame_span, *refs),
        out_shape=(
            jax.ShapeDtypeStruct((4, NY, NZ, NX, 96, 768), bf16),
            jax.ShapeDtypeStruct((NZ, NX, 96, 3072), bf16),
            jax.ShapeDtypeStruct((NY, NC, 192, 3072), bf16),
            jax.ShapeDtypeStruct(frames_shape, bf16),
            jax.ShapeDtypeStruct((16, 768), f32),
            jax.ShapeDtypeStruct((1, 3072), f32),
        ) + tuple(jax.ShapeDtypeStruct(shape, kind) for shape, kind in kept),
        in_specs=[scalar] * 2 + [anywhere] * 6,
        out_specs=(anywhere,) * 4 + (inside,) * 2 + (anywhere,) * len(kept),
        scratch_shapes=[
            pltpu.VMEM((4,) + tokens.shape, bf16),
            pltpu.VMEM((8,) + small.shape, bf16),
            pltpu.VMEM((4, NY, NZ, NX, 96, 768), bf16),
            pltpu.VMEM(frames_shape, bf16),
        ] + [pltpu.VMEM(shape, kind) for shape, kind in kept] + [
            pltpu.VMEM((2, 4, span, 768), bf16),
            pltpu.VMEM((2 * span, 1536), f32),
            pltpu.VMEM((2 * span, 512), f32),
            pltpu.VMEM((2, 2 * span, 512), f32),
            pltpu.VMEM((2, 1, 1536), f32),
            pltpu.SemaphoreType.DMA((number,)),
            pltpu.SemaphoreType.DMA((number,)),
            pltpu.SemaphoreType.DMA((GROUPS + 3,)),
            pltpu.SemaphoreType.DMA((5,)),
            pltpu.SemaphoreType.DMA((26,)),
        ],
        compiler_params=pltpu.CompilerParams(
            collective_id=1, has_side_effects=True, vmem_limit_bytes=60 << 20
        ),
        name="gather_forward",
    )(lengths, counts, pairs, wide, tall, small, frames, tokens)


def reduce_kernel(
    pairs, wide, tall, small,
    total, small_total,
    own_acc, core_in, diag_in, x_in, y_in, z_in, small_in, small_sum, small_seq,
    send_sems, recv_sems, local_sems,
):
    z, x, y, c = where_am_i()
    greet(z, x, y, c)
    mail = Mail(send_sems, recv_sems)
    bank = (pairs, wide, tall)
    x_mate, y_mate = device_at(z, 1 - x, y, c), device_at(z, x, 1 - y, c)
    c_mate = device_at(z, x, y, 1 - c)
    z_mates = [device_at(lax.rem(z + k, NZ), x, y, c) for k in range(1, NZ)]
    grp = z * NX + x
    seq = y * NC + c

    small_slots = mail.slots(2 * NZ - 1)
    small_to = [(lax.rem(z + k, NZ), x) for k in range(1, NZ)]
    small_to += [(lax.rem(z + k, NZ), 1 - x) for k in range(NZ)]
    for number, (zz, xx) in enumerate(small_to):
        mail.post(small.at[zz * NX + xx], small_in.at[number], small_slots[number], device_at(zz, xx, y, c))

    core_slots = [mail.slots(4 * parts_in(g, 4)) for g in range(GROUPS)]
    local = []
    count = 0
    columns = [(0, 0), (1, 0), (0, 1), (1, 1)]

    def column(dx, dy):
        return jnp.where(dx, 1 - x, x), jnp.where(dy, 1 - y, y)

    for group in range(GROUPS):
        mine = []
        for place, (dx, dy) in enumerate(columns):
            xx, yy = (1 - x if dx else x), (1 - y if dy else y)
            targets = [core_in.at[group, place]] if group < 6 else [core_in.at[group, place, k] for k in range(4)]
            sources = pieces_of(bank, group, yy, 1 - c, xx, 0, 4)
            many = len(sources)
            for k in range(many):
                mail.post(sources[k], targets[k], core_slots[group][place * many + k], c_mate)
            sources = pieces_of(bank, group, yy, c, xx, 0, 4)
            targets = [own_acc.at[group, place]] if group < 6 else [own_acc.at[group, place, k] for k in range(4)]
            for k in range(many):
                copy = pltpu.make_async_copy(sources[k], targets[k], local_sems.at[count])
                copy.start()
                mine.append(copy)
                count += 1
        local.append(mine)

    dx_slots = [mail.slots(1) for _ in range(GROUPS)]
    dy_slots = [mail.slots(1) for _ in range(GROUPS)]
    x_slots = [mail.slots(1) for _ in range(GROUPS)]
    y_slots = [mail.slots(1) for _ in range(GROUPS)]
    z_slots = [mail.slots(NZ - 1) for _ in range(GROUPS)]

    def core_step(group):
        for copy in local[group]:
            copy.wait()
        many = 4 if group >= 6 else 1
        for place in (3, 1, 2, 0):
            for k in range(many):
                target = core_in.at[group, place] if many == 1 else core_in.at[group, place, k]
                mail.arrive(target, core_slots[group][place * many + k], c_mate)

            def add(k, carry):
                own_acc[group, place, k] = own_acc[group, place, k] + core_in[group, place, k]
                return carry

            lax.fori_loop(0, 4, add, 0)
            if place == 3:
                mail.post(own_acc.at[group, 3, pl.ds(0, 2)], diag_in.at[group, 0], dx_slots[group][0], x_mate)
                mail.post(own_acc.at[group, 3, pl.ds(2, 2)], diag_in.at[group, 1], dy_slots[group][0], y_mate)

    def side_step(group):
        mail.arrive(diag_in.at[group, 0], dx_slots[group][0], x_mate)

        def add_y(k, carry):
            own_acc[group, 2, k] = own_acc[group, 2, k] + diag_in[group, 0, k]
            return carry

        lax.fori_loop(0, 2, add_y, 0)
        mail.post(own_acc.at[group, 2], y_in.at[group], y_slots[group][0], y_mate)
        mail.arrive(diag_in.at[group, 1], dy_slots[group][0], y_mate)

        def add_x(k, carry):
            own_acc[group, 1, k + 2] = own_acc[group, 1, k + 2] + diag_in[group, 1, k]
            return carry

        lax.fori_loop(0, 2, add_x, 0)
        mail.post(own_acc.at[group, 1], x_in.at[group], x_slots[group][0], x_mate)

    def column_step(group):
        mail.arrive(y_in.at[group], y_slots[group][0], y_mate)
        mail.arrive(x_in.at[group], x_slots[group][0], x_mate)

        def add(k, carry):
            own_acc[group, 0, k] = (
                own_acc[group, 0, k].astype(jnp.float32)
                + x_in[group, k].astype(jnp.float32)
                + y_in[group, k].astype(jnp.float32)
            ).astype(jnp.bfloat16)
            return carry

        lax.fori_loop(0, 4, add, 0)
        for k in range(1, NZ):
            zz = lax.rem(z + k, NZ)
            mail.post(own_acc.at[group, 0, zz], z_in.at[group, k - 1], z_slots[group][k - 1], z_mates[k - 1])

    def last_step(group):
        for k in range(1, NZ):
            mail.arrive(z_in.at[group, k - 1], z_slots[group][k - 1], z_mates[k - 1])
        total[group] = own_acc[group, 0, z].astype(jnp.float32) + (
            z_in[group, 0].astype(jnp.float32) + z_in[group, 1].astype(jnp.float32)
        ) + z_in[group, 2].astype(jnp.float32)

    seq_slots = mail.slots(3)
    for step in range(GROUPS + 3):
        if step < GROUPS:
            core_step(step)
        if 0 <= step - 1 < GROUPS:
            side_step(step - 1)
        if 0 <= step - 2 < GROUPS:
            column_step(step - 2)
        if 0 <= step - 3 < GROUPS:
            last_step(step - 3)
        if step == 3:
            for number in range(2 * NZ - 1):
                mail.arrive(small_in.at[number], small_slots[number], x_mate)
            small_sum[...] = (
                (small[grp] + small_in[0]) + (small_in[1] + small_in[2])
                + ((small_in[3] + small_in[4]) + (small_in[5] + small_in[6]))
            )
            mail.post(small_sum, small_seq.at[0], seq_slots[0], c_mate)
        if step == 5:
            mail.arrive(small_seq.at[0], seq_slots[0], c_mate)
            small_seq[1] = small_sum[...] + small_seq[0]
            mail.post(small_seq.at[1], small_seq.at[2], seq_slots[1], y_mate)
        if step == 7:
            mail.arrive(small_seq.at[2], seq_slots[1], y_mate)
            small_total[...] = small_seq[1] + small_seq[2]
    mail.finish()


def reduce_everything(pairs, wide, tall, small):
    bf16 = jnp.bfloat16
    piece = (96, 384)
    number = 7 + 3 + sum(4 * parts_in(g, 4) + 4 + 3 for g in range(GROUPS))
    anywhere = pl.BlockSpec(memory_space=pl.ANY)
    inside = pl.BlockSpec(memory_space=pltpu.VMEM)
    small_piece = small.shape[1:]
    return pl.pallas_call(
        reduce_kernel,
        out_shape=(
            jax.ShapeDtypeStruct((GROUPS,) + piece, jnp.float32),
            jax.ShapeDtypeStruct(small_piece, jnp.float32),
        ),
        in_specs=[anywhere] * 3 + [inside],
        out_specs=(inside, inside),
        scratch_shapes=[
            pltpu.VMEM((GROUPS, 4, NZ) + piece, bf16),
            pltpu.VMEM((GROUPS, 4, NZ) + piece, bf16),
            pltpu.VMEM((GROUPS, 2, 2) + piece, bf16),
            pltpu.VMEM((GROUPS, NZ) + piece, bf16),
            pltpu.VMEM((GROUPS, NZ) + piece, bf16),
            pltpu.VMEM((GROUPS, NZ - 1) + piece, bf16),
            pltpu.VMEM((7,) + small_piece, jnp.float32),
            pltpu.VMEM(small_piece, jnp.float32),
            pltpu.VMEM((3,) + small_piece, jnp.float32),
            pltpu.SemaphoreType.DMA((number,)),
            pltpu.SemaphoreType.DMA((number,)),
            pltpu.SemaphoreType.DMA((4 * sum(parts_in(g, 4) for g in range(GROUPS)),)),
        ],
        compiler_params=pltpu.CompilerParams(
            collective_id=2, has_side_effects=True, vmem_limit_bytes=58 << 20
        ),
        name="reduce_all",
    )(pairs, wide, tall, small)


def joined(first, second):
    return jnp.concatenate([first, second], axis=1)


def mm(left, right):
    return lax.dot_general(left, right, (((1,), (0,)), ((), ())), preferred_element_type=jnp.float32)


def mm_back(left, right):
    return lax.dot_general(left, right, (((1,), (1,)), ((), ())), preferred_element_type=jnp.float32)


def mm_rows(left, right):
    return lax.dot_general(left, right, (((0,), (0,)), ((), ())), preferred_element_type=jnp.float32)


def low_lanes(rows):
    return lax.broadcasted_iota(jnp.int32, (rows, 128), 1) < 64


def turned(tile):
    return pltpu.roll(tile, 64, 1)


def tile_of(values, number):
    return values[:, number * 128:(number + 1) * 128]


def split_first(near, far):
    low = low_lanes(near.shape[0])
    return [tile_of(near, 0), jnp.where(low, tile_of(near, 1), tile_of(far, 1)), tile_of(far, 0)]


def split_second(near, far):
    low = low_lanes(near.shape[0])
    return [tile_of(near, 1), turned(jnp.where(low, tile_of(far, 0), tile_of(near, 0))), tile_of(far, 1)]


def join_first(values):
    low = low_lanes(values.shape[0])
    middle = tile_of(values, 1)
    nothing = jnp.zeros_like(middle)
    near = jnp.concatenate([tile_of(values, 0), jnp.where(low, middle, nothing)], axis=1)
    far = jnp.concatenate([tile_of(values, 2), jnp.where(low, nothing, middle)], axis=1)
    return near.astype(jnp.bfloat16), far.astype(jnp.bfloat16)


def join_second(values):
    low = low_lanes(values.shape[0])
    middle = turned(tile_of(values, 1))
    nothing = jnp.zeros_like(middle)
    near = jnp.concatenate([jnp.where(low, nothing, middle), tile_of(values, 0)], axis=1)
    far = jnp.concatenate([jnp.where(low, middle, nothing), tile_of(values, 2)], axis=1)
    return near.astype(jnp.bfloat16), far.astype(jnp.bfloat16)


def join_both(first, second):
    low = low_lanes(first.shape[0])
    mine, other = tile_of(first, 1), turned(tile_of(second, 1))
    return jnp.concatenate(
        [
            tile_of(first, 0), jnp.where(low, mine, other), tile_of(second, 0),
            tile_of(first, 2), jnp.where(low, other, mine), tile_of(second, 2),
        ],
        axis=1,
    ).astype(jnp.bfloat16)


def block_of(pair, y, at):
    if len(pair.shape) == 3:
        return pair[y, :, at]
    return pair[y, :, :, :, at].reshape(768, -1)


def times_first(values, pair):
    tiles = []
    for y in range(2):
        tiles += split_first(mm(values, block_of(pair, y, slice(0, 256))), mm(values, block_of(pair, y, slice(384, 640))))
    return tiles


def times_second(values, pair):
    tiles = []
    for y in range(2):
        tiles += split_second(mm(values, block_of(pair, y, slice(128, 384))), mm(values, block_of(pair, y, slice(512, 768))))
    return tiles


def back_first(grads, pair):
    out = None
    for y in range(2):
        near, far = join_first(grads[:, y * 384:(y + 1) * 384])
        part = mm_back(near, block_of(pair, y, slice(0, 256))) + mm_back(far, block_of(pair, y, slice(384, 640)))
        out = part if out is None else out + part
    return out


def back_second(grads, pair):
    out = None
    for y in range(2):
        near, far = join_second(grads[:, y * 384:(y + 1) * 384])
        part = mm_back(near, block_of(pair, y, slice(128, 384))) + mm_back(far, block_of(pair, y, slice(512, 768)))
        out = part if out is None else out + part
    return out


def outer_second(out, inputs, grads):
    for y in range(2):
        near, far = join_second(grads[:, y * 384:(y + 1) * 384])
        out[y, :, 128:384] = mm_rows(inputs, near).astype(jnp.bfloat16)
        out[y, :, 512:768] = mm_rows(inputs, far).astype(jnp.bfloat16)


def outer_first_after(out, inputs, grads):
    for y in range(2):
        near, far = join_first(grads[:, y * 384:(y + 1) * 384])
        near, far = mm_rows(inputs, near), mm_rows(inputs, far)
        out[y, :, 0:128] = tile_of(near, 0).astype(jnp.bfloat16)
        out[y, :, 128:256] = (out[y, :, 128:256].astype(jnp.float32) + tile_of(near, 1)).astype(jnp.bfloat16)
        out[y, :, 384:512] = tile_of(far, 0).astype(jnp.bfloat16)
        out[y, :, 512:640] = (out[y, :, 512:640].astype(jnp.float32) + tile_of(far, 1)).astype(jnp.bfloat16)


def normed(values, gain, bias):
    return norm_rows(values, gain, bias).astype(jnp.bfloat16)


def normed_back(values, gain, grads):
    centre = values - jnp.mean(values, axis=-1, keepdims=True)
    scale = lax.rsqrt(jnp.mean(centre * centre, axis=-1, keepdims=True) + EPS)
    unit = centre * scale
    inner = grads * gain
    back = scale * (
        inner - jnp.mean(inner, axis=-1, keepdims=True) - unit * jnp.mean(inner * unit, axis=-1, keepdims=True)
    )
    return back, jnp.sum(grads * unit, axis=0, keepdims=True), jnp.sum(grads, axis=0, keepdims=True)


def column_sum(values):
    return jnp.sum(values.astype(jnp.float32), axis=0, keepdims=True)


def stacked(values, t, pair):
    both = values[t, :, pair * 128:(pair + 1) * 128]
    low = low_lanes(both.shape[0])
    nothing = jnp.zeros_like(both)
    return jnp.concatenate([jnp.where(low, both, nothing), jnp.where(low, nothing, both)], axis=0)


def unstacked(values):
    half = values.shape[0] // 2
    return jnp.where(low_lanes(half), values[:half], values[half:])


CHUNK = 16


def soften(scores, bias, chances, rows):
    def one(number, carry):
        first = pl.multiple_of(number * CHUNK, CHUNK)
        values = scores[pl.ds(first, CHUNK), :] + bias(first)
        raised = jnp.exp(values - jnp.max(values, axis=1, keepdims=True))
        share = raised * (1.0 / jnp.sum(raised, axis=1, keepdims=True))
        chances[pl.ds(first, CHUNK), :] = share.astype(jnp.bfloat16)
        return carry

    lax.fori_loop(0, rows // CHUNK, one, 0, unroll=2)


def soften_back(chances, slopes, grads, rows):
    def one(number, carry):
        first = pl.multiple_of(number * CHUNK, CHUNK)
        share = chances[pl.ds(first, CHUNK), :].astype(jnp.float32)
        slope = slopes[pl.ds(first, CHUNK), :]
        inner = jnp.sum(share * slope, axis=1, keepdims=True)
        grads[pl.ds(first, CHUNK), :] = (share * (slope - inner)).astype(jnp.bfloat16)
        return carry

    lax.fori_loop(0, rows // CHUNK, one, 0, unroll=2)


def self_forward(lengths, tokens, vec, qk, vo, q_out, k_out, v_out, a_out, o_out, h1_out, c_out, p_out, a_all, scores, bias):
    span = tokens.shape[2]
    seq = lax.axis_index("seq")
    factor = 1.0 / math.sqrt(HEAD_DIM)
    for s in range(4):
        for t in range(2):
            a_all[t, s] = normed(tokens[s, t].astype(jnp.float32), vec[0:1], vec[1:2])
    for t in range(2):
        row = lax.broadcasted_iota(jnp.int32, (span, 512), 0)
        lane = lax.broadcasted_iota(jnp.int32, (span, 512), 1)
        inside = lax.bitwise_and(lane, 127)
        place = lax.shift_right_logical(lane, 7) * span + inside
        good = (inside < span) & (place <= row + seq * span) & (place < lengths[t])
        block = jnp.where(good, 0.0, NEG)
        bias[t, 0:span] = block
        bias[t, span:2 * span] = block
    yield
    for t in range(2):
        a_out[t] = a_all[t, seq]
        rows = a_all[t].reshape(4 * span, 768)
        for number, tile in enumerate(times_second(rows, qk)):
            tile = tile.astype(jnp.bfloat16)
            for s in range(4):
                k_out[t, s, 0:span, number * 128:(number + 1) * 128] = tile[s * span:(s + 1) * span]
        yield
        for number, tile in enumerate(times_first(rows, vo)):
            at = slice(number * 128, (number + 1) * 128)
            tile = (tile + vec[3:4, at]).astype(jnp.bfloat16)
            for s in range(4):
                v_out[t, s, 0:span, at] = tile[s * span:(s + 1) * span]
        for s in range(4):
            k_out[t, s, span:128, :] = jnp.zeros((128 - span, 768), jnp.bfloat16)
            v_out[t, s, span:128, :] = jnp.zeros((128 - span, 768), jnp.bfloat16)
        yield
    own = a_out[...].reshape(2 * span, 768)
    for number, tile in enumerate(times_first(own, qk)):
        at = slice(number * 128, (number + 1) * 128)
        tile = ((tile + vec[2:3, at]) * factor).astype(jnp.bfloat16)
        for t in range(2):
            q_out[t, :, at] = tile[t * span:(t + 1) * span]
    yield
    for t in range(2):
        for pair in range(6):
            at = slice(pair * 128, (pair + 1) * 128)
            scores[...] = mm_back(stacked(q_out, t, pair), k_out[t, :, :, at].reshape(512, 128))
            chances = p_out.at[t, pair]
            soften(scores, lambda first: bias[t, pl.ds(first, CHUNK), :], chances, 2 * span)
            o_out[t, :, at] = unstacked(mm(chances[...], v_out[t, :, :, at].reshape(512, 128))).astype(jnp.bfloat16)
            yield
    out = o_out[...].reshape(2 * span, 768)
    for number, tile in enumerate(times_second(out, vo)):
        at = slice(number * 128, (number + 1) * 128)
        for t in range(2):
            h1_out[t, :, at] = (
                tokens[seq, t, :, at].astype(jnp.float32) + tile[t * span:(t + 1) * span] + vec[4:5, at]
            )
    for t in range(2):
        c_out[t] = normed(h1_out[t], vec[5:6], vec[6:7])
    yield


def cross_keys(frames, vec, kv, ck_out, cv_out):
    for t in range(2):
        for s in range(4):
            block = frames[t, s]
            rows = slice(s * 384, (s + 1) * 384)
            for y in range(2):
                product = mm(block, block_of(kv, y, slice(0, 768)))
                near, far = product[:, 0:384], product[:, 384:768]
                keys = split_first(near[:, 0:256], far[:, 0:256])
                values = split_second(near[:, 128:384], far[:, 128:384])
                for place in range(3):
                    at = slice(y * 384 + place * 128, y * 384 + (place + 1) * 128)
                    ck_out[t, rows, at] = keys[place].astype(jnp.bfloat16)
                    cv_out[t, rows, at] = (values[place] + vec[8:9, at]).astype(jnp.bfloat16)
            yield


def cross_forward(counts, frame_span, c, vec, xqo, ck, cv, h1, cq_out, o2_out, h2_out, m_out, p_out, scores, bias):
    span = c.shape[1]
    factor = 1.0 / math.sqrt(HEAD_DIM)
    rows = c[...].reshape(2 * span, 768)
    for number, tile in enumerate(times_first(rows, xqo)):
        at = slice(number * 128, (number + 1) * 128)
        tile = ((tile + vec[7:8, at]) * factor).astype(jnp.bfloat16)
        for t in range(2):
            cq_out[t, :, at] = tile[t * span:(t + 1) * span]
    for t in range(2):
        for s in range(4):
            inside = lax.broadcasted_iota(jnp.int32, (1, 384), 1)
            good = (inside < frame_span) & (s * frame_span + inside < counts[t])
            bias[t, :, s * 384:(s + 1) * 384] = jnp.where(good, 0.0, NEG)
    yield
    for t in range(2):
        for pair in range(6):
            at = slice(pair * 128, (pair + 1) * 128)
            scores[...] = mm_back(stacked(cq_out, t, pair), ck[t, :, at])
            chances = p_out.at[t, pair]
            soften(scores, lambda first: bias[t], chances, 2 * span)
            o2_out[t, :, at] = unstacked(mm(chances[...], cv[t, :, at])).astype(jnp.bfloat16)
            yield
    out = o2_out[...].reshape(2 * span, 768)
    for number, tile in enumerate(times_second(out, xqo)):
        at = slice(number * 128, (number + 1) * 128)
        for t in range(2):
            h2_out[t, :, at] = h1[t, :, at] + tile[t * span:(t + 1) * span] + vec[9:10, at]
    for t in range(2):
        m_out[t] = normed(h2_out[t], vec[10:11], vec[11:12])
    yield


def feed_forward(
    lengths, ids, weights, cotangent, vec, wide_bias, wide, tall, h2, m,
    y_out, dh2_out, wide_grad, tall_grad, small_out, wide_small, dy, z_sum, dm_sum,
):
    span = m.shape[1]
    seq = lax.axis_index("seq")
    for t in range(2):
        weight = 0.0
        for corpus in range(weights.shape[0]):
            weight = weight + jnp.where(ids[t] == corpus, weights[corpus], 0.0)
        row = lax.broadcasted_iota(jnp.int32, (span, 1), 0) + seq * span
        scale = jnp.where(row < lengths[t], weight, 0.0)
        dy[t * span:(t + 1) * span] = cotangent[t].astype(jnp.float32) * scale
    dz = dy[...].astype(jnp.bfloat16)
    rows = m[...].reshape(2 * span, 768)
    small_out[0:1] = column_sum(dz)
    z_sum[...] = jnp.zeros_like(z_sum)
    dm_sum[...] = jnp.zeros_like(dm_sum)

    def one(number, carry):
        at = lanes(number * 768, 768)
        hidden = mm(rows, wide[:, at]) + wide_bias[:, at]
        bell = 0.5 * (1.0 + lax.erf(hidden * 0.7071067811865476))
        gate = (hidden * bell).astype(jnp.bfloat16)
        z_sum[...] += mm_back(gate, tall[:, at])
        slope = bell + hidden * (jnp.exp(-0.5 * hidden * hidden) * 0.3989422804014327)
        back = (mm(dz, tall[:, at]) * slope).astype(jnp.bfloat16)
        dm_sum[...] += mm_back(back, wide[:, at])
        tall_grad[:, at] = mm_rows(dz, gate).astype(jnp.bfloat16)
        wide_grad[:, at] = mm_rows(rows, back).astype(jnp.bfloat16)
        wide_small[:, at] = column_sum(back)
        return carry

    lax.fori_loop(0, 4, one, 0)
    h2_rows = h2[...].reshape(2 * span, 768)
    out = h2_rows + z_sum[...] + vec[12:13]
    back, gain, offset = normed_back(h2_rows, vec[10:11], dm_sum[...])
    small_out[1:2] = gain
    small_out[2:3] = offset
    result = dy[...] + back
    for t in range(2):
        y_out[t] = out[t * span:(t + 1) * span].astype(jnp.bfloat16)
        dh2_out[t] = result[t * span:(t + 1) * span]


def cross_back(dh2, o2, c, h1, cq, ck, cv, p, vec, xqo, dh1_out, dkt_out, dvt_out, grad_out, small_out, do, dq, scores, dscores):
    span = c.shape[1]
    factor = 1.0 / math.sqrt(HEAD_DIM)
    dh2_rows = dh2[...].reshape(2 * span, 768)
    low_rows = dh2_rows.astype(jnp.bfloat16)
    low_wide = low_rows.astype(jnp.float32)
    small_out[0:1] = column_sum(low_wide)
    heard = back_second(low_wide, xqo)
    small_out[1:2] = column_sum(heard.astype(jnp.bfloat16))
    for t in range(2):
        do[t] = heard[t * span:(t + 1) * span].astype(jnp.bfloat16)
    outer_second(grad_out, o2[...].reshape(2 * span, 768), low_wide)
    for t in range(2):
        def one(pair, carry):
            at = lanes(pair * 128, 128)
            low = low_lanes(span)

            def both_heads(ref):
                both = ref[t, :, at]
                nothing = jnp.zeros_like(both)
                return jnp.concatenate([jnp.where(low, both, nothing), jnp.where(low, nothing, both)], axis=0)

            slopes, query = both_heads(do), both_heads(cq)
            scores[...] = mm_back(slopes, cv[t, :, at])
            chances = p.at[t, pair]
            soften_back(chances, scores, dscores, 2 * span)
            dq[t, :, at] = unstacked(mm(dscores[...], ck[t, :, at])) * factor
            first = pl.multiple_of(pair * 128, 128)
            dkt_out[t, pl.ds(first, 128), :] = mm_rows(query, dscores[...]).astype(jnp.bfloat16)
            dvt_out[t, pl.ds(first, 128), :] = mm_rows(slopes, chances[...]).astype(jnp.bfloat16)
            return carry

        lax.fori_loop(0, 6, one, 0)
    low_q = dq[...].reshape(2 * span, 768).astype(jnp.bfloat16)
    wide_q = low_q.astype(jnp.float32)
    small_out[2:3] = column_sum(wide_q)
    outer_first_after(grad_out, c[...].reshape(2 * span, 768), wide_q)
    back, gain, offset = normed_back(h1[...].reshape(2 * span, 768), vec[5:6], back_first(wide_q, xqo))
    small_out[3:4] = gain
    small_out[4:5] = offset
    for t in range(2):
        dh1_out[t] = dh2[t] + back[t * span:(t + 1) * span]


def cross_key_grads(dkt, dvt, frames, grad_out):
    for y in range(2):
        at = slice(y * 384, (y + 1) * 384)
        keys = mm(dkt[0, at, :], frames[0]) + mm(dkt[1, at, :], frames[1])
        values = mm(dvt[0, at, :], frames[0]) + mm(dvt[1, at, :], frames[1])
        grad_out[y] = join_both(keys.T, values.T)


def self_back(dh1, q, k, v, p, o, vo, dq_out, dkt_out, dvt_out, grad_out, small_out, do, scores, dscores):
    span = q.shape[1]
    factor = 1.0 / math.sqrt(HEAD_DIM)
    low_wide = dh1[...].reshape(2 * span, 768).astype(jnp.bfloat16).astype(jnp.float32)
    small_out[0:1] = column_sum(low_wide)
    heard = back_second(low_wide, vo)
    for t in range(2):
        do[t] = heard[t * span:(t + 1) * span].astype(jnp.bfloat16)
    outer_second(grad_out, o[...].reshape(2 * span, 768), low_wide)
    for t in range(2):
        for pair in range(6):
            at = slice(pair * 128, (pair + 1) * 128)
            slopes, query = stacked(do, t, pair), stacked(q, t, pair)
            scores[...] = mm_back(slopes, v[t, :, :, at].reshape(512, 128))
            chances = p.at[t, pair]
            soften_back(chances, scores, dscores, 2 * span)
            dq_out[t, :, at] = (unstacked(mm(dscores[...], k[t, :, :, at].reshape(512, 128))) * factor).astype(
                jnp.bfloat16
            )
            keys = mm_rows(query, dscores[...]).astype(jnp.bfloat16)
            values = mm_rows(slopes, chances[...]).astype(jnp.bfloat16)
            for s in range(4):
                dkt_out[s, t, at, :] = keys[:, s * 128:(s + 1) * 128]
                dvt_out[s, t, at, :] = values[:, s * 128:(s + 1) * 128]


def self_finish(tokens, dh1, a, dq, dkt, dvt, vec, qk, vo, vo_grad_in, dx_out, qk_grad, vo_grad, small_out, dk, dv):
    span = a.shape[1]
    for t in range(2):
        dk[t * span:(t + 1) * span] = dkt[t].astype(jnp.float32).T[0:span]
        dv[t * span:(t + 1) * span] = dvt[t].astype(jnp.float32).T[0:span]
    inputs = a[...].reshape(2 * span, 768)
    wide_q = dq[...].reshape(2 * span, 768).astype(jnp.float32)
    small_out[0:1] = column_sum(wide_q)
    small_out[1:2] = column_sum(dv[...])
    vo_grad[...] = vo_grad_in[...]
    outer_first_after(vo_grad, inputs, dv[...])
    back = back_first(dv[...], vo)
    for y in range(2):
        at = slice(y * 384, (y + 1) * 384)
        both = join_both(wide_q[:, at], dk[:, at])
        qk_grad[y] = mm_rows(inputs, both).astype(jnp.bfloat16)
        back = back + mm_back(both, qk[y])
    for t in range(2):
        part, gain, offset = normed_back(
            tokens[t].astype(jnp.float32), vec[0:1], back[t * span:(t + 1) * span]
        )
        dx_out[t] = (dh1[t] + part).astype(jnp.bfloat16)
        if t == 0:
            small_out[2:3] = gain
            small_out[3:4] = offset
        else:
            small_out[2:3] += gain
            small_out[3:4] += offset


def call(body, name, scalars, arrays, shapes, scratch):
    inside = pl.BlockSpec(memory_space=pltpu.VMEM)
    return pl.pallas_call(
        body,
        out_shape=tuple(jax.ShapeDtypeStruct(shape, kind) for shape, kind in shapes),
        in_specs=[pl.BlockSpec(memory_space=pltpu.SMEM)] * len(scalars) + [inside] * len(arrays),
        out_specs=(inside,) * len(shapes),
        scratch_shapes=[pltpu.VMEM(shape, kind) for shape, kind in scratch],
        compiler_params=pltpu.CompilerParams(vmem_limit_bytes=60 << 20),
        name=name,
    )(*scalars, *arrays)


def mixed(first, second, core):
    even = joined(joined(first[:, :128], joined(first[:, 128:], second[:, 128:])), second[:, :128])
    odd = joined(joined(first[:, 64:], joined(second[:, :64], first[:, :64])), second[:, 64:])
    return jnp.where(core == 0, even, odd)


def unmixed(piece, core):
    first = jnp.where(core == 0, piece[:, :192], joined(piece[:, 192:256], piece[:, :128]))
    second = jnp.where(
        core == 0, joined(piece[:, 256:], piece[:, 192:256]), joined(piece[:, 128:192], piece[:, 256:])
    )
    return first, second


def on_device_fast(*arguments):
    (
        tokens, encoder_states, lengths, frame_counts, corpus_ids, corpus_weights, cotangent,
        first_gain, first_bias, query_weight, query_bias, key_weight, value_weight, value_bias,
        output_weight, output_bias, second_gain, second_bias, cross_query_weight, cross_query_bias,
        cross_key_weight, cross_value_weight, cross_value_bias, cross_output_weight, cross_output_bias,
        third_gain, third_bias, expand_weight, expand_bias, reduce_weight, reduce_bias,
    ) = arguments
    bf16, f32 = jnp.bfloat16, jnp.float32
    core = lax.rem(lax.axis_index("seq"), NC)
    frame_span = encoder_states.shape[1]
    span = tokens.shape[1]
    small_vectors = (
        first_gain, first_bias, query_bias, value_bias, output_bias, second_gain, second_bias,
        cross_query_bias, cross_value_bias, cross_output_bias, third_gain, third_bias, reduce_bias, expand_bias,
    )
    small = jnp.concatenate([
        jnp.pad(jnp.stack(small_vectors[:13]), ((0, 3), (0, 32))), jnp.pad(expand_bias.reshape(3, 128), ((0, 13), (0, 0)))
    ])
    pairs = jnp.stack([
        mixed(query_weight, key_weight, core),
        mixed(value_weight, output_weight, core),
        mixed(cross_key_weight, cross_value_weight, core),
        mixed(cross_query_weight, cross_output_weight, core),
    ])
    frames_padded = jnp.pad(encoder_states, ((0, 0), (0, 384 - frame_span), (0, 0)))
    (
        pairs_all, wide_all, tall_all, frames_all, vec, wide_bias,
        q, k, v, a, o, h1, c, p_self, ck, cv, cq, o2, h2, m, p_cross,
    ) = run_forward(
        frame_span, lengths, frame_counts, pairs, expand_weight, reduce_weight.T, small, frames_padded, tokens
    )
    pairs_all = pairs_all.reshape(4, NY, 768, 768)
    w_qk, w_vo, w_kv, w_xqo = [pairs_all[p] for p in range(4)]
    wide = wide_all.reshape(768, 3072)
    tall = tall_all.reshape(768, 3072)
    rows3 = (2, span, 768)
    layer_output, dh2, wide_grads, tall_grads, small_ff, wide_small = call(
        feed_forward, "feed_forward", [lengths, corpus_ids, corpus_weights],
        [cotangent, vec, wide_bias, wide, tall, h2, m],
        [
            (rows3, bf16), (rows3, f32), ((768, 3072), bf16), ((768, 3072), bf16), ((8, 768), f32), ((1, 3072), f32),
        ],
        [((2 * span, 768), f32)] * 3,
    )
    dh1, dck, dcv, grad_xqo, small_cross = call(
        cross_back, "cross_back", [], [dh2, o2, c, h1, cq, ck, cv, p_cross, vec, w_xqo],
        [
            (rows3, f32), ((2, 768, 1536), bf16), ((2, 768, 1536), bf16), ((2, 768, 768), bf16), ((8, 768), f32),
        ],
        [(rows3, bf16), (rows3, f32), ((2 * span, 1536), f32), ((2 * span, 1536), bf16)],
    )
    (grad_kv,) = call(
        cross_key_grads, "cross_key_grads", [], [dck, dcv, frames_all.reshape(2, 1536, 768)],
        [((2, 768, 768), bf16)], [],
    )
    dq, dkt, dvt, grad_o, small_self = call(
        self_back, "self_back", [], [dh1, q, k, v, p_self, o, w_vo],
        [
            (rows3, bf16), ((4, 2, 768, 128), bf16), ((4, 2, 768, 128), bf16), ((2, 768, 768), bf16), ((8, 768), f32),
        ],
        [(rows3, bf16), ((2 * span, 512), f32), ((2 * span, 512), bf16)],
    )
    dkt, dvt = (
        lax.psum_scatter(dkt, "seq", scatter_dimension=0, tiled=False),
        lax.psum_scatter(dvt, "seq", scatter_dimension=0, tiled=False),
    )
    tokens_gradient, grad_qk, grad_vo, small_last = call(
        self_finish, "self_finish", [], [tokens, dh1, a, dq, dkt, dvt, vec, w_qk, w_vo, grad_o],
        [(rows3, bf16), ((2, 768, 768), bf16), ((2, 768, 768), bf16), ((8, 768), f32)],
        [((2 * span, 768), f32), ((2 * span, 768), f32)],
    )
    pair_grads = jnp.stack([grad_qk, grad_vo, grad_kv, grad_xqo]).reshape(4, NY, NZ, NX, 96, 768)
    small_grads = jnp.concatenate([
        small_last[2:4], small_last[0:2], small_self[0:1], small_cross[3:5], small_cross[2:3], small_cross[1:2],
        small_cross[0:1], small_ff[1:3], small_ff[0:1],
    ])
    small_flat = jnp.concatenate(
        [small_grads.reshape(13, 8, 96).transpose(1, 0, 2).reshape(8, 13 * 96), wide_small.reshape(8, 384)], axis=1
    )
    small_flat = jnp.pad(small_flat, ((0, 0), (0, 2048 - 17 * 96))).reshape(8, 16, 128)
    total, small_total = reduce_everything(
        pair_grads, wide_grads.reshape(NZ, NX, 96, 3072), tall_grads.reshape(NY, NC, 192, 3072), small_flat
    )
    (m_query, m_key), (m_value, m_mixer), (m_xkey, m_xvalue), (m_xquery, m_xmixer) = [
        unmixed(total[p], core) for p in range(4)
    ]
    expand_grad = jnp.concatenate([total[4], total[5]], axis=1)
    reduce_grad = jnp.concatenate([total[6], total[7]], axis=0).T
    flat_total = small_total.reshape(-1)
    smaller = [flat_total[i * 96:(i + 1) * 96] for i in range(13)]
    expand_bias_grad = flat_total[13 * 96:17 * 96]
    return (
        layer_output, tokens_gradient, smaller[0], smaller[1], m_query, smaller[2], m_key, m_value, smaller[3],
        m_mixer, smaller[4], smaller[5], smaller[6], m_xquery, smaller[7], m_xkey, m_xvalue, smaller[8],
        m_xmixer, smaller[9], smaller[10], smaller[11], expand_grad, expand_bias_grad, reduce_grad, smaller[12],
    )


def solution(mesh):
    placed = (
        P("grp", "seq", None),
        P("grp", "seq", None),
        P("grp"),
        P("grp"),
        P("grp"),
        P(),
        P("grp", "seq", None),
        P("grp"),
        P("grp"),
        P("grp", "seq"),
        P("grp"),
        P("grp", "seq"),
        P("grp", "seq"),
        P("grp"),
        P("grp", "seq"),
        P("grp"),
        P("grp"),
        P("grp"),
        P("grp", "seq"),
        P("grp"),
        P("grp", "seq"),
        P("grp", "seq"),
        P("grp"),
        P("grp", "seq"),
        P("grp"),
        P("grp"),
        P("grp"),
        P("grp", "seq"),
        P("grp"),
        P("grp", "seq"),
        P("grp"),
    )
    small_slice = mesh.shape["grp"] == NZ * NX and mesh.shape["seq"] == NY * NC
    return jax.shard_map(
        on_device_fast if small_slice else on_device_plain,
        mesh=mesh,
        in_specs=placed,
        out_specs=(
            P("grp", "seq", None),
            P("grp", "seq", None),
            P("grp"),
            P("grp"),
            P("grp", "seq"),
            P("grp"),
            P("grp", "seq"),
            P("grp", "seq"),
            P("grp"),
            P("grp", "seq"),
            P("grp"),
            P("grp"),
            P("grp"),
            P("grp", "seq"),
            P("grp"),
            P("grp", "seq"),
            P("grp", "seq"),
            P("grp"),
            P("grp", "seq"),
            P("grp"),
            P("grp"),
            P("grp"),
            P("grp", "seq"),
            P("grp"),
            P("grp", "seq"),
            P("grp"),
        ),
        check_vma=False,
    )
```

```python
import math

import jax
import jax.numpy as jnp
from jax import lax
from jax.experimental import pallas as pl
from jax.experimental.pallas import tpu as pltpu
from jax.sharding import PartitionSpec as P

HEADS = 12
HEAD_DIM = 64


NEG = -1e30
EPS = 1e-05


def norm_rows(values, scaling, offset):
    centre = values - jnp.mean(values, axis=-1, keepdims=True)
    spread = jnp.mean(centre * centre, axis=-1, keepdims=True)
    return centre * lax.rsqrt(spread + EPS) * scaling + offset


def smooth_gate(values):
    return 0.5 * values * (1.0 + lax.erf(values * 0.7071067811865476))


def linear(inputs, weight):
    return jnp.einsum("bri,ij->brj", inputs, weight, preferred_element_type=jnp.float32)


def linear_back(gradient, weight):
    return jnp.einsum("brj,ij->bri", gradient, weight, preferred_element_type=jnp.float32)


def outer_sum(inputs, gradient):
    return jnp.einsum("bri,brj->ij", inputs, gradient, preferred_element_type=jnp.float32)


def row_total(gradient):
    return jnp.sum(gradient.astype(jnp.float32), axis=(0, 1))


def split_heads(values):
    return values.reshape(values.shape[0], values.shape[1], HEADS, HEAD_DIM)


def scores_of(query, key_rows, allowed):
    scores = jnp.einsum(
        "bqhd,bkhd->bhqk",
        split_heads(query),
        split_heads(key_rows),
        preferred_element_type=jnp.float32,
    )
    return jnp.where(allowed[:, None], scores, NEG)


def attend(query, key_rows, values, allowed):
    scores = scores_of(query, key_rows, allowed)
    maximum = jnp.max(scores, axis=-1, keepdims=True)
    raised = jnp.exp(scores - maximum)
    summed = jnp.sum(raised, axis=-1, keepdims=True)
    chances = (raised / summed).astype(jnp.bfloat16)
    blended = jnp.einsum(
        "bhqk,bkhd->bqhd", chances, split_heads(values), preferred_element_type=jnp.float32
    )
    return (blended.reshape(query.shape).astype(jnp.bfloat16), maximum + jnp.log(summed))


def attend_back(grad_low, query, key_rows, values, allowed, logsum):
    scores = scores_of(query, key_rows, allowed)
    chances = jnp.exp(scores - logsum)
    grad_heads = split_heads(grad_low)
    grad_chance = jnp.einsum(
        "bqhd,bkhd->bhqk", grad_heads, split_heads(values), preferred_element_type=jnp.float32
    )
    offset = jnp.sum(chances * grad_chance, axis=-1, keepdims=True)
    grad_score = (chances * (grad_chance - offset)).astype(jnp.bfloat16)
    grad_query = jnp.einsum(
        "bhqk,bkhd->bqhd", grad_score, split_heads(key_rows), preferred_element_type=jnp.float32
    )
    grad_keys = jnp.einsum(
        "bhqk,bqhd->bkhd", grad_score, split_heads(query), preferred_element_type=jnp.float32
    )
    grad_values = jnp.einsum(
        "bhqk,bqhd->bkhd",
        chances.astype(jnp.bfloat16),
        grad_heads,
        preferred_element_type=jnp.float32,
    )
    return (
        grad_query.reshape(query.shape),
        grad_keys.reshape(key_rows.shape),
        grad_values.reshape(values.shape),
    )


def on_device_plain(
    tokens,
    encoder_states,
    lengths,
    frame_counts,
    corpus_ids,
    corpus_weights,
    cotangent,
    first_gain,
    first_bias,
    query_weight,
    query_bias,
    key_weight,
    value_weight,
    value_bias,
    output_weight,
    output_bias,
    second_gain,
    second_bias,
    cross_query_weight,
    cross_query_bias,
    cross_key_weight,
    cross_value_weight,
    cross_value_bias,
    cross_output_weight,
    cross_output_bias,
    third_gain,
    third_bias,
    expand_weight,
    expand_bias,
    reduce_weight,
    reduce_bias,
):
    row_parts = (
        lax.all_gather(query_weight, "grp", axis=0, tiled=True),
        lax.all_gather(key_weight, "grp", axis=0, tiled=True),
        lax.all_gather(value_weight, "grp", axis=0, tiled=True),
        lax.all_gather(output_weight, "grp", axis=0, tiled=True),
        lax.all_gather(cross_query_weight, "grp", axis=0, tiled=True),
        lax.all_gather(cross_key_weight, "grp", axis=0, tiled=True),
        lax.all_gather(cross_value_weight, "grp", axis=0, tiled=True),
        lax.all_gather(cross_output_weight, "grp", axis=0, tiled=True),
        lax.all_gather(expand_weight, "grp", axis=0, tiled=True),
        lax.all_gather(reduce_weight, "grp", axis=0, tiled=True),
        lax.all_gather(first_gain, "grp", axis=0, tiled=True),
        lax.all_gather(first_bias, "grp", axis=0, tiled=True),
        lax.all_gather(query_bias, "grp", axis=0, tiled=True),
        lax.all_gather(value_bias, "grp", axis=0, tiled=True),
        lax.all_gather(output_bias, "grp", axis=0, tiled=True),
        lax.all_gather(second_gain, "grp", axis=0, tiled=True),
        lax.all_gather(second_bias, "grp", axis=0, tiled=True),
        lax.all_gather(cross_query_bias, "grp", axis=0, tiled=True),
        lax.all_gather(cross_value_bias, "grp", axis=0, tiled=True),
        lax.all_gather(cross_output_bias, "grp", axis=0, tiled=True),
        lax.all_gather(third_gain, "grp", axis=0, tiled=True),
        lax.all_gather(third_bias, "grp", axis=0, tiled=True),
        lax.all_gather(expand_bias, "grp", axis=0, tiled=True),
        lax.all_gather(reduce_bias, "grp", axis=0, tiled=True),
    )
    gathered = (
        lax.all_gather(row_parts[0], "seq", axis=1, tiled=True),
        lax.all_gather(row_parts[1], "seq", axis=1, tiled=True),
        lax.all_gather(row_parts[2], "seq", axis=1, tiled=True),
        lax.all_gather(row_parts[3], "seq", axis=1, tiled=True),
        lax.all_gather(row_parts[4], "seq", axis=1, tiled=True),
        lax.all_gather(row_parts[5], "seq", axis=1, tiled=True),
        lax.all_gather(row_parts[6], "seq", axis=1, tiled=True),
        lax.all_gather(row_parts[7], "seq", axis=1, tiled=True),
        lax.all_gather(row_parts[8], "seq", axis=1, tiled=True),
        lax.all_gather(row_parts[9], "seq", axis=1, tiled=True),
    )
    w_query, w_key, w_value, w_mixer, x_query, x_key, x_value, x_mixer, w_expand, w_reduce = (
        gathered
    )
    vectors = [piece.astype(jnp.float32) for piece in row_parts[10:]]
    factor = 1.0 / math.sqrt(HEAD_DIM)
    seq_count = lax.axis_size("seq")
    span_rows = tokens.shape[1]
    query_pos = lax.axis_index("seq") * span_rows + jnp.arange(span_rows, dtype=jnp.int32)
    key_pos = jnp.arange(span_rows * seq_count, dtype=jnp.int32)
    self_mask = (key_pos[None, None, :] <= query_pos[None, :, None]) & (
        key_pos[None, None, :] < lengths[:, None, None]
    )
    frame_pos = jnp.arange(encoder_states.shape[1] * seq_count, dtype=jnp.int32)
    cross_mask = frame_pos[None, None, :] < frame_counts[:, None, None]
    layer_in = tokens.astype(jnp.float32)
    normed_one, norm_back_one = jax.vjp(norm_rows, layer_in, vectors[0], vectors[1])
    normed_one = normed_one.astype(jnp.bfloat16)
    query_low = ((linear(normed_one, w_query) + vectors[2]) * factor).astype(jnp.bfloat16)
    key_low = linear(normed_one, w_key).astype(jnp.bfloat16)
    value_low = (linear(normed_one, w_value) + vectors[3]).astype(jnp.bfloat16)
    key_all, value_all = (
        lax.all_gather(key_low, "seq", axis=1, tiled=True),
        lax.all_gather(value_low, "seq", axis=1, tiled=True),
    )
    self_out, self_logsum = attend(query_low, key_all, value_all, self_mask)
    after_self = layer_in + linear(self_out, w_mixer) + vectors[4]
    normed_two, norm_back_two = jax.vjp(norm_rows, after_self, vectors[5], vectors[6])
    normed_two = normed_two.astype(jnp.bfloat16)
    cross_query = ((linear(normed_two, x_query) + vectors[7]) * factor).astype(jnp.bfloat16)
    frames_all = lax.all_gather(encoder_states, "seq", axis=1, tiled=True)
    cross_keys_all = linear(frames_all, x_key).astype(jnp.bfloat16)
    cross_values_all = (linear(frames_all, x_value) + vectors[8]).astype(jnp.bfloat16)
    cross_out, cross_logsum = attend(cross_query, cross_keys_all, cross_values_all, cross_mask)
    after_cross = after_self + linear(cross_out, x_mixer) + vectors[9]
    normed_three, norm_back_three = jax.vjp(norm_rows, after_cross, vectors[10], vectors[11])
    normed_three = normed_three.astype(jnp.bfloat16)
    hidden = linear(normed_three, w_expand) + vectors[12]
    gated, gate_back = jax.vjp(smooth_gate, hidden)
    gated_low = gated.astype(jnp.bfloat16)
    result = after_cross + linear(gated_low, w_reduce) + vectors[13]
    layer_output = result.astype(jnp.bfloat16)
    present = (query_pos[None, :] < lengths[:, None]).astype(jnp.float32)
    corpus_index = jnp.arange(corpus_weights.shape[0], dtype=jnp.int32)
    corpus_scale = jnp.sum(
        jnp.where(corpus_ids[:, None] == corpus_index[None, :], corpus_weights[None, :], 0.0),
        axis=1,
    )
    grad_out = cotangent.astype(jnp.float32) * (present * corpus_scale[:, None])[:, :, None]
    reduce_low = grad_out.astype(jnp.bfloat16)
    slope_reduce_bias = row_total(reduce_low)
    slope_reduce = outer_sum(gated_low, reduce_low)
    grad_hidden = gate_back(linear_back(reduce_low, w_reduce))[0]
    hidden_low = grad_hidden.astype(jnp.bfloat16)
    slope_expand_bias = row_total(hidden_low)
    slope_expand = outer_sum(normed_three, hidden_low)
    grad_norm_in, slope_gain_three, slope_bias_three = norm_back_three(
        linear_back(hidden_low, w_expand)
    )
    grad_cross = grad_out + grad_norm_in
    cross_low = grad_cross.astype(jnp.bfloat16)
    slope_xmixer_bias = row_total(cross_low)
    slope_xmixer = outer_sum(cross_out, cross_low)
    grad_heard = linear_back(cross_low, x_mixer).astype(jnp.bfloat16)
    grad_cq, part_ck, part_cv = attend_back(
        grad_heard, cross_query, cross_keys_all, cross_values_all, cross_mask, cross_logsum
    )
    slope_xkey = outer_sum(frames_all, part_ck)
    slope_xvalue = outer_sum(frames_all, part_cv)
    slope_xvalue_bias = row_total(part_cv)
    low_cq = (grad_cq * factor).astype(jnp.bfloat16)
    slope_xquery_bias = row_total(low_cq)
    slope_xquery = outer_sum(normed_two, low_cq)
    grad_norm_two, slope_gain_two, slope_bias_two = norm_back_two(linear_back(low_cq, x_query))
    grad_self = grad_cross + grad_norm_two
    self_low = grad_self.astype(jnp.bfloat16)
    slope_mixer_bias = row_total(self_low)
    slope_mixer = outer_sum(self_out, self_low)
    grad_mixed = linear_back(self_low, w_mixer).astype(jnp.bfloat16)
    grad_q, part_k, part_v = attend_back(
        grad_mixed, query_low, key_all, value_all, self_mask, self_logsum
    )
    summed_k, summed_v = (
        lax.psum_scatter(
            part_k.astype(jnp.bfloat16), "seq", scatter_dimension=1, tiled=True
        ).astype(jnp.float32),
        lax.psum_scatter(
            part_v.astype(jnp.bfloat16), "seq", scatter_dimension=1, tiled=True
        ).astype(jnp.float32),
    )
    low_k = summed_k.astype(jnp.bfloat16)
    low_v = summed_v.astype(jnp.bfloat16)
    low_q = (grad_q * factor).astype(jnp.bfloat16)
    slope_query = outer_sum(normed_one, low_q)
    slope_query_bias = row_total(low_q)
    slope_key = outer_sum(normed_one, low_k)
    slope_value = outer_sum(normed_one, low_v)
    slope_value_bias = row_total(low_v)
    grad_normed = (
        linear_back(low_q, w_query) + linear_back(low_k, w_key) + linear_back(low_v, w_value)
    )
    grad_norm_one, slope_gain_one, slope_bias_one = norm_back_one(grad_normed)
    tokens_gradient = (grad_self + grad_norm_one).astype(jnp.bfloat16)
    owned = (
        lax.psum_scatter(slope_query, "grp", scatter_dimension=0, tiled=True),
        lax.psum_scatter(slope_key, "grp", scatter_dimension=0, tiled=True),
        lax.psum_scatter(slope_value, "grp", scatter_dimension=0, tiled=True),
        lax.psum_scatter(slope_mixer, "grp", scatter_dimension=0, tiled=True),
        lax.psum_scatter(slope_xquery, "grp", scatter_dimension=0, tiled=True),
        lax.psum_scatter(slope_xkey, "grp", scatter_dimension=0, tiled=True),
        lax.psum_scatter(slope_xvalue, "grp", scatter_dimension=0, tiled=True),
        lax.psum_scatter(slope_xmixer, "grp", scatter_dimension=0, tiled=True),
        lax.psum_scatter(slope_expand, "grp", scatter_dimension=0, tiled=True),
        lax.psum_scatter(slope_reduce, "grp", scatter_dimension=0, tiled=True),
        lax.psum_scatter(slope_gain_one, "grp", scatter_dimension=0, tiled=True),
        lax.psum_scatter(slope_bias_one, "grp", scatter_dimension=0, tiled=True),
        lax.psum_scatter(slope_query_bias, "grp", scatter_dimension=0, tiled=True),
        lax.psum_scatter(slope_value_bias, "grp", scatter_dimension=0, tiled=True),
        lax.psum_scatter(slope_mixer_bias, "grp", scatter_dimension=0, tiled=True),
        lax.psum_scatter(slope_gain_two, "grp", scatter_dimension=0, tiled=True),
        lax.psum_scatter(slope_bias_two, "grp", scatter_dimension=0, tiled=True),
        lax.psum_scatter(slope_xquery_bias, "grp", scatter_dimension=0, tiled=True),
        lax.psum_scatter(slope_xvalue_bias, "grp", scatter_dimension=0, tiled=True),
        lax.psum_scatter(slope_xmixer_bias, "grp", scatter_dimension=0, tiled=True),
        lax.psum_scatter(slope_gain_three, "grp", scatter_dimension=0, tiled=True),
        lax.psum_scatter(slope_bias_three, "grp", scatter_dimension=0, tiled=True),
        lax.psum_scatter(slope_expand_bias, "grp", scatter_dimension=0, tiled=True),
        lax.psum_scatter(slope_reduce_bias, "grp", scatter_dimension=0, tiled=True),
    )
    matrices = (
        lax.psum_scatter(
            owned[0].astype(jnp.bfloat16), "seq", scatter_dimension=1, tiled=True
        ).astype(jnp.float32),
        lax.psum_scatter(
            owned[1].astype(jnp.bfloat16), "seq", scatter_dimension=1, tiled=True
        ).astype(jnp.float32),
        lax.psum_scatter(
            owned[2].astype(jnp.bfloat16), "seq", scatter_dimension=1, tiled=True
        ).astype(jnp.float32),
        lax.psum_scatter(
            owned[3].astype(jnp.bfloat16), "seq", scatter_dimension=1, tiled=True
        ).astype(jnp.float32),
        lax.psum_scatter(
            owned[4].astype(jnp.bfloat16), "seq", scatter_dimension=1, tiled=True
        ).astype(jnp.float32),
        lax.psum_scatter(
            owned[5].astype(jnp.bfloat16), "seq", scatter_dimension=1, tiled=True
        ).astype(jnp.float32),
        lax.psum_scatter(
            owned[6].astype(jnp.bfloat16), "seq", scatter_dimension=1, tiled=True
        ).astype(jnp.float32),
        lax.psum_scatter(
            owned[7].astype(jnp.bfloat16), "seq", scatter_dimension=1, tiled=True
        ).astype(jnp.float32),
        lax.psum_scatter(
            owned[8].astype(jnp.bfloat16), "seq", scatter_dimension=1, tiled=True
        ).astype(jnp.float32),
        lax.psum_scatter(
            owned[9].astype(jnp.bfloat16), "seq", scatter_dimension=1, tiled=True
        ).astype(jnp.float32),
    )
    smaller = lax.psum(
        (
            owned[10],
            owned[11],
            owned[12],
            owned[13],
            owned[14],
            owned[15],
            owned[16],
            owned[17],
            owned[18],
            owned[19],
            owned[20],
            owned[21],
            owned[22],
            owned[23],
        ),
        "seq",
    )
    return (
        layer_output,
        tokens_gradient,
        smaller[0],
        smaller[1],
        matrices[0],
        smaller[2],
        matrices[1],
        matrices[2],
        smaller[3],
        matrices[3],
        smaller[4],
        smaller[5],
        smaller[6],
        matrices[4],
        smaller[7],
        matrices[5],
        matrices[6],
        smaller[8],
        matrices[7],
        smaller[9],
        smaller[10],
        smaller[11],
        matrices[8],
        smaller[12],
        matrices[9],
        smaller[13],
    )


MESH_ID = pl.DeviceIdType.MESH
NZ, NX, NY, NC = 4, 2, 2, 2
GROUPS = 8


def where_am_i():
    grp = lax.axis_index("grp")
    seq = lax.axis_index("seq")
    return grp // NX, lax.rem(grp, NX), seq // NC, lax.rem(seq, NC)


def device_at(z, x, y, c):
    return (z * NX + x, y * NC + c)


def lanes(start, size):
    return pl.ds(pl.multiple_of(start, 128), size)


def pieces_of(bank, group, y, c, x, z_from, z_to):
    pairs, wide, tall = bank
    if group < 4:
        return [pairs.at[group, y, pl.ds(z_from, z_to - z_from), x, :, lanes(c * 384, 384)]]
    if group < 6:
        start = (y * NC + c) * 768 + (group - 4) * 384
        return [wide.at[pl.ds(z_from, z_to - z_from), x, :, lanes(start, 384)]]
    return [
        tall.at[y, c, pl.ds((group - 6) * 96, 96), lanes((z * NX + x) * 384, 384)]
        for z in range(z_from, z_to)
    ]


def piece_at(bank, group, y, c, x, z):
    pairs, wide, tall = bank
    if group < 4:
        return pairs.at[group, y, z, x, :, lanes(c * 384, 384)]
    if group < 6:
        return wide.at[z, x, :, lanes((y * NC + c) * 768 + (group - 4) * 384, 384)]
    return tall.at[y, c, pl.ds((group - 6) * 96, 96), lanes((z * NX + x) * 384, 384)]


def own_piece(bank, group):
    pairs, wide, tall = bank
    if group < 4:
        return pairs.at[group]
    if group < 6:
        return wide.at[:, pl.ds((group - 4) * 384, 384)]
    return tall.at[pl.ds((group - 6) * 96, 96), :]


class Mail:
    def __init__(self, send_sems, recv_sems):
        self.send_sems, self.recv_sems, self.count, self.sent = send_sems, recv_sems, 0, []

    def slots(self, number):
        first = self.count
        self.count += number
        return list(range(first, first + number))

    def post(self, source, target, slot, device):
        copy = pltpu.make_async_remote_copy(
            src_ref=source,
            dst_ref=target,
            send_sem=self.send_sems.at[slot],
            recv_sem=self.recv_sems.at[slot],
            device_id=device,
            device_id_type=MESH_ID,
        )
        copy.start()
        self.sent.append(copy)

    def arrive(self, target, slot, device):
        pltpu.make_async_remote_copy(
            src_ref=target,
            dst_ref=target,
            send_sem=self.send_sems.at[slot],
            recv_sem=self.recv_sems.at[slot],
            device_id=device,
            device_id_type=MESH_ID,
        ).wait_recv()

    def finish(self):
        for copy in self.sent:
            copy.wait_send()


def greet(z, x, y, c):
    barrier = pltpu.get_barrier_semaphore()
    friends = [device_at(lax.rem(z + k, NZ), x, y, c) for k in range(1, NZ)]
    friends += [device_at(lax.rem(z + k, NZ), 1 - x, y, c) for k in range(NZ)]
    friends += [device_at(z, x, 1 - y, c), device_at(z, x, y, 1 - c)]
    for friend in friends:
        pl.semaphore_signal(barrier, inc=1, device_id=friend, device_id_type=MESH_ID)
    pl.semaphore_wait(barrier, len(friends))


def parts_in(group, number):
    return number if group >= 6 else 1


def joined(first, second):
    return jnp.concatenate([first, second], axis=1)


def mixed(first, second, core):
    even = joined(joined(first[:, :128], joined(first[:, 128:], second[:, 128:])), second[:, :128])
    odd = joined(joined(first[:, 64:], joined(second[:, :64], first[:, :64])), second[:, 64:])
    return jnp.where(core == 0, even, odd).astype(jnp.bfloat16)


ORDER = (2, 0, 1, 3, 4, 5, 6, 7)


def forward_kernel(
    frame_span, lengths, counts,
    query_in, key_in, value_in, mixer_in, xkey_in, xvalue_in, xquery_in, xmixer_in, wide_in, reduce_in,
    small_in, frames_short, tokens_in,
    pairs, wide, tall, frames, vec_out, wide_bias,
    q_to, k_to, v_to, a_to, o_to, h1_to, c_to, p_self_to, ck_to, cv_to, cq_to, o2_to, h2_to, m_to, p_cross_to,
    tokens_got, small, pairs_here, frames_here, q, k, v, a, o, h1, c, p_self, ck, cv, cq, o2, h2, m, p_cross,
    a_all, scores, self_scores, self_bias, cross_bias, pairs_in, tall_in, frames_in,
    send_sems, recv_sems, local_sems, load_sems, save_sems,
):
    z, x, y, c_own = where_am_i()
    for number, (first, second) in enumerate((
        (query_in, key_in), (value_in, mixer_in), (xkey_in, xvalue_in), (xquery_in, xmixer_in)
    )):
        pairs_in[number] = mixed(first[...].astype(jnp.float32), second[...].astype(jnp.float32), c_own)
    tall_in[...] = reduce_in[...].astype(jnp.float32).T.astype(jnp.bfloat16)
    frames_in[:, 368:384] = jnp.zeros((2, 16, 768), jnp.bfloat16)
    frames_in[:, 0:frame_span] = frames_short[...]
    greet(z, x, y, c_own)
    mail = Mail(send_sems, recv_sems)
    own = (pairs_in, wide_in, tall_in)
    bank = (pairs, wide, tall)
    x_mate, y_mate = device_at(z, 1 - x, y, c_own), device_at(z, x, 1 - y, c_own)
    c_mate = device_at(z, x, y, 1 - c_own)
    z_mates = [device_at(lax.rem(z + n, NZ), x, y, c_own) for n in range(1, NZ)]
    grp = z * NX + x
    seq = y * NC + c_own

    local = []

    def keep(source, target):
        copy = pltpu.make_async_copy(source, target, local_sems.at[len(local)])
        copy.start()
        local.append(copy)

    small_slots = mail.slots(2 * NZ - 1)
    small_to = z_mates + [device_at(lax.rem(z + n, NZ), 1 - x, y, c_own) for n in range(NZ)]
    token_slots = mail.slots(3)
    frame_slots = mail.slots(3)
    z_slots = [mail.slots(NZ - 1) for _ in range(GROUPS)]
    x_slots = [mail.slots(parts_in(g, 4)) for g in range(GROUPS)]
    y_slots = [mail.slots(parts_in(g, 4)) for g in range(GROUPS)]
    dy_slots = [mail.slots(parts_in(g, VIA_X)) for g in range(GROUPS)]
    dx_slots = [mail.slots(parts_in(g, 4 - VIA_X)) for g in range(GROUPS)]
    co_slots = [mail.slots(parts_in(g, 4)) for g in range(GROUPS)]
    cx_slots = [mail.slots(parts_in(g, 4)) for g in range(GROUPS)]
    cy_slots = [mail.slots(parts_in(g, 4)) for g in range(GROUPS)]
    cdy_slots = [mail.slots(parts_in(g, VIA_X)) for g in range(GROUPS)]
    cdx_slots = [mail.slots(parts_in(g, 4 - VIA_X)) for g in range(GROUPS)]

    def to_column(group):
        for n in range(1, NZ):
            mail.post(
                own_piece(own, group), piece_at(bank, group, y, c_own, x, z), z_slots[group][n - 1], z_mates[n - 1]
            )

    def post_all(group, slots, device, yy, cc, xx, z_from, z_to):
        for slot, ref in zip(slots, pieces_of(bank, group, yy, cc, xx, z_from, z_to)):
            mail.post(ref, ref, slot, device)

    def arrive_all(group, slots, device, yy, cc, xx, z_from, z_to):
        for slot, ref in zip(slots, pieces_of(bank, group, yy, cc, xx, z_from, z_to)):
            mail.arrive(ref, slot, device)

    def spread(group):
        for n in range(1, NZ):
            zz = lax.rem(z + NZ - n, NZ)
            mail.arrive(piece_at(bank, group, y, c_own, x, zz), z_slots[group][n - 1], z_mates[n - 1])
        local[group].wait()
        post_all(group, x_slots[group], x_mate, y, c_own, x, 0, 4)
        post_all(group, y_slots[group], y_mate, y, c_own, x, 0, 4)
        post_all(group, co_slots[group], c_mate, y, c_own, x, 0, 4)

    def turn(group):
        arrive_all(group, y_slots[group], y_mate, 1 - y, c_own, x, 0, 4)
        post_all(group, dx_slots[group], x_mate, 1 - y, c_own, x, VIA_X, 4)
        post_all(group, cy_slots[group], c_mate, 1 - y, c_own, x, 0, 4)
        arrive_all(group, x_slots[group], x_mate, y, c_own, 1 - x, 0, 4)
        post_all(group, dy_slots[group], y_mate, y, c_own, 1 - x, 0, VIA_X)
        post_all(group, cx_slots[group], c_mate, y, c_own, 1 - x, 0, 4)

    def share(group):
        arrive_all(group, dy_slots[group], y_mate, 1 - y, c_own, 1 - x, 0, VIA_X)
        post_all(group, cdy_slots[group], c_mate, 1 - y, c_own, 1 - x, 0, VIA_X)
        arrive_all(group, dx_slots[group], x_mate, 1 - y, c_own, 1 - x, VIA_X, 4)
        post_all(group, cdx_slots[group], c_mate, 1 - y, c_own, 1 - x, VIA_X, 4)

    def complete(group):
        arrive_all(group, co_slots[group], c_mate, y, 1 - c_own, x, 0, 4)
        arrive_all(group, cx_slots[group], c_mate, y, 1 - c_own, 1 - x, 0, 4)
        arrive_all(group, cy_slots[group], c_mate, 1 - y, 1 - c_own, x, 0, 4)
        arrive_all(group, cdy_slots[group], c_mate, 1 - y, 1 - c_own, 1 - x, 0, VIA_X)
        arrive_all(group, cdx_slots[group], c_mate, 1 - y, 1 - c_own, 1 - x, VIA_X, 4)

    def frame_rows(number):
        return frames.at[:, number]

    loads = []

    def load(source, target):
        copy = pltpu.make_async_copy(source, target, load_sems.at[len(loads)])
        copy.start()
        loads.append(copy)
        return copy

    def load_pair(group):
        complete(group)
        return load(pairs.at[group], pairs_here.at[group])

    saves = []

    def save(source, target):
        copy = pltpu.make_async_copy(source, target, save_sems.at[len(saves)])
        copy.start()
        saves.append(copy)

    for group in range(GROUPS):
        keep(own_piece(own, group), piece_at(bank, group, y, c_own, x, z))
    keep(small_in, small.at[grp])
    keep(frames_in, frame_rows(seq))
    keep(tokens_in, tokens_got.at[seq])
    to_column(ORDER[0])
    for slot, device in zip(small_slots, small_to):
        mail.post(small_in, small.at[grp], slot, device)
    to_column(ORDER[1])
    mail.post(frames_in, frame_rows(seq), frame_slots[0], y_mate)
    mail.post(frames_in, frame_rows(seq), frame_slots[1], c_mate)
    mail.post(tokens_in, tokens_got.at[seq], token_slots[0], y_mate)
    mail.post(tokens_in, tokens_got.at[seq], token_slots[1], c_mate)
    to_column(ORDER[2])

    pending = []
    for step in range(GROUPS + 2):
        if step + 3 < GROUPS:
            pending.append((to_column, ORDER[step + 3]))
        if step < GROUPS:
            pending.append((spread, ORDER[step]))
        if 0 <= step - 1 < GROUPS:
            pending.append((turn, ORDER[step - 1]))
        if 0 <= step - 2 < GROUPS:
            pending.append((share, ORDER[step - 2]))

    def tick(number=1):
        while number > 0 and pending:
            action, group = pending.pop(0)
            action(group)
            if action is not to_column:
                number -= 1

    def until(action, group):
        while (action, group) in pending:
            tick()

    for n in range(1, NZ):
        zz = lax.rem(z + NZ - n, NZ)
        mail.arrive(small.at[zz * NX + x], small_slots[n - 1], z_mates[n - 1])
    for n in range(NZ):
        zz = lax.rem(z + NZ - n, NZ)
        mail.arrive(small.at[zz * NX + 1 - x], small_slots[NZ - 1 + n], x_mate)
    local[GROUPS].wait()
    vec_out[...] = jnp.concatenate([small[g, 0:16, 0:96].astype(jnp.float32) for g in range(8)], axis=1)
    for g in range(8):
        three = small[g, 16:24, :].astype(jnp.float32)
        for n in range(3):
            at = g * 384 + n * 128
            wide_bias[:, at:at + 128] = three[n:n + 1]

    until(spread, ORDER[1])
    other = (1 - y) * NC + c_own
    mail.arrive(tokens_got.at[other], token_slots[0], y_mate)
    mail.post(tokens_got.at[other], tokens_got.at[other], token_slots[2], c_mate)
    until(turn, ORDER[0])
    mail.arrive(frame_rows(other), frame_slots[0], y_mate)
    mail.post(frame_rows(other), frame_rows(other), frame_slots[2], c_mate)
    until(share, ORDER[0])
    mail.arrive(tokens_got.at[y * NC + 1 - c_own], token_slots[1], c_mate)
    mail.arrive(tokens_got.at[(1 - y) * NC + 1 - c_own], token_slots[2], c_mate)
    mail.arrive(frame_rows(y * NC + 1 - c_own), frame_slots[1], c_mate)
    mail.arrive(frame_rows((1 - y) * NC + 1 - c_own), frame_slots[2], c_mate)
    for copy in local[GROUPS + 1:]:
        copy.wait()
    frames_loaded = load(frames, frames_here)
    kv_loaded = load_pair(2)
    frames_loaded.wait()
    kv_loaded.wait()
    for number, _ in enumerate(cross_keys(frames_here, vec_out, pairs_here.at[2], ck, cv)):
        if number % 2 == 1:
            tick()
    save(ck, ck_to)
    save(cv, cv_to)
    until(share, 1)
    first = load_pair(0)
    second = load_pair(1)
    first.wait()
    second.wait()
    phase = self_forward(
        lengths, tokens_got, vec_out, pairs_here.at[0], pairs_here.at[1], q, k, v, a, o, h1, c, p_self,
        a_all, self_scores, self_bias,
    )
    for number, _ in enumerate(phase):
        if number % 2 == 1:
            tick()
    until(share, 3)
    third = load_pair(3)
    for source, target in (
        (q, q_to), (k, k_to), (v, v_to), (a, a_to), (o, o_to), (h1, h1_to), (c, c_to), (p_self, p_self_to)
    ):
        save(source, target)
    third.wait()
    phase = cross_forward(
        counts, frame_span, c, vec_out, pairs_here.at[3], ck, cv, h1, cq, o2, h2, m, p_cross, scores, cross_bias
    )
    for number, _ in enumerate(phase):
        if 1 <= number <= 12:
            t, pair = (number - 1) // 6, (number - 1) % 6
            save(p_cross.at[t, pair], p_cross_to.at[t, pair])
        if number % 2 == 1:
            tick()
    for source, target in ((cq, cq_to), (o2, o2_to), (h2, h2_to), (m, m_to)):
        save(source, target)
    tick(100)
    for group in (4, 5, 6, 7):
        complete(group)
    for copy in saves:
        copy.wait()
    mail.finish()


VIA_X = 2


def slots_needed():
    return (2 * NZ - 1) + 6 + sum(
        3 + parts_in(g, 4) * 5 + 2 * (parts_in(g, VIA_X) + parts_in(g, 4 - VIA_X)) for g in range(GROUPS)
    )


def run_forward(lengths, counts, matrices, small, frames, tokens):
    bf16, f32 = jnp.bfloat16, jnp.float32
    number = slots_needed()
    span = tokens.shape[1]
    anywhere = pl.BlockSpec(memory_space=pl.ANY)
    inside = pl.BlockSpec(memory_space=pltpu.VMEM)
    scalar = pl.BlockSpec(memory_space=pltpu.SMEM)
    rows = (2, span, 768)
    keys = (2, 4, 128, 768)
    kept = [
        (rows, bf16), (keys, bf16), (keys, bf16), (rows, bf16), (rows, bf16), (rows, f32), (rows, bf16),
        ((2, 6, 2 * span, 512), bf16), ((2, 6, 1536, 128), bf16), ((2, 6, 1536, 128), bf16), (rows, bf16), (rows, bf16),
        (rows, f32), (rows, bf16), ((2, 6, 2 * span, 1536), bf16),
    ]
    frame_span = frames.shape[1]
    frames_shape = (2, NY * NC, 384, 768)
    return pl.pallas_call(
        lambda *refs: forward_kernel(frame_span, *refs),
        out_shape=(
            jax.ShapeDtypeStruct((4, NY, NZ, NX, 96, 768), bf16),
            jax.ShapeDtypeStruct((NZ, NX, 96, 3072), bf16),
            jax.ShapeDtypeStruct((NY, NC, 192, 3072), bf16),
            jax.ShapeDtypeStruct(frames_shape, bf16),
            jax.ShapeDtypeStruct((16, 768), f32),
            jax.ShapeDtypeStruct((1, 3072), f32),
        ) + tuple(jax.ShapeDtypeStruct(shape, kind) for shape, kind in kept),
        in_specs=[scalar] * 2 + [inside] * 13,
        out_specs=(anywhere,) * 4 + (inside,) * 2 + (anywhere,) * len(kept),
        scratch_shapes=[
            pltpu.VMEM((4,) + tokens.shape, bf16),
            pltpu.VMEM((8,) + small.shape, bf16),
            pltpu.VMEM((4, NY, NZ, NX, 96, 768), bf16),
            pltpu.VMEM(frames_shape, bf16),
        ] + [pltpu.VMEM(shape, kind) for shape, kind in kept] + [
            pltpu.VMEM((2, 4, span, 768), bf16),
            pltpu.VMEM((2 * span, 1536), f32),
            pltpu.VMEM((2 * span, 512), f32),
            pltpu.VMEM((2, 2 * span, 512), f32),
            pltpu.VMEM((2, 1, 1536), f32),
            pltpu.VMEM((4, 96, 384), bf16),
            pltpu.VMEM((192, 384), bf16),
            pltpu.VMEM((2, 384, 768), bf16),
            pltpu.SemaphoreType.DMA((number,)),
            pltpu.SemaphoreType.DMA((number,)),
            pltpu.SemaphoreType.DMA((GROUPS + 3,)),
            pltpu.SemaphoreType.DMA((5,)),
            pltpu.SemaphoreType.DMA((26,)),
        ],
        compiler_params=pltpu.CompilerParams(
            collective_id=1, has_side_effects=True, vmem_limit_bytes=60 << 20
        ),
        name="gather_forward",
    )(lengths, counts, *matrices, small, frames, tokens)


def mm(left, right):
    return lax.dot_general(left, right, (((1,), (0,)), ((), ())), preferred_element_type=jnp.float32)


def mm_back(left, right):
    return lax.dot_general(left, right, (((1,), (1,)), ((), ())), preferred_element_type=jnp.float32)


def mm_rows(left, right):
    return lax.dot_general(left, right, (((0,), (0,)), ((), ())), preferred_element_type=jnp.float32)


def low_lanes(rows):
    return lax.broadcasted_iota(jnp.int32, (rows, 128), 1) < 64


def turned(tile):
    return pltpu.roll(tile, 64, 1)


def tile_of(values, number):
    return values[:, number * 128:(number + 1) * 128]


def split_first(near, far):
    low = low_lanes(near.shape[0])
    return [tile_of(near, 0), jnp.where(low, tile_of(near, 1), tile_of(far, 1)), tile_of(far, 0)]


def split_second(near, far):
    low = low_lanes(near.shape[0])
    return [tile_of(near, 1), turned(jnp.where(low, tile_of(far, 0), tile_of(near, 0))), tile_of(far, 1)]


def join_first(values):
    low = low_lanes(values.shape[0])
    middle = tile_of(values, 1)
    nothing = jnp.zeros_like(middle)
    near = jnp.concatenate([tile_of(values, 0), jnp.where(low, middle, nothing)], axis=1)
    far = jnp.concatenate([tile_of(values, 2), jnp.where(low, nothing, middle)], axis=1)
    return near.astype(jnp.bfloat16), far.astype(jnp.bfloat16)


def join_second(values):
    low = low_lanes(values.shape[0])
    middle = turned(tile_of(values, 1))
    nothing = jnp.zeros_like(middle)
    near = jnp.concatenate([jnp.where(low, nothing, middle), tile_of(values, 0)], axis=1)
    far = jnp.concatenate([jnp.where(low, middle, nothing), tile_of(values, 2)], axis=1)
    return near.astype(jnp.bfloat16), far.astype(jnp.bfloat16)


def join_both(first, second):
    low = low_lanes(first.shape[0])
    mine, other = tile_of(first, 1), turned(tile_of(second, 1))
    return jnp.concatenate(
        [
            tile_of(first, 0), jnp.where(low, mine, other), tile_of(second, 0),
            tile_of(first, 2), jnp.where(low, other, mine), tile_of(second, 2),
        ],
        axis=1,
    ).astype(jnp.bfloat16)


def block_of(pair, y, at):
    if len(pair.shape) == 3:
        return pair[y, :, at]
    return pair[y, :, :, :, at].reshape(768, -1)


def times_first(values, pair):
    tiles = []
    for y in range(2):
        tiles += split_first(mm(values, block_of(pair, y, slice(0, 256))), mm(values, block_of(pair, y, slice(384, 640))))
    return tiles


def times_second(values, pair):
    tiles = []
    for y in range(2):
        tiles += split_second(mm(values, block_of(pair, y, slice(128, 384))), mm(values, block_of(pair, y, slice(512, 768))))
    return tiles


def back_first(grads, pair):
    out = None
    for y in range(2):
        near, far = join_first(grads[:, y * 384:(y + 1) * 384])
        part = mm_back(near, block_of(pair, y, slice(0, 256))) + mm_back(far, block_of(pair, y, slice(384, 640)))
        out = part if out is None else out + part
    return out


def back_second(grads, pair):
    out = None
    for y in range(2):
        near, far = join_second(grads[:, y * 384:(y + 1) * 384])
        part = mm_back(near, block_of(pair, y, slice(128, 384))) + mm_back(far, block_of(pair, y, slice(512, 768)))
        out = part if out is None else out + part
    return out


def normed(values, gain, bias):
    return norm_rows(values, gain, bias).astype(jnp.bfloat16)


def normed_back(values, gain, grads):
    centre = values - jnp.mean(values, axis=-1, keepdims=True)
    scale = lax.rsqrt(jnp.mean(centre * centre, axis=-1, keepdims=True) + EPS)
    unit = centre * scale
    inner = grads * gain
    back = scale * (
        inner - jnp.mean(inner, axis=-1, keepdims=True) - unit * jnp.mean(inner * unit, axis=-1, keepdims=True)
    )
    return back, jnp.sum(grads * unit, axis=0, keepdims=True), jnp.sum(grads, axis=0, keepdims=True)


def column_sum(values):
    return jnp.sum(values.astype(jnp.float32), axis=0, keepdims=True)


def stacked(values, t, pair):
    both = values[t, :, pair * 128:(pair + 1) * 128]
    low = low_lanes(both.shape[0])
    nothing = jnp.zeros_like(both)
    return jnp.concatenate([jnp.where(low, both, nothing), jnp.where(low, nothing, both)], axis=0)


def unstacked(values):
    half = values.shape[0] // 2
    return jnp.where(low_lanes(half), values[:half], values[half:])


CHUNK = 16


def soften(scores, bias, chances, rows):
    def one(number, carry):
        first = pl.multiple_of(number * CHUNK, CHUNK)
        values = scores[pl.ds(first, CHUNK), :] + bias(first)
        raised = jnp.exp(values - jnp.max(values, axis=1, keepdims=True))
        share = raised * (1.0 / jnp.sum(raised, axis=1, keepdims=True))
        chances[pl.ds(first, CHUNK), :] = share.astype(jnp.bfloat16)
        return carry

    lax.fori_loop(0, rows // CHUNK, one, 0, unroll=2)


def soften_back(chances, slopes, grads, rows):
    def one(number, carry):
        first = pl.multiple_of(number * CHUNK, CHUNK)
        share = chances[pl.ds(first, CHUNK), :].astype(jnp.float32)
        slope = slopes[pl.ds(first, CHUNK), :]
        inner = jnp.sum(share * slope, axis=1, keepdims=True)
        grads[pl.ds(first, CHUNK), :] = (share * (slope - inner)).astype(jnp.bfloat16)
        return carry

    lax.fori_loop(0, rows // CHUNK, one, 0, unroll=2)


def self_forward(lengths, tokens, vec, qk, vo, q_out, k_out, v_out, a_out, o_out, h1_out, c_out, p_out, a_all, scores, bias):
    span = tokens.shape[2]
    seq = lax.axis_index("seq")
    factor = 1.0 / math.sqrt(HEAD_DIM)
    for s in range(4):
        for t in range(2):
            a_all[t, s] = normed(tokens[s, t].astype(jnp.float32), vec[0:1], vec[1:2])
    for t in range(2):
        row = lax.broadcasted_iota(jnp.int32, (span, 512), 0)
        lane = lax.broadcasted_iota(jnp.int32, (span, 512), 1)
        inside = lax.bitwise_and(lane, 127)
        place = lax.shift_right_logical(lane, 7) * span + inside
        good = (inside < span) & (place <= row + seq * span) & (place < lengths[t])
        block = jnp.where(good, 0.0, NEG)
        bias[t, 0:span] = block
        bias[t, span:2 * span] = block
    yield
    for t in range(2):
        a_out[t] = a_all[t, seq]
        rows = a_all[t].reshape(4 * span, 768)
        for number, tile in enumerate(times_second(rows, qk)):
            tile = tile.astype(jnp.bfloat16)
            for s in range(4):
                k_out[t, s, 0:span, number * 128:(number + 1) * 128] = tile[s * span:(s + 1) * span]
        yield
        for number, tile in enumerate(times_first(rows, vo)):
            at = slice(number * 128, (number + 1) * 128)
            tile = (tile + vec[3:4, at]).astype(jnp.bfloat16)
            for s in range(4):
                v_out[t, s, 0:span, at] = tile[s * span:(s + 1) * span]
        for s in range(4):
            k_out[t, s, span:128, :] = jnp.zeros((128 - span, 768), jnp.bfloat16)
            v_out[t, s, span:128, :] = jnp.zeros((128 - span, 768), jnp.bfloat16)
        yield
    own = a_out[...].reshape(2 * span, 768)
    for number, tile in enumerate(times_first(own, qk)):
        at = slice(number * 128, (number + 1) * 128)
        tile = ((tile + vec[2:3, at]) * factor).astype(jnp.bfloat16)
        for t in range(2):
            q_out[t, :, at] = tile[t * span:(t + 1) * span]
    yield
    for t in range(2):
        for pair in range(6):
            at = slice(pair * 128, (pair + 1) * 128)
            scores[...] = mm_back(stacked(q_out, t, pair), k_out[t, :, :, at].reshape(512, 128))
            chances = p_out.at[t, pair]
            soften(scores, lambda first: bias[t, pl.ds(first, CHUNK), :], chances, 2 * span)
            o_out[t, :, at] = unstacked(mm(chances[...], v_out[t, :, :, at].reshape(512, 128))).astype(jnp.bfloat16)
            yield
    out = o_out[...].reshape(2 * span, 768)
    for number, tile in enumerate(times_second(out, vo)):
        at = slice(number * 128, (number + 1) * 128)
        for t in range(2):
            h1_out[t, :, at] = (
                tokens[seq, t, :, at].astype(jnp.float32) + tile[t * span:(t + 1) * span] + vec[4:5, at]
            )
    for t in range(2):
        c_out[t] = normed(h1_out[t], vec[5:6], vec[6:7])
    yield


def cross_keys(frames, vec, kv, ck_out, cv_out):
    for t in range(2):
        for s in range(4):
            block = frames[t, s]
            rows = slice(s * 384, (s + 1) * 384)
            for y in range(2):
                product = mm(block, block_of(kv, y, slice(0, 768)))
                near, far = product[:, 0:384], product[:, 384:768]
                keys = split_first(near[:, 0:256], far[:, 0:256])
                values = split_second(near[:, 128:384], far[:, 128:384])
                for place in range(3):
                    at = slice(y * 384 + place * 128, y * 384 + (place + 1) * 128)
                    ck_out[t, y * 3 + place, rows] = keys[place].astype(jnp.bfloat16)
                    cv_out[t, y * 3 + place, rows] = (values[place] + vec[8:9, at]).astype(jnp.bfloat16)
            yield


def cross_forward(counts, frame_span, c, vec, xqo, ck, cv, h1, cq_out, o2_out, h2_out, m_out, p_out, scores, bias):
    span = c.shape[1]
    factor = 1.0 / math.sqrt(HEAD_DIM)
    rows = c[...].reshape(2 * span, 768)
    for number, tile in enumerate(times_first(rows, xqo)):
        at = slice(number * 128, (number + 1) * 128)
        tile = ((tile + vec[7:8, at]) * factor).astype(jnp.bfloat16)
        for t in range(2):
            cq_out[t, :, at] = tile[t * span:(t + 1) * span]
    for t in range(2):
        for s in range(4):
            inside = lax.broadcasted_iota(jnp.int32, (1, 384), 1)
            good = (inside < frame_span) & (s * frame_span + inside < counts[t])
            bias[t, :, s * 384:(s + 1) * 384] = jnp.where(good, 0.0, NEG)
    yield
    for t in range(2):
        for pair in range(6):
            at = slice(pair * 128, (pair + 1) * 128)
            scores[...] = mm_back(stacked(cq_out, t, pair), ck[t, pair])
            chances = p_out.at[t, pair]
            soften(scores, lambda first: bias[t], chances, 2 * span)
            o2_out[t, :, at] = unstacked(mm(chances[...], cv[t, pair])).astype(jnp.bfloat16)
            yield
    out = o2_out[...].reshape(2 * span, 768)
    for number, tile in enumerate(times_second(out, xqo)):
        at = slice(number * 128, (number + 1) * 128)
        for t in range(2):
            h2_out[t, :, at] = h1[t, :, at] + tile[t * span:(t + 1) * span] + vec[9:10, at]
    for t in range(2):
        m_out[t] = normed(h2_out[t], vec[10:11], vec[11:12])
    yield


class Summing:
    def __init__(self, mail, place, mates, acc, diag_x, diag_y, x_in, y_in, z_in, total):
        self.mail, self.place, self.mates = mail, place, mates
        self.acc, self.diag_x, self.diag_y = acc, diag_x, diag_y
        self.x_in, self.y_in, self.z_in, self.total = x_in, y_in, z_in, total
        self.slots = [mail.slots(4 + NZ - 1) for _ in range(acc.shape[0])]

    def begin(self, n):
        z, x, y = self.place
        x_mate, y_mate, _ = self.mates
        self.mail.post(self.acc.at[n, 1 - y, pl.ds(0, 2), 1 - x], self.diag_x.at[n], self.slots[n][0], x_mate)
        self.mail.post(self.acc.at[n, 1 - y, pl.ds(2, 2), 1 - x], self.diag_y.at[n], self.slots[n][1], y_mate)

    def side(self, n):
        z, x, y = self.place
        x_mate, y_mate, _ = self.mates
        self.mail.arrive(self.diag_x.at[n], self.slots[n][0], x_mate)
        for k in range(2):
            self.acc[n, 1 - y, k, x] = self.acc[n, 1 - y, k, x] + self.diag_x[n, k]
        self.mail.post(self.acc.at[n, 1 - y, :, x], self.y_in.at[n], self.slots[n][2], y_mate)
        self.mail.arrive(self.diag_y.at[n], self.slots[n][1], y_mate)
        for k in range(2):
            self.acc[n, y, 2 + k, 1 - x] = self.acc[n, y, 2 + k, 1 - x] + self.diag_y[n, k]
        self.mail.post(self.acc.at[n, y, :, 1 - x], self.x_in.at[n], self.slots[n][3], x_mate)

    def column(self, n):
        z, x, y = self.place
        x_mate, y_mate, z_mates = self.mates
        self.mail.arrive(self.y_in.at[n], self.slots[n][2], y_mate)
        self.mail.arrive(self.x_in.at[n], self.slots[n][3], x_mate)
        for k in range(NZ):
            self.acc[n, y, k, x] = (
                self.acc[n, y, k, x].astype(jnp.float32)
                + self.x_in[n, k].astype(jnp.float32)
                + self.y_in[n, k].astype(jnp.float32)
            ).astype(jnp.bfloat16)
        for k in range(1, NZ):
            zz = lax.rem(z + k, NZ)
            self.mail.post(self.acc.at[n, y, zz, x], self.z_in.at[n, k - 1], self.slots[n][3 + k], z_mates[k - 1])

    def last(self, n):
        z, x, y = self.place
        _, _, z_mates = self.mates
        for k in range(1, NZ):
            self.mail.arrive(self.z_in.at[n, k - 1], self.slots[n][3 + k], z_mates[k - 1])
        self.total[n] = self.acc[n, y, z, x].astype(jnp.float32) + (
            self.z_in[n, 0].astype(jnp.float32) + self.z_in[n, 1].astype(jnp.float32)
        ) + self.z_in[n, 2].astype(jnp.float32)


def summing_scratch(n):
    piece = (96, 384)
    shapes = [
        (n, NY, NZ, NX) + piece, (n, 2) + piece, (n, 2) + piece, (n, NZ) + piece, (n, NZ) + piece, (n, NZ - 1) + piece
    ]
    return [pltpu.VMEM(shape, jnp.bfloat16) for shape in shapes]


class Loads:
    def __init__(self, sems):
        self.sems, self.count = sems, 0

    def start(self, source, target):
        copy = pltpu.make_async_copy(source, target, self.sems.at[self.count])
        copy.start()
        self.count += 1
        return copy


def two(first, second):
    return jnp.concatenate([first, second], axis=0)


def feed_kernel(
    lengths, ids, weights, cotangent, vec, wide_bias, h2, m, o2, c, h1, cq,
    wide_far, tall_far, pairs_far, frames_far, ck_far, cv_far, p_far,
    y_out, dh1_out, total, acc_kv, acc_xqo, small_out, wide_small,
    acc, diag_x, diag_y, x_in, y_in, z_in,
    wide, tall, xqo, frames, keys_here, values_here, p_here,
    m_sib, g_own, g_sib, du_own, du_send, du_sib, dz_own, dz_send, dz_sib,
    o2_sib, c_sib, xb_own, xb_send, xb_sib, xa_own, xa_send, xa_sib, gkv, kv_in,
    dy, dh2, do, dq, scores, dscores,
    send_sems, recv_sems, load_sems, unit_sems,
):
    z, x, y, core = where_am_i()
    span = m.shape[1]
    seq = y * NC + core
    factor = 1.0 / math.sqrt(HEAD_DIM)
    low = low_lanes(2 * span)
    x_mate, y_mate, c_mate = device_at(z, 1 - x, y, core), device_at(z, x, 1 - y, core), device_at(z, x, y, 1 - core)
    z_mates = [device_at(lax.rem(z + n, NZ), x, y, core) for n in range(1, NZ)]
    loads = Loads(load_sems)
    order = [(yy, side) for yy in range(2) for side in range(2)]
    block_loads = []
    for yy, side in order:
        at = lanes((2 * yy + (core if side == 0 else 1 - core)) * 768, 768)
        block_loads.append((
            loads.start(wide_far.at[:, :, :, at], wide.at[:, :, :, at]),
            loads.start(tall_far.at[:, :, :, at], tall.at[:, :, :, at]),
        ))
    xqo_load = loads.start(pairs_far.at[3], xqo)
    frames_load = loads.start(frames_far, frames)
    units = [(pair, t) for pair in range(6) for t in range(2)]

    def unit_copies(n):
        pair, t = units[n]
        slot = n % 2
        return [
            pltpu.make_async_copy(ck_far.at[t, pair], keys_here.at[slot], unit_sems.at[slot, 0]),
            pltpu.make_async_copy(cv_far.at[t, pair], values_here.at[slot], unit_sems.at[slot, 1]),
            pltpu.make_async_copy(p_far.at[t, pair], p_here.at[slot], unit_sems.at[slot, 2]),
        ]

    for copy in unit_copies(0):
        copy.start()
    greet(z, x, y, core)
    mail = Mail(send_sems, recv_sems)
    sums = Summing(mail, (z, x, y), (x_mate, y_mate, z_mates), acc, diag_x, diag_y, x_in, y_in, z_in, total)
    swap = mail.slots(1 + 2 + 4 + 2 + 2 + 2 + 1)
    m_slot, dz_slots, g_slots, du_slots = swap[0], swap[1:3], swap[3:7], swap[7:9]
    xb_slots, xa_slots, kv_slot = swap[9:11], swap[11:13], swap[13]
    o2_slot, c_slot = mail.slots(2)
    mail.post(m, m_sib, m_slot, c_mate)
    mail.post(o2, o2_sib, o2_slot, c_mate)
    mail.post(c, c_sib, c_slot, c_mate)

    for t in range(2):
        weight = 0.0
        for corpus in range(weights.shape[0]):
            weight = weight + jnp.where(ids[t] == corpus, weights[corpus], 0.0)
        row = lax.broadcasted_iota(jnp.int32, (span, 1), 0) + seq * span
        scale = jnp.where(row < lengths[t], weight, 0.0)
        dy[t * span:(t + 1) * span] = cotangent[t].astype(jnp.float32) * scale
    dz = dy[...].astype(jnp.bfloat16)
    dz_wide = dz.astype(jnp.float32)
    small_out[...] = jnp.zeros_like(small_out)
    small_out[12:13] = column_sum(dz_wide)
    for yy in range(2):
        tiles = [dz_wide[:, yy * 384 + n * 128:yy * 384 + (n + 1) * 128] for n in range(3)]
        even = jnp.concatenate([tiles[0], tiles[1]], axis=1)
        last = turned(tiles[2])
        odd = jnp.concatenate([jnp.where(low, turned(tiles[1]), last), last], axis=1)
        dz_own[yy] = jnp.where(core == 0, even, odd).astype(jnp.bfloat16)
        dz_send[yy] = jnp.where(core == 0, odd, even).astype(jnp.bfloat16)
        mail.post(dz_send.at[yy], dz_sib.at[yy], dz_slots[yy], c_mate)
    rows = m[...].reshape(2 * span, 768)
    z_sum, dm_sum = None, None
    for number, (yy, side) in enumerate(order):
        at = lanes((2 * yy + (core if side == 0 else 1 - core)) * 768, 768)
        for copy in block_loads[number]:
            copy.wait()
        wide_here = wide[:, :, :, at].reshape(768, 768)
        tall_here = tall[:, :, :, at].reshape(768, 768)
        hidden = mm(rows, wide_here) + wide_bias[:, at]
        bell = 0.5 * (1.0 + lax.erf(hidden * 0.7071067811865476))
        gate = (hidden * bell).astype(jnp.bfloat16)
        g_own[:, at] = gate
        mail.post(g_own.at[:, at], g_sib.at[:, at], g_slots[number], c_mate)
        slope = bell + hidden * (jnp.exp(-0.5 * hidden * hidden) * 0.3989422804014327)
        back = (mm(dz, tall_here) * slope).astype(jnp.bfloat16)
        if side == 0:
            du_own[yy] = back
        else:
            du_send[yy] = back
            mail.post(du_send.at[yy], du_sib.at[yy], du_slots[yy], c_mate)
        part = mm_back(gate, tall_here)
        z_sum = part if z_sum is None else z_sum + part
        part = mm_back(back, wide_here)
        dm_sum = part if dm_sum is None else dm_sum + part
        wide_small[:, at] = column_sum(back)
    h2_rows = h2[...].reshape(2 * span, 768)
    out = h2_rows + z_sum + vec[12:13]
    back, gain, offset = normed_back(h2_rows, vec[10:11], dm_sum)
    small_out[10:11] = gain
    small_out[11:12] = offset
    dh2[...] = dy[...] + back
    for t in range(2):
        y_out[t] = out[t * span:(t + 1) * span].astype(jnp.bfloat16)

    for number, (yy, side) in enumerate(order):
        at = lanes((2 * yy + (1 - core if side == 0 else core)) * 768, 768)
        mail.arrive(g_sib.at[:, at], g_slots[number], c_mate)
    for yy in range(2):
        mail.arrive(dz_sib.at[yy], dz_slots[yy], c_mate)
    for yy in range(2):
        slopes = two(dz_own[yy], dz_sib[yy])
        for zz in range(NZ):
            at = slice(zz * 768, (zz + 1) * 768)
            product = mm_rows(slopes, two(g_own[:, at], g_sib[:, at])).astype(jnp.bfloat16)
            for xx in range(NX):
                acc[2, yy, zz, xx] = product[0:96, xx * 384:(xx + 1) * 384]
                acc[3, yy, zz, xx] = product[96:192, xx * 384:(xx + 1) * 384]
    sums.begin(2)
    sums.begin(3)
    mail.arrive(m_sib, m_slot, c_mate)
    both_rows = two(rows, m_sib[...].reshape(2 * span, 768))
    for yy in range(2):
        mail.arrive(du_sib.at[yy], du_slots[yy], c_mate)
        product = mm_rows(both_rows, two(du_own[yy], du_sib[yy])).astype(jnp.bfloat16)
        acc[0, yy] = product[:, 0:384].reshape(NZ, NX, 96, 384)
        acc[1, yy] = product[:, 384:768].reshape(NZ, NX, 96, 384)
    sums.begin(0)
    sums.begin(1)
    pending = []
    for step in range(6):
        for lag, action in ((0, sums.side), (1, sums.column), (2, sums.last)):
            if 0 <= step - lag < 4:
                pending.append((action, (2, 3, 0, 1)[step - lag]))

    def tick(number=1):
        for _ in range(number):
            if pending:
                action, group = pending.pop(0)
                action(group)

    low_wide = dh2[...].astype(jnp.bfloat16).astype(jnp.float32)
    small_out[9:10] = column_sum(low_wide)
    xqo_load.wait()
    for yy in range(2):
        near, far = join_second(low_wide[:, yy * 384:(yy + 1) * 384])
        xb_own[yy] = jnp.where(core == 0, near, far)
        xb_send[yy] = jnp.where(core == 0, far, near)
        mail.post(xb_send.at[yy], xb_sib.at[yy], xb_slots[yy], c_mate)
    heard = back_second(low_wide, xqo)
    small_out[8:9] = column_sum(heard.astype(jnp.bfloat16))
    for t in range(2):
        do[t] = heard[t * span:(t + 1) * span].astype(jnp.bfloat16)
    tick()
    frames_load.wait()
    total_kv = None
    for number, (pair, t) in enumerate(units):
        at = slice(pair * 128, (pair + 1) * 128)
        slot = number % 2
        if number + 1 < len(units):
            for copy in unit_copies(number + 1):
                copy.start()
        for copy in unit_copies(number):
            copy.wait()
        slopes, query = stacked(do, t, pair), stacked(cq, t, pair)
        scores[...] = mm_back(slopes, values_here[slot])
        chances = p_here.at[slot]
        soften_back(chances, scores, dscores, 2 * span)
        dq[t * span:(t + 1) * span, at] = unstacked(mm(dscores[...], keys_here[slot])) * factor
        turned_grads = two(mm_rows(query, dscores[...]), mm_rows(slopes, chances[...])).astype(jnp.bfloat16)
        part = mm(turned_grads, frames[t].reshape(1536, 768))
        total_kv = part if t == 0 else total_kv + part
        if t == 1:
            keys, values = total_kv[0:128].T, total_kv[128:256].T
            yy, place = pair // 3, pair % 3
            if place == 1:
                values = turned(values)
                half = low_lanes(768)
                gkv[0, yy, :, 128:256] = jnp.where(half, keys, values).astype(jnp.bfloat16)
                gkv[1, yy, :, 128:256] = jnp.where(half, values, keys).astype(jnp.bfloat16)
            else:
                gkv[place // 2, yy, :, 0:128] = keys.astype(jnp.bfloat16)
                gkv[place // 2, yy, :, 256:384] = values.astype(jnp.bfloat16)
        tick()
    mail.post(gkv.at[1 - core], kv_in, kv_slot, c_mate)
    low_q = dq[...].astype(jnp.bfloat16).astype(jnp.float32)
    small_out[7:8] = column_sum(low_q)
    for yy in range(2):
        near, far = join_first(low_q[:, yy * 384:(yy + 1) * 384])
        xa_own[yy] = jnp.where(core == 0, near, far)
        xa_send[yy] = jnp.where(core == 0, far, near)
        mail.post(xa_send.at[yy], xa_sib.at[yy], xa_slots[yy], c_mate)
    back, gain, offset = normed_back(h1[...].reshape(2 * span, 768), vec[5:6], back_first(low_q, xqo))
    small_out[5:6] = gain
    small_out[6:7] = offset
    for t in range(2):
        dh1_out[t] = dh2[t * span:(t + 1) * span] + back[t * span:(t + 1) * span]
    mail.arrive(o2_sib, o2_slot, c_mate)
    mail.arrive(c_sib, c_slot, c_mate)
    o2_both = two(o2[...].reshape(2 * span, 768), o2_sib[...].reshape(2 * span, 768))
    c_both = two(c[...].reshape(2 * span, 768), c_sib[...].reshape(2 * span, 768))
    for yy in range(2):
        mail.arrive(xb_sib.at[yy], xb_slots[yy], c_mate)
        mail.arrive(xa_sib.at[yy], xa_slots[yy], c_mate)
        second = mm_rows(o2_both, two(xb_own[yy], xb_sib[yy]))
        first = mm_rows(c_both, two(xa_own[yy], xa_sib[yy]))
        store_pair(acc_xqo.at[yy], first, second)
    mail.arrive(kv_in, kv_slot, c_mate)
    for yy in range(2):
        acc_kv[yy] = (gkv[core, yy] + kv_in[yy]).reshape(NZ, NX, 96, 384)
    tick(100)
    mail.finish()


def store_pair(out, first, second):
    shape = (NZ, NX, 96, 128)
    out[:, :, :, 0:128] = tile_of(first, 0).astype(jnp.bfloat16).reshape(shape)
    out[:, :, :, 128:256] = (tile_of(first, 1) + tile_of(second, 0)).astype(jnp.bfloat16).reshape(shape)
    out[:, :, :, 256:384] = tile_of(second, 1).astype(jnp.bfloat16).reshape(shape)


def run_feed(lengths, ids, weights, near, far):
    bf16, f32 = jnp.bfloat16, jnp.float32
    span = near[4].shape[1]
    rows, flat = (2, span, 768), 2 * span
    inside, anywhere = pl.BlockSpec(memory_space=pltpu.VMEM), pl.BlockSpec(memory_space=pl.ANY)
    scalar = pl.BlockSpec(memory_space=pltpu.SMEM)
    piece = (NY, NZ, NX, 96, 384)
    number = 4 * 7 + 16
    scratch = [
        ((NZ, NX, 96, 3072), bf16), ((NY, NC, 192, 3072), bf16), ((NY, NZ, NX, 96, 768), bf16), (far[3].shape, bf16),
        ((2, 1536, 128), bf16), ((2, 1536, 128), bf16), ((2, flat, 1536), bf16),
        (rows, bf16), ((flat, 3072), bf16), ((flat, 3072), bf16),
        ((2, flat, 768), bf16), ((2, flat, 768), bf16), ((2, flat, 768), bf16),
        ((2, flat, 256), bf16), ((2, flat, 256), bf16), ((2, flat, 256), bf16),
        (rows, bf16), (rows, bf16),
    ] + [((2, flat, 256), bf16)] * 6 + [
        ((2, 2, 768, 384), bf16), ((2, 768, 384), bf16),
        ((flat, 768), f32), ((flat, 768), f32), (rows, bf16), ((flat, 768), f32), ((flat, 1536), f32),
        ((flat, 1536), bf16),
    ]
    return pl.pallas_call(
        feed_kernel,
        out_shape=(
            jax.ShapeDtypeStruct(rows, bf16), jax.ShapeDtypeStruct(rows, f32),
            jax.ShapeDtypeStruct((4, 96, 384), f32),
            jax.ShapeDtypeStruct(piece, bf16), jax.ShapeDtypeStruct(piece, bf16),
            jax.ShapeDtypeStruct((16, 768), f32), jax.ShapeDtypeStruct((1, 3072), f32),
        ),
        in_specs=[scalar] * 3 + [inside] * len(near) + [anywhere] * len(far),
        out_specs=(inside,) * 7,
        scratch_shapes=summing_scratch(4) + [pltpu.VMEM(shape, kind) for shape, kind in scratch] + [
            pltpu.SemaphoreType.DMA((number,)),
            pltpu.SemaphoreType.DMA((number,)),
            pltpu.SemaphoreType.DMA((10,)),
            pltpu.SemaphoreType.DMA((2, 3)),
        ],
        compiler_params=pltpu.CompilerParams(
            collective_id=2, has_side_effects=True, vmem_limit_bytes=60 << 20
        ),
        name="feed_cross_back",
    )(lengths, ids, weights, *near, *far)


def last_kernel(
    tokens, dh1, q, k, v, a, o, p, vec, small_before, wide_small,
    pairs_far, kv_far, xqo_far,
    dx_out, total, small_total,
    acc, diag_x, diag_y, x_in, y_in, z_in,
    qk, vo, a_sib, o_sib, ob_own, ob_send, ob_sib, va_own, va_send, va_sib, qk_own, qk_send, qk_sib,
    dkv, dkv_core, dkv_side, do, dq, dk, dv, scores, dscores,
    small, pack, pack_in, pack_sum, pack_seq,
    send_sems, recv_sems, load_sems,
):
    z, x, y, core = where_am_i()
    span = q.shape[1]
    seq = y * NC + core
    grp = z * NX + x
    factor = 1.0 / math.sqrt(HEAD_DIM)
    x_mate, y_mate, c_mate = device_at(z, 1 - x, y, core), device_at(z, x, 1 - y, core), device_at(z, x, y, 1 - core)
    z_mates = [device_at(lax.rem(z + n, NZ), x, y, core) for n in range(1, NZ)]
    loads = Loads(load_sems)
    acc_loads = [loads.start(kv_far, acc.at[2]), loads.start(xqo_far, acc.at[3])]
    vo_load = loads.start(pairs_far.at[1], vo)
    qk_load = loads.start(pairs_far.at[0], qk)
    greet(z, x, y, core)
    mail = Mail(send_sems, recv_sems)
    sums = Summing(mail, (z, x, y), (x_mate, y_mate, z_mates), acc, diag_x, diag_y, x_in, y_in, z_in, total)
    a_slot, o_slot = mail.slots(2)
    ob_slots, va_slots, qk_slots = mail.slots(2), mail.slots(2), mail.slots(2)
    core_slots, side_slots = mail.slots(4), mail.slots(2)
    pack_slots, seq_slots = mail.slots(2 * NZ - 1), mail.slots(2)
    for copy in acc_loads:
        copy.wait()
    sums.begin(2)
    sums.begin(3)
    mail.post(a, a_sib, a_slot, c_mate)
    mail.post(o, o_sib, o_slot, c_mate)
    pending = [
        (sums.side, 2), (sums.side, 3), (sums.column, 2), (sums.column, 3), (sums.last, 2), (sums.last, 3)
    ]

    def tick(number=1):
        for _ in range(number):
            if pending:
                action, group = pending.pop(0)
                action(group)

    small[...] = small_before[...]
    low_wide = dh1[...].reshape(2 * span, 768).astype(jnp.bfloat16).astype(jnp.float32)
    small[4:5] = column_sum(low_wide)
    for yy in range(2):
        near, far = join_second(low_wide[:, yy * 384:(yy + 1) * 384])
        ob_own[yy] = jnp.where(core == 0, near, far)
        ob_send[yy] = jnp.where(core == 0, far, near)
        mail.post(ob_send.at[yy], ob_sib.at[yy], ob_slots[yy], c_mate)
    vo_load.wait()
    heard = back_second(low_wide, vo)
    for t in range(2):
        do[t] = heard[t * span:(t + 1) * span].astype(jnp.bfloat16)

    def core_target(t, side):
        return dkv_core.at[t, side]

    def exchange_core(t):
        mail.post(dkv.at[t, y * NC + 1 - core], core_target(t, 0), core_slots[2 * t], c_mate)
        mail.post(dkv.at[t, (1 - y) * NC + 1 - core], core_target(t, 1), core_slots[2 * t + 1], c_mate)

    def add_blocks(target, source):
        def one(n, carry):
            at = pl.ds(pl.multiple_of(n * 128, 128), 128)
            for kind in range(2):
                target[kind, at, :] = target[kind, at, :] + source[kind, at, :]
            return carry

        lax.fori_loop(0, 6, one, 0)

    def exchange_side(t):
        mail.arrive(core_target(t, 1), core_slots[2 * t + 1], c_mate)
        add_blocks(dkv.at[t, (1 - y) * NC + core], core_target(t, 1))
        mail.post(dkv.at[t, (1 - y) * NC + core], dkv_side.at[t], side_slots[t], y_mate)
        mail.arrive(core_target(t, 0), core_slots[2 * t], c_mate)
        add_blocks(dkv.at[t, seq], core_target(t, 0))

    for t in range(2):
        for pair in range(6):
            at = slice(pair * 128, (pair + 1) * 128)
            slopes, query = stacked(do, t, pair), stacked(q, t, pair)
            scores[...] = mm_back(slopes, v[t, :, :, at].reshape(512, 128))
            chances = p.at[t, pair]
            soften_back(chances, scores, dscores, 2 * span)
            dq[t * span:(t + 1) * span, at] = unstacked(mm(dscores[...], k[t, :, :, at].reshape(512, 128))) * factor
            keys = mm_rows(query, dscores[...]).astype(jnp.bfloat16)
            values = mm_rows(slopes, chances[...]).astype(jnp.bfloat16)
            for s in range(4):
                dkv[t, s, 0, at, :] = keys[:, s * 128:(s + 1) * 128]
                dkv[t, s, 1, at, :] = values[:, s * 128:(s + 1) * 128]
            if t == 1 and pair == 0:
                exchange_side(0)
            elif pair % 2 == 1:
                tick()
        exchange_core(t)
    low_q = dq[...].astype(jnp.bfloat16).astype(jnp.float32)
    small[2:3] = column_sum(low_q)
    qk_load.wait()
    exchange_side(1)
    tick()
    for t in range(2):
        mail.arrive(dkv_side.at[t], side_slots[t], y_mate)
        for kind, out in ((0, dk), (1, dv)):
            whole = dkv[t, seq, kind].astype(jnp.float32) + dkv_side[t, kind].astype(jnp.float32)
            out[t * span:(t + 1) * span] = whole.T[0:span]
    dk_wide, dv_wide = [ref[...].astype(jnp.bfloat16).astype(jnp.float32) for ref in (dk, dv)]
    small[3:4] = column_sum(dv_wide)
    joined_qk = []
    for yy in range(2):
        at = slice(yy * 384, (yy + 1) * 384)
        near, far = join_first(dv_wide[:, at])
        va_own[yy] = jnp.where(core == 0, near, far)
        va_send[yy] = jnp.where(core == 0, far, near)
        mail.post(va_send.at[yy], va_sib.at[yy], va_slots[yy], c_mate)
        both = join_both(low_q[:, at], dk_wide[:, at])
        joined_qk.append(both)
        near, far = both[:, 0:384], both[:, 384:768]
        qk_own[yy] = jnp.where(core == 0, near, far)
        qk_send[yy] = jnp.where(core == 0, far, near)
        mail.post(qk_send.at[yy], qk_sib.at[yy], qk_slots[yy], c_mate)
    mail.arrive(a_sib, a_slot, c_mate)
    mail.arrive(o_sib, o_slot, c_mate)
    a_both = two(a[...].reshape(2 * span, 768), a_sib[...].reshape(2 * span, 768))
    o_both = two(o[...].reshape(2 * span, 768), o_sib[...].reshape(2 * span, 768))
    for yy in range(2):
        mail.arrive(ob_sib.at[yy], ob_slots[yy], c_mate)
        mail.arrive(va_sib.at[yy], va_slots[yy], c_mate)
        second = mm_rows(o_both, two(ob_own[yy], ob_sib[yy]))
        first = mm_rows(a_both, two(va_own[yy], va_sib[yy]))
        store_pair(acc.at[1, yy], first, second)
    sums.begin(1)
    for yy in range(2):
        mail.arrive(qk_sib.at[yy], qk_slots[yy], c_mate)
        product = mm_rows(a_both, two(qk_own[yy], qk_sib[yy])).astype(jnp.bfloat16)
        acc[0, yy] = product.reshape(NZ, NX, 96, 384)
    sums.begin(0)
    back = back_first(dv_wide, vo)
    for yy in range(2):
        back = back + mm_back(joined_qk[yy], block_of(qk, yy, slice(0, 768)))
    gain, offset = None, None
    for t in range(2):
        part, gain_part, offset_part = normed_back(
            tokens[t].astype(jnp.float32), vec[0:1], back[t * span:(t + 1) * span]
        )
        dx_out[t] = (dh1[t] + part).astype(jnp.bfloat16)
        gain = gain_part if t == 0 else gain + gain_part
        offset = offset_part if t == 0 else offset + offset_part
    small[0:1] = gain
    small[1:2] = offset
    for g in range(8):
        pack[g, 0:16, 0:96] = small[:, g * 96:(g + 1) * 96]
        pack[g, 0:16, 96:128] = jnp.zeros((16, 32), jnp.float32)
        for n in range(3):
            at = g * 384 + n * 128
            pack[g, 16 + n:17 + n, :] = wide_small[:, at:at + 128]
        pack[g, 19:24, :] = jnp.zeros((5, 128), jnp.float32)
    pack_to = [(lax.rem(z + n, NZ), x) for n in range(1, NZ)]
    pack_to += [(lax.rem(z + n, NZ), 1 - x) for n in range(NZ)]
    for number, (zz, xx) in enumerate(pack_to):
        mail.post(pack.at[zz * NX + xx], pack_in.at[number], pack_slots[number], device_at(zz, xx, y, core))
    tick(100)
    sums.side(1)
    for number in range(2 * NZ - 1):
        mail.arrive(pack_in.at[number], pack_slots[number], x_mate)
    pack_sum[...] = (
        (pack[grp] + pack_in[0]) + (pack_in[1] + pack_in[2])
        + ((pack_in[3] + pack_in[4]) + (pack_in[5] + pack_in[6]))
    )
    mail.post(pack_sum, pack_seq.at[0], seq_slots[0], c_mate)
    sums.side(0)
    mail.arrive(pack_seq.at[0], seq_slots[0], c_mate)
    pack_seq[1] = pack_sum[...] + pack_seq[0]
    mail.post(pack_seq.at[1], pack_seq.at[2], seq_slots[1], y_mate)
    sums.column(1)
    mail.arrive(pack_seq.at[2], seq_slots[1], y_mate)
    small_total[...] = pack_seq[1] + pack_seq[2]
    sums.column(0)
    sums.last(1)
    sums.last(0)
    mail.finish()


def run_last(near, far):
    bf16, f32 = jnp.bfloat16, jnp.float32
    span = near[0].shape[1]
    rows, flat = (2, span, 768), 2 * span
    inside, anywhere = pl.BlockSpec(memory_space=pltpu.VMEM), pl.BlockSpec(memory_space=pl.ANY)
    number = 4 * 7 + 8 + 6 + 9
    scratch = [
        ((NY, NZ, NX, 96, 768), bf16), ((NY, NZ, NX, 96, 768), bf16), (rows, bf16), (rows, bf16),
    ] + [((2, flat, 256), bf16)] * 6 + [((2, flat, 384), bf16)] * 3 + [
        ((2, 4, 2, 768, 128), bf16), ((2, 2, 2, 768, 128), bf16), ((2, 2, 768, 128), bf16),
        (rows, bf16), ((flat, 768), f32), ((flat, 768), f32), ((flat, 768), f32), ((flat, 512), f32),
        ((flat, 512), bf16),
        ((16, 768), f32), ((8, 24, 128), f32), ((7, 24, 128), f32), ((24, 128), f32), ((3, 24, 128), f32),
    ]
    return pl.pallas_call(
        last_kernel,
        out_shape=(
            jax.ShapeDtypeStruct(rows, bf16), jax.ShapeDtypeStruct((4, 96, 384), f32),
            jax.ShapeDtypeStruct((24, 128), f32),
        ),
        in_specs=[inside] * len(near) + [anywhere] * len(far),
        out_specs=(inside,) * 3,
        scratch_shapes=summing_scratch(4) + [pltpu.VMEM(shape, kind) for shape, kind in scratch] + [
            pltpu.SemaphoreType.DMA((number,)),
            pltpu.SemaphoreType.DMA((number,)),
            pltpu.SemaphoreType.DMA((4,)),
        ],
        compiler_params=pltpu.CompilerParams(
            collective_id=3, has_side_effects=True, vmem_limit_bytes=60 << 20
        ),
        name="self_back_sum",
    )(*near, *far)


def unmixed(piece, core):
    first = jnp.where(core == 0, piece[:, :192], joined(piece[:, 192:256], piece[:, :128]))
    second = jnp.where(
        core == 0, joined(piece[:, 256:], piece[:, 192:256]), joined(piece[:, 128:192], piece[:, 256:])
    )
    return first, second


def on_device_fast(*arguments):
    (
        tokens, encoder_states, lengths, frame_counts, corpus_ids, corpus_weights, cotangent,
        first_gain, first_bias, query_weight, query_bias, key_weight, value_weight, value_bias,
        output_weight, output_bias, second_gain, second_bias, cross_query_weight, cross_query_bias,
        cross_key_weight, cross_value_weight, cross_value_bias, cross_output_weight, cross_output_bias,
        third_gain, third_bias, expand_weight, expand_bias, reduce_weight, reduce_bias,
    ) = arguments
    bf16, f32 = jnp.bfloat16, jnp.float32
    core = lax.rem(lax.axis_index("seq"), NC)
    small_vectors = (
        first_gain, first_bias, query_bias, value_bias, output_bias, second_gain, second_bias,
        cross_query_bias, cross_value_bias, cross_output_bias, third_gain, third_bias, reduce_bias, expand_bias,
    )
    small = jnp.concatenate([
        jnp.pad(jnp.stack(small_vectors[:13]), ((0, 3), (0, 32))), jnp.pad(expand_bias.reshape(3, 128), ((0, 13), (0, 0)))
    ])
    matrices = (
        query_weight, key_weight, value_weight, output_weight, cross_key_weight, cross_value_weight,
        cross_query_weight, cross_output_weight, expand_weight, reduce_weight,
    )
    (
        pairs_all, wide_all, tall_all, frames_all, vec, wide_bias,
        q, k, v, a, o, h1, c, p_self, ck, cv, cq, o2, h2, m, p_cross,
    ) = run_forward(lengths, frame_counts, matrices, small, encoder_states, tokens)
    layer_output, dh1, total_ff, acc_kv, acc_xqo, small_before, wide_small = run_feed(
        lengths, corpus_ids, corpus_weights,
        [cotangent, vec, wide_bias, h2, m, o2, c, h1, cq],
        [wide_all, tall_all, pairs_all, frames_all, ck, cv, p_cross],
    )
    tokens_gradient, total, small_total = run_last(
        [tokens, dh1, q, k, v, a, o, p_self, vec, small_before, wide_small], [pairs_all, acc_kv, acc_xqo]
    )
    (m_query, m_key), (m_value, m_mixer), (m_xkey, m_xvalue), (m_xquery, m_xmixer) = [
        unmixed(total[p], core) for p in range(4)
    ]
    expand_grad = jnp.concatenate([total_ff[0], total_ff[1]], axis=1)
    reduce_grad = jnp.concatenate([total_ff[2], total_ff[3]], axis=0).T
    smaller = [small_total[i, :96] for i in range(13)]
    expand_bias_grad = small_total[16:19].reshape(384)
    return (
        layer_output, tokens_gradient, smaller[0], smaller[1], m_query, smaller[2], m_key, m_value, smaller[3],
        m_mixer, smaller[4], smaller[5], smaller[6], m_xquery, smaller[7], m_xkey, m_xvalue, smaller[8],
        m_xmixer, smaller[9], smaller[10], smaller[11], expand_grad, expand_bias_grad, reduce_grad, smaller[12],
    )


def solution(mesh):
    placed = (
        P("grp", "seq", None),
        P("grp", "seq", None),
        P("grp"),
        P("grp"),
        P("grp"),
        P(),
        P("grp", "seq", None),
        P("grp"),
        P("grp"),
        P("grp", "seq"),
        P("grp"),
        P("grp", "seq"),
        P("grp", "seq"),
        P("grp"),
        P("grp", "seq"),
        P("grp"),
        P("grp"),
        P("grp"),
        P("grp", "seq"),
        P("grp"),
        P("grp", "seq"),
        P("grp", "seq"),
        P("grp"),
        P("grp", "seq"),
        P("grp"),
        P("grp"),
        P("grp"),
        P("grp", "seq"),
        P("grp"),
        P("grp", "seq"),
        P("grp"),
    )
    small_slice = mesh.shape["grp"] == NZ * NX and mesh.shape["seq"] == NY * NC
    return jax.shard_map(
        on_device_fast if small_slice else on_device_plain,
        mesh=mesh,
        in_specs=placed,
        out_specs=(
            P("grp", "seq", None),
            P("grp", "seq", None),
            P("grp"),
            P("grp"),
            P("grp", "seq"),
            P("grp"),
            P("grp", "seq"),
            P("grp", "seq"),
            P("grp"),
            P("grp", "seq"),
            P("grp"),
            P("grp"),
            P("grp"),
            P("grp", "seq"),
            P("grp"),
            P("grp", "seq"),
            P("grp", "seq"),
            P("grp"),
            P("grp", "seq"),
            P("grp"),
            P("grp"),
            P("grp"),
            P("grp", "seq"),
            P("grp"),
            P("grp", "seq"),
            P("grp"),
        ),
        check_vma=False,
    )
```

```python
import math

import jax
import jax.numpy as jnp
from jax import lax
from jax.experimental import pallas as pl
from jax.experimental.pallas import tpu as pltpu
from jax.sharding import PartitionSpec as P

HEADS = 12
HEAD_DIM = 64


NEG = -1e30
EPS = 1e-05


def norm_rows(values, scaling, offset):
    centre = values - jnp.mean(values, axis=-1, keepdims=True)
    spread = jnp.mean(centre * centre, axis=-1, keepdims=True)
    return centre * lax.rsqrt(spread + EPS) * scaling + offset


def smooth_gate(values):
    return 0.5 * values * (1.0 + lax.erf(values * 0.7071067811865476))


def linear(inputs, weight):
    return jnp.einsum("bri,ij->brj", inputs, weight, preferred_element_type=jnp.float32)


def linear_back(gradient, weight):
    return jnp.einsum("brj,ij->bri", gradient, weight, preferred_element_type=jnp.float32)


def outer_sum(inputs, gradient):
    return jnp.einsum("bri,brj->ij", inputs, gradient, preferred_element_type=jnp.float32)


def row_total(gradient):
    return jnp.sum(gradient.astype(jnp.float32), axis=(0, 1))


def split_heads(values):
    return values.reshape(values.shape[0], values.shape[1], HEADS, HEAD_DIM)


def scores_of(query, key_rows, allowed):
    scores = jnp.einsum(
        "bqhd,bkhd->bhqk",
        split_heads(query),
        split_heads(key_rows),
        preferred_element_type=jnp.float32,
    )
    return jnp.where(allowed[:, None], scores, NEG)


def attend(query, key_rows, values, allowed):
    scores = scores_of(query, key_rows, allowed)
    maximum = jnp.max(scores, axis=-1, keepdims=True)
    raised = jnp.exp(scores - maximum)
    summed = jnp.sum(raised, axis=-1, keepdims=True)
    chances = (raised / summed).astype(jnp.bfloat16)
    blended = jnp.einsum(
        "bhqk,bkhd->bqhd", chances, split_heads(values), preferred_element_type=jnp.float32
    )
    return (blended.reshape(query.shape).astype(jnp.bfloat16), maximum + jnp.log(summed))


def attend_back(grad_low, query, key_rows, values, allowed, logsum):
    scores = scores_of(query, key_rows, allowed)
    chances = jnp.exp(scores - logsum)
    grad_heads = split_heads(grad_low)
    grad_chance = jnp.einsum(
        "bqhd,bkhd->bhqk", grad_heads, split_heads(values), preferred_element_type=jnp.float32
    )
    offset = jnp.sum(chances * grad_chance, axis=-1, keepdims=True)
    grad_score = (chances * (grad_chance - offset)).astype(jnp.bfloat16)
    grad_query = jnp.einsum(
        "bhqk,bkhd->bqhd", grad_score, split_heads(key_rows), preferred_element_type=jnp.float32
    )
    grad_keys = jnp.einsum(
        "bhqk,bqhd->bkhd", grad_score, split_heads(query), preferred_element_type=jnp.float32
    )
    grad_values = jnp.einsum(
        "bhqk,bqhd->bkhd",
        chances.astype(jnp.bfloat16),
        grad_heads,
        preferred_element_type=jnp.float32,
    )
    return (
        grad_query.reshape(query.shape),
        grad_keys.reshape(key_rows.shape),
        grad_values.reshape(values.shape),
    )


def on_device_plain(
    tokens,
    encoder_states,
    lengths,
    frame_counts,
    corpus_ids,
    corpus_weights,
    cotangent,
    first_gain,
    first_bias,
    query_weight,
    query_bias,
    key_weight,
    value_weight,
    value_bias,
    output_weight,
    output_bias,
    second_gain,
    second_bias,
    cross_query_weight,
    cross_query_bias,
    cross_key_weight,
    cross_value_weight,
    cross_value_bias,
    cross_output_weight,
    cross_output_bias,
    third_gain,
    third_bias,
    expand_weight,
    expand_bias,
    reduce_weight,
    reduce_bias,
):
    row_parts = (
        lax.all_gather(query_weight, "grp", axis=0, tiled=True),
        lax.all_gather(key_weight, "grp", axis=0, tiled=True),
        lax.all_gather(value_weight, "grp", axis=0, tiled=True),
        lax.all_gather(output_weight, "grp", axis=0, tiled=True),
        lax.all_gather(cross_query_weight, "grp", axis=0, tiled=True),
        lax.all_gather(cross_key_weight, "grp", axis=0, tiled=True),
        lax.all_gather(cross_value_weight, "grp", axis=0, tiled=True),
        lax.all_gather(cross_output_weight, "grp", axis=0, tiled=True),
        lax.all_gather(expand_weight, "grp", axis=0, tiled=True),
        lax.all_gather(reduce_weight, "grp", axis=0, tiled=True),
        lax.all_gather(first_gain, "grp", axis=0, tiled=True),
        lax.all_gather(first_bias, "grp", axis=0, tiled=True),
        lax.all_gather(query_bias, "grp", axis=0, tiled=True),
        lax.all_gather(value_bias, "grp", axis=0, tiled=True),
        lax.all_gather(output_bias, "grp", axis=0, tiled=True),
        lax.all_gather(second_gain, "grp", axis=0, tiled=True),
        lax.all_gather(second_bias, "grp", axis=0, tiled=True),
        lax.all_gather(cross_query_bias, "grp", axis=0, tiled=True),
        lax.all_gather(cross_value_bias, "grp", axis=0, tiled=True),
        lax.all_gather(cross_output_bias, "grp", axis=0, tiled=True),
        lax.all_gather(third_gain, "grp", axis=0, tiled=True),
        lax.all_gather(third_bias, "grp", axis=0, tiled=True),
        lax.all_gather(expand_bias, "grp", axis=0, tiled=True),
        lax.all_gather(reduce_bias, "grp", axis=0, tiled=True),
    )
    gathered = (
        lax.all_gather(row_parts[0], "seq", axis=1, tiled=True),
        lax.all_gather(row_parts[1], "seq", axis=1, tiled=True),
        lax.all_gather(row_parts[2], "seq", axis=1, tiled=True),
        lax.all_gather(row_parts[3], "seq", axis=1, tiled=True),
        lax.all_gather(row_parts[4], "seq", axis=1, tiled=True),
        lax.all_gather(row_parts[5], "seq", axis=1, tiled=True),
        lax.all_gather(row_parts[6], "seq", axis=1, tiled=True),
        lax.all_gather(row_parts[7], "seq", axis=1, tiled=True),
        lax.all_gather(row_parts[8], "seq", axis=1, tiled=True),
        lax.all_gather(row_parts[9], "seq", axis=1, tiled=True),
    )
    w_query, w_key, w_value, w_mixer, x_query, x_key, x_value, x_mixer, w_expand, w_reduce = (
        gathered
    )
    vectors = [piece.astype(jnp.float32) for piece in row_parts[10:]]
    factor = 1.0 / math.sqrt(HEAD_DIM)
    seq_count = lax.axis_size("seq")
    span_rows = tokens.shape[1]
    query_pos = lax.axis_index("seq") * span_rows + jnp.arange(span_rows, dtype=jnp.int32)
    key_pos = jnp.arange(span_rows * seq_count, dtype=jnp.int32)
    self_mask = (key_pos[None, None, :] <= query_pos[None, :, None]) & (
        key_pos[None, None, :] < lengths[:, None, None]
    )
    frame_pos = jnp.arange(encoder_states.shape[1] * seq_count, dtype=jnp.int32)
    cross_mask = frame_pos[None, None, :] < frame_counts[:, None, None]
    layer_in = tokens.astype(jnp.float32)
    normed_one, norm_back_one = jax.vjp(norm_rows, layer_in, vectors[0], vectors[1])
    normed_one = normed_one.astype(jnp.bfloat16)
    query_low = ((linear(normed_one, w_query) + vectors[2]) * factor).astype(jnp.bfloat16)
    key_low = linear(normed_one, w_key).astype(jnp.bfloat16)
    value_low = (linear(normed_one, w_value) + vectors[3]).astype(jnp.bfloat16)
    key_all, value_all = (
        lax.all_gather(key_low, "seq", axis=1, tiled=True),
        lax.all_gather(value_low, "seq", axis=1, tiled=True),
    )
    self_out, self_logsum = attend(query_low, key_all, value_all, self_mask)
    after_self = layer_in + linear(self_out, w_mixer) + vectors[4]
    normed_two, norm_back_two = jax.vjp(norm_rows, after_self, vectors[5], vectors[6])
    normed_two = normed_two.astype(jnp.bfloat16)
    cross_query = ((linear(normed_two, x_query) + vectors[7]) * factor).astype(jnp.bfloat16)
    frames_all = lax.all_gather(encoder_states, "seq", axis=1, tiled=True)
    cross_keys_all = linear(frames_all, x_key).astype(jnp.bfloat16)
    cross_values_all = (linear(frames_all, x_value) + vectors[8]).astype(jnp.bfloat16)
    cross_out, cross_logsum = attend(cross_query, cross_keys_all, cross_values_all, cross_mask)
    after_cross = after_self + linear(cross_out, x_mixer) + vectors[9]
    normed_three, norm_back_three = jax.vjp(norm_rows, after_cross, vectors[10], vectors[11])
    normed_three = normed_three.astype(jnp.bfloat16)
    hidden = linear(normed_three, w_expand) + vectors[12]
    gated, gate_back = jax.vjp(smooth_gate, hidden)
    gated_low = gated.astype(jnp.bfloat16)
    result = after_cross + linear(gated_low, w_reduce) + vectors[13]
    layer_output = result.astype(jnp.bfloat16)
    present = (query_pos[None, :] < lengths[:, None]).astype(jnp.float32)
    corpus_index = jnp.arange(corpus_weights.shape[0], dtype=jnp.int32)
    corpus_scale = jnp.sum(
        jnp.where(corpus_ids[:, None] == corpus_index[None, :], corpus_weights[None, :], 0.0),
        axis=1,
    )
    grad_out = cotangent.astype(jnp.float32) * (present * corpus_scale[:, None])[:, :, None]
    reduce_low = grad_out.astype(jnp.bfloat16)
    slope_reduce_bias = row_total(reduce_low)
    slope_reduce = outer_sum(gated_low, reduce_low)
    grad_hidden = gate_back(linear_back(reduce_low, w_reduce))[0]
    hidden_low = grad_hidden.astype(jnp.bfloat16)
    slope_expand_bias = row_total(hidden_low)
    slope_expand = outer_sum(normed_three, hidden_low)
    grad_norm_in, slope_gain_three, slope_bias_three = norm_back_three(
        linear_back(hidden_low, w_expand)
    )
    grad_cross = grad_out + grad_norm_in
    cross_low = grad_cross.astype(jnp.bfloat16)
    slope_xmixer_bias = row_total(cross_low)
    slope_xmixer = outer_sum(cross_out, cross_low)
    grad_heard = linear_back(cross_low, x_mixer).astype(jnp.bfloat16)
    grad_cq, part_ck, part_cv = attend_back(
        grad_heard, cross_query, cross_keys_all, cross_values_all, cross_mask, cross_logsum
    )
    slope_xkey = outer_sum(frames_all, part_ck)
    slope_xvalue = outer_sum(frames_all, part_cv)
    slope_xvalue_bias = row_total(part_cv)
    low_cq = (grad_cq * factor).astype(jnp.bfloat16)
    slope_xquery_bias = row_total(low_cq)
    slope_xquery = outer_sum(normed_two, low_cq)
    grad_norm_two, slope_gain_two, slope_bias_two = norm_back_two(linear_back(low_cq, x_query))
    grad_self = grad_cross + grad_norm_two
    self_low = grad_self.astype(jnp.bfloat16)
    slope_mixer_bias = row_total(self_low)
    slope_mixer = outer_sum(self_out, self_low)
    grad_mixed = linear_back(self_low, w_mixer).astype(jnp.bfloat16)
    grad_q, part_k, part_v = attend_back(
        grad_mixed, query_low, key_all, value_all, self_mask, self_logsum
    )
    summed_k, summed_v = (
        lax.psum_scatter(
            part_k.astype(jnp.bfloat16), "seq", scatter_dimension=1, tiled=True
        ).astype(jnp.float32),
        lax.psum_scatter(
            part_v.astype(jnp.bfloat16), "seq", scatter_dimension=1, tiled=True
        ).astype(jnp.float32),
    )
    low_k = summed_k.astype(jnp.bfloat16)
    low_v = summed_v.astype(jnp.bfloat16)
    low_q = (grad_q * factor).astype(jnp.bfloat16)
    slope_query = outer_sum(normed_one, low_q)
    slope_query_bias = row_total(low_q)
    slope_key = outer_sum(normed_one, low_k)
    slope_value = outer_sum(normed_one, low_v)
    slope_value_bias = row_total(low_v)
    grad_normed = (
        linear_back(low_q, w_query) + linear_back(low_k, w_key) + linear_back(low_v, w_value)
    )
    grad_norm_one, slope_gain_one, slope_bias_one = norm_back_one(grad_normed)
    tokens_gradient = (grad_self + grad_norm_one).astype(jnp.bfloat16)
    owned = (
        lax.psum_scatter(slope_query, "grp", scatter_dimension=0, tiled=True),
        lax.psum_scatter(slope_key, "grp", scatter_dimension=0, tiled=True),
        lax.psum_scatter(slope_value, "grp", scatter_dimension=0, tiled=True),
        lax.psum_scatter(slope_mixer, "grp", scatter_dimension=0, tiled=True),
        lax.psum_scatter(slope_xquery, "grp", scatter_dimension=0, tiled=True),
        lax.psum_scatter(slope_xkey, "grp", scatter_dimension=0, tiled=True),
        lax.psum_scatter(slope_xvalue, "grp", scatter_dimension=0, tiled=True),
        lax.psum_scatter(slope_xmixer, "grp", scatter_dimension=0, tiled=True),
        lax.psum_scatter(slope_expand, "grp", scatter_dimension=0, tiled=True),
        lax.psum_scatter(slope_reduce, "grp", scatter_dimension=0, tiled=True),
        lax.psum_scatter(slope_gain_one, "grp", scatter_dimension=0, tiled=True),
        lax.psum_scatter(slope_bias_one, "grp", scatter_dimension=0, tiled=True),
        lax.psum_scatter(slope_query_bias, "grp", scatter_dimension=0, tiled=True),
        lax.psum_scatter(slope_value_bias, "grp", scatter_dimension=0, tiled=True),
        lax.psum_scatter(slope_mixer_bias, "grp", scatter_dimension=0, tiled=True),
        lax.psum_scatter(slope_gain_two, "grp", scatter_dimension=0, tiled=True),
        lax.psum_scatter(slope_bias_two, "grp", scatter_dimension=0, tiled=True),
        lax.psum_scatter(slope_xquery_bias, "grp", scatter_dimension=0, tiled=True),
        lax.psum_scatter(slope_xvalue_bias, "grp", scatter_dimension=0, tiled=True),
        lax.psum_scatter(slope_xmixer_bias, "grp", scatter_dimension=0, tiled=True),
        lax.psum_scatter(slope_gain_three, "grp", scatter_dimension=0, tiled=True),
        lax.psum_scatter(slope_bias_three, "grp", scatter_dimension=0, tiled=True),
        lax.psum_scatter(slope_expand_bias, "grp", scatter_dimension=0, tiled=True),
        lax.psum_scatter(slope_reduce_bias, "grp", scatter_dimension=0, tiled=True),
    )
    matrices = (
        lax.psum_scatter(
            owned[0].astype(jnp.bfloat16), "seq", scatter_dimension=1, tiled=True
        ).astype(jnp.float32),
        lax.psum_scatter(
            owned[1].astype(jnp.bfloat16), "seq", scatter_dimension=1, tiled=True
        ).astype(jnp.float32),
        lax.psum_scatter(
            owned[2].astype(jnp.bfloat16), "seq", scatter_dimension=1, tiled=True
        ).astype(jnp.float32),
        lax.psum_scatter(
            owned[3].astype(jnp.bfloat16), "seq", scatter_dimension=1, tiled=True
        ).astype(jnp.float32),
        lax.psum_scatter(
            owned[4].astype(jnp.bfloat16), "seq", scatter_dimension=1, tiled=True
        ).astype(jnp.float32),
        lax.psum_scatter(
            owned[5].astype(jnp.bfloat16), "seq", scatter_dimension=1, tiled=True
        ).astype(jnp.float32),
        lax.psum_scatter(
            owned[6].astype(jnp.bfloat16), "seq", scatter_dimension=1, tiled=True
        ).astype(jnp.float32),
        lax.psum_scatter(
            owned[7].astype(jnp.bfloat16), "seq", scatter_dimension=1, tiled=True
        ).astype(jnp.float32),
        lax.psum_scatter(
            owned[8].astype(jnp.bfloat16), "seq", scatter_dimension=1, tiled=True
        ).astype(jnp.float32),
        lax.psum_scatter(
            owned[9].astype(jnp.bfloat16), "seq", scatter_dimension=1, tiled=True
        ).astype(jnp.float32),
    )
    smaller = lax.psum(
        (
            owned[10],
            owned[11],
            owned[12],
            owned[13],
            owned[14],
            owned[15],
            owned[16],
            owned[17],
            owned[18],
            owned[19],
            owned[20],
            owned[21],
            owned[22],
            owned[23],
        ),
        "seq",
    )
    return (
        layer_output,
        tokens_gradient,
        smaller[0],
        smaller[1],
        matrices[0],
        smaller[2],
        matrices[1],
        matrices[2],
        smaller[3],
        matrices[3],
        smaller[4],
        smaller[5],
        smaller[6],
        matrices[4],
        smaller[7],
        matrices[5],
        matrices[6],
        smaller[8],
        matrices[7],
        smaller[9],
        smaller[10],
        smaller[11],
        matrices[8],
        smaller[12],
        matrices[9],
        smaller[13],
    )


MESH_ID = pl.DeviceIdType.MESH
NZ, NX, NY, NC = 4, 2, 2, 2
GROUPS = 8


def where_am_i():
    grp = lax.axis_index("grp")
    seq = lax.axis_index("seq")
    return grp // NX, lax.rem(grp, NX), seq // NC, lax.rem(seq, NC)


def device_at(z, x, y, c):
    return (z * NX + x, y * NC + c)


def lanes(start, size):
    return pl.ds(pl.multiple_of(start, 128), size)


def pieces_of(bank, group, y, c, x, z_from, z_to):
    heads, mixer, pairs, wide, tall = bank
    column = pl.ds(z_from, z_to - z_from)
    if group == 0:
        return [heads.at[column, x]]
    if group == 1:
        return [mixer.at[y, column, x, :, lanes(c * 256, 256)]]
    if group < 4:
        return [pairs.at[group - 2, y, column, x, :, lanes(c * 384, 384)]]
    if group < 6:
        start = (y * NC + c) * 768 + (group - 4) * 384
        return [wide.at[column, x, :, lanes(start, 384)]]
    return [
        tall.at[y, c, pl.ds((group - 6) * 96, 96), lanes((z * NX + x) * 384, 384)]
        for z in range(z_from, z_to)
    ]


def piece_at(bank, group, y, c, x, z):
    heads, mixer, pairs, wide, tall = bank
    if group == 0:
        return heads.at[z, x]
    if group == 1:
        return mixer.at[y, z, x, :, lanes(c * 256, 256)]
    if group < 4:
        return pairs.at[group - 2, y, z, x, :, lanes(c * 384, 384)]
    if group < 6:
        return wide.at[z, x, :, lanes((y * NC + c) * 768 + (group - 4) * 384, 384)]
    return tall.at[y, c, pl.ds((group - 6) * 96, 96), lanes((z * NX + x) * 384, 384)]


def own_piece(own, group):
    heads, mixer, pairs, wide, tall = own
    if group == 0:
        return heads
    if group == 1:
        return mixer
    if group < 4:
        return pairs.at[group - 2]
    if group < 6:
        return wide.at[:, pl.ds((group - 4) * 384, 384)]
    return tall.at[pl.ds((group - 6) * 96, 96), :]


class Mail:
    def __init__(self, send_sems, recv_sems):
        self.send_sems, self.recv_sems, self.count, self.sent = send_sems, recv_sems, 0, []

    def slots(self, number):
        first = self.count
        self.count += number
        return list(range(first, first + number))

    def post(self, source, target, slot, device):
        copy = pltpu.make_async_remote_copy(
            src_ref=source,
            dst_ref=target,
            send_sem=self.send_sems.at[slot],
            recv_sem=self.recv_sems.at[slot],
            device_id=device,
            device_id_type=MESH_ID,
        )
        copy.start()
        self.sent.append(copy)

    def arrive(self, target, slot, device):
        pltpu.make_async_remote_copy(
            src_ref=target,
            dst_ref=target,
            send_sem=self.send_sems.at[slot],
            recv_sem=self.recv_sems.at[slot],
            device_id=device,
            device_id_type=MESH_ID,
        ).wait_recv()

    def finish(self):
        for copy in self.sent:
            copy.wait_send()


def greet(z, x, y, c):
    barrier = pltpu.get_barrier_semaphore()
    friends = [device_at(lax.rem(z + k, NZ), x, y, c) for k in range(1, NZ)]
    friends += [device_at(lax.rem(z + k, NZ), 1 - x, y, c) for k in range(NZ)]
    friends += [device_at(z, x, 1 - y, c), device_at(z, x, y, 1 - c), device_at(z, x, 1 - y, 1 - c)]
    for friend in friends:
        pl.semaphore_signal(barrier, inc=1, device_id=friend, device_id_type=MESH_ID)
    pl.semaphore_wait(barrier, len(friends))


def parts_in(group, number):
    return number if group >= 6 else 1


def joined(first, second):
    return jnp.concatenate([first, second], axis=1)


def mixed(first, second, core):
    even = joined(joined(first[:, :128], joined(first[:, 128:], second[:, 128:])), second[:, :128])
    odd = joined(joined(first[:, 64:], joined(second[:, :64], first[:, :64])), second[:, 64:])
    return jnp.where(core == 0, even, odd).astype(jnp.bfloat16)


def packed_heads(query, key, value, core):
    nothing = jnp.zeros_like(value[:, :64])
    even = [query[:, :128], key[:, :128], value[:, :128], query[:, 128:], key[:, 128:], value[:, 128:], nothing]
    odd = [query[:, 64:], key[:, 64:], value[:, 64:], key[:, :64], query[:, :64], nothing, value[:, :64]]
    even, odd = jnp.concatenate(even, axis=1), jnp.concatenate(odd, axis=1)
    return jnp.where(core == 0, even, odd).astype(jnp.bfloat16)


def packed_mixer(mixer, core):
    nothing = jnp.zeros_like(mixer[:, :64])
    even = joined(mixer, nothing)
    odd = joined(mixer[:, 64:], joined(nothing, mixer[:, :64]))
    return jnp.where(core == 0, even, odd).astype(jnp.bfloat16)


def own_tiles(row, y, core):
    block = jnp.where(y == 0, row[:, :384], row[:, 384:])
    lane = lax.broadcasted_iota(jnp.int32, (1, 128), 1)
    mine = lax.shift_right_logical(lane, 6) == core
    return (
        jnp.where(core == 0, block[:, :128], block[:, 256:]),
        jnp.where(mine, block[:, 128:256], jnp.zeros((1, 128), jnp.float32)),
    )


def natural_row(pair, third, y, core):
    nothing = jnp.zeros_like(pair)
    first, last = jnp.where(core == 0, pair, nothing), jnp.where(core == 0, nothing, pair)
    block = jnp.concatenate([first, third, last], axis=1)
    empty = jnp.zeros_like(block)
    return jnp.concatenate([jnp.where(y == 0, block, empty), jnp.where(y == 0, empty, block)], axis=1)


ORDER = (0, 2, 1, 3, 4, 5, 6, 7)


def forward_kernel(
    frame_span, lengths, counts,
    query_in, key_in, value_in, mixer_in, xkey_in, xvalue_in, xquery_in, xmixer_in, wide_in, tall_in,
    vectors_in, wide_bias_in, frames_short, tokens_in,
    heads, mixer, pairs, wide, tall, frames, vec_out, wide_bias,
    a_to, rows_to, third_to, o_to, h1_to, c_to, p_self_to, ck_to, cv_to, cq_to, o2_to, h2_to, m_to, p_cross_to,
    tokens_got, small, heads_here, mixer_here, pairs_here, frames_here,
    a_all, head_rows, third, o, h1, c, p_self, ck, cv, cq, o2, h2, m, p_cross,
    o_send, o_got, scores, self_scores, self_bias, cross_bias, heads_in, mixer_in_v, pairs_in, frames_in, small_in,
    send_sems, recv_sems, local_sems, load_sems, save_sems,
):
    z, x, y, c_own = where_am_i()
    heads_in[...] = packed_heads(*[ref[...].astype(jnp.float32) for ref in (query_in, key_in, value_in)], c_own)
    mixer_in_v[...] = packed_mixer(mixer_in[...].astype(jnp.float32), c_own)
    for number, (first, second) in enumerate(((xkey_in, xvalue_in), (xquery_in, xmixer_in))):
        pairs_in[number] = mixed(first[...].astype(jnp.float32), second[...].astype(jnp.float32), c_own)
    small_in[...] = jnp.zeros((32, 128), jnp.bfloat16)
    small_in[0:13, 0:96] = vectors_in[...]
    small_in[16:19, :] = wide_bias_in[...]
    frames_in[:, 368:384] = jnp.zeros((2, 16, 768), jnp.bfloat16)
    frames_in[:, 0:frame_span] = frames_short[...]
    greet(z, x, y, c_own)
    mail = Mail(send_sems, recv_sems)
    own = (heads_in, mixer_in_v, pairs_in, wide_in, tall_in)
    bank = (heads, mixer, pairs, wide, tall)
    far_mate = device_at(z, x, 1 - y, 1 - c_own)
    x_mate, y_mate = device_at(z, 1 - x, y, c_own), device_at(z, x, 1 - y, c_own)
    c_mate = device_at(z, x, y, 1 - c_own)
    z_mates = [device_at(lax.rem(z + n, NZ), x, y, c_own) for n in range(1, NZ)]
    grp = z * NX + x
    seq = y * NC + c_own

    local = []

    def keep(source, target):
        copy = pltpu.make_async_copy(source, target, local_sems.at[len(local)])
        copy.start()
        local.append(copy)

    small_slots = mail.slots(2 * NZ - 1)
    small_to = z_mates + [device_at(lax.rem(z + n, NZ), 1 - x, y, c_own) for n in range(NZ)]
    token_slots = mail.slots(3)
    frame_slots = mail.slots(3)
    z_slots = [mail.slots(NZ - 1) for _ in range(GROUPS)]
    x_slots = [mail.slots(parts_in(g, 4)) for g in range(GROUPS)]
    y_slots = [mail.slots(parts_in(g, 4)) for g in range(GROUPS)]
    dy_slots = [mail.slots(parts_in(g, VIA_X)) for g in range(GROUPS)]
    dx_slots = [mail.slots(parts_in(g, 4 - VIA_X)) for g in range(GROUPS)]
    co_slots = [mail.slots(parts_in(g, 4)) for g in range(GROUPS)]
    cx_slots = [mail.slots(parts_in(g, 4)) for g in range(GROUPS)]
    cy_slots = [mail.slots(parts_in(g, 4)) for g in range(GROUPS)]
    cdy_slots = [mail.slots(parts_in(g, VIA_X)) for g in range(GROUPS)]
    cdx_slots = [mail.slots(parts_in(g, 4 - VIA_X)) for g in range(GROUPS)]

    def to_column(group):
        for n in range(1, NZ):
            mail.post(
                own_piece(own, group), piece_at(bank, group, y, c_own, x, z), z_slots[group][n - 1], z_mates[n - 1]
            )

    def post_all(group, slots, device, yy, cc, xx, z_from, z_to):
        for slot, ref in zip(slots, pieces_of(bank, group, yy, cc, xx, z_from, z_to)):
            mail.post(ref, ref, slot, device)

    def arrive_all(group, slots, device, yy, cc, xx, z_from, z_to):
        for slot, ref in zip(slots, pieces_of(bank, group, yy, cc, xx, z_from, z_to)):
            mail.arrive(ref, slot, device)

    def spread(group):
        for n in range(1, NZ):
            zz = lax.rem(z + NZ - n, NZ)
            mail.arrive(piece_at(bank, group, y, c_own, x, zz), z_slots[group][n - 1], z_mates[n - 1])
        local[group].wait()
        post_all(group, x_slots[group], x_mate, y, c_own, x, 0, 4)
        if group == 0:
            return
        post_all(group, y_slots[group], y_mate, y, c_own, x, 0, 4)
        post_all(group, co_slots[group], c_mate, y, c_own, x, 0, 4)

    def turn(group):
        if group == 0:
            arrive_all(group, x_slots[group], x_mate, y, c_own, 1 - x, 0, 4)
            return
        arrive_all(group, y_slots[group], y_mate, 1 - y, c_own, x, 0, 4)
        post_all(group, dx_slots[group], x_mate, 1 - y, c_own, x, VIA_X, 4)
        post_all(group, cy_slots[group], c_mate, 1 - y, c_own, x, 0, 4)
        arrive_all(group, x_slots[group], x_mate, y, c_own, 1 - x, 0, 4)
        post_all(group, dy_slots[group], y_mate, y, c_own, 1 - x, 0, VIA_X)
        post_all(group, cx_slots[group], c_mate, y, c_own, 1 - x, 0, 4)

    def share(group):
        if group == 0:
            return
        arrive_all(group, dy_slots[group], y_mate, 1 - y, c_own, 1 - x, 0, VIA_X)
        post_all(group, cdy_slots[group], c_mate, 1 - y, c_own, 1 - x, 0, VIA_X)
        arrive_all(group, dx_slots[group], x_mate, 1 - y, c_own, 1 - x, VIA_X, 4)
        post_all(group, cdx_slots[group], c_mate, 1 - y, c_own, 1 - x, VIA_X, 4)

    def complete(group):
        arrive_all(group, co_slots[group], c_mate, y, 1 - c_own, x, 0, 4)
        arrive_all(group, cx_slots[group], c_mate, y, 1 - c_own, 1 - x, 0, 4)
        arrive_all(group, cy_slots[group], c_mate, 1 - y, 1 - c_own, x, 0, 4)
        arrive_all(group, cdy_slots[group], c_mate, 1 - y, 1 - c_own, 1 - x, 0, VIA_X)
        arrive_all(group, cdx_slots[group], c_mate, 1 - y, 1 - c_own, 1 - x, VIA_X, 4)

    def frame_rows(number):
        return frames.at[:, number]

    loads = []

    def load(source, target):
        copy = pltpu.make_async_copy(source, target, load_sems.at[len(loads)])
        copy.start()
        loads.append(copy)
        return copy

    def load_pair(group):
        complete(group)
        return load(pairs.at[group - 2], pairs_here.at[group - 2])

    saves = []

    def save(source, target):
        copy = pltpu.make_async_copy(source, target, save_sems.at[len(saves)])
        copy.start()
        saves.append(copy)

    for group in range(GROUPS):
        keep(own_piece(own, group), piece_at(bank, group, y, c_own, x, z))
    keep(small_in, small.at[grp])
    keep(frames_in, frame_rows(seq))
    keep(tokens_in, tokens_got.at[seq])
    to_column(ORDER[0])
    for slot, device in zip(small_slots, small_to):
        mail.post(small_in, small.at[grp], slot, device)
    to_column(ORDER[1])
    mail.post(frames_in, frame_rows(seq), frame_slots[0], y_mate)
    mail.post(frames_in, frame_rows(seq), frame_slots[1], c_mate)
    mail.post(tokens_in, tokens_got.at[seq], token_slots[0], y_mate)
    mail.post(tokens_in, tokens_got.at[seq], token_slots[1], c_mate)
    to_column(ORDER[2])

    pending = []
    for step in range(GROUPS + 2):
        if step + 3 < GROUPS:
            pending.append((to_column, ORDER[step + 3]))
        if step < GROUPS:
            pending.append((spread, ORDER[step]))
        if 0 <= step - 1 < GROUPS:
            pending.append((turn, ORDER[step - 1]))
        if 0 <= step - 2 < GROUPS:
            pending.append((share, ORDER[step - 2]))

    def tick(number=1):
        while number > 0 and pending:
            action, group = pending.pop(0)
            action(group)
            if action is not to_column:
                number -= 1

    def until(action, group):
        while (action, group) in pending:
            tick()

    for n in range(1, NZ):
        zz = lax.rem(z + NZ - n, NZ)
        mail.arrive(small.at[zz * NX + x], small_slots[n - 1], z_mates[n - 1])
    for n in range(NZ):
        zz = lax.rem(z + NZ - n, NZ)
        mail.arrive(small.at[zz * NX + 1 - x], small_slots[NZ - 1 + n], x_mate)
    local[GROUPS].wait()
    vec_out[...] = jnp.concatenate([small[g, 0:16, 0:96].astype(jnp.float32) for g in range(8)], axis=1)
    for g in range(8):
        three = small[g, 16:24, :].astype(jnp.float32)
        for n in range(3):
            at = g * 384 + n * 128
            wide_bias[:, at:at + 128] = three[n:n + 1]

    o_slots = mail.slots(6)
    until(turn, 0)
    other = (1 - y) * NC + c_own
    mail.arrive(tokens_got.at[other], token_slots[0], y_mate)
    mail.post(tokens_got.at[other], tokens_got.at[other], token_slots[2], c_mate)
    heads_loaded = load(heads, heads_here)
    mail.arrive(frame_rows(other), frame_slots[0], y_mate)
    mail.post(frame_rows(other), frame_rows(other), frame_slots[2], c_mate)
    mail.arrive(tokens_got.at[y * NC + 1 - c_own], token_slots[1], c_mate)
    mail.arrive(tokens_got.at[(1 - y) * NC + 1 - c_own], token_slots[2], c_mate)
    for copy in local[GROUPS + 1:]:
        copy.wait()
    heads_loaded.wait()
    phase = self_forward(lengths, tokens_got, vec_out, heads_here, a_all, head_rows, third, p_self, o_send, self_scores, self_bias)
    mates = ((c_mate, y * NC + 1 - c_own), (y_mate, other), (far_mate, (1 - y) * NC + 1 - c_own))
    for number, t in enumerate(phase):
        if t is not None:
            for place, (mate, mate_seq) in enumerate(mates):
                mail.post(o_send.at[mate_seq, t], o_got.at[seq, t], o_slots[3 * t + place], mate)
            o_got[seq, t] = o_send[seq, t]
        if number % 2 == 1:
            tick()
    mail.arrive(frame_rows(y * NC + 1 - c_own), frame_slots[1], c_mate)
    mail.arrive(frame_rows((1 - y) * NC + 1 - c_own), frame_slots[2], c_mate)
    frames_loaded = load(frames, frames_here)
    for source, target in ((a_all, a_to), (head_rows, rows_to), (third, third_to), (p_self, p_self_to)):
        save(source, target)
    until(share, 2)
    kv_loaded = load_pair(2)
    frames_loaded.wait()
    kv_loaded.wait()
    for number, _ in enumerate(cross_keys(frames_here, vec_out, pairs_here.at[0], ck, cv)):
        if number % 2 == 1:
            tick()
    save(ck, ck_to)
    save(cv, cv_to)
    until(share, 1)
    complete(1)
    mixer_loaded = load(mixer, mixer_here)
    for t in range(2):
        for place, (mate, mate_seq) in enumerate(mates):
            mail.arrive(o_got.at[mate_seq, t], o_slots[3 * t + place], mate)
    mixer_loaded.wait()
    self_out(tokens_got, vec_out, mixer_here, o_got, o, h1, c)
    until(share, 3)
    third_loaded = load_pair(3)
    for source, target in ((o, o_to), (h1, h1_to), (c, c_to)):
        save(source, target)
    third_loaded.wait()
    phase = cross_forward(
        counts, frame_span, c, vec_out, pairs_here.at[1], ck, cv, h1, cq, o2, h2, m, p_cross, scores, cross_bias
    )
    for number, _ in enumerate(phase):
        if 1 <= number <= 12:
            t, pair = (number - 1) // 6, (number - 1) % 6
            save(p_cross.at[t, pair], p_cross_to.at[t, pair])
        if number % 2 == 1:
            tick()
    for source, target in ((cq, cq_to), (o2, o2_to), (h2, h2_to), (m, m_to)):
        save(source, target)
    tick(100)
    for group in (4, 5, 6, 7):
        complete(group)
    for copy in saves:
        copy.wait()
    mail.finish()


VIA_X = 2


def slots_needed():
    return (2 * NZ - 1) + 12 + sum(
        3 + parts_in(g, 4) * 5 + 2 * (parts_in(g, VIA_X) + parts_in(g, 4 - VIA_X)) for g in range(GROUPS)
    )


def run_forward(lengths, counts, matrices, vectors, wide_bias, frames, tokens):
    bf16, f32 = jnp.bfloat16, jnp.float32
    number = slots_needed()
    span = tokens.shape[1]
    anywhere = pl.BlockSpec(memory_space=pl.ANY)
    inside = pl.BlockSpec(memory_space=pltpu.VMEM)
    scalar = pl.BlockSpec(memory_space=pltpu.SMEM)
    rows = (2, span, 768)
    kept = [
        ((2, 4, span, 768), bf16), ((2, 512, 640), bf16), ((2, 512, 128), bf16), (rows, bf16), (rows, f32),
        (rows, bf16), ((2, 4, 3 * span, 512), bf16), ((2, 6, 1536, 128), bf16), ((2, 6, 1536, 128), bf16), (rows, bf16),
        (rows, bf16), (rows, f32), (rows, bf16), ((2, 6, 2 * span, 1536), bf16),
    ]
    frame_span = frames.shape[1]
    frames_shape = (2, NY * NC, 384, 768)
    return pl.pallas_call(
        lambda *refs: forward_kernel(frame_span, *refs),
        out_shape=(
            jax.ShapeDtypeStruct((NZ, NX, 96, 640), bf16),
            jax.ShapeDtypeStruct((NY, NZ, NX, 96, 512), bf16),
            jax.ShapeDtypeStruct((2, NY, NZ, NX, 96, 768), bf16),
            jax.ShapeDtypeStruct((NZ, NX, 96, 3072), bf16),
            jax.ShapeDtypeStruct((NY, NC, 192, 3072), bf16),
            jax.ShapeDtypeStruct(frames_shape, bf16),
            jax.ShapeDtypeStruct((16, 768), f32),
            jax.ShapeDtypeStruct((1, 3072), f32),
        ) + tuple(jax.ShapeDtypeStruct(shape, kind) for shape, kind in kept),
        in_specs=[scalar] * 2 + [inside] * 14,
        out_specs=(anywhere,) * 6 + (inside,) * 2 + (anywhere,) * len(kept),
        scratch_shapes=[
            pltpu.VMEM((4,) + tokens.shape, bf16),
            pltpu.VMEM((8, 32, 128), bf16),
            pltpu.VMEM((NZ, NX, 96, 640), bf16),
            pltpu.VMEM((NY, NZ, NX, 96, 512), bf16),
            pltpu.VMEM((2, NY, NZ, NX, 96, 768), bf16),
            pltpu.VMEM(frames_shape, bf16),
        ] + [pltpu.VMEM(shape, kind) for shape, kind in kept] + [
            pltpu.VMEM((4, 2, span, 256), bf16),
            pltpu.VMEM((4, 2, span, 256), bf16),
            pltpu.VMEM((2 * span, 1536), f32),
            pltpu.VMEM((3 * span, 512), f32),
            pltpu.VMEM((2, 4 * span, 512), f32),
            pltpu.VMEM((2, 1, 1536), f32),
            pltpu.VMEM((96, 640), bf16),
            pltpu.VMEM((96, 256), bf16),
            pltpu.VMEM((2, 96, 384), bf16),
            pltpu.VMEM((2, 384, 768), bf16),
            pltpu.VMEM((32, 128), bf16),
            pltpu.SemaphoreType.DMA((number,)),
            pltpu.SemaphoreType.DMA((number,)),
            pltpu.SemaphoreType.DMA((GROUPS + 3,)),
            pltpu.SemaphoreType.DMA((5,)),
            pltpu.SemaphoreType.DMA((26,)),
        ],
        compiler_params=pltpu.CompilerParams(
            collective_id=1, has_side_effects=True, vmem_limit_bytes=60 << 20
        ),
        name="gather_forward",
    )(lengths, counts, *matrices, vectors, wide_bias, frames, tokens)


def mm(left, right):
    return lax.dot_general(left, right, (((1,), (0,)), ((), ())), preferred_element_type=jnp.float32)


def mm_back(left, right):
    return lax.dot_general(left, right, (((1,), (1,)), ((), ())), preferred_element_type=jnp.float32)


def mm_rows(left, right):
    return lax.dot_general(left, right, (((0,), (0,)), ((), ())), preferred_element_type=jnp.float32)


def low_lanes(rows):
    return lax.broadcasted_iota(jnp.int32, (rows, 128), 1) < 64


def turned(tile):
    return pltpu.roll(tile, 64, 1)


def tile_of(values, number):
    return values[:, number * 128:(number + 1) * 128]


def split_first(near, far):
    low = low_lanes(near.shape[0])
    return [tile_of(near, 0), jnp.where(low, tile_of(near, 1), tile_of(far, 1)), tile_of(far, 0)]


def split_second(near, far):
    low = low_lanes(near.shape[0])
    return [tile_of(near, 1), turned(jnp.where(low, tile_of(far, 0), tile_of(near, 0))), tile_of(far, 1)]


def join_first(values):
    low = low_lanes(values.shape[0])
    middle = tile_of(values, 1)
    nothing = jnp.zeros_like(middle)
    near = jnp.concatenate([tile_of(values, 0), jnp.where(low, middle, nothing)], axis=1)
    far = jnp.concatenate([tile_of(values, 2), jnp.where(low, nothing, middle)], axis=1)
    return near.astype(jnp.bfloat16), far.astype(jnp.bfloat16)


def join_second(values):
    low = low_lanes(values.shape[0])
    middle = turned(tile_of(values, 1))
    nothing = jnp.zeros_like(middle)
    near = jnp.concatenate([jnp.where(low, nothing, middle), tile_of(values, 0)], axis=1)
    far = jnp.concatenate([jnp.where(low, middle, nothing), tile_of(values, 2)], axis=1)
    return near.astype(jnp.bfloat16), far.astype(jnp.bfloat16)


def join_both(first, second):
    low = low_lanes(first.shape[0])
    mine, other = tile_of(first, 1), turned(tile_of(second, 1))
    return jnp.concatenate(
        [
            tile_of(first, 0), jnp.where(low, mine, other), tile_of(second, 0),
            tile_of(first, 2), jnp.where(low, other, mine), tile_of(second, 2),
        ],
        axis=1,
    ).astype(jnp.bfloat16)


def block_of(pair, y, at):
    if len(pair.shape) == 3:
        return pair[y, :, at]
    return pair[y, :, :, :, at].reshape(768, -1)


def times_first(values, pair):
    tiles = []
    for y in range(2):
        tiles += split_first(mm(values, block_of(pair, y, slice(0, 256))), mm(values, block_of(pair, y, slice(384, 640))))
    return tiles


def times_second(values, pair):
    tiles = []
    for y in range(2):
        tiles += split_second(mm(values, block_of(pair, y, slice(128, 384))), mm(values, block_of(pair, y, slice(512, 768))))
    return tiles


def back_first(grads, pair):
    out = None
    for y in range(2):
        near, far = join_first(grads[:, y * 384:(y + 1) * 384])
        part = mm_back(near, block_of(pair, y, slice(0, 256))) + mm_back(far, block_of(pair, y, slice(384, 640)))
        out = part if out is None else out + part
    return out


def back_second(grads, pair):
    out = None
    for y in range(2):
        near, far = join_second(grads[:, y * 384:(y + 1) * 384])
        part = mm_back(near, block_of(pair, y, slice(128, 384))) + mm_back(far, block_of(pair, y, slice(512, 768)))
        out = part if out is None else out + part
    return out


def normed(values, gain, bias):
    return norm_rows(values, gain, bias).astype(jnp.bfloat16)


def normed_back(values, gain, grads):
    centre = values - jnp.mean(values, axis=-1, keepdims=True)
    scale = lax.rsqrt(jnp.mean(centre * centre, axis=-1, keepdims=True) + EPS)
    unit = centre * scale
    inner = grads * gain
    back = scale * (
        inner - jnp.mean(inner, axis=-1, keepdims=True) - unit * jnp.mean(inner * unit, axis=-1, keepdims=True)
    )
    return back, jnp.sum(grads * unit, axis=0, keepdims=True), jnp.sum(grads, axis=0, keepdims=True)


def column_sum(values):
    return jnp.sum(values.astype(jnp.float32), axis=0, keepdims=True)


def both_heads(both):
    low = low_lanes(both.shape[0])
    nothing = jnp.zeros_like(both)
    return jnp.concatenate([jnp.where(low, both, nothing), jnp.where(low, nothing, both)], axis=0)


def stacked(values, t, pair):
    return both_heads(values[t, :, pair * 128:(pair + 1) * 128])


def third_head(tile, core):
    lane = lax.broadcasted_iota(jnp.int32, tile.shape, 1)
    return jnp.where(lax.shift_right_logical(lane, 6) == core, tile, jnp.zeros_like(tile))


def unstacked(values):
    half = values.shape[0] // 2
    return jnp.where(low_lanes(half), values[:half], values[half:])


CHUNK = 16


def soften(scores, bias, chances, rows, width):
    def one(number, carry):
        first = pl.multiple_of(number * CHUNK, CHUNK)
        values = scores[pl.ds(first, CHUNK), 0:width] + bias(first)
        raised = jnp.exp(values - jnp.max(values, axis=1, keepdims=True))
        share = raised * (1.0 / jnp.sum(raised, axis=1, keepdims=True))
        chances[pl.ds(first, CHUNK), 0:width] = share.astype(jnp.bfloat16)
        return carry

    lax.fori_loop(0, rows // CHUNK, one, 0, unroll=2 if rows // CHUNK % 2 == 0 else 3)


def soften_back(chances, slopes, grads, rows, width):
    def one(number, carry):
        first = pl.multiple_of(number * CHUNK, CHUNK)
        share = chances[pl.ds(first, CHUNK), 0:width].astype(jnp.float32)
        slope = slopes[pl.ds(first, CHUNK), 0:width]
        inner = jnp.sum(share * slope, axis=1, keepdims=True)
        grads[pl.ds(first, CHUNK), 0:width] = (share * (slope - inner)).astype(jnp.bfloat16)
        return carry

    lax.fori_loop(0, rows // CHUNK, one, 0, unroll=2 if rows // CHUNK % 2 == 0 else 3)


def self_forward(lengths, tokens, vec, heads, a_out, rows_out, third_out, p_out, o_out, scores, bias):
    span = tokens.shape[2]
    z, x, y, core = where_am_i()
    factor = 1.0 / math.sqrt(HEAD_DIM)
    for s in range(4):
        for t in range(2):
            a_out[t, s] = normed(tokens[s, t].astype(jnp.float32), vec[0:1], vec[1:2])
    yield None
    lane = lax.broadcasted_iota(jnp.int32, (1, 128), 1)
    mine = lax.shift_right_logical(lane, 6) == core
    nothing = jnp.zeros((1, 128), jnp.float32)
    query_pair, query_third = own_tiles(vec[2:3], y, core)
    value_pair, value_third = own_tiles(vec[3:4], y, core)
    offset = jnp.concatenate([query_pair, nothing, value_pair, query_third, value_third], axis=1)
    ones = nothing + 1.0
    scale = jnp.concatenate([ones * factor, ones, ones, jnp.where(mine, ones * factor, ones), ones], axis=1)
    for t in range(2):
        row = lax.broadcasted_iota(jnp.int32, (4 * span, 512), 0)
        place = lax.broadcasted_iota(jnp.int32, (4 * span, 512), 1)
        bias[t] = jnp.where((place <= row) & (place < lengths[t]), 0.0, NEG)
        product = mm(a_out[t].reshape(4 * span, 768), heads[...].reshape(768, 640))
        product = (product + offset) * scale
        rows_out[t, 0:4 * span] = product.astype(jnp.bfloat16)
        rows_out[t, 4 * span:512] = jnp.zeros((512 - 4 * span, 640), jnp.bfloat16)
        third_out[t, 0:4 * span] = turned(product[:, 384:512]).astype(jnp.bfloat16)
        third_out[t, 4 * span:512] = jnp.zeros((512 - 4 * span, 128), jnp.bfloat16)
        yield None
    for t in range(2):
        for block in range(4):
            rows, width = slice(block * span, (block + 1) * span), 128 * (block + 1)
            scores[0:2 * span, 0:width] = mm_back(
                both_heads(rows_out[t, rows, 0:128]), rows_out[t, 0:width, 128:256]
            )
            scores[2 * span:3 * span, 0:width] = mm_back(
                third_head(rows_out[t, rows, 384:512], core), third_out[t, 0:width]
            )
            chances = p_out.at[t, block]
            soften(
                scores, lambda first: bias[t, pl.ds(block * span + lax.rem(first, span), CHUNK), 0:width], chances,
                3 * span, width,
            )
            blended = mm(chances[0:2 * span, 0:width], rows_out[t, 0:width, 256:384])
            o_out[block, t, :, 0:128] = unstacked(blended).astype(jnp.bfloat16)
            blended = mm(chances[2 * span:3 * span, 0:width], rows_out[t, 0:width, 512:640])
            o_out[block, t, :, 128:256] = blended.astype(jnp.bfloat16)
            yield t if block == 3 else None


def self_out(tokens, vec, mixer, o_got, o_out, h1_out, c_out):
    span = tokens.shape[2]
    seq = lax.axis_index("seq")
    low = low_lanes(span)
    for t in range(2):
        for y in range(2):
            even, odd = o_got[2 * y, t], o_got[2 * y + 1, t]
            tiles = [even[:, 0:128], jnp.where(low, even[:, 128:256], odd[:, 128:256]), odd[:, 0:128]]
            for number, tile in enumerate(tiles):
                at = slice(y * 384 + number * 128, y * 384 + (number + 1) * 128)
                o_out[t, :, at] = tile
    rows = o_out[...].reshape(2 * span, 768)
    low = low_lanes(2 * span)
    for y in range(2):
        product = mm(rows, mixer[y].reshape(768, 512))
        tiles = [product[:, 0:128], jnp.where(low, product[:, 128:256], product[:, 384:512]), product[:, 256:384]]
        for number, tile in enumerate(tiles):
            at = slice(y * 384 + number * 128, y * 384 + (number + 1) * 128)
            for t in range(2):
                h1_out[t, :, at] = (
                    tokens[seq, t, :, at].astype(jnp.float32) + tile[t * span:(t + 1) * span] + vec[4:5, at]
                )
    for t in range(2):
        c_out[t] = normed(h1_out[t], vec[5:6], vec[6:7])


def cross_keys(frames, vec, kv, ck_out, cv_out):
    for t in range(2):
        for s in range(4):
            block = frames[t, s]
            rows = slice(s * 384, (s + 1) * 384)
            for y in range(2):
                product = mm(block, block_of(kv, y, slice(0, 768)))
                near, far = product[:, 0:384], product[:, 384:768]
                keys = split_first(near[:, 0:256], far[:, 0:256])
                values = split_second(near[:, 128:384], far[:, 128:384])
                for place in range(3):
                    at = slice(y * 384 + place * 128, y * 384 + (place + 1) * 128)
                    ck_out[t, y * 3 + place, rows] = keys[place].astype(jnp.bfloat16)
                    cv_out[t, y * 3 + place, rows] = (values[place] + vec[8:9, at]).astype(jnp.bfloat16)
            yield


def cross_forward(counts, frame_span, c, vec, xqo, ck, cv, h1, cq_out, o2_out, h2_out, m_out, p_out, scores, bias):
    span = c.shape[1]
    factor = 1.0 / math.sqrt(HEAD_DIM)
    rows = c[...].reshape(2 * span, 768)
    for number, tile in enumerate(times_first(rows, xqo)):
        at = slice(number * 128, (number + 1) * 128)
        tile = ((tile + vec[7:8, at]) * factor).astype(jnp.bfloat16)
        for t in range(2):
            cq_out[t, :, at] = tile[t * span:(t + 1) * span]
    for t in range(2):
        for s in range(4):
            inside = lax.broadcasted_iota(jnp.int32, (1, 384), 1)
            good = (inside < frame_span) & (s * frame_span + inside < counts[t])
            bias[t, :, s * 384:(s + 1) * 384] = jnp.where(good, 0.0, NEG)
    yield
    for t in range(2):
        for pair in range(6):
            at = slice(pair * 128, (pair + 1) * 128)
            scores[...] = mm_back(stacked(cq_out, t, pair), ck[t, pair])
            chances = p_out.at[t, pair]
            soften(scores, lambda first: bias[t], chances, 2 * span, 1536)
            o2_out[t, :, at] = unstacked(mm(chances[...], cv[t, pair])).astype(jnp.bfloat16)
            yield
    out = o2_out[...].reshape(2 * span, 768)
    for number, tile in enumerate(times_second(out, xqo)):
        at = slice(number * 128, (number + 1) * 128)
        for t in range(2):
            h2_out[t, :, at] = h1[t, :, at] + tile[t * span:(t + 1) * span] + vec[9:10, at]
    for t in range(2):
        m_out[t] = normed(h2_out[t], vec[10:11], vec[11:12])
    yield


class Summing:
    def __init__(self, mail, place, mates, acc, diag_x, diag_y, x_in, y_in, z_in, total):
        self.mail, self.place, self.mates = mail, place, mates
        self.acc, self.diag_x, self.diag_y = acc, diag_x, diag_y
        self.x_in, self.y_in, self.z_in, self.total = x_in, y_in, z_in, total
        self.slots = [mail.slots(4 + NZ - 1) for _ in range(acc.shape[0])]

    def begin(self, n):
        z, x, y = self.place
        x_mate, y_mate, _ = self.mates
        self.mail.post(self.acc.at[n, 1 - y, pl.ds(0, 2), 1 - x], self.diag_x.at[n], self.slots[n][0], x_mate)
        self.mail.post(self.acc.at[n, 1 - y, pl.ds(2, 2), 1 - x], self.diag_y.at[n], self.slots[n][1], y_mate)

    def side(self, n):
        z, x, y = self.place
        x_mate, y_mate, _ = self.mates
        self.mail.arrive(self.diag_x.at[n], self.slots[n][0], x_mate)
        for k in range(2):
            self.acc[n, 1 - y, k, x] = self.acc[n, 1 - y, k, x] + self.diag_x[n, k]
        self.mail.post(self.acc.at[n, 1 - y, :, x], self.y_in.at[n], self.slots[n][2], y_mate)
        self.mail.arrive(self.diag_y.at[n], self.slots[n][1], y_mate)
        for k in range(2):
            self.acc[n, y, 2 + k, 1 - x] = self.acc[n, y, 2 + k, 1 - x] + self.diag_y[n, k]
        self.mail.post(self.acc.at[n, y, :, 1 - x], self.x_in.at[n], self.slots[n][3], x_mate)

    def column(self, n):
        z, x, y = self.place
        x_mate, y_mate, z_mates = self.mates
        self.mail.arrive(self.y_in.at[n], self.slots[n][2], y_mate)
        self.mail.arrive(self.x_in.at[n], self.slots[n][3], x_mate)
        for k in range(NZ):
            self.acc[n, y, k, x] = (
                self.acc[n, y, k, x].astype(jnp.float32)
                + self.x_in[n, k].astype(jnp.float32)
                + self.y_in[n, k].astype(jnp.float32)
            ).astype(jnp.bfloat16)
        for k in range(1, NZ):
            zz = lax.rem(z + k, NZ)
            self.mail.post(self.acc.at[n, y, zz, x], self.z_in.at[n, k - 1], self.slots[n][3 + k], z_mates[k - 1])

    def last(self, n):
        z, x, y = self.place
        _, _, z_mates = self.mates
        for k in range(1, NZ):
            self.mail.arrive(self.z_in.at[n, k - 1], self.slots[n][3 + k], z_mates[k - 1])
        self.total[n] = self.acc[n, y, z, x].astype(jnp.float32) + (
            self.z_in[n, 0].astype(jnp.float32) + self.z_in[n, 1].astype(jnp.float32)
        ) + self.z_in[n, 2].astype(jnp.float32)


def summing_scratch(n, width=384):
    piece = (96, width)
    shapes = [
        (n, NY, NZ, NX) + piece, (n, 2) + piece, (n, 2) + piece, (n, NZ) + piece, (n, NZ) + piece, (n, NZ - 1) + piece
    ]
    return [pltpu.VMEM(shape, jnp.bfloat16) for shape in shapes]


class Loads:
    def __init__(self, sems):
        self.sems, self.count = sems, 0

    def start(self, source, target):
        copy = pltpu.make_async_copy(source, target, self.sems.at[self.count])
        copy.start()
        self.count += 1
        return copy


def two(first, second):
    return jnp.concatenate([first, second], axis=0)


def feed_kernel(
    lengths, ids, weights, cotangent, vec, wide_bias, h2, m, o2, c, h1, cq,
    wide_far, tall_far, pairs_far, frames_far, ck_far, cv_far, p_far,
    y_out, dh1_out, total, acc_kv, acc_xqo, small_out, wide_small,
    acc, diag_x, diag_y, x_in, y_in, z_in,
    wide, tall, xqo, frames, keys_here, values_here, p_here,
    m_sib, g_own, g_sib, du_own, du_send, du_sib, dz_own, dz_send, dz_sib,
    o2_sib, c_sib, xb_own, xb_send, xb_sib, xa_own, xa_send, xa_sib, gkv, kv_in,
    dy, dh2, do, dq, scores, dscores,
    send_sems, recv_sems, load_sems, unit_sems,
):
    z, x, y, core = where_am_i()
    span = m.shape[1]
    seq = y * NC + core
    factor = 1.0 / math.sqrt(HEAD_DIM)
    low = low_lanes(2 * span)
    x_mate, y_mate, c_mate = device_at(z, 1 - x, y, core), device_at(z, x, 1 - y, core), device_at(z, x, y, 1 - core)
    z_mates = [device_at(lax.rem(z + n, NZ), x, y, core) for n in range(1, NZ)]
    loads = Loads(load_sems)
    order = [(yy, side) for yy in range(2) for side in range(2)]
    block_loads = []
    for yy, side in order:
        at = lanes((2 * yy + (core if side == 0 else 1 - core)) * 768, 768)
        block_loads.append((
            loads.start(wide_far.at[:, :, :, at], wide.at[:, :, :, at]),
            loads.start(tall_far.at[:, :, :, at], tall.at[:, :, :, at]),
        ))
    xqo_load = loads.start(pairs_far.at[1], xqo)
    frames_load = loads.start(frames_far, frames)
    units = [(pair, t) for pair in range(6) for t in range(2)]

    def unit_copies(n):
        pair, t = units[n]
        slot = n % 2
        return [
            pltpu.make_async_copy(ck_far.at[t, pair], keys_here.at[slot], unit_sems.at[slot, 0]),
            pltpu.make_async_copy(cv_far.at[t, pair], values_here.at[slot], unit_sems.at[slot, 1]),
            pltpu.make_async_copy(p_far.at[t, pair], p_here.at[slot], unit_sems.at[slot, 2]),
        ]

    for copy in unit_copies(0):
        copy.start()
    greet(z, x, y, core)
    mail = Mail(send_sems, recv_sems)
    sums = Summing(mail, (z, x, y), (x_mate, y_mate, z_mates), acc, diag_x, diag_y, x_in, y_in, z_in, total)
    swap = mail.slots(1 + 2 + 4 + 2 + 2 + 2 + 1)
    m_slot, dz_slots, g_slots, du_slots = swap[0], swap[1:3], swap[3:7], swap[7:9]
    xb_slots, xa_slots, kv_slot = swap[9:11], swap[11:13], swap[13]
    o2_slot, c_slot = mail.slots(2)
    mail.post(m, m_sib, m_slot, c_mate)
    mail.post(o2, o2_sib, o2_slot, c_mate)
    mail.post(c, c_sib, c_slot, c_mate)

    for t in range(2):
        weight = 0.0
        for corpus in range(weights.shape[0]):
            weight = weight + jnp.where(ids[t] == corpus, weights[corpus], 0.0)
        row = lax.broadcasted_iota(jnp.int32, (span, 1), 0) + seq * span
        scale = jnp.where(row < lengths[t], weight, 0.0)
        dy[t * span:(t + 1) * span] = cotangent[t].astype(jnp.float32) * scale
    dz = dy[...].astype(jnp.bfloat16)
    dz_wide = dz.astype(jnp.float32)
    small_out[...] = jnp.zeros_like(small_out)
    small_out[12:13] = column_sum(dz_wide)
    for yy in range(2):
        tiles = [dz_wide[:, yy * 384 + n * 128:yy * 384 + (n + 1) * 128] for n in range(3)]
        even = jnp.concatenate([tiles[0], tiles[1]], axis=1)
        last = turned(tiles[2])
        odd = jnp.concatenate([jnp.where(low, turned(tiles[1]), last), last], axis=1)
        dz_own[yy] = jnp.where(core == 0, even, odd).astype(jnp.bfloat16)
        dz_send[yy] = jnp.where(core == 0, odd, even).astype(jnp.bfloat16)
        mail.post(dz_send.at[yy], dz_sib.at[yy], dz_slots[yy], c_mate)
    rows = m[...].reshape(2 * span, 768)
    z_sum, dm_sum = None, None
    for number, (yy, side) in enumerate(order):
        at = lanes((2 * yy + (core if side == 0 else 1 - core)) * 768, 768)
        for copy in block_loads[number]:
            copy.wait()
        wide_here = wide[:, :, :, at].reshape(768, 768)
        tall_here = tall[:, :, :, at].reshape(768, 768)
        hidden = mm(rows, wide_here) + wide_bias[:, at]
        bell = 0.5 * (1.0 + lax.erf(hidden * 0.7071067811865476))
        gate = (hidden * bell).astype(jnp.bfloat16)
        g_own[:, at] = gate
        mail.post(g_own.at[:, at], g_sib.at[:, at], g_slots[number], c_mate)
        slope = bell + hidden * (jnp.exp(-0.5 * hidden * hidden) * 0.3989422804014327)
        back = (mm(dz, tall_here) * slope).astype(jnp.bfloat16)
        if side == 0:
            du_own[yy] = back
        else:
            du_send[yy] = back
            mail.post(du_send.at[yy], du_sib.at[yy], du_slots[yy], c_mate)
        part = mm_back(gate, tall_here)
        z_sum = part if z_sum is None else z_sum + part
        part = mm_back(back, wide_here)
        dm_sum = part if dm_sum is None else dm_sum + part
        wide_small[:, at] = column_sum(back)
    h2_rows = h2[...].reshape(2 * span, 768)
    out = h2_rows + z_sum + vec[12:13]
    back, gain, offset = normed_back(h2_rows, vec[10:11], dm_sum)
    small_out[10:11] = gain
    small_out[11:12] = offset
    dh2[...] = dy[...] + back
    for t in range(2):
        y_out[t] = out[t * span:(t + 1) * span].astype(jnp.bfloat16)

    for number, (yy, side) in enumerate(order):
        at = lanes((2 * yy + (1 - core if side == 0 else core)) * 768, 768)
        mail.arrive(g_sib.at[:, at], g_slots[number], c_mate)
    for yy in range(2):
        mail.arrive(dz_sib.at[yy], dz_slots[yy], c_mate)
    for yy in range(2):
        slopes = two(dz_own[yy], dz_sib[yy])
        for zz in range(NZ):
            at = slice(zz * 768, (zz + 1) * 768)
            product = mm_rows(slopes, two(g_own[:, at], g_sib[:, at])).astype(jnp.bfloat16)
            for xx in range(NX):
                acc[2, yy, zz, xx] = product[0:96, xx * 384:(xx + 1) * 384]
                acc[3, yy, zz, xx] = product[96:192, xx * 384:(xx + 1) * 384]
    sums.begin(2)
    sums.begin(3)
    mail.arrive(m_sib, m_slot, c_mate)
    both_rows = two(rows, m_sib[...].reshape(2 * span, 768))
    for yy in range(2):
        mail.arrive(du_sib.at[yy], du_slots[yy], c_mate)
        product = mm_rows(both_rows, two(du_own[yy], du_sib[yy])).astype(jnp.bfloat16)
        acc[0, yy] = product[:, 0:384].reshape(NZ, NX, 96, 384)
        acc[1, yy] = product[:, 384:768].reshape(NZ, NX, 96, 384)
    sums.begin(0)
    sums.begin(1)
    pending = []
    for step in range(6):
        for lag, action in ((0, sums.side), (1, sums.column), (2, sums.last)):
            if 0 <= step - lag < 4:
                pending.append((action, (2, 3, 0, 1)[step - lag]))

    def tick(number=1):
        for _ in range(number):
            if pending:
                action, group = pending.pop(0)
                action(group)

    low_wide = dh2[...].astype(jnp.bfloat16).astype(jnp.float32)
    small_out[9:10] = column_sum(low_wide)
    xqo_load.wait()
    for yy in range(2):
        near, far = join_second(low_wide[:, yy * 384:(yy + 1) * 384])
        xb_own[yy] = jnp.where(core == 0, near, far)
        xb_send[yy] = jnp.where(core == 0, far, near)
        mail.post(xb_send.at[yy], xb_sib.at[yy], xb_slots[yy], c_mate)
    heard = back_second(low_wide, xqo)
    small_out[8:9] = column_sum(heard.astype(jnp.bfloat16))
    for t in range(2):
        do[t] = heard[t * span:(t + 1) * span].astype(jnp.bfloat16)
    tick()
    frames_load.wait()
    total_kv = None
    for number, (pair, t) in enumerate(units):
        at = slice(pair * 128, (pair + 1) * 128)
        slot = number % 2
        if number + 1 < len(units):
            for copy in unit_copies(number + 1):
                copy.start()
        for copy in unit_copies(number):
            copy.wait()
        slopes, query = stacked(do, t, pair), stacked(cq, t, pair)
        scores[...] = mm_back(slopes, values_here[slot])
        chances = p_here.at[slot]
        soften_back(chances, scores, dscores, 2 * span, 1536)
        dq[t * span:(t + 1) * span, at] = unstacked(mm(dscores[...], keys_here[slot])) * factor
        turned_grads = two(mm_rows(query, dscores[...]), mm_rows(slopes, chances[...])).astype(jnp.bfloat16)
        part = mm(turned_grads, frames[t].reshape(1536, 768))
        total_kv = part if t == 0 else total_kv + part
        if t == 1:
            keys, values = total_kv[0:128].T, total_kv[128:256].T
            yy, place = pair // 3, pair % 3
            if place == 1:
                values = turned(values)
                half = low_lanes(768)
                gkv[0, yy, :, 128:256] = jnp.where(half, keys, values).astype(jnp.bfloat16)
                gkv[1, yy, :, 128:256] = jnp.where(half, values, keys).astype(jnp.bfloat16)
            else:
                gkv[place // 2, yy, :, 0:128] = keys.astype(jnp.bfloat16)
                gkv[place // 2, yy, :, 256:384] = values.astype(jnp.bfloat16)
        tick()
    mail.post(gkv.at[1 - core], kv_in, kv_slot, c_mate)
    low_q = dq[...].astype(jnp.bfloat16).astype(jnp.float32)
    small_out[7:8] = column_sum(low_q)
    for yy in range(2):
        near, far = join_first(low_q[:, yy * 384:(yy + 1) * 384])
        xa_own[yy] = jnp.where(core == 0, near, far)
        xa_send[yy] = jnp.where(core == 0, far, near)
        mail.post(xa_send.at[yy], xa_sib.at[yy], xa_slots[yy], c_mate)
    back, gain, offset = normed_back(h1[...].reshape(2 * span, 768), vec[5:6], back_first(low_q, xqo))
    small_out[5:6] = gain
    small_out[6:7] = offset
    for t in range(2):
        dh1_out[t] = dh2[t * span:(t + 1) * span] + back[t * span:(t + 1) * span]
    mail.arrive(o2_sib, o2_slot, c_mate)
    mail.arrive(c_sib, c_slot, c_mate)
    o2_both = two(o2[...].reshape(2 * span, 768), o2_sib[...].reshape(2 * span, 768))
    c_both = two(c[...].reshape(2 * span, 768), c_sib[...].reshape(2 * span, 768))
    for yy in range(2):
        mail.arrive(xb_sib.at[yy], xb_slots[yy], c_mate)
        mail.arrive(xa_sib.at[yy], xa_slots[yy], c_mate)
        second = mm_rows(o2_both, two(xb_own[yy], xb_sib[yy]))
        first = mm_rows(c_both, two(xa_own[yy], xa_sib[yy]))
        store_pair(acc_xqo.at[yy], first, second)
    mail.arrive(kv_in, kv_slot, c_mate)
    for yy in range(2):
        acc_kv[yy] = (gkv[core, yy] + kv_in[yy]).reshape(NZ, NX, 96, 384)
    tick(100)
    mail.finish()


def store_pair(out, first, second):
    shape = (NZ, NX, 96, 128)
    out[:, :, :, 0:128] = tile_of(first, 0).astype(jnp.bfloat16).reshape(shape)
    out[:, :, :, 128:256] = (tile_of(first, 1) + tile_of(second, 0)).astype(jnp.bfloat16).reshape(shape)
    out[:, :, :, 256:384] = tile_of(second, 1).astype(jnp.bfloat16).reshape(shape)


def run_feed(lengths, ids, weights, near, far):
    bf16, f32 = jnp.bfloat16, jnp.float32
    span = near[4].shape[1]
    rows, flat = (2, span, 768), 2 * span
    inside, anywhere = pl.BlockSpec(memory_space=pltpu.VMEM), pl.BlockSpec(memory_space=pl.ANY)
    scalar = pl.BlockSpec(memory_space=pltpu.SMEM)
    piece = (NY, NZ, NX, 96, 384)
    number = 4 * 7 + 16
    scratch = [
        ((NZ, NX, 96, 3072), bf16), ((NY, NC, 192, 3072), bf16), ((NY, NZ, NX, 96, 768), bf16), (far[3].shape, bf16),
        ((2, 1536, 128), bf16), ((2, 1536, 128), bf16), ((2, flat, 1536), bf16),
        (rows, bf16), ((flat, 3072), bf16), ((flat, 3072), bf16),
        ((2, flat, 768), bf16), ((2, flat, 768), bf16), ((2, flat, 768), bf16),
        ((2, flat, 256), bf16), ((2, flat, 256), bf16), ((2, flat, 256), bf16),
        (rows, bf16), (rows, bf16),
    ] + [((2, flat, 256), bf16)] * 6 + [
        ((2, 2, 768, 384), bf16), ((2, 768, 384), bf16),
        ((flat, 768), f32), ((flat, 768), f32), (rows, bf16), ((flat, 768), f32), ((flat, 1536), f32),
        ((flat, 1536), bf16),
    ]
    return pl.pallas_call(
        feed_kernel,
        out_shape=(
            jax.ShapeDtypeStruct(rows, bf16), jax.ShapeDtypeStruct(rows, f32),
            jax.ShapeDtypeStruct((4, 96, 384), f32),
            jax.ShapeDtypeStruct(piece, bf16), jax.ShapeDtypeStruct(piece, bf16),
            jax.ShapeDtypeStruct((16, 768), f32), jax.ShapeDtypeStruct((1, 3072), f32),
        ),
        in_specs=[scalar] * 3 + [inside] * len(near) + [anywhere] * len(far),
        out_specs=(inside,) * 7,
        scratch_shapes=summing_scratch(4) + [pltpu.VMEM(shape, kind) for shape, kind in scratch] + [
            pltpu.SemaphoreType.DMA((number,)),
            pltpu.SemaphoreType.DMA((number,)),
            pltpu.SemaphoreType.DMA((10,)),
            pltpu.SemaphoreType.DMA((2, 3)),
        ],
        compiler_params=pltpu.CompilerParams(
            collective_id=2, has_side_effects=True, vmem_limit_bytes=60 << 20
        ),
        name="feed_cross_back",
    )(lengths, ids, weights, *near, *far)


def last_kernel(
    tokens, dh1, a, head_rows, third, o, p, vec, small_before, wide_small,
    heads_far, mixer_far, kv_far, xqo_far,
    dx_out, total, total_o, total_q, small_total,
    acc, diag_x, diag_y, x_in, y_in, z_in,
    acc_o, diag_x_o, diag_y_o, x_in_o, y_in_o, z_in_o,
    acc_q, x_in_q, z_in_q,
    heads, mixer, o_sib, ob_own, ob_send, ob_sib, do_send, do_got, kv_sum, dq_third, dheads,
    da_send, da_core, da_side, scores, dscores,
    small, pack, pack_in, pack_sum, pack_seq,
    send_sems, recv_sems, load_sems,
):
    z, x, y, core = where_am_i()
    span = o.shape[1]
    seq = y * NC + core
    grp = z * NX + x
    factor = 1.0 / math.sqrt(HEAD_DIM)
    x_mate, y_mate, c_mate = device_at(z, 1 - x, y, core), device_at(z, x, 1 - y, core), device_at(z, x, y, 1 - core)
    far_mate = device_at(z, x, 1 - y, 1 - core)
    z_mates = [device_at(lax.rem(z + n, NZ), x, y, core) for n in range(1, NZ)]
    loads = Loads(load_sems)
    mixer_load = loads.start(mixer_far, mixer)
    acc_loads = [loads.start(kv_far, acc.at[0]), loads.start(xqo_far, acc.at[1])]
    heads_load = loads.start(heads_far, heads)
    greet(z, x, y, core)
    mail = Mail(send_sems, recv_sems)
    mates3 = (x_mate, y_mate, z_mates)
    sums = Summing(mail, (z, x, y), mates3, acc, diag_x, diag_y, x_in, y_in, z_in, total)
    sums_o = Summing(mail, (z, x, y), mates3, acc_o, diag_x_o, diag_y_o, x_in_o, y_in_o, z_in_o, total_o)
    (o_slot,) = mail.slots(1)
    ob_slots, do_slots = mail.slots(2), mail.slots(6)
    core_slots, side_slots = mail.slots(4), mail.slots(2)
    xq_slots, zq_slots = mail.slots(2), mail.slots(6)
    pack_slots, seq_slots = mail.slots(2 * NZ - 1), mail.slots(2)
    mail.post(o, o_sib, o_slot, c_mate)
    small[...] = small_before[...]
    low_wide = dh1[...].reshape(2 * span, 768).astype(jnp.bfloat16).astype(jnp.float32)
    small[4:5] = column_sum(low_wide)
    heard = None
    mixer_load.wait()
    for yy in range(2):
        near, far = join_first(low_wide[:, yy * 384:(yy + 1) * 384])
        ob_own[yy] = jnp.where(core == 0, near, far)
        ob_send[yy] = jnp.where(core == 0, far, near)
        mail.post(ob_send.at[yy], ob_sib.at[yy], ob_slots[yy], c_mate)
        part = mm_back(jnp.concatenate([near, far], axis=1), mixer[yy].reshape(768, 512))
        heard = part if heard is None else heard + part
    for yy in range(2):
        near, far = join_first(heard[:, yy * 384:(yy + 1) * 384])
        for t in range(2):
            do_send[2 * yy, t] = near[t * span:(t + 1) * span]
            do_send[2 * yy + 1, t] = far[t * span:(t + 1) * span]
    mates = (
        (c_mate, y * NC + 1 - core), (y_mate, (1 - y) * NC + core), (far_mate, (1 - y) * NC + 1 - core)
    )
    for t in range(2):
        for place in (2, 1, 0):
            mate, mate_seq = mates[place]
            mail.post(do_send.at[mate_seq, t], do_got.at[seq, t], do_slots[3 * t + place], mate)
        do_got[seq, t] = do_send[seq, t]
    for copy in acc_loads:
        copy.wait()
    sums.begin(0)
    sums.begin(1)
    mail.arrive(o_sib, o_slot, c_mate)
    o_both = two(o[...].reshape(2 * span, 768), o_sib[...].reshape(2 * span, 768))
    for yy in range(2):
        mail.arrive(ob_sib.at[yy], ob_slots[yy], c_mate)
        product = mm_rows(o_both, two(ob_own[yy], ob_sib[yy])).astype(jnp.bfloat16)
        acc_o[0, yy] = product.reshape(NZ, NX, 96, 256)
    sums_o.begin(0)
    pending = [
        (sums.side, 0), (sums.side, 1), (sums_o.side, 0), (sums.column, 0), (sums.column, 1), (sums_o.column, 0),
        (sums.last, 0), (sums.last, 1), (sums_o.last, 0),
    ]

    def tick(number=1):
        for _ in range(number):
            if pending:
                action, group = pending.pop(0)
                action(group)

    def exchange_core(t):
        mail.post(da_send.at[y * NC + 1 - core, t], da_core.at[t, 0], core_slots[2 * t], c_mate)
        mail.post(da_send.at[(1 - y) * NC + 1 - core, t], da_core.at[t, 1], core_slots[2 * t + 1], c_mate)

    def exchange_side(t):
        mail.arrive(da_core.at[t, 1], core_slots[2 * t + 1], c_mate)
        across = (1 - y) * NC + core
        da_send[across, t] = da_send[across, t] + da_core[t, 1]
        mail.post(da_send.at[across, t], da_side.at[t], side_slots[t], y_mate)

    heads_load.wait()
    for t in range(2):
        for place, (mate, mate_seq) in enumerate(mates):
            mail.arrive(do_got.at[mate_seq, t], do_slots[3 * t + place], mate)
        for block in (3, 2, 1, 0):
            rows, width = slice(block * span, (block + 1) * span), 128 * (block + 1)
            slopes, slopes_third = both_heads(do_got[block, t, :, 0:128]), do_got[block, t, :, 128:256]
            query = both_heads(head_rows[t, rows, 0:128])
            query_third = third_head(head_rows[t, rows, 384:512], core)
            scores[0:2 * span, 0:width] = mm_back(slopes, head_rows[t, 0:width, 256:384])
            scores[2 * span:3 * span, 0:width] = mm_back(slopes_third, head_rows[t, 0:width, 512:640])
            chances = p.at[t, block]
            soften_back(chances, scores, dscores, 3 * span, width)
            pair_grads, third_grads = dscores[0:2 * span, 0:width], dscores[2 * span:3 * span, 0:width]
            dheads[t, rows, 0:128] = (
                unstacked(mm(pair_grads, head_rows[t, 0:width, 128:256])) * factor
            ).astype(jnp.bfloat16)
            dq_third[rows] = third_head(mm(third_grads, third[t, 0:width]) * factor, core)
            parts = (
                mm_rows(query, pair_grads), mm_rows(query_third, third_grads),
                mm_rows(slopes, chances[0:2 * span, 0:width]), mm_rows(slopes_third, chances[2 * span:3 * span, 0:width]),
            )
            for number, part in enumerate(parts):
                if block == 3:
                    kv_sum[number] = part
                else:
                    kv_sum[number, :, 0:width] += part
            if t == 1 and block == 3:
                exchange_side(0)
            elif (t, block) in ((0, 1), (0, 0), (1, 1), (1, 0)):
                tick()
        keys, keys_third, values, values_third = [kv_sum[number].T[0:4 * span] for number in range(4)]
        dheads[t, :, 128:256] = keys.astype(jnp.bfloat16)
        dheads[t, :, 256:384] = values.astype(jnp.bfloat16)
        dheads[t, :, 384:512] = (dq_third[...] + turned(keys_third)).astype(jnp.bfloat16)
        dheads[t, :, 512:640] = values_third.astype(jnp.bfloat16)
        if t == 1:
            inputs = two(a[0].reshape(4 * span, 768), a[1].reshape(4 * span, 768))
            product = mm_rows(inputs, two(dheads[0], dheads[1])).astype(jnp.bfloat16)
            acc_q[...] = product.reshape(NZ, NX, 96, 640)
            for part, at in enumerate((slice(0, 384), slice(384, 640))):
                mail.post(acc_q.at[:, 1 - x, :, at], x_in_q.at[:, :, at], xq_slots[part], x_mate)
        back = mm_back(dheads[t], heads[...].reshape(768, 640)).astype(jnp.bfloat16)
        for s in range(4):
            da_send[s, t] = back[s * span:(s + 1) * span]
        exchange_core(t)
    tick(2)
    exchange_side(1)
    tick()
    sums_q = [column_sum(two(dheads[0, :, n * 128:(n + 1) * 128], dheads[1, :, n * 128:(n + 1) * 128])) for n in (0, 2, 3, 4)]
    small[2:3] = natural_row(sums_q[0], third_head(sums_q[2], core), y, core)
    small[3:4] = natural_row(sums_q[1], sums_q[3], y, core)
    for part, at in enumerate((slice(0, 384), slice(384, 640))):
        mail.arrive(x_in_q.at[:, :, at], xq_slots[part], x_mate)
        for k in range(NZ):
            acc_q[k, x, :, at] = acc_q[k, x, :, at] + x_in_q[k, :, at]
        for k in range(1, NZ):
            zz = lax.rem(z + k, NZ)
            mail.post(
                acc_q.at[zz, x, :, at], z_in_q.at[k - 1, :, at], zq_slots[3 * part + k - 1], z_mates[k - 1]
            )
    gain, offset = None, None
    for t in range(2):
        mail.arrive(da_core.at[t, 0], core_slots[2 * t], c_mate)
        mail.arrive(da_side.at[t], side_slots[t], y_mate)
        back = (
            da_send[seq, t].astype(jnp.float32) + da_core[t, 0].astype(jnp.float32) + da_side[t].astype(jnp.float32)
        )
        part, gain_part, offset_part = normed_back(tokens[t].astype(jnp.float32), vec[0:1], back)
        dx_out[t] = (dh1[t] + part).astype(jnp.bfloat16)
        gain = gain_part if t == 0 else gain + gain_part
        offset = offset_part if t == 0 else offset + offset_part
    small[0:1] = gain
    small[1:2] = offset
    for g in range(8):
        pack[g, 0:16, 0:96] = small[:, g * 96:(g + 1) * 96]
        pack[g, 0:16, 96:128] = jnp.zeros((16, 32), jnp.float32)
        for n in range(3):
            at = g * 384 + n * 128
            pack[g, 16 + n:17 + n, :] = wide_small[:, at:at + 128]
        pack[g, 19:24, :] = jnp.zeros((5, 128), jnp.float32)
    pack_to = [(lax.rem(z + n, NZ), x) for n in range(1, NZ)]
    pack_to += [(lax.rem(z + n, NZ), 1 - x) for n in range(NZ)]
    for number, (zz, xx) in enumerate(pack_to):
        mail.post(pack.at[zz * NX + xx], pack_in.at[number], pack_slots[number], device_at(zz, xx, y, core))
    tick(100)
    for number in range(2 * NZ - 1):
        mail.arrive(pack_in.at[number], pack_slots[number], x_mate)
    pack_sum[...] = (
        (pack[grp] + pack_in[0]) + (pack_in[1] + pack_in[2])
        + ((pack_in[3] + pack_in[4]) + (pack_in[5] + pack_in[6]))
    )
    mail.post(pack_sum, pack_seq.at[0], seq_slots[0], c_mate)
    mail.arrive(pack_seq.at[0], seq_slots[0], c_mate)
    pack_seq[1] = pack_sum[...] + pack_seq[0]
    mail.post(pack_seq.at[1], pack_seq.at[2], seq_slots[1], y_mate)
    for part, at in enumerate((slice(0, 384), slice(384, 640))):
        for k in range(1, NZ):
            mail.arrive(z_in_q.at[k - 1, :, at], zq_slots[3 * part + k - 1], z_mates[k - 1])
        total_q[:, at] = (acc_q[z, x, :, at].astype(jnp.float32) + z_in_q[0, :, at].astype(jnp.float32)) + (
            z_in_q[1, :, at].astype(jnp.float32) + z_in_q[2, :, at].astype(jnp.float32)
        )
    mail.arrive(pack_seq.at[2], seq_slots[1], y_mate)
    small_total[...] = pack_seq[1] + pack_seq[2]
    mail.finish()


def run_last(near, far):
    bf16, f32 = jnp.bfloat16, jnp.float32
    span = near[0].shape[1]
    rows, flat = (2, span, 768), 2 * span
    inside, anywhere = pl.BlockSpec(memory_space=pltpu.VMEM), pl.BlockSpec(memory_space=pl.ANY)
    number = 3 * 7 + 1 + 2 + 6 + 6 + 8 + 9
    scratch = [
        ((NZ, NX, 96, 640), bf16), ((NZ, 96, 640), bf16), ((NZ - 1, 96, 640), bf16),
        ((NZ, NX, 96, 640), bf16), ((NY, NZ, NX, 96, 512), bf16), (rows, bf16),
        ((2, flat, 256), bf16), ((2, flat, 256), bf16), ((2, flat, 256), bf16),
        ((4, 2, span, 256), bf16), ((4, 2, span, 256), bf16), ((4, 128, 512), f32), ((4 * span, 128), f32),
        ((2, 4 * span, 640), bf16), ((4, 2, span, 768), bf16), ((2, 2, span, 768), bf16), ((2, span, 768), bf16),
        ((3 * span, 512), f32), ((3 * span, 512), bf16),
        ((16, 768), f32), ((8, 24, 128), f32), ((7, 24, 128), f32), ((24, 128), f32), ((3, 24, 128), f32),
    ]
    return pl.pallas_call(
        last_kernel,
        out_shape=(
            jax.ShapeDtypeStruct(rows, bf16), jax.ShapeDtypeStruct((2, 96, 384), f32),
            jax.ShapeDtypeStruct((1, 96, 256), f32), jax.ShapeDtypeStruct((96, 640), f32),
            jax.ShapeDtypeStruct((24, 128), f32),
        ),
        in_specs=[inside] * len(near) + [anywhere] * len(far),
        out_specs=(inside,) * 5,
        scratch_shapes=summing_scratch(2) + summing_scratch(1, 256) + [
            pltpu.VMEM(shape, kind) for shape, kind in scratch
        ] + [
            pltpu.SemaphoreType.DMA((number,)),
            pltpu.SemaphoreType.DMA((number,)),
            pltpu.SemaphoreType.DMA((4,)),
        ],
        compiler_params=pltpu.CompilerParams(
            collective_id=3, has_side_effects=True, vmem_limit_bytes=60 << 20
        ),
        name="self_back_sum",
    )(*near, *far)


def place_kernel(
    y, dx, total, total_o, total_q, total_ff, small,
    y_out, dx_out, query, key, value, mixer, xkey, xvalue, xquery, xmixer, wide, tall, *more,
):
    vectors, wide_bias = more[:13], more[13]
    core = lax.rem(lax.axis_index("seq"), NC)
    y_out[...] = y[...]
    dx_out[...] = dx[...]

    def put(out, even, odd):
        @pl.when(core == 0)
        def _():
            out[...] = jnp.concatenate(even, axis=1)

        @pl.when(core != 0)
        def _():
            out[...] = jnp.concatenate(odd, axis=1)

    heads = total_q[...]
    for out, pair, even, odd in ((query, 0, 384, 448), (key, 128, 448, 384), (value, 256, 512, 576)):
        whole = heads[:, pair:pair + 128]
        put(out, [whole, heads[:, even:even + 64]], [heads[:, odd:odd + 64], whole])
    piece = total_o[0]
    put(mixer, [piece[:, :192]], [piece[:, 192:], piece[:, :128]])
    for number, (first, second) in enumerate(((xkey, xvalue), (xquery, xmixer))):
        piece = total[number]
        put(first, [piece[:, :192]], [piece[:, 192:256], piece[:, :128]])
        put(second, [piece[:, 256:], piece[:, 192:256]], [piece[:, 128:192], piece[:, 256:]])
    wide[:, :384] = total_ff[0]
    wide[:, 384:] = total_ff[1]
    tall[:96] = total_ff[2]
    tall[96:] = total_ff[3]
    for number, out in enumerate(vectors):
        out[...] = small[number:number + 1, 0:96]
    for number in range(3):
        wide_bias[:, number * 128:(number + 1) * 128] = small[16 + number:17 + number]


def run_place(y, dx, *totals):
    f32 = jnp.float32
    inside = pl.BlockSpec(memory_space=pltpu.VMEM)
    like = jax.ShapeDtypeStruct(y.shape, y.dtype)
    return pl.pallas_call(
        place_kernel,
        out_shape=(like, like) + (jax.ShapeDtypeStruct((96, 192), f32),) * 8 + (
            jax.ShapeDtypeStruct((96, 768), f32), jax.ShapeDtypeStruct((192, 384), f32),
        ) + (jax.ShapeDtypeStruct((1, 96), f32),) * 13 + (jax.ShapeDtypeStruct((1, 384), f32),),
        in_specs=[inside] * 7,
        out_specs=(inside,) * 26,
        compiler_params=pltpu.CompilerParams(vmem_limit_bytes=60 << 20),
        name="place",
    )(y, dx, *totals)


def on_device_fast(*arguments):
    (
        tokens, encoder_states, lengths, frame_counts, corpus_ids, corpus_weights, cotangent,
        first_gain, first_bias, query_weight, query_bias, key_weight, value_weight, value_bias,
        output_weight, output_bias, second_gain, second_bias, cross_query_weight, cross_query_bias,
        cross_key_weight, cross_value_weight, cross_value_bias, cross_output_weight, cross_output_bias,
        third_gain, third_bias, expand_weight, expand_bias, reduce_weight, reduce_bias,
    ) = arguments
    bf16, f32 = jnp.bfloat16, jnp.float32
    small_vectors = (
        first_gain, first_bias, query_bias, value_bias, output_bias, second_gain, second_bias,
        cross_query_bias, cross_value_bias, cross_output_bias, third_gain, third_bias, reduce_bias, expand_bias,
    )
    matrices = (
        query_weight, key_weight, value_weight, output_weight, cross_key_weight, cross_value_weight,
        cross_query_weight, cross_output_weight, expand_weight, reduce_weight.T,
    )
    (
        heads_all, mixer_all, pairs_all, wide_all, tall_all, frames_all, vec, wide_bias,
        a_all, head_rows, third, o, h1, c, p_self, ck, cv, cq, o2, h2, m, p_cross,
    ) = run_forward(
        lengths, frame_counts, matrices, jnp.stack(small_vectors[:13]), expand_bias.reshape(3, 128), encoder_states, tokens
    )
    layer_output, dh1, total_ff, acc_kv, acc_xqo, small_before, wide_small = run_feed(
        lengths, corpus_ids, corpus_weights,
        [cotangent, vec, wide_bias, h2, m, o2, c, h1, cq],
        [wide_all, tall_all, pairs_all, frames_all, ck, cv, p_cross],
    )
    tokens_gradient, total, total_o, total_q, small_total = run_last(
        [tokens, dh1, a_all, head_rows, third, o, p_self, vec, small_before, wide_small],
        [heads_all, mixer_all, acc_kv, acc_xqo],
    )
    (
        layer_output, tokens_gradient, m_query, m_key, m_value, m_mixer, m_xkey, m_xvalue, m_xquery, m_xmixer,
        expand_grad, reduce_grad, *smaller,
    ) = run_place(layer_output, tokens_gradient, total, total_o, total_q, total_ff, small_total)
    reduce_grad = reduce_grad.T
    smaller = [row.reshape(-1) for row in smaller]
    expand_bias_grad = smaller[13]
    return (
        layer_output, tokens_gradient, smaller[0], smaller[1], m_query, smaller[2], m_key, m_value, smaller[3],
        m_mixer, smaller[4], smaller[5], smaller[6], m_xquery, smaller[7], m_xkey, m_xvalue, smaller[8],
        m_xmixer, smaller[9], smaller[10], smaller[11], expand_grad, expand_bias_grad, reduce_grad, smaller[12],
    )


def solution(mesh):
    placed = (
        P("grp", "seq", None),
        P("grp", "seq", None),
        P("grp"),
        P("grp"),
        P("grp"),
        P(),
        P("grp", "seq", None),
        P("grp"),
        P("grp"),
        P("grp", "seq"),
        P("grp"),
        P("grp", "seq"),
        P("grp", "seq"),
        P("grp"),
        P("grp", "seq"),
        P("grp"),
        P("grp"),
        P("grp"),
        P("grp", "seq"),
        P("grp"),
        P("grp", "seq"),
        P("grp", "seq"),
        P("grp"),
        P("grp", "seq"),
        P("grp"),
        P("grp"),
        P("grp"),
        P("grp", "seq"),
        P("grp"),
        P("grp", "seq"),
        P("grp"),
    )
    small_slice = mesh.shape["grp"] == NZ * NX and mesh.shape["seq"] == NY * NC
    return jax.shard_map(
        on_device_fast if small_slice else on_device_plain,
        mesh=mesh,
        in_specs=placed,
        out_specs=(
            P("grp", "seq", None),
            P("grp", "seq", None),
            P("grp"),
            P("grp"),
            P("grp", "seq"),
            P("grp"),
            P("grp", "seq"),
            P("grp", "seq"),
            P("grp"),
            P("grp", "seq"),
            P("grp"),
            P("grp"),
            P("grp"),
            P("grp", "seq"),
            P("grp"),
            P("grp", "seq"),
            P("grp", "seq"),
            P("grp"),
            P("grp", "seq"),
            P("grp"),
            P("grp"),
            P("grp"),
            P("grp", "seq"),
            P("grp"),
            P("grp", "seq"),
            P("grp"),
        ),
        check_vma=False,
    )
```

```python
import math

import jax
import jax.numpy as jnp
from jax import lax
from jax.experimental import pallas as pl
from jax.experimental.pallas import tpu as pltpu
from jax.sharding import PartitionSpec as P

HEADS = 12
HEAD_DIM = 64


NEG = -1e30
EPS = 1e-05


def norm_rows(values, scaling, offset):
    centre = values - jnp.mean(values, axis=-1, keepdims=True)
    spread = jnp.mean(centre * centre, axis=-1, keepdims=True)
    return centre * lax.rsqrt(spread + EPS) * scaling + offset


def smooth_gate(values):
    return 0.5 * values * (1.0 + lax.erf(values * 0.7071067811865476))


def linear(inputs, weight):
    return jnp.einsum("bri,ij->brj", inputs, weight, preferred_element_type=jnp.float32)


def linear_back(gradient, weight):
    return jnp.einsum("brj,ij->bri", gradient, weight, preferred_element_type=jnp.float32)


def outer_sum(inputs, gradient):
    return jnp.einsum("bri,brj->ij", inputs, gradient, preferred_element_type=jnp.float32)


def row_total(gradient):
    return jnp.sum(gradient.astype(jnp.float32), axis=(0, 1))


def split_heads(values):
    return values.reshape(values.shape[0], values.shape[1], HEADS, HEAD_DIM)


def scores_of(query, key_rows, allowed):
    scores = jnp.einsum(
        "bqhd,bkhd->bhqk",
        split_heads(query),
        split_heads(key_rows),
        preferred_element_type=jnp.float32,
    )
    return jnp.where(allowed[:, None], scores, NEG)


def attend(query, key_rows, values, allowed):
    scores = scores_of(query, key_rows, allowed)
    maximum = jnp.max(scores, axis=-1, keepdims=True)
    raised = jnp.exp(scores - maximum)
    summed = jnp.sum(raised, axis=-1, keepdims=True)
    chances = (raised / summed).astype(jnp.bfloat16)
    blended = jnp.einsum(
        "bhqk,bkhd->bqhd", chances, split_heads(values), preferred_element_type=jnp.float32
    )
    return (blended.reshape(query.shape).astype(jnp.bfloat16), maximum + jnp.log(summed))


def attend_back(grad_low, query, key_rows, values, allowed, logsum):
    scores = scores_of(query, key_rows, allowed)
    chances = jnp.exp(scores - logsum)
    grad_heads = split_heads(grad_low)
    grad_chance = jnp.einsum(
        "bqhd,bkhd->bhqk", grad_heads, split_heads(values), preferred_element_type=jnp.float32
    )
    offset = jnp.sum(chances * grad_chance, axis=-1, keepdims=True)
    grad_score = (chances * (grad_chance - offset)).astype(jnp.bfloat16)
    grad_query = jnp.einsum(
        "bhqk,bkhd->bqhd", grad_score, split_heads(key_rows), preferred_element_type=jnp.float32
    )
    grad_keys = jnp.einsum(
        "bhqk,bqhd->bkhd", grad_score, split_heads(query), preferred_element_type=jnp.float32
    )
    grad_values = jnp.einsum(
        "bhqk,bqhd->bkhd",
        chances.astype(jnp.bfloat16),
        grad_heads,
        preferred_element_type=jnp.float32,
    )
    return (
        grad_query.reshape(query.shape),
        grad_keys.reshape(key_rows.shape),
        grad_values.reshape(values.shape),
    )


def on_device_plain(
    tokens,
    encoder_states,
    lengths,
    frame_counts,
    corpus_ids,
    corpus_weights,
    cotangent,
    first_gain,
    first_bias,
    query_weight,
    query_bias,
    key_weight,
    value_weight,
    value_bias,
    output_weight,
    output_bias,
    second_gain,
    second_bias,
    cross_query_weight,
    cross_query_bias,
    cross_key_weight,
    cross_value_weight,
    cross_value_bias,
    cross_output_weight,
    cross_output_bias,
    third_gain,
    third_bias,
    expand_weight,
    expand_bias,
    reduce_weight,
    reduce_bias,
):
    row_parts = (
        lax.all_gather(query_weight, "grp", axis=0, tiled=True),
        lax.all_gather(key_weight, "grp", axis=0, tiled=True),
        lax.all_gather(value_weight, "grp", axis=0, tiled=True),
        lax.all_gather(output_weight, "grp", axis=0, tiled=True),
        lax.all_gather(cross_query_weight, "grp", axis=0, tiled=True),
        lax.all_gather(cross_key_weight, "grp", axis=0, tiled=True),
        lax.all_gather(cross_value_weight, "grp", axis=0, tiled=True),
        lax.all_gather(cross_output_weight, "grp", axis=0, tiled=True),
        lax.all_gather(expand_weight, "grp", axis=0, tiled=True),
        lax.all_gather(reduce_weight, "grp", axis=0, tiled=True),
        lax.all_gather(first_gain, "grp", axis=0, tiled=True),
        lax.all_gather(first_bias, "grp", axis=0, tiled=True),
        lax.all_gather(query_bias, "grp", axis=0, tiled=True),
        lax.all_gather(value_bias, "grp", axis=0, tiled=True),
        lax.all_gather(output_bias, "grp", axis=0, tiled=True),
        lax.all_gather(second_gain, "grp", axis=0, tiled=True),
        lax.all_gather(second_bias, "grp", axis=0, tiled=True),
        lax.all_gather(cross_query_bias, "grp", axis=0, tiled=True),
        lax.all_gather(cross_value_bias, "grp", axis=0, tiled=True),
        lax.all_gather(cross_output_bias, "grp", axis=0, tiled=True),
        lax.all_gather(third_gain, "grp", axis=0, tiled=True),
        lax.all_gather(third_bias, "grp", axis=0, tiled=True),
        lax.all_gather(expand_bias, "grp", axis=0, tiled=True),
        lax.all_gather(reduce_bias, "grp", axis=0, tiled=True),
    )
    gathered = (
        lax.all_gather(row_parts[0], "seq", axis=1, tiled=True),
        lax.all_gather(row_parts[1], "seq", axis=1, tiled=True),
        lax.all_gather(row_parts[2], "seq", axis=1, tiled=True),
        lax.all_gather(row_parts[3], "seq", axis=1, tiled=True),
        lax.all_gather(row_parts[4], "seq", axis=1, tiled=True),
        lax.all_gather(row_parts[5], "seq", axis=1, tiled=True),
        lax.all_gather(row_parts[6], "seq", axis=1, tiled=True),
        lax.all_gather(row_parts[7], "seq", axis=1, tiled=True),
        lax.all_gather(row_parts[8], "seq", axis=1, tiled=True),
        lax.all_gather(row_parts[9], "seq", axis=1, tiled=True),
    )
    w_query, w_key, w_value, w_mixer, x_query, x_key, x_value, x_mixer, w_expand, w_reduce = (
        gathered
    )
    vectors = [piece.astype(jnp.float32) for piece in row_parts[10:]]
    factor = 1.0 / math.sqrt(HEAD_DIM)
    seq_count = lax.axis_size("seq")
    span_rows = tokens.shape[1]
    query_pos = lax.axis_index("seq") * span_rows + jnp.arange(span_rows, dtype=jnp.int32)
    key_pos = jnp.arange(span_rows * seq_count, dtype=jnp.int32)
    self_mask = (key_pos[None, None, :] <= query_pos[None, :, None]) & (
        key_pos[None, None, :] < lengths[:, None, None]
    )
    frame_pos = jnp.arange(encoder_states.shape[1] * seq_count, dtype=jnp.int32)
    cross_mask = frame_pos[None, None, :] < frame_counts[:, None, None]
    layer_in = tokens.astype(jnp.float32)
    normed_one, norm_back_one = jax.vjp(norm_rows, layer_in, vectors[0], vectors[1])
    normed_one = normed_one.astype(jnp.bfloat16)
    query_low = ((linear(normed_one, w_query) + vectors[2]) * factor).astype(jnp.bfloat16)
    key_low = linear(normed_one, w_key).astype(jnp.bfloat16)
    value_low = (linear(normed_one, w_value) + vectors[3]).astype(jnp.bfloat16)
    key_all, value_all = (
        lax.all_gather(key_low, "seq", axis=1, tiled=True),
        lax.all_gather(value_low, "seq", axis=1, tiled=True),
    )
    self_out, self_logsum = attend(query_low, key_all, value_all, self_mask)
    after_self = layer_in + linear(self_out, w_mixer) + vectors[4]
    normed_two, norm_back_two = jax.vjp(norm_rows, after_self, vectors[5], vectors[6])
    normed_two = normed_two.astype(jnp.bfloat16)
    cross_query = ((linear(normed_two, x_query) + vectors[7]) * factor).astype(jnp.bfloat16)
    frames_all = lax.all_gather(encoder_states, "seq", axis=1, tiled=True)
    cross_keys_all = linear(frames_all, x_key).astype(jnp.bfloat16)
    cross_values_all = (linear(frames_all, x_value) + vectors[8]).astype(jnp.bfloat16)
    cross_out, cross_logsum = attend(cross_query, cross_keys_all, cross_values_all, cross_mask)
    after_cross = after_self + linear(cross_out, x_mixer) + vectors[9]
    normed_three, norm_back_three = jax.vjp(norm_rows, after_cross, vectors[10], vectors[11])
    normed_three = normed_three.astype(jnp.bfloat16)
    hidden = linear(normed_three, w_expand) + vectors[12]
    gated, gate_back = jax.vjp(smooth_gate, hidden)
    gated_low = gated.astype(jnp.bfloat16)
    result = after_cross + linear(gated_low, w_reduce) + vectors[13]
    layer_output = result.astype(jnp.bfloat16)
    present = (query_pos[None, :] < lengths[:, None]).astype(jnp.float32)
    corpus_index = jnp.arange(corpus_weights.shape[0], dtype=jnp.int32)
    corpus_scale = jnp.sum(
        jnp.where(corpus_ids[:, None] == corpus_index[None, :], corpus_weights[None, :], 0.0),
        axis=1,
    )
    grad_out = cotangent.astype(jnp.float32) * (present * corpus_scale[:, None])[:, :, None]
    reduce_low = grad_out.astype(jnp.bfloat16)
    slope_reduce_bias = row_total(reduce_low)
    slope_reduce = outer_sum(gated_low, reduce_low)
    grad_hidden = gate_back(linear_back(reduce_low, w_reduce))[0]
    hidden_low = grad_hidden.astype(jnp.bfloat16)
    slope_expand_bias = row_total(hidden_low)
    slope_expand = outer_sum(normed_three, hidden_low)
    grad_norm_in, slope_gain_three, slope_bias_three = norm_back_three(
        linear_back(hidden_low, w_expand)
    )
    grad_cross = grad_out + grad_norm_in
    cross_low = grad_cross.astype(jnp.bfloat16)
    slope_xmixer_bias = row_total(cross_low)
    slope_xmixer = outer_sum(cross_out, cross_low)
    grad_heard = linear_back(cross_low, x_mixer).astype(jnp.bfloat16)
    grad_cq, part_ck, part_cv = attend_back(
        grad_heard, cross_query, cross_keys_all, cross_values_all, cross_mask, cross_logsum
    )
    slope_xkey = outer_sum(frames_all, part_ck)
    slope_xvalue = outer_sum(frames_all, part_cv)
    slope_xvalue_bias = row_total(part_cv)
    low_cq = (grad_cq * factor).astype(jnp.bfloat16)
    slope_xquery_bias = row_total(low_cq)
    slope_xquery = outer_sum(normed_two, low_cq)
    grad_norm_two, slope_gain_two, slope_bias_two = norm_back_two(linear_back(low_cq, x_query))
    grad_self = grad_cross + grad_norm_two
    self_low = grad_self.astype(jnp.bfloat16)
    slope_mixer_bias = row_total(self_low)
    slope_mixer = outer_sum(self_out, self_low)
    grad_mixed = linear_back(self_low, w_mixer).astype(jnp.bfloat16)
    grad_q, part_k, part_v = attend_back(
        grad_mixed, query_low, key_all, value_all, self_mask, self_logsum
    )
    summed_k, summed_v = (
        lax.psum_scatter(
            part_k.astype(jnp.bfloat16), "seq", scatter_dimension=1, tiled=True
        ).astype(jnp.float32),
        lax.psum_scatter(
            part_v.astype(jnp.bfloat16), "seq", scatter_dimension=1, tiled=True
        ).astype(jnp.float32),
    )
    low_k = summed_k.astype(jnp.bfloat16)
    low_v = summed_v.astype(jnp.bfloat16)
    low_q = (grad_q * factor).astype(jnp.bfloat16)
    slope_query = outer_sum(normed_one, low_q)
    slope_query_bias = row_total(low_q)
    slope_key = outer_sum(normed_one, low_k)
    slope_value = outer_sum(normed_one, low_v)
    slope_value_bias = row_total(low_v)
    grad_normed = (
        linear_back(low_q, w_query) + linear_back(low_k, w_key) + linear_back(low_v, w_value)
    )
    grad_norm_one, slope_gain_one, slope_bias_one = norm_back_one(grad_normed)
    tokens_gradient = (grad_self + grad_norm_one).astype(jnp.bfloat16)
    owned = (
        lax.psum_scatter(slope_query, "grp", scatter_dimension=0, tiled=True),
        lax.psum_scatter(slope_key, "grp", scatter_dimension=0, tiled=True),
        lax.psum_scatter(slope_value, "grp", scatter_dimension=0, tiled=True),
        lax.psum_scatter(slope_mixer, "grp", scatter_dimension=0, tiled=True),
        lax.psum_scatter(slope_xquery, "grp", scatter_dimension=0, tiled=True),
        lax.psum_scatter(slope_xkey, "grp", scatter_dimension=0, tiled=True),
        lax.psum_scatter(slope_xvalue, "grp", scatter_dimension=0, tiled=True),
        lax.psum_scatter(slope_xmixer, "grp", scatter_dimension=0, tiled=True),
        lax.psum_scatter(slope_expand, "grp", scatter_dimension=0, tiled=True),
        lax.psum_scatter(slope_reduce, "grp", scatter_dimension=0, tiled=True),
        lax.psum_scatter(slope_gain_one, "grp", scatter_dimension=0, tiled=True),
        lax.psum_scatter(slope_bias_one, "grp", scatter_dimension=0, tiled=True),
        lax.psum_scatter(slope_query_bias, "grp", scatter_dimension=0, tiled=True),
        lax.psum_scatter(slope_value_bias, "grp", scatter_dimension=0, tiled=True),
        lax.psum_scatter(slope_mixer_bias, "grp", scatter_dimension=0, tiled=True),
        lax.psum_scatter(slope_gain_two, "grp", scatter_dimension=0, tiled=True),
        lax.psum_scatter(slope_bias_two, "grp", scatter_dimension=0, tiled=True),
        lax.psum_scatter(slope_xquery_bias, "grp", scatter_dimension=0, tiled=True),
        lax.psum_scatter(slope_xvalue_bias, "grp", scatter_dimension=0, tiled=True),
        lax.psum_scatter(slope_xmixer_bias, "grp", scatter_dimension=0, tiled=True),
        lax.psum_scatter(slope_gain_three, "grp", scatter_dimension=0, tiled=True),
        lax.psum_scatter(slope_bias_three, "grp", scatter_dimension=0, tiled=True),
        lax.psum_scatter(slope_expand_bias, "grp", scatter_dimension=0, tiled=True),
        lax.psum_scatter(slope_reduce_bias, "grp", scatter_dimension=0, tiled=True),
    )
    matrices = (
        lax.psum_scatter(
            owned[0].astype(jnp.bfloat16), "seq", scatter_dimension=1, tiled=True
        ).astype(jnp.float32),
        lax.psum_scatter(
            owned[1].astype(jnp.bfloat16), "seq", scatter_dimension=1, tiled=True
        ).astype(jnp.float32),
        lax.psum_scatter(
            owned[2].astype(jnp.bfloat16), "seq", scatter_dimension=1, tiled=True
        ).astype(jnp.float32),
        lax.psum_scatter(
            owned[3].astype(jnp.bfloat16), "seq", scatter_dimension=1, tiled=True
        ).astype(jnp.float32),
        lax.psum_scatter(
            owned[4].astype(jnp.bfloat16), "seq", scatter_dimension=1, tiled=True
        ).astype(jnp.float32),
        lax.psum_scatter(
            owned[5].astype(jnp.bfloat16), "seq", scatter_dimension=1, tiled=True
        ).astype(jnp.float32),
        lax.psum_scatter(
            owned[6].astype(jnp.bfloat16), "seq", scatter_dimension=1, tiled=True
        ).astype(jnp.float32),
        lax.psum_scatter(
            owned[7].astype(jnp.bfloat16), "seq", scatter_dimension=1, tiled=True
        ).astype(jnp.float32),
        lax.psum_scatter(
            owned[8].astype(jnp.bfloat16), "seq", scatter_dimension=1, tiled=True
        ).astype(jnp.float32),
        lax.psum_scatter(
            owned[9].astype(jnp.bfloat16), "seq", scatter_dimension=1, tiled=True
        ).astype(jnp.float32),
    )
    smaller = lax.psum(
        (
            owned[10],
            owned[11],
            owned[12],
            owned[13],
            owned[14],
            owned[15],
            owned[16],
            owned[17],
            owned[18],
            owned[19],
            owned[20],
            owned[21],
            owned[22],
            owned[23],
        ),
        "seq",
    )
    return (
        layer_output,
        tokens_gradient,
        smaller[0],
        smaller[1],
        matrices[0],
        smaller[2],
        matrices[1],
        matrices[2],
        smaller[3],
        matrices[3],
        smaller[4],
        smaller[5],
        smaller[6],
        matrices[4],
        smaller[7],
        matrices[5],
        matrices[6],
        smaller[8],
        matrices[7],
        smaller[9],
        smaller[10],
        smaller[11],
        matrices[8],
        smaller[12],
        matrices[9],
        smaller[13],
    )


MESH_ID = pl.DeviceIdType.MESH
NZ, NX, NY, NC = 4, 2, 2, 2
GROUPS = 8


def where_am_i():
    grp = lax.axis_index("grp")
    seq = lax.axis_index("seq")
    return grp // NX, lax.rem(grp, NX), seq // NC, lax.rem(seq, NC)


def device_at(z, x, y, c):
    return (z * NX + x, y * NC + c)


def lanes(start, size):
    return pl.ds(pl.multiple_of(start, 128), size)


def pieces_of(bank, group, y, c, x, z_from, z_to):
    heads, mixer, pairs, wide, tall = bank
    column = pl.ds(z_from, z_to - z_from)
    if group == 0:
        return [heads.at[column, x]]
    if group == 1:
        return [mixer.at[y, column, x, :, lanes(c * 256, 256)]]
    if group < 4:
        return [pairs.at[group - 2, y, column, x, :, lanes(c * 384, 384)]]
    if group < 6:
        start = (y * NC + c) * 768 + (group - 4) * 384
        return [wide.at[column, x, :, lanes(start, 384)]]
    return [
        tall.at[y, c, pl.ds((group - 6) * 96, 96), lanes((z * NX + x) * 384, 384)]
        for z in range(z_from, z_to)
    ]


def piece_at(bank, group, y, c, x, z):
    heads, mixer, pairs, wide, tall = bank
    if group == 0:
        return heads.at[z, x]
    if group == 1:
        return mixer.at[y, z, x, :, lanes(c * 256, 256)]
    if group < 4:
        return pairs.at[group - 2, y, z, x, :, lanes(c * 384, 384)]
    if group < 6:
        return wide.at[z, x, :, lanes((y * NC + c) * 768 + (group - 4) * 384, 384)]
    return tall.at[y, c, pl.ds((group - 6) * 96, 96), lanes((z * NX + x) * 384, 384)]


def own_piece(own, group):
    heads, mixer, pairs, wide, tall = own
    if group == 0:
        return heads
    if group == 1:
        return mixer
    if group < 4:
        return pairs.at[group - 2]
    if group < 6:
        return wide.at[:, pl.ds((group - 4) * 384, 384)]
    return tall.at[pl.ds((group - 6) * 96, 96), :]


class Mail:
    def __init__(self, send_sems, recv_sems):
        self.send_sems, self.recv_sems, self.count, self.sent = send_sems, recv_sems, 0, []

    def slots(self, number):
        first = self.count
        self.count += number
        return list(range(first, first + number))

    def post(self, source, target, slot, device):
        copy = pltpu.make_async_remote_copy(
            src_ref=source,
            dst_ref=target,
            send_sem=self.send_sems.at[slot],
            recv_sem=self.recv_sems.at[slot],
            device_id=device,
            device_id_type=MESH_ID,
        )
        copy.start()
        self.sent.append(copy)

    def arrive(self, target, slot, device):
        pltpu.make_async_remote_copy(
            src_ref=target,
            dst_ref=target,
            send_sem=self.send_sems.at[slot],
            recv_sem=self.recv_sems.at[slot],
            device_id=device,
            device_id_type=MESH_ID,
        ).wait_recv()

    def finish(self):
        for copy in self.sent:
            copy.wait_send()


def greet(z, x, y, c):
    barrier = pltpu.get_barrier_semaphore()
    friends = [device_at(lax.rem(z + k, NZ), x, y, c) for k in range(1, NZ)]
    friends += [device_at(lax.rem(z + k, NZ), 1 - x, y, c) for k in range(NZ)]
    friends += [device_at(z, x, 1 - y, c), device_at(z, x, y, 1 - c), device_at(z, x, 1 - y, 1 - c)]
    for friend in friends:
        pl.semaphore_signal(barrier, inc=1, device_id=friend, device_id_type=MESH_ID)
    pl.semaphore_wait(barrier, len(friends))


def parts_in(group, number):
    return number if group >= 6 else 1


def joined(first, second):
    return jnp.concatenate([first, second], axis=1)


def mixed(first, second, core):
    even = joined(joined(first[:, :128], joined(first[:, 128:], second[:, 128:])), second[:, :128])
    odd = joined(joined(first[:, 64:], joined(second[:, :64], first[:, :64])), second[:, 64:])
    return jnp.where(core == 0, even, odd).astype(jnp.bfloat16)


def packed_heads(query, key, value, core):
    nothing = jnp.zeros_like(value[:, :64])
    even = [query[:, :128], key[:, :128], value[:, :128], query[:, 128:], key[:, 128:], value[:, 128:], nothing]
    odd = [query[:, 64:], key[:, 64:], value[:, 64:], key[:, :64], query[:, :64], nothing, value[:, :64]]
    even, odd = jnp.concatenate(even, axis=1), jnp.concatenate(odd, axis=1)
    return jnp.where(core == 0, even, odd).astype(jnp.bfloat16)


def packed_mixer(mixer, core):
    nothing = jnp.zeros_like(mixer[:, :64])
    even = joined(mixer, nothing)
    odd = joined(mixer[:, 64:], joined(nothing, mixer[:, :64]))
    return jnp.where(core == 0, even, odd).astype(jnp.bfloat16)


def own_tiles(row, y, core):
    block = jnp.where(y == 0, row[:, :384], row[:, 384:])
    lane = lax.broadcasted_iota(jnp.int32, (1, 128), 1)
    mine = lax.shift_right_logical(lane, 6) == core
    return (
        jnp.where(core == 0, block[:, :128], block[:, 256:]),
        jnp.where(mine, block[:, 128:256], jnp.zeros((1, 128), jnp.float32)),
    )


def natural_row(pair, third, y, core):
    nothing = jnp.zeros_like(pair)
    first, last = jnp.where(core == 0, pair, nothing), jnp.where(core == 0, nothing, pair)
    block = jnp.concatenate([first, third, last], axis=1)
    empty = jnp.zeros_like(block)
    return jnp.concatenate([jnp.where(y == 0, block, empty), jnp.where(y == 0, empty, block)], axis=1)


ORDER = (0, 2, 1, 3, 4, 5, 6, 7)


def forward_kernel(
    frame_span, lengths, counts,
    query_in, key_in, value_in, mixer_in, xkey_in, xvalue_in, xquery_in, xmixer_in, wide_in, tall_in,
    vectors_in, wide_bias_in, frames_short, tokens_in,
    heads, mixer, pairs, wide, tall, frames, vec_out, wide_bias,
    a_to, rows_to, third_to, o_to, h1_to, c_to, p_self_to, ck_to, cv_to, cq_to, o2_to, h2_to, m_to, p_cross_to,
    tokens_got, small, heads_here, mixer_here, pairs_here, frames_here,
    a_all, head_rows, third, o, h1, c, p_self, ck, cv, cq, o2, h2, m, p_cross,
    o_send, o_got, scores, self_scores, self_bias, cross_bias, heads_in, mixer_in_v, pairs_in, frames_in, small_in,
    send_sems, recv_sems, local_sems, load_sems, save_sems,
):
    z, x, y, c_own = where_am_i()
    heads_in[...] = packed_heads(*[ref[...].astype(jnp.float32) for ref in (query_in, key_in, value_in)], c_own)
    mixer_in_v[...] = packed_mixer(mixer_in[...].astype(jnp.float32), c_own)
    for number, (first, second) in enumerate(((xkey_in, xvalue_in), (xquery_in, xmixer_in))):
        pairs_in[number] = mixed(first[...].astype(jnp.float32), second[...].astype(jnp.float32), c_own)
    small_in[...] = jnp.zeros((32, 128), jnp.bfloat16)
    small_in[0:13, 0:96] = vectors_in[...]
    small_in[16:19, :] = wide_bias_in[...]
    frames_in[:, 368:384] = jnp.zeros((2, 16, 768), jnp.bfloat16)
    frames_in[:, 0:frame_span] = frames_short[...]
    greet(z, x, y, c_own)
    mail = Mail(send_sems, recv_sems)
    own = (heads_in, mixer_in_v, pairs_in, wide_in, tall_in)
    bank = (heads, mixer, pairs, wide, tall)
    far_mate = device_at(z, x, 1 - y, 1 - c_own)
    x_mate, y_mate = device_at(z, 1 - x, y, c_own), device_at(z, x, 1 - y, c_own)
    c_mate = device_at(z, x, y, 1 - c_own)
    z_mates = [device_at(lax.rem(z + n, NZ), x, y, c_own) for n in range(1, NZ)]
    grp = z * NX + x
    seq = y * NC + c_own

    local = []

    def keep(source, target):
        copy = pltpu.make_async_copy(source, target, local_sems.at[len(local)])
        copy.start()
        local.append(copy)

    small_slots = mail.slots(2 * NZ - 1)
    small_to = z_mates + [device_at(lax.rem(z + n, NZ), 1 - x, y, c_own) for n in range(NZ)]
    token_slots = mail.slots(3)
    frame_slots = mail.slots(3)
    z_slots = [mail.slots(NZ - 1) for _ in range(GROUPS)]
    x_slots = [mail.slots(parts_in(g, 4)) for g in range(GROUPS)]
    y_slots = [mail.slots(parts_in(g, 4)) for g in range(GROUPS)]
    dy_slots = [mail.slots(parts_in(g, VIA_X)) for g in range(GROUPS)]
    dx_slots = [mail.slots(parts_in(g, 4 - VIA_X)) for g in range(GROUPS)]
    co_slots = [mail.slots(parts_in(g, 4)) for g in range(GROUPS)]
    cx_slots = [mail.slots(parts_in(g, 4)) for g in range(GROUPS)]
    cy_slots = [mail.slots(parts_in(g, 4)) for g in range(GROUPS)]
    cdy_slots = [mail.slots(parts_in(g, VIA_X)) for g in range(GROUPS)]
    cdx_slots = [mail.slots(parts_in(g, 4 - VIA_X)) for g in range(GROUPS)]

    def to_column(group):
        for n in range(1, NZ):
            mail.post(
                own_piece(own, group), piece_at(bank, group, y, c_own, x, z), z_slots[group][n - 1], z_mates[n - 1]
            )

    def post_all(group, slots, device, yy, cc, xx, z_from, z_to):
        for slot, ref in zip(slots, pieces_of(bank, group, yy, cc, xx, z_from, z_to)):
            mail.post(ref, ref, slot, device)

    def arrive_all(group, slots, device, yy, cc, xx, z_from, z_to):
        for slot, ref in zip(slots, pieces_of(bank, group, yy, cc, xx, z_from, z_to)):
            mail.arrive(ref, slot, device)

    def spread(group):
        for n in range(1, NZ):
            zz = lax.rem(z + NZ - n, NZ)
            mail.arrive(piece_at(bank, group, y, c_own, x, zz), z_slots[group][n - 1], z_mates[n - 1])
        local[group].wait()
        post_all(group, x_slots[group], x_mate, y, c_own, x, 0, 4)
        if group == 0:
            return
        post_all(group, y_slots[group], y_mate, y, c_own, x, 0, 4)
        post_all(group, co_slots[group], c_mate, y, c_own, x, 0, 4)

    def turn(group):
        if group == 0:
            arrive_all(group, x_slots[group], x_mate, y, c_own, 1 - x, 0, 4)
            return
        arrive_all(group, y_slots[group], y_mate, 1 - y, c_own, x, 0, 4)
        post_all(group, dx_slots[group], x_mate, 1 - y, c_own, x, VIA_X, 4)
        post_all(group, cy_slots[group], c_mate, 1 - y, c_own, x, 0, 4)
        arrive_all(group, x_slots[group], x_mate, y, c_own, 1 - x, 0, 4)
        post_all(group, dy_slots[group], y_mate, y, c_own, 1 - x, 0, VIA_X)
        post_all(group, cx_slots[group], c_mate, y, c_own, 1 - x, 0, 4)

    def share(group):
        if group == 0:
            return
        arrive_all(group, dy_slots[group], y_mate, 1 - y, c_own, 1 - x, 0, VIA_X)
        post_all(group, cdy_slots[group], c_mate, 1 - y, c_own, 1 - x, 0, VIA_X)
        arrive_all(group, dx_slots[group], x_mate, 1 - y, c_own, 1 - x, VIA_X, 4)
        post_all(group, cdx_slots[group], c_mate, 1 - y, c_own, 1 - x, VIA_X, 4)

    def complete(group):
        arrive_all(group, co_slots[group], c_mate, y, 1 - c_own, x, 0, 4)
        arrive_all(group, cx_slots[group], c_mate, y, 1 - c_own, 1 - x, 0, 4)
        arrive_all(group, cy_slots[group], c_mate, 1 - y, 1 - c_own, x, 0, 4)
        arrive_all(group, cdy_slots[group], c_mate, 1 - y, 1 - c_own, 1 - x, 0, VIA_X)
        arrive_all(group, cdx_slots[group], c_mate, 1 - y, 1 - c_own, 1 - x, VIA_X, 4)

    def frame_rows(number):
        return frames.at[:, number]

    loads = []

    def load(source, target):
        copy = pltpu.make_async_copy(source, target, load_sems.at[len(loads)])
        copy.start()
        loads.append(copy)
        return copy

    def load_pair(group):
        complete(group)
        return load(pairs.at[group - 2], pairs_here.at[group - 2])

    saves = []

    def save(source, target):
        copy = pltpu.make_async_copy(source, target, save_sems.at[len(saves)])
        copy.start()
        saves.append(copy)

    for group in range(GROUPS):
        keep(own_piece(own, group), piece_at(bank, group, y, c_own, x, z))
    keep(small_in, small.at[grp])
    keep(frames_in, frame_rows(seq))
    keep(tokens_in, tokens_got.at[seq])
    to_column(ORDER[0])
    for slot, device in zip(small_slots, small_to):
        mail.post(small_in, small.at[grp], slot, device)
    to_column(ORDER[1])
    mail.post(frames_in, frame_rows(seq), frame_slots[0], y_mate)
    mail.post(frames_in, frame_rows(seq), frame_slots[1], c_mate)
    mail.post(tokens_in, tokens_got.at[seq], token_slots[0], y_mate)
    mail.post(tokens_in, tokens_got.at[seq], token_slots[1], c_mate)
    to_column(ORDER[2])

    pending = []
    for step in range(GROUPS + 2):
        if step + 3 < GROUPS:
            pending.append((to_column, ORDER[step + 3]))
        if step < GROUPS:
            pending.append((spread, ORDER[step]))
        if 0 <= step - 1 < GROUPS:
            pending.append((turn, ORDER[step - 1]))
        if 0 <= step - 2 < GROUPS:
            pending.append((share, ORDER[step - 2]))

    def tick(number=1):
        while number > 0 and pending:
            action, group = pending.pop(0)
            action(group)
            if action is not to_column:
                number -= 1

    def until(action, group):
        while (action, group) in pending:
            tick()

    for n in range(1, NZ):
        zz = lax.rem(z + NZ - n, NZ)
        mail.arrive(small.at[zz * NX + x], small_slots[n - 1], z_mates[n - 1])
    for n in range(NZ):
        zz = lax.rem(z + NZ - n, NZ)
        mail.arrive(small.at[zz * NX + 1 - x], small_slots[NZ - 1 + n], x_mate)
    local[GROUPS].wait()
    vec_out[...] = jnp.concatenate([small[g, 0:16, 0:96].astype(jnp.float32) for g in range(8)], axis=1)
    for g in range(8):
        three = small[g, 16:24, :].astype(jnp.float32)
        for n in range(3):
            at = g * 384 + n * 128
            wide_bias[:, at:at + 128] = three[n:n + 1]

    o_slots = mail.slots(6)
    until(turn, 0)
    other = (1 - y) * NC + c_own
    mail.arrive(tokens_got.at[other], token_slots[0], y_mate)
    mail.post(tokens_got.at[other], tokens_got.at[other], token_slots[2], c_mate)
    heads_loaded = load(heads, heads_here)
    mail.arrive(frame_rows(other), frame_slots[0], y_mate)
    mail.post(frame_rows(other), frame_rows(other), frame_slots[2], c_mate)
    mail.arrive(tokens_got.at[y * NC + 1 - c_own], token_slots[1], c_mate)
    mail.arrive(tokens_got.at[(1 - y) * NC + 1 - c_own], token_slots[2], c_mate)
    for copy in local[GROUPS + 1:]:
        copy.wait()
    heads_loaded.wait()
    phase = self_forward(lengths, tokens_got, vec_out, heads_here, a_all, head_rows, third, p_self, o_send, self_scores, self_bias)
    mates = ((c_mate, y * NC + 1 - c_own), (y_mate, other), (far_mate, (1 - y) * NC + 1 - c_own))
    for number, t in enumerate(phase):
        if t is not None:
            for place, (mate, mate_seq) in enumerate(mates):
                mail.post(o_send.at[mate_seq, t], o_got.at[seq, t], o_slots[3 * t + place], mate)
            o_got[seq, t] = o_send[seq, t]
        if number % 2 == 1:
            tick()
    mail.arrive(frame_rows(y * NC + 1 - c_own), frame_slots[1], c_mate)
    mail.arrive(frame_rows((1 - y) * NC + 1 - c_own), frame_slots[2], c_mate)
    frames_loaded = load(frames, frames_here)
    for source, target in ((a_all, a_to), (head_rows, rows_to), (third, third_to), (p_self, p_self_to)):
        save(source, target)
    until(share, 2)
    kv_loaded = load_pair(2)
    frames_loaded.wait()
    kv_loaded.wait()
    for number, _ in enumerate(cross_keys(frames_here, vec_out, pairs_here.at[0], ck, cv)):
        if number % 2 == 1:
            tick()
    save(ck, ck_to)
    save(cv, cv_to)
    until(share, 1)
    complete(1)
    mixer_loaded = load(mixer, mixer_here)
    for t in range(2):
        for place, (mate, mate_seq) in enumerate(mates):
            mail.arrive(o_got.at[mate_seq, t], o_slots[3 * t + place], mate)
    mixer_loaded.wait()
    self_out(tokens_got, vec_out, mixer_here, o_got, o, h1, c)
    until(share, 3)
    third_loaded = load_pair(3)
    for source, target in ((o, o_to), (h1, h1_to), (c, c_to)):
        save(source, target)
    third_loaded.wait()
    phase = cross_forward(
        counts, frame_span, c, vec_out, pairs_here.at[1], ck, cv, h1, cq, o2, h2, m, p_cross, scores, cross_bias
    )
    for number, _ in enumerate(phase):
        if 1 <= number <= 12:
            t, pair = (number - 1) // 6, (number - 1) % 6
            save(p_cross.at[t, pair], p_cross_to.at[t, pair])
        if number % 2 == 1:
            tick()
    for source, target in ((cq, cq_to), (o2, o2_to), (h2, h2_to), (m, m_to)):
        save(source, target)
    tick(100)
    for group in (4, 5, 6, 7):
        complete(group)
    for copy in saves:
        copy.wait()
    mail.finish()


VIA_X = 2


def slots_needed():
    return (2 * NZ - 1) + 12 + sum(
        3 + parts_in(g, 4) * 5 + 2 * (parts_in(g, VIA_X) + parts_in(g, 4 - VIA_X)) for g in range(GROUPS)
    )


def run_forward(lengths, counts, matrices, vectors, wide_bias, frames, tokens):
    bf16, f32 = jnp.bfloat16, jnp.float32
    number = slots_needed()
    span = tokens.shape[1]
    anywhere = pl.BlockSpec(memory_space=pl.ANY)
    inside = pl.BlockSpec(memory_space=pltpu.VMEM)
    scalar = pl.BlockSpec(memory_space=pltpu.SMEM)
    rows = (2, span, 768)
    kept = [
        ((2, 4, span, 768), bf16), ((2, 512, 640), bf16), ((2, 512, 128), bf16), (rows, bf16), (rows, f32),
        (rows, bf16), ((2, 4, 3 * span, 512), bf16), ((2, 6, 1536, 128), bf16), ((2, 6, 1536, 128), bf16), (rows, bf16),
        (rows, bf16), (rows, f32), (rows, bf16), ((2, 6, 2 * span, 1536), bf16),
    ]
    frame_span = frames.shape[1]
    frames_shape = (2, NY * NC, 384, 768)
    return pl.pallas_call(
        lambda *refs: forward_kernel(frame_span, *refs),
        out_shape=(
            jax.ShapeDtypeStruct((NZ, NX, 96, 640), bf16),
            jax.ShapeDtypeStruct((NY, NZ, NX, 96, 512), bf16),
            jax.ShapeDtypeStruct((2, NY, NZ, NX, 96, 768), bf16),
            jax.ShapeDtypeStruct((NZ, NX, 96, 3072), bf16),
            jax.ShapeDtypeStruct((NY, NC, 192, 3072), bf16),
            jax.ShapeDtypeStruct(frames_shape, bf16),
            jax.ShapeDtypeStruct((16, 768), f32),
            jax.ShapeDtypeStruct((1, 3072), f32),
        ) + tuple(jax.ShapeDtypeStruct(shape, kind) for shape, kind in kept),
        in_specs=[scalar] * 2 + [inside] * 14,
        out_specs=(anywhere,) * 6 + (inside,) * 2 + (anywhere,) * len(kept),
        scratch_shapes=[
            pltpu.VMEM((4,) + tokens.shape, bf16),
            pltpu.VMEM((8, 32, 128), bf16),
            pltpu.VMEM((NZ, NX, 96, 640), bf16),
            pltpu.VMEM((NY, NZ, NX, 96, 512), bf16),
            pltpu.VMEM((2, NY, NZ, NX, 96, 768), bf16),
            pltpu.VMEM(frames_shape, bf16),
        ] + [pltpu.VMEM(shape, kind) for shape, kind in kept] + [
            pltpu.VMEM((4, 2, span, 256), bf16),
            pltpu.VMEM((4, 2, span, 256), bf16),
            pltpu.VMEM((2 * span, 1536), f32),
            pltpu.VMEM((3 * span, 512), f32),
            pltpu.VMEM((2, 4 * span, 512), f32),
            pltpu.VMEM((2, 1, 1536), f32),
            pltpu.VMEM((96, 640), bf16),
            pltpu.VMEM((96, 256), bf16),
            pltpu.VMEM((2, 96, 384), bf16),
            pltpu.VMEM((2, 384, 768), bf16),
            pltpu.VMEM((32, 128), bf16),
            pltpu.SemaphoreType.DMA((number,)),
            pltpu.SemaphoreType.DMA((number,)),
            pltpu.SemaphoreType.DMA((GROUPS + 3,)),
            pltpu.SemaphoreType.DMA((5,)),
            pltpu.SemaphoreType.DMA((26,)),
        ],
        compiler_params=pltpu.CompilerParams(
            collective_id=1, has_side_effects=True, vmem_limit_bytes=60 << 20
        ),
        name="gather_forward",
    )(lengths, counts, *matrices, vectors, wide_bias, frames, tokens)


def mm(left, right):
    return lax.dot_general(left, right, (((1,), (0,)), ((), ())), preferred_element_type=jnp.float32)


def mm_back(left, right):
    return lax.dot_general(left, right, (((1,), (1,)), ((), ())), preferred_element_type=jnp.float32)


def mm_rows(left, right):
    return lax.dot_general(left, right, (((0,), (0,)), ((), ())), preferred_element_type=jnp.float32)


def low_lanes(rows):
    return lax.broadcasted_iota(jnp.int32, (rows, 128), 1) < 64


def turned(tile):
    return pltpu.roll(tile, 64, 1)


def tile_of(values, number):
    return values[:, number * 128:(number + 1) * 128]


def split_first(near, far):
    low = low_lanes(near.shape[0])
    return [tile_of(near, 0), jnp.where(low, tile_of(near, 1), tile_of(far, 1)), tile_of(far, 0)]


def split_second(near, far):
    low = low_lanes(near.shape[0])
    return [tile_of(near, 1), turned(jnp.where(low, tile_of(far, 0), tile_of(near, 0))), tile_of(far, 1)]


def join_first(values):
    low = low_lanes(values.shape[0])
    middle = tile_of(values, 1)
    nothing = jnp.zeros_like(middle)
    near = jnp.concatenate([tile_of(values, 0), jnp.where(low, middle, nothing)], axis=1)
    far = jnp.concatenate([tile_of(values, 2), jnp.where(low, nothing, middle)], axis=1)
    return near.astype(jnp.bfloat16), far.astype(jnp.bfloat16)


def join_second(values):
    low = low_lanes(values.shape[0])
    middle = turned(tile_of(values, 1))
    nothing = jnp.zeros_like(middle)
    near = jnp.concatenate([jnp.where(low, nothing, middle), tile_of(values, 0)], axis=1)
    far = jnp.concatenate([jnp.where(low, middle, nothing), tile_of(values, 2)], axis=1)
    return near.astype(jnp.bfloat16), far.astype(jnp.bfloat16)


def join_both(first, second):
    low = low_lanes(first.shape[0])
    mine, other = tile_of(first, 1), turned(tile_of(second, 1))
    return jnp.concatenate(
        [
            tile_of(first, 0), jnp.where(low, mine, other), tile_of(second, 0),
            tile_of(first, 2), jnp.where(low, other, mine), tile_of(second, 2),
        ],
        axis=1,
    ).astype(jnp.bfloat16)


def block_of(pair, y, at):
    if len(pair.shape) == 3:
        return pair[y, :, at]
    return pair[y, :, :, :, at].reshape(768, -1)


def times_first(values, pair):
    tiles = []
    for y in range(2):
        tiles += split_first(mm(values, block_of(pair, y, slice(0, 256))), mm(values, block_of(pair, y, slice(384, 640))))
    return tiles


def times_second(values, pair):
    tiles = []
    for y in range(2):
        tiles += split_second(mm(values, block_of(pair, y, slice(128, 384))), mm(values, block_of(pair, y, slice(512, 768))))
    return tiles


def back_first(grads, pair):
    out = None
    for y in range(2):
        near, far = join_first(grads[:, y * 384:(y + 1) * 384])
        part = mm_back(near, block_of(pair, y, slice(0, 256))) + mm_back(far, block_of(pair, y, slice(384, 640)))
        out = part if out is None else out + part
    return out


def back_second(grads, pair):
    out = None
    for y in range(2):
        near, far = join_second(grads[:, y * 384:(y + 1) * 384])
        part = mm_back(near, block_of(pair, y, slice(128, 384))) + mm_back(far, block_of(pair, y, slice(512, 768)))
        out = part if out is None else out + part
    return out


def normed(values, gain, bias):
    return norm_rows(values, gain, bias).astype(jnp.bfloat16)


def normed_back(values, gain, grads):
    centre = values - jnp.mean(values, axis=-1, keepdims=True)
    scale = lax.rsqrt(jnp.mean(centre * centre, axis=-1, keepdims=True) + EPS)
    unit = centre * scale
    inner = grads * gain
    back = scale * (
        inner - jnp.mean(inner, axis=-1, keepdims=True) - unit * jnp.mean(inner * unit, axis=-1, keepdims=True)
    )
    return back, jnp.sum(grads * unit, axis=0, keepdims=True), jnp.sum(grads, axis=0, keepdims=True)


def column_sum(values):
    return jnp.sum(values.astype(jnp.float32), axis=0, keepdims=True)


def both_heads(both):
    low = low_lanes(both.shape[0])
    nothing = jnp.zeros_like(both)
    return jnp.concatenate([jnp.where(low, both, nothing), jnp.where(low, nothing, both)], axis=0)


def stacked(values, t, pair):
    return both_heads(values[t, :, pair * 128:(pair + 1) * 128])


def third_head(tile, core):
    lane = lax.broadcasted_iota(jnp.int32, tile.shape, 1)
    return jnp.where(lax.shift_right_logical(lane, 6) == core, tile, jnp.zeros_like(tile))


def unstacked(values):
    half = values.shape[0] // 2
    return jnp.where(low_lanes(half), values[:half], values[half:])


CHUNK = 16


def soften(scores, bias, chances, rows, width):
    def one(number, carry):
        first = pl.multiple_of(number * CHUNK, CHUNK)
        values = scores[pl.ds(first, CHUNK), 0:width] + bias(first)
        raised = jnp.exp(values - jnp.max(values, axis=1, keepdims=True))
        share = raised * (1.0 / jnp.sum(raised, axis=1, keepdims=True))
        chances[pl.ds(first, CHUNK), 0:width] = share.astype(jnp.bfloat16)
        return carry

    lax.fori_loop(0, rows // CHUNK, one, 0, unroll=2 if rows // CHUNK % 2 == 0 else 3)


def soften_back(chances, slopes, grads, rows, width):
    def one(number, carry):
        first = pl.multiple_of(number * CHUNK, CHUNK)
        share = chances[pl.ds(first, CHUNK), 0:width].astype(jnp.float32)
        slope = slopes[pl.ds(first, CHUNK), 0:width]
        inner = jnp.sum(share * slope, axis=1, keepdims=True)
        grads[pl.ds(first, CHUNK), 0:width] = (share * (slope - inner)).astype(jnp.bfloat16)
        return carry

    lax.fori_loop(0, rows // CHUNK, one, 0, unroll=2 if rows // CHUNK % 2 == 0 else 3)


def self_forward(lengths, tokens, vec, heads, a_out, rows_out, third_out, p_out, o_out, scores, bias):
    span = tokens.shape[2]
    z, x, y, core = where_am_i()
    factor = 1.0 / math.sqrt(HEAD_DIM)
    for s in range(4):
        for t in range(2):
            a_out[t, s] = normed(tokens[s, t].astype(jnp.float32), vec[0:1], vec[1:2])
    yield None
    lane = lax.broadcasted_iota(jnp.int32, (1, 128), 1)
    mine = lax.shift_right_logical(lane, 6) == core
    nothing = jnp.zeros((1, 128), jnp.float32)
    query_pair, query_third = own_tiles(vec[2:3], y, core)
    value_pair, value_third = own_tiles(vec[3:4], y, core)
    offset = jnp.concatenate([query_pair, nothing, value_pair, query_third, value_third], axis=1)
    ones = nothing + 1.0
    scale = jnp.concatenate([ones * factor, ones, ones, jnp.where(mine, ones * factor, ones), ones], axis=1)
    for t in range(2):
        row = lax.broadcasted_iota(jnp.int32, (4 * span, 512), 0)
        place = lax.broadcasted_iota(jnp.int32, (4 * span, 512), 1)
        bias[t] = jnp.where((place <= row) & (place < lengths[t]), 0.0, NEG)
        product = mm(a_out[t].reshape(4 * span, 768), heads[...].reshape(768, 640))
        product = (product + offset) * scale
        rows_out[t, 0:4 * span] = product.astype(jnp.bfloat16)
        rows_out[t, 4 * span:512] = jnp.zeros((512 - 4 * span, 640), jnp.bfloat16)
        third_out[t, 0:4 * span] = turned(product[:, 384:512]).astype(jnp.bfloat16)
        third_out[t, 4 * span:512] = jnp.zeros((512 - 4 * span, 128), jnp.bfloat16)
        yield None
    for t in range(2):
        for block in range(4):
            rows, width = slice(block * span, (block + 1) * span), 128 * (block + 1)
            scores[0:2 * span, 0:width] = mm_back(
                both_heads(rows_out[t, rows, 0:128]), rows_out[t, 0:width, 128:256]
            )
            scores[2 * span:3 * span, 0:width] = mm_back(
                third_head(rows_out[t, rows, 384:512], core), third_out[t, 0:width]
            )
            chances = p_out.at[t, block]
            soften(
                scores, lambda first: bias[t, pl.ds(block * span + lax.rem(first, span), CHUNK), 0:width], chances,
                3 * span, width,
            )
            blended = mm(chances[0:2 * span, 0:width], rows_out[t, 0:width, 256:384])
            o_out[block, t, :, 0:128] = unstacked(blended).astype(jnp.bfloat16)
            blended = mm(chances[2 * span:3 * span, 0:width], rows_out[t, 0:width, 512:640])
            o_out[block, t, :, 128:256] = blended.astype(jnp.bfloat16)
            yield t if block == 3 else None


def self_out(tokens, vec, mixer, o_got, o_out, h1_out, c_out):
    span = tokens.shape[2]
    seq = lax.axis_index("seq")
    low = low_lanes(span)
    for t in range(2):
        for y in range(2):
            even, odd = o_got[2 * y, t], o_got[2 * y + 1, t]
            tiles = [even[:, 0:128], jnp.where(low, even[:, 128:256], odd[:, 128:256]), odd[:, 0:128]]
            for number, tile in enumerate(tiles):
                at = slice(y * 384 + number * 128, y * 384 + (number + 1) * 128)
                o_out[t, :, at] = tile
    rows = o_out[...].reshape(2 * span, 768)
    low = low_lanes(2 * span)
    for y in range(2):
        product = mm(rows, mixer[y].reshape(768, 512))
        tiles = [product[:, 0:128], jnp.where(low, product[:, 128:256], product[:, 384:512]), product[:, 256:384]]
        for number, tile in enumerate(tiles):
            at = slice(y * 384 + number * 128, y * 384 + (number + 1) * 128)
            for t in range(2):
                h1_out[t, :, at] = (
                    tokens[seq, t, :, at].astype(jnp.float32) + tile[t * span:(t + 1) * span] + vec[4:5, at]
                )
    for t in range(2):
        c_out[t] = normed(h1_out[t], vec[5:6], vec[6:7])


def cross_keys(frames, vec, kv, ck_out, cv_out):
    for t in range(2):
        for s in range(4):
            block = frames[t, s]
            rows = slice(s * 384, (s + 1) * 384)
            for y in range(2):
                product = mm(block, block_of(kv, y, slice(0, 768)))
                near, far = product[:, 0:384], product[:, 384:768]
                keys = split_first(near[:, 0:256], far[:, 0:256])
                values = split_second(near[:, 128:384], far[:, 128:384])
                for place in range(3):
                    at = slice(y * 384 + place * 128, y * 384 + (place + 1) * 128)
                    ck_out[t, y * 3 + place, rows] = keys[place].astype(jnp.bfloat16)
                    cv_out[t, y * 3 + place, rows] = (values[place] + vec[8:9, at]).astype(jnp.bfloat16)
            yield


def cross_forward(counts, frame_span, c, vec, xqo, ck, cv, h1, cq_out, o2_out, h2_out, m_out, p_out, scores, bias):
    span = c.shape[1]
    factor = 1.0 / math.sqrt(HEAD_DIM)
    rows = c[...].reshape(2 * span, 768)
    for number, tile in enumerate(times_first(rows, xqo)):
        at = slice(number * 128, (number + 1) * 128)
        tile = ((tile + vec[7:8, at]) * factor).astype(jnp.bfloat16)
        for t in range(2):
            cq_out[t, :, at] = tile[t * span:(t + 1) * span]
    for t in range(2):
        for s in range(4):
            inside = lax.broadcasted_iota(jnp.int32, (1, 384), 1)
            good = (inside < frame_span) & (s * frame_span + inside < counts[t])
            bias[t, :, s * 384:(s + 1) * 384] = jnp.where(good, 0.0, NEG)
    yield
    for t in range(2):
        for pair in range(6):
            at = slice(pair * 128, (pair + 1) * 128)
            scores[...] = mm_back(stacked(cq_out, t, pair), ck[t, pair])
            chances = p_out.at[t, pair]
            soften(scores, lambda first: bias[t], chances, 2 * span, 1536)
            o2_out[t, :, at] = unstacked(mm(chances[...], cv[t, pair])).astype(jnp.bfloat16)
            yield
    out = o2_out[...].reshape(2 * span, 768)
    for number, tile in enumerate(times_second(out, xqo)):
        at = slice(number * 128, (number + 1) * 128)
        for t in range(2):
            h2_out[t, :, at] = h1[t, :, at] + tile[t * span:(t + 1) * span] + vec[9:10, at]
    for t in range(2):
        m_out[t] = normed(h2_out[t], vec[10:11], vec[11:12])
    yield


class Summing:
    def __init__(self, mail, place, mates, acc, diag_x, diag_y, x_in, y_in, z_in, total):
        self.mail, self.place, self.mates = mail, place, mates
        self.acc, self.diag_x, self.diag_y = acc, diag_x, diag_y
        self.x_in, self.y_in, self.z_in, self.total = x_in, y_in, z_in, total
        self.slots = [mail.slots(4 + NZ - 1) for _ in range(acc.shape[0])]

    def begin(self, n):
        z, x, y = self.place
        x_mate, y_mate, _ = self.mates
        self.mail.post(self.acc.at[n, 1 - y, pl.ds(0, 2), 1 - x], self.diag_x.at[n], self.slots[n][0], x_mate)
        self.mail.post(self.acc.at[n, 1 - y, pl.ds(2, 2), 1 - x], self.diag_y.at[n], self.slots[n][1], y_mate)

    def side(self, n):
        z, x, y = self.place
        x_mate, y_mate, _ = self.mates
        self.mail.arrive(self.diag_x.at[n], self.slots[n][0], x_mate)
        for k in range(2):
            self.acc[n, 1 - y, k, x] = self.acc[n, 1 - y, k, x] + self.diag_x[n, k]
        self.mail.post(self.acc.at[n, 1 - y, :, x], self.y_in.at[n], self.slots[n][2], y_mate)
        self.mail.arrive(self.diag_y.at[n], self.slots[n][1], y_mate)
        for k in range(2):
            self.acc[n, y, 2 + k, 1 - x] = self.acc[n, y, 2 + k, 1 - x] + self.diag_y[n, k]
        self.mail.post(self.acc.at[n, y, :, 1 - x], self.x_in.at[n], self.slots[n][3], x_mate)

    def column(self, n):
        z, x, y = self.place
        x_mate, y_mate, z_mates = self.mates
        self.mail.arrive(self.y_in.at[n], self.slots[n][2], y_mate)
        self.mail.arrive(self.x_in.at[n], self.slots[n][3], x_mate)
        for k in range(NZ):
            self.acc[n, y, k, x] = (
                self.acc[n, y, k, x].astype(jnp.float32)
                + self.x_in[n, k].astype(jnp.float32)
                + self.y_in[n, k].astype(jnp.float32)
            ).astype(jnp.bfloat16)
        for k in range(1, NZ):
            zz = lax.rem(z + k, NZ)
            self.mail.post(self.acc.at[n, y, zz, x], self.z_in.at[n, k - 1], self.slots[n][3 + k], z_mates[k - 1])

    def last(self, n):
        z, x, y = self.place
        _, _, z_mates = self.mates
        for k in range(1, NZ):
            self.mail.arrive(self.z_in.at[n, k - 1], self.slots[n][3 + k], z_mates[k - 1])
        self.total[n] = self.acc[n, y, z, x].astype(jnp.float32) + (
            self.z_in[n, 0].astype(jnp.float32) + self.z_in[n, 1].astype(jnp.float32)
        ) + self.z_in[n, 2].astype(jnp.float32)


def summing_scratch(n, width=384):
    piece = (96, width)
    shapes = [
        (n, NY, NZ, NX) + piece, (n, 2) + piece, (n, 2) + piece, (n, NZ) + piece, (n, NZ) + piece, (n, NZ - 1) + piece
    ]
    return [pltpu.VMEM(shape, jnp.bfloat16) for shape in shapes]


class Loads:
    def __init__(self, sems):
        self.sems, self.count = sems, 0

    def start(self, source, target):
        copy = pltpu.make_async_copy(source, target, self.sems.at[self.count])
        copy.start()
        self.count += 1
        return copy


def two(first, second):
    return jnp.concatenate([first, second], axis=0)


def feed_kernel(
    lengths, ids, weights, cotangent, vec, wide_bias, h2, m, o2, c, h1, cq,
    wide_far, tall_far, pairs_far, frames_far, ck_far, cv_far, p_far,
    y_out, dh1_out, total, acc_kv, acc_xqo, small_out, wide_small,
    acc, diag_x, diag_y, x_in, y_in, z_in,
    wide, tall, xqo, frames, keys_here, values_here, p_here,
    m_sib, g_own, g_sib, du_own, du_send, du_sib, dz_own, dz_send, dz_sib,
    o2_sib, c_sib, xb_own, xb_send, xb_sib, xa_own, xa_send, xa_sib, gkv, kv_in,
    dy, dh2, do, dq, scores, dscores, gate_slope,
    send_sems, recv_sems, load_sems, unit_sems,
):
    z, x, y, core = where_am_i()
    span = m.shape[1]
    seq = y * NC + core
    factor = 1.0 / math.sqrt(HEAD_DIM)
    low = low_lanes(2 * span)
    x_mate, y_mate, c_mate = device_at(z, 1 - x, y, core), device_at(z, x, 1 - y, core), device_at(z, x, y, 1 - core)
    z_mates = [device_at(lax.rem(z + n, NZ), x, y, core) for n in range(1, NZ)]
    loads = Loads(load_sems)
    order = [(yy, side) for yy in range(2) for side in range(2)]
    block_loads = []
    for yy, side in order:
        at = lanes((2 * yy + (core if side == 0 else 1 - core)) * 768, 768)
        block_loads.append((
            loads.start(wide_far.at[:, :, :, at], wide.at[:, :, :, at]),
            loads.start(tall_far.at[:, :, :, at], tall.at[:, :, :, at]),
        ))
    xqo_load = loads.start(pairs_far.at[1], xqo)
    frames_load = loads.start(frames_far, frames)
    units = [(pair, t) for pair in range(6) for t in range(2)]

    def unit_copies(n):
        pair, t = units[n]
        slot = n % 2
        return [
            pltpu.make_async_copy(ck_far.at[t, pair], keys_here.at[slot], unit_sems.at[slot, 0]),
            pltpu.make_async_copy(cv_far.at[t, pair], values_here.at[slot], unit_sems.at[slot, 1]),
            pltpu.make_async_copy(p_far.at[t, pair], p_here.at[slot], unit_sems.at[slot, 2]),
        ]

    for copy in unit_copies(0):
        copy.start()
    greet(z, x, y, core)
    mail = Mail(send_sems, recv_sems)
    sums = Summing(mail, (z, x, y), (x_mate, y_mate, z_mates), acc, diag_x, diag_y, x_in, y_in, z_in, total)
    swap = mail.slots(1 + 2 + 4 + 2 + 2 + 2 + 1)
    m_slot, dz_slots, g_slots, du_slots = swap[0], swap[1:3], swap[3:7], swap[7:9]
    xb_slots, xa_slots, kv_slot = swap[9:11], swap[11:13], swap[13]
    o2_slot, c_slot = mail.slots(2)
    mail.post(m, m_sib, m_slot, c_mate)
    mail.post(o2, o2_sib, o2_slot, c_mate)
    mail.post(c, c_sib, c_slot, c_mate)

    for t in range(2):
        weight = 0.0
        for corpus in range(weights.shape[0]):
            weight = weight + jnp.where(ids[t] == corpus, weights[corpus], 0.0)
        row = lax.broadcasted_iota(jnp.int32, (span, 1), 0) + seq * span
        scale = jnp.where(row < lengths[t], weight, 0.0)
        dy[t * span:(t + 1) * span] = cotangent[t].astype(jnp.float32) * scale
    dz = dy[...].astype(jnp.bfloat16)
    dz_wide = dz.astype(jnp.float32)
    small_out[...] = jnp.zeros_like(small_out)
    small_out[12:13] = column_sum(dz_wide)
    for yy in range(2):
        tiles = [dz_wide[:, yy * 384 + n * 128:yy * 384 + (n + 1) * 128] for n in range(3)]
        even = jnp.concatenate([tiles[0], tiles[1]], axis=1)
        last = turned(tiles[2])
        odd = jnp.concatenate([jnp.where(low, turned(tiles[1]), last), last], axis=1)
        dz_own[yy] = jnp.where(core == 0, even, odd).astype(jnp.bfloat16)
        dz_send[yy] = jnp.where(core == 0, odd, even).astype(jnp.bfloat16)
        mail.post(dz_send.at[yy], dz_sib.at[yy], dz_slots[yy], c_mate)
    rows = m[...].reshape(2 * span, 768)
    for number, (yy, side) in enumerate(order):
        at = lanes((2 * yy + (core if side == 0 else 1 - core)) * 768, 768)
        for copy in block_loads[number]:
            copy.wait()
        hidden = mm(rows, wide[:, :, :, at].reshape(768, 768)) + wide_bias[:, at]
        bell = 0.5 * (1.0 + lax.erf(hidden * 0.7071067811865476))
        g_own[:, at] = (hidden * bell).astype(jnp.bfloat16)
        mail.post(g_own.at[:, at], g_sib.at[:, at], g_slots[number], c_mate)
        gate_slope[:, at] = bell + hidden * (jnp.exp(-0.5 * hidden * hidden) * 0.3989422804014327)
    for number, (yy, side) in enumerate(order):
        at = lanes((2 * yy + (1 - core if side == 0 else core)) * 768, 768)
        mail.arrive(g_sib.at[:, at], g_slots[number], c_mate)
    for yy in range(2):
        mail.arrive(dz_sib.at[yy], dz_slots[yy], c_mate)
    for yy in range(2):
        slopes = two(dz_own[yy], dz_sib[yy])
        for zz in range(NZ):
            at = slice(zz * 768, (zz + 1) * 768)
            product = mm_rows(slopes, two(g_own[:, at], g_sib[:, at])).astype(jnp.bfloat16)
            for xx in range(NX):
                acc[2, yy, zz, xx] = product[0:96, xx * 384:(xx + 1) * 384]
                acc[3, yy, zz, xx] = product[96:192, xx * 384:(xx + 1) * 384]
    sums.begin(2)
    sums.begin(3)
    z_sum, dm_sum = None, None
    for number, (yy, side) in enumerate(order):
        at = lanes((2 * yy + (core if side == 0 else 1 - core)) * 768, 768)
        wide_here = wide[:, :, :, at].reshape(768, 768)
        tall_here = tall[:, :, :, at].reshape(768, 768)
        back = (mm(dz, tall_here) * gate_slope[:, at]).astype(jnp.bfloat16)
        if side == 0:
            du_own[yy] = back
        else:
            du_send[yy] = back
            mail.post(du_send.at[yy], du_sib.at[yy], du_slots[yy], c_mate)
        part = mm_back(g_own[:, at], tall_here)
        z_sum = part if z_sum is None else z_sum + part
        part = mm_back(back, wide_here)
        dm_sum = part if dm_sum is None else dm_sum + part
        wide_small[:, at] = column_sum(back)
    mail.arrive(m_sib, m_slot, c_mate)
    both_rows = two(rows, m_sib[...].reshape(2 * span, 768))
    for yy in range(2):
        mail.arrive(du_sib.at[yy], du_slots[yy], c_mate)
        product = mm_rows(both_rows, two(du_own[yy], du_sib[yy])).astype(jnp.bfloat16)
        acc[0, yy] = product[:, 0:384].reshape(NZ, NX, 96, 384)
        acc[1, yy] = product[:, 384:768].reshape(NZ, NX, 96, 384)
    sums.begin(0)
    sums.begin(1)
    h2_rows = h2[...].reshape(2 * span, 768)
    out = h2_rows + z_sum + vec[12:13]
    back, gain, offset = normed_back(h2_rows, vec[10:11], dm_sum)
    small_out[10:11] = gain
    small_out[11:12] = offset
    dh2[...] = dy[...] + back
    for t in range(2):
        y_out[t] = out[t * span:(t + 1) * span].astype(jnp.bfloat16)

    pending = []
    for step in range(6):
        for lag, action in ((0, sums.side), (1, sums.column), (2, sums.last)):
            if 0 <= step - lag < 4:
                pending.append((action, (2, 3, 0, 1)[step - lag]))

    def tick(number=1):
        for _ in range(number):
            if pending:
                action, group = pending.pop(0)
                action(group)

    low_wide = dh2[...].astype(jnp.bfloat16).astype(jnp.float32)
    small_out[9:10] = column_sum(low_wide)
    xqo_load.wait()
    for yy in range(2):
        near, far = join_second(low_wide[:, yy * 384:(yy + 1) * 384])
        xb_own[yy] = jnp.where(core == 0, near, far)
        xb_send[yy] = jnp.where(core == 0, far, near)
        mail.post(xb_send.at[yy], xb_sib.at[yy], xb_slots[yy], c_mate)
    heard = back_second(low_wide, xqo)
    small_out[8:9] = column_sum(heard.astype(jnp.bfloat16))
    for t in range(2):
        do[t] = heard[t * span:(t + 1) * span].astype(jnp.bfloat16)
    tick()
    frames_load.wait()
    total_kv = None
    for number, (pair, t) in enumerate(units):
        at = slice(pair * 128, (pair + 1) * 128)
        slot = number % 2
        if number + 1 < len(units):
            for copy in unit_copies(number + 1):
                copy.start()
        for copy in unit_copies(number):
            copy.wait()
        slopes, query = stacked(do, t, pair), stacked(cq, t, pair)
        scores[...] = mm_back(slopes, values_here[slot])
        chances = p_here.at[slot]
        soften_back(chances, scores, dscores, 2 * span, 1536)
        dq[t * span:(t + 1) * span, at] = unstacked(mm(dscores[...], keys_here[slot])) * factor
        turned_grads = two(mm_rows(query, dscores[...]), mm_rows(slopes, chances[...])).astype(jnp.bfloat16)
        part = mm(turned_grads, frames[t].reshape(1536, 768))
        total_kv = part if t == 0 else total_kv + part
        if t == 1:
            keys, values = total_kv[0:128].T, total_kv[128:256].T
            yy, place = pair // 3, pair % 3
            if place == 1:
                values = turned(values)
                half = low_lanes(768)
                gkv[0, yy, :, 128:256] = jnp.where(half, keys, values).astype(jnp.bfloat16)
                gkv[1, yy, :, 128:256] = jnp.where(half, values, keys).astype(jnp.bfloat16)
            else:
                gkv[place // 2, yy, :, 0:128] = keys.astype(jnp.bfloat16)
                gkv[place // 2, yy, :, 256:384] = values.astype(jnp.bfloat16)
        if number >= 2:
            tick()
    mail.post(gkv.at[1 - core], kv_in, kv_slot, c_mate)
    low_q = dq[...].astype(jnp.bfloat16).astype(jnp.float32)
    small_out[7:8] = column_sum(low_q)
    for yy in range(2):
        near, far = join_first(low_q[:, yy * 384:(yy + 1) * 384])
        xa_own[yy] = jnp.where(core == 0, near, far)
        xa_send[yy] = jnp.where(core == 0, far, near)
        mail.post(xa_send.at[yy], xa_sib.at[yy], xa_slots[yy], c_mate)
    back, gain, offset = normed_back(h1[...].reshape(2 * span, 768), vec[5:6], back_first(low_q, xqo))
    small_out[5:6] = gain
    small_out[6:7] = offset
    for t in range(2):
        dh1_out[t] = dh2[t * span:(t + 1) * span] + back[t * span:(t + 1) * span]
    mail.arrive(o2_sib, o2_slot, c_mate)
    mail.arrive(c_sib, c_slot, c_mate)
    o2_both = two(o2[...].reshape(2 * span, 768), o2_sib[...].reshape(2 * span, 768))
    c_both = two(c[...].reshape(2 * span, 768), c_sib[...].reshape(2 * span, 768))
    for yy in range(2):
        mail.arrive(xb_sib.at[yy], xb_slots[yy], c_mate)
        mail.arrive(xa_sib.at[yy], xa_slots[yy], c_mate)
        second = mm_rows(o2_both, two(xb_own[yy], xb_sib[yy]))
        first = mm_rows(c_both, two(xa_own[yy], xa_sib[yy]))
        store_pair(acc_xqo.at[yy], first, second)
    mail.arrive(kv_in, kv_slot, c_mate)
    for yy in range(2):
        acc_kv[yy] = (gkv[core, yy] + kv_in[yy]).reshape(NZ, NX, 96, 384)
    tick(100)
    mail.finish()


def store_pair(out, first, second):
    shape = (NZ, NX, 96, 128)
    out[:, :, :, 0:128] = tile_of(first, 0).astype(jnp.bfloat16).reshape(shape)
    out[:, :, :, 128:256] = (tile_of(first, 1) + tile_of(second, 0)).astype(jnp.bfloat16).reshape(shape)
    out[:, :, :, 256:384] = tile_of(second, 1).astype(jnp.bfloat16).reshape(shape)


def run_feed(lengths, ids, weights, near, far):
    bf16, f32 = jnp.bfloat16, jnp.float32
    span = near[4].shape[1]
    rows, flat = (2, span, 768), 2 * span
    inside, anywhere = pl.BlockSpec(memory_space=pltpu.VMEM), pl.BlockSpec(memory_space=pl.ANY)
    scalar = pl.BlockSpec(memory_space=pltpu.SMEM)
    piece = (NY, NZ, NX, 96, 384)
    number = 4 * 7 + 16
    scratch = [
        ((NZ, NX, 96, 3072), bf16), ((NY, NC, 192, 3072), bf16), ((NY, NZ, NX, 96, 768), bf16), (far[3].shape, bf16),
        ((2, 1536, 128), bf16), ((2, 1536, 128), bf16), ((2, flat, 1536), bf16),
        (rows, bf16), ((flat, 3072), bf16), ((flat, 3072), bf16),
        ((2, flat, 768), bf16), ((2, flat, 768), bf16), ((2, flat, 768), bf16),
        ((2, flat, 256), bf16), ((2, flat, 256), bf16), ((2, flat, 256), bf16),
        (rows, bf16), (rows, bf16),
    ] + [((2, flat, 256), bf16)] * 6 + [
        ((2, 2, 768, 384), bf16), ((2, 768, 384), bf16),
        ((flat, 768), f32), ((flat, 768), f32), (rows, bf16), ((flat, 768), f32), ((flat, 1536), f32),
        ((flat, 1536), bf16), ((flat, 3072), f32),
    ]
    return pl.pallas_call(
        feed_kernel,
        out_shape=(
            jax.ShapeDtypeStruct(rows, bf16), jax.ShapeDtypeStruct(rows, f32),
            jax.ShapeDtypeStruct((4, 96, 384), f32),
            jax.ShapeDtypeStruct(piece, bf16), jax.ShapeDtypeStruct(piece, bf16),
            jax.ShapeDtypeStruct((16, 768), f32), jax.ShapeDtypeStruct((1, 3072), f32),
        ),
        in_specs=[scalar] * 3 + [inside] * len(near) + [anywhere] * len(far),
        out_specs=(inside,) * 7,
        scratch_shapes=summing_scratch(4) + [pltpu.VMEM(shape, kind) for shape, kind in scratch] + [
            pltpu.SemaphoreType.DMA((number,)),
            pltpu.SemaphoreType.DMA((number,)),
            pltpu.SemaphoreType.DMA((10,)),
            pltpu.SemaphoreType.DMA((2, 3)),
        ],
        compiler_params=pltpu.CompilerParams(
            collective_id=2, has_side_effects=True, vmem_limit_bytes=60 << 20
        ),
        name="feed_cross_back",
    )(lengths, ids, weights, *near, *far)


def last_kernel(
    tokens, dh1, a, head_rows, third, o, p, vec, small_before, wide_small,
    heads_far, mixer_far, kv_far, xqo_far,
    dx_out, total, total_o, total_q, small_total,
    acc, diag_x, diag_y, x_in, y_in, z_in,
    acc_o, diag_x_o, diag_y_o, x_in_o, y_in_o, z_in_o,
    acc_q, x_in_q, z_in_q,
    heads, mixer, o_sib, ob_own, ob_send, ob_sib, do_send, do_got, kv_sum, dq_third, dheads,
    da_send, da_core, da_side, scores, dscores,
    small, pack, pack_in, pack_sum, pack_seq,
    send_sems, recv_sems, load_sems,
):
    z, x, y, core = where_am_i()
    span = o.shape[1]
    seq = y * NC + core
    grp = z * NX + x
    factor = 1.0 / math.sqrt(HEAD_DIM)
    x_mate, y_mate, c_mate = device_at(z, 1 - x, y, core), device_at(z, x, 1 - y, core), device_at(z, x, y, 1 - core)
    far_mate = device_at(z, x, 1 - y, 1 - core)
    z_mates = [device_at(lax.rem(z + n, NZ), x, y, core) for n in range(1, NZ)]
    loads = Loads(load_sems)
    mixer_load = loads.start(mixer_far, mixer)
    acc_loads = [loads.start(kv_far, acc.at[0]), loads.start(xqo_far, acc.at[1])]
    heads_load = loads.start(heads_far, heads)
    greet(z, x, y, core)
    mail = Mail(send_sems, recv_sems)
    mates3 = (x_mate, y_mate, z_mates)
    sums = Summing(mail, (z, x, y), mates3, acc, diag_x, diag_y, x_in, y_in, z_in, total)
    sums_o = Summing(mail, (z, x, y), mates3, acc_o, diag_x_o, diag_y_o, x_in_o, y_in_o, z_in_o, total_o)
    (o_slot,) = mail.slots(1)
    ob_slots, do_slots = mail.slots(2), mail.slots(6)
    core_slots, side_slots = mail.slots(4), mail.slots(2)
    xq_slots, zq_slots = mail.slots(2), mail.slots(6)
    pack_slots, seq_slots = mail.slots(2 * NZ - 1), mail.slots(2)
    mail.post(o, o_sib, o_slot, c_mate)
    small[...] = small_before[...]
    low_wide = dh1[...].reshape(2 * span, 768).astype(jnp.bfloat16).astype(jnp.float32)
    small[4:5] = column_sum(low_wide)
    heard = None
    mixer_load.wait()
    for yy in range(2):
        near, far = join_first(low_wide[:, yy * 384:(yy + 1) * 384])
        ob_own[yy] = jnp.where(core == 0, near, far)
        ob_send[yy] = jnp.where(core == 0, far, near)
        mail.post(ob_send.at[yy], ob_sib.at[yy], ob_slots[yy], c_mate)
        part = mm_back(jnp.concatenate([near, far], axis=1), mixer[yy].reshape(768, 512))
        heard = part if heard is None else heard + part
    for yy in range(2):
        near, far = join_first(heard[:, yy * 384:(yy + 1) * 384])
        for t in range(2):
            do_send[2 * yy, t] = near[t * span:(t + 1) * span]
            do_send[2 * yy + 1, t] = far[t * span:(t + 1) * span]
    mates = (
        (c_mate, y * NC + 1 - core), (y_mate, (1 - y) * NC + core), (far_mate, (1 - y) * NC + 1 - core)
    )
    for t in range(2):
        for place in (2, 1, 0):
            mate, mate_seq = mates[place]
            mail.post(do_send.at[mate_seq, t], do_got.at[seq, t], do_slots[3 * t + place], mate)
        do_got[seq, t] = do_send[seq, t]
    for copy in acc_loads:
        copy.wait()
    sums.begin(0)
    sums.begin(1)
    mail.arrive(o_sib, o_slot, c_mate)
    o_both = two(o[...].reshape(2 * span, 768), o_sib[...].reshape(2 * span, 768))
    for yy in range(2):
        mail.arrive(ob_sib.at[yy], ob_slots[yy], c_mate)
        product = mm_rows(o_both, two(ob_own[yy], ob_sib[yy])).astype(jnp.bfloat16)
        acc_o[0, yy] = product.reshape(NZ, NX, 96, 256)
    sums_o.begin(0)
    pending = [
        (sums.side, 0), (sums.side, 1), (sums_o.side, 0), (sums.column, 0), (sums.column, 1), (sums_o.column, 0),
        (sums.last, 0), (sums.last, 1), (sums_o.last, 0),
    ]

    def tick(number=1):
        for _ in range(number):
            if pending:
                action, group = pending.pop(0)
                action(group)

    def exchange_core(t):
        mail.post(da_send.at[y * NC + 1 - core, t], da_core.at[t, 0], core_slots[2 * t], c_mate)
        mail.post(da_send.at[(1 - y) * NC + 1 - core, t], da_core.at[t, 1], core_slots[2 * t + 1], c_mate)

    def exchange_side(t):
        mail.arrive(da_core.at[t, 1], core_slots[2 * t + 1], c_mate)
        across = (1 - y) * NC + core
        da_send[across, t] = da_send[across, t] + da_core[t, 1]
        mail.post(da_send.at[across, t], da_side.at[t], side_slots[t], y_mate)

    heads_load.wait()
    for t in range(2):
        for place, (mate, mate_seq) in enumerate(mates):
            mail.arrive(do_got.at[mate_seq, t], do_slots[3 * t + place], mate)
        for block in (3, 2, 1, 0):
            rows, width = slice(block * span, (block + 1) * span), 128 * (block + 1)
            slopes, slopes_third = both_heads(do_got[block, t, :, 0:128]), do_got[block, t, :, 128:256]
            query = both_heads(head_rows[t, rows, 0:128])
            query_third = third_head(head_rows[t, rows, 384:512], core)
            scores[0:2 * span, 0:width] = mm_back(slopes, head_rows[t, 0:width, 256:384])
            scores[2 * span:3 * span, 0:width] = mm_back(slopes_third, head_rows[t, 0:width, 512:640])
            chances = p.at[t, block]
            soften_back(chances, scores, dscores, 3 * span, width)
            pair_grads, third_grads = dscores[0:2 * span, 0:width], dscores[2 * span:3 * span, 0:width]
            dheads[t, rows, 0:128] = (
                unstacked(mm(pair_grads, head_rows[t, 0:width, 128:256])) * factor
            ).astype(jnp.bfloat16)
            dq_third[rows] = third_head(mm(third_grads, third[t, 0:width]) * factor, core)
            parts = (
                mm_rows(query, pair_grads), mm_rows(query_third, third_grads),
                mm_rows(slopes, chances[0:2 * span, 0:width]), mm_rows(slopes_third, chances[2 * span:3 * span, 0:width]),
            )
            for number, part in enumerate(parts):
                if block == 3:
                    kv_sum[number] = part
                else:
                    kv_sum[number, :, 0:width] += part
            if t == 1 and block == 3:
                exchange_side(0)
            elif (t, block) in ((0, 1), (0, 0), (1, 1), (1, 0)):
                tick()
        keys, keys_third, values, values_third = [kv_sum[number].T[0:4 * span] for number in range(4)]
        dheads[t, :, 128:256] = keys.astype(jnp.bfloat16)
        dheads[t, :, 256:384] = values.astype(jnp.bfloat16)
        dheads[t, :, 384:512] = (dq_third[...] + turned(keys_third)).astype(jnp.bfloat16)
        dheads[t, :, 512:640] = values_third.astype(jnp.bfloat16)
        if t == 1:
            inputs = two(a[0].reshape(4 * span, 768), a[1].reshape(4 * span, 768))
            product = mm_rows(inputs, two(dheads[0], dheads[1])).astype(jnp.bfloat16)
            acc_q[...] = product.reshape(NZ, NX, 96, 640)
            for part, at in enumerate((slice(0, 384), slice(384, 640))):
                mail.post(acc_q.at[:, 1 - x, :, at], x_in_q.at[:, :, at], xq_slots[part], x_mate)
        back = mm_back(dheads[t], heads[...].reshape(768, 640)).astype(jnp.bfloat16)
        for s in range(4):
            da_send[s, t] = back[s * span:(s + 1) * span]
        exchange_core(t)
    tick(2)
    exchange_side(1)
    tick()
    sums_q = [column_sum(two(dheads[0, :, n * 128:(n + 1) * 128], dheads[1, :, n * 128:(n + 1) * 128])) for n in (0, 2, 3, 4)]
    small[2:3] = natural_row(sums_q[0], third_head(sums_q[2], core), y, core)
    small[3:4] = natural_row(sums_q[1], sums_q[3], y, core)
    for part, at in enumerate((slice(0, 384), slice(384, 640))):
        mail.arrive(x_in_q.at[:, :, at], xq_slots[part], x_mate)
        for k in range(NZ):
            acc_q[k, x, :, at] = acc_q[k, x, :, at] + x_in_q[k, :, at]
        for k in range(1, NZ):
            zz = lax.rem(z + k, NZ)
            mail.post(
                acc_q.at[zz, x, :, at], z_in_q.at[k - 1, :, at], zq_slots[3 * part + k - 1], z_mates[k - 1]
            )
    gain, offset = None, None
    for t in range(2):
        mail.arrive(da_core.at[t, 0], core_slots[2 * t], c_mate)
        mail.arrive(da_side.at[t], side_slots[t], y_mate)
        back = (
            da_send[seq, t].astype(jnp.float32) + da_core[t, 0].astype(jnp.float32) + da_side[t].astype(jnp.float32)
        )
        part, gain_part, offset_part = normed_back(tokens[t].astype(jnp.float32), vec[0:1], back)
        dx_out[t] = (dh1[t] + part).astype(jnp.bfloat16)
        gain = gain_part if t == 0 else gain + gain_part
        offset = offset_part if t == 0 else offset + offset_part
    small[0:1] = gain
    small[1:2] = offset
    for g in range(8):
        pack[g, 0:16, 0:96] = small[:, g * 96:(g + 1) * 96]
        pack[g, 0:16, 96:128] = jnp.zeros((16, 32), jnp.float32)
        for n in range(3):
            at = g * 384 + n * 128
            pack[g, 16 + n:17 + n, :] = wide_small[:, at:at + 128]
        pack[g, 19:24, :] = jnp.zeros((5, 128), jnp.float32)
    pack_to = [(lax.rem(z + n, NZ), x) for n in range(1, NZ)]
    pack_to += [(lax.rem(z + n, NZ), 1 - x) for n in range(NZ)]
    for number, (zz, xx) in enumerate(pack_to):
        mail.post(pack.at[zz * NX + xx], pack_in.at[number], pack_slots[number], device_at(zz, xx, y, core))
    tick(100)
    for number in range(2 * NZ - 1):
        mail.arrive(pack_in.at[number], pack_slots[number], x_mate)
    pack_sum[...] = (
        (pack[grp] + pack_in[0]) + (pack_in[1] + pack_in[2])
        + ((pack_in[3] + pack_in[4]) + (pack_in[5] + pack_in[6]))
    )
    mail.post(pack_sum, pack_seq.at[0], seq_slots[0], c_mate)
    mail.arrive(pack_seq.at[0], seq_slots[0], c_mate)
    pack_seq[1] = pack_sum[...] + pack_seq[0]
    mail.post(pack_seq.at[1], pack_seq.at[2], seq_slots[1], y_mate)
    for part, at in enumerate((slice(0, 384), slice(384, 640))):
        for k in range(1, NZ):
            mail.arrive(z_in_q.at[k - 1, :, at], zq_slots[3 * part + k - 1], z_mates[k - 1])
        total_q[:, at] = (acc_q[z, x, :, at].astype(jnp.float32) + z_in_q[0, :, at].astype(jnp.float32)) + (
            z_in_q[1, :, at].astype(jnp.float32) + z_in_q[2, :, at].astype(jnp.float32)
        )
    mail.arrive(pack_seq.at[2], seq_slots[1], y_mate)
    small_total[...] = pack_seq[1] + pack_seq[2]
    mail.finish()


def run_last(near, far):
    bf16, f32 = jnp.bfloat16, jnp.float32
    span = near[0].shape[1]
    rows, flat = (2, span, 768), 2 * span
    inside, anywhere = pl.BlockSpec(memory_space=pltpu.VMEM), pl.BlockSpec(memory_space=pl.ANY)
    number = 3 * 7 + 1 + 2 + 6 + 6 + 8 + 9
    scratch = [
        ((NZ, NX, 96, 640), bf16), ((NZ, 96, 640), bf16), ((NZ - 1, 96, 640), bf16),
        ((NZ, NX, 96, 640), bf16), ((NY, NZ, NX, 96, 512), bf16), (rows, bf16),
        ((2, flat, 256), bf16), ((2, flat, 256), bf16), ((2, flat, 256), bf16),
        ((4, 2, span, 256), bf16), ((4, 2, span, 256), bf16), ((4, 128, 512), f32), ((4 * span, 128), f32),
        ((2, 4 * span, 640), bf16), ((4, 2, span, 768), bf16), ((2, 2, span, 768), bf16), ((2, span, 768), bf16),
        ((3 * span, 512), f32), ((3 * span, 512), bf16),
        ((16, 768), f32), ((8, 24, 128), f32), ((7, 24, 128), f32), ((24, 128), f32), ((3, 24, 128), f32),
    ]
    return pl.pallas_call(
        last_kernel,
        out_shape=(
            jax.ShapeDtypeStruct(rows, bf16), jax.ShapeDtypeStruct((2, 96, 384), f32),
            jax.ShapeDtypeStruct((1, 96, 256), f32), jax.ShapeDtypeStruct((96, 640), f32),
            jax.ShapeDtypeStruct((24, 128), f32),
        ),
        in_specs=[inside] * len(near) + [anywhere] * len(far),
        out_specs=(inside,) * 5,
        scratch_shapes=summing_scratch(2) + summing_scratch(1, 256) + [
            pltpu.VMEM(shape, kind) for shape, kind in scratch
        ] + [
            pltpu.SemaphoreType.DMA((number,)),
            pltpu.SemaphoreType.DMA((number,)),
            pltpu.SemaphoreType.DMA((4,)),
        ],
        compiler_params=pltpu.CompilerParams(
            collective_id=3, has_side_effects=True, vmem_limit_bytes=60 << 20
        ),
        name="self_back_sum",
    )(*near, *far)


def place_kernel(
    y, dx, total, total_o, total_q, total_ff, small,
    y_out, dx_out, query, key, value, mixer, xkey, xvalue, xquery, xmixer, wide, tall, *more,
):
    vectors, wide_bias = more[:13], more[13]
    core = lax.rem(lax.axis_index("seq"), NC)
    y_out[...] = y[...]
    dx_out[...] = dx[...]

    def put(out, even, odd):
        @pl.when(core == 0)
        def _():
            out[...] = jnp.concatenate(even, axis=1)

        @pl.when(core != 0)
        def _():
            out[...] = jnp.concatenate(odd, axis=1)

    heads = total_q[...]
    for out, pair, even, odd in ((query, 0, 384, 448), (key, 128, 448, 384), (value, 256, 512, 576)):
        whole = heads[:, pair:pair + 128]
        put(out, [whole, heads[:, even:even + 64]], [heads[:, odd:odd + 64], whole])
    piece = total_o[0]
    put(mixer, [piece[:, :192]], [piece[:, 192:], piece[:, :128]])
    for number, (first, second) in enumerate(((xkey, xvalue), (xquery, xmixer))):
        piece = total[number]
        put(first, [piece[:, :192]], [piece[:, 192:256], piece[:, :128]])
        put(second, [piece[:, 256:], piece[:, 192:256]], [piece[:, 128:192], piece[:, 256:]])
    wide[:, :384] = total_ff[0]
    wide[:, 384:] = total_ff[1]
    tall[:96] = total_ff[2]
    tall[96:] = total_ff[3]
    for number, out in enumerate(vectors):
        out[...] = small[number:number + 1, 0:96]
    for number in range(3):
        wide_bias[:, number * 128:(number + 1) * 128] = small[16 + number:17 + number]


def run_place(y, dx, *totals):
    f32 = jnp.float32
    inside = pl.BlockSpec(memory_space=pltpu.VMEM)
    like = jax.ShapeDtypeStruct(y.shape, y.dtype)
    return pl.pallas_call(
        place_kernel,
        out_shape=(like, like) + (jax.ShapeDtypeStruct((96, 192), f32),) * 8 + (
            jax.ShapeDtypeStruct((96, 768), f32), jax.ShapeDtypeStruct((192, 384), f32),
        ) + (jax.ShapeDtypeStruct((1, 96), f32),) * 13 + (jax.ShapeDtypeStruct((1, 384), f32),),
        in_specs=[inside] * 7,
        out_specs=(inside,) * 26,
        compiler_params=pltpu.CompilerParams(vmem_limit_bytes=60 << 20),
        name="place",
    )(y, dx, *totals)


def on_device_fast(*arguments):
    (
        tokens, encoder_states, lengths, frame_counts, corpus_ids, corpus_weights, cotangent,
        first_gain, first_bias, query_weight, query_bias, key_weight, value_weight, value_bias,
        output_weight, output_bias, second_gain, second_bias, cross_query_weight, cross_query_bias,
        cross_key_weight, cross_value_weight, cross_value_bias, cross_output_weight, cross_output_bias,
        third_gain, third_bias, expand_weight, expand_bias, reduce_weight, reduce_bias,
    ) = arguments
    bf16, f32 = jnp.bfloat16, jnp.float32
    small_vectors = (
        first_gain, first_bias, query_bias, value_bias, output_bias, second_gain, second_bias,
        cross_query_bias, cross_value_bias, cross_output_bias, third_gain, third_bias, reduce_bias, expand_bias,
    )
    matrices = (
        query_weight, key_weight, value_weight, output_weight, cross_key_weight, cross_value_weight,
        cross_query_weight, cross_output_weight, expand_weight, reduce_weight.T,
    )
    (
        heads_all, mixer_all, pairs_all, wide_all, tall_all, frames_all, vec, wide_bias,
        a_all, head_rows, third, o, h1, c, p_self, ck, cv, cq, o2, h2, m, p_cross,
    ) = run_forward(
        lengths, frame_counts, matrices, jnp.stack(small_vectors[:13]), expand_bias.reshape(3, 128), encoder_states, tokens
    )
    layer_output, dh1, total_ff, acc_kv, acc_xqo, small_before, wide_small = run_feed(
        lengths, corpus_ids, corpus_weights,
        [cotangent, vec, wide_bias, h2, m, o2, c, h1, cq],
        [wide_all, tall_all, pairs_all, frames_all, ck, cv, p_cross],
    )
    tokens_gradient, total, total_o, total_q, small_total = run_last(
        [tokens, dh1, a_all, head_rows, third, o, p_self, vec, small_before, wide_small],
        [heads_all, mixer_all, acc_kv, acc_xqo],
    )
    (
        layer_output, tokens_gradient, m_query, m_key, m_value, m_mixer, m_xkey, m_xvalue, m_xquery, m_xmixer,
        expand_grad, reduce_grad, *smaller,
    ) = run_place(layer_output, tokens_gradient, total, total_o, total_q, total_ff, small_total)
    reduce_grad = reduce_grad.T
    smaller = [row.reshape(-1) for row in smaller]
    expand_bias_grad = smaller[13]
    return (
        layer_output, tokens_gradient, smaller[0], smaller[1], m_query, smaller[2], m_key, m_value, smaller[3],
        m_mixer, smaller[4], smaller[5], smaller[6], m_xquery, smaller[7], m_xkey, m_xvalue, smaller[8],
        m_xmixer, smaller[9], smaller[10], smaller[11], expand_grad, expand_bias_grad, reduce_grad, smaller[12],
    )


def solution(mesh):
    placed = (
        P("grp", "seq", None),
        P("grp", "seq", None),
        P("grp"),
        P("grp"),
        P("grp"),
        P(),
        P("grp", "seq", None),
        P("grp"),
        P("grp"),
        P("grp", "seq"),
        P("grp"),
        P("grp", "seq"),
        P("grp", "seq"),
        P("grp"),
        P("grp", "seq"),
        P("grp"),
        P("grp"),
        P("grp"),
        P("grp", "seq"),
        P("grp"),
        P("grp", "seq"),
        P("grp", "seq"),
        P("grp"),
        P("grp", "seq"),
        P("grp"),
        P("grp"),
        P("grp"),
        P("grp", "seq"),
        P("grp"),
        P("grp", "seq"),
        P("grp"),
    )
    small_slice = mesh.shape["grp"] == NZ * NX and mesh.shape["seq"] == NY * NC
    return jax.shard_map(
        on_device_fast if small_slice else on_device_plain,
        mesh=mesh,
        in_specs=placed,
        out_specs=(
            P("grp", "seq", None),
            P("grp", "seq", None),
            P("grp"),
            P("grp"),
            P("grp", "seq"),
            P("grp"),
            P("grp", "seq"),
            P("grp", "seq"),
            P("grp"),
            P("grp", "seq"),
            P("grp"),
            P("grp"),
            P("grp"),
            P("grp", "seq"),
            P("grp"),
            P("grp", "seq"),
            P("grp", "seq"),
            P("grp"),
            P("grp", "seq"),
            P("grp"),
            P("grp"),
            P("grp"),
            P("grp", "seq"),
            P("grp"),
            P("grp", "seq"),
            P("grp"),
        ),
        check_vma=False,
    )
```

```python
import math

import jax
import jax.numpy as jnp
from jax import lax
from jax.experimental import pallas as pl
from jax.experimental.pallas import tpu as pltpu
from jax.sharding import PartitionSpec as P

HEADS = 12
HEAD_DIM = 64


NEG = -1e30
EPS = 1e-05


def norm_rows(values, scaling, offset):
    centre = values - jnp.mean(values, axis=-1, keepdims=True)
    spread = jnp.mean(centre * centre, axis=-1, keepdims=True)
    return centre * lax.rsqrt(spread + EPS) * scaling + offset


def smooth_gate(values):
    return 0.5 * values * (1.0 + lax.erf(values * 0.7071067811865476))


def linear(inputs, weight):
    return jnp.einsum("bri,ij->brj", inputs, weight, preferred_element_type=jnp.float32)


def linear_back(gradient, weight):
    return jnp.einsum("brj,ij->bri", gradient, weight, preferred_element_type=jnp.float32)


def outer_sum(inputs, gradient):
    return jnp.einsum("bri,brj->ij", inputs, gradient, preferred_element_type=jnp.float32)


def row_total(gradient):
    return jnp.sum(gradient.astype(jnp.float32), axis=(0, 1))


def split_heads(values):
    return values.reshape(values.shape[0], values.shape[1], HEADS, HEAD_DIM)


def scores_of(query, key_rows, allowed):
    scores = jnp.einsum(
        "bqhd,bkhd->bhqk",
        split_heads(query),
        split_heads(key_rows),
        preferred_element_type=jnp.float32,
    )
    return jnp.where(allowed[:, None], scores, NEG)


def attend(query, key_rows, values, allowed):
    scores = scores_of(query, key_rows, allowed)
    maximum = jnp.max(scores, axis=-1, keepdims=True)
    raised = jnp.exp(scores - maximum)
    summed = jnp.sum(raised, axis=-1, keepdims=True)
    chances = (raised / summed).astype(jnp.bfloat16)
    blended = jnp.einsum(
        "bhqk,bkhd->bqhd", chances, split_heads(values), preferred_element_type=jnp.float32
    )
    return (blended.reshape(query.shape).astype(jnp.bfloat16), maximum + jnp.log(summed))


def attend_back(grad_low, query, key_rows, values, allowed, logsum):
    scores = scores_of(query, key_rows, allowed)
    chances = jnp.exp(scores - logsum)
    grad_heads = split_heads(grad_low)
    grad_chance = jnp.einsum(
        "bqhd,bkhd->bhqk", grad_heads, split_heads(values), preferred_element_type=jnp.float32
    )
    offset = jnp.sum(chances * grad_chance, axis=-1, keepdims=True)
    grad_score = (chances * (grad_chance - offset)).astype(jnp.bfloat16)
    grad_query = jnp.einsum(
        "bhqk,bkhd->bqhd", grad_score, split_heads(key_rows), preferred_element_type=jnp.float32
    )
    grad_keys = jnp.einsum(
        "bhqk,bqhd->bkhd", grad_score, split_heads(query), preferred_element_type=jnp.float32
    )
    grad_values = jnp.einsum(
        "bhqk,bqhd->bkhd",
        chances.astype(jnp.bfloat16),
        grad_heads,
        preferred_element_type=jnp.float32,
    )
    return (
        grad_query.reshape(query.shape),
        grad_keys.reshape(key_rows.shape),
        grad_values.reshape(values.shape),
    )


def on_device_plain(
    tokens,
    encoder_states,
    lengths,
    frame_counts,
    corpus_ids,
    corpus_weights,
    cotangent,
    first_gain,
    first_bias,
    query_weight,
    query_bias,
    key_weight,
    value_weight,
    value_bias,
    output_weight,
    output_bias,
    second_gain,
    second_bias,
    cross_query_weight,
    cross_query_bias,
    cross_key_weight,
    cross_value_weight,
    cross_value_bias,
    cross_output_weight,
    cross_output_bias,
    third_gain,
    third_bias,
    expand_weight,
    expand_bias,
    reduce_weight,
    reduce_bias,
):
    row_parts = (
        lax.all_gather(query_weight, "grp", axis=0, tiled=True),
        lax.all_gather(key_weight, "grp", axis=0, tiled=True),
        lax.all_gather(value_weight, "grp", axis=0, tiled=True),
        lax.all_gather(output_weight, "grp", axis=0, tiled=True),
        lax.all_gather(cross_query_weight, "grp", axis=0, tiled=True),
        lax.all_gather(cross_key_weight, "grp", axis=0, tiled=True),
        lax.all_gather(cross_value_weight, "grp", axis=0, tiled=True),
        lax.all_gather(cross_output_weight, "grp", axis=0, tiled=True),
        lax.all_gather(expand_weight, "grp", axis=0, tiled=True),
        lax.all_gather(reduce_weight, "grp", axis=0, tiled=True),
        lax.all_gather(first_gain, "grp", axis=0, tiled=True),
        lax.all_gather(first_bias, "grp", axis=0, tiled=True),
        lax.all_gather(query_bias, "grp", axis=0, tiled=True),
        lax.all_gather(value_bias, "grp", axis=0, tiled=True),
        lax.all_gather(output_bias, "grp", axis=0, tiled=True),
        lax.all_gather(second_gain, "grp", axis=0, tiled=True),
        lax.all_gather(second_bias, "grp", axis=0, tiled=True),
        lax.all_gather(cross_query_bias, "grp", axis=0, tiled=True),
        lax.all_gather(cross_value_bias, "grp", axis=0, tiled=True),
        lax.all_gather(cross_output_bias, "grp", axis=0, tiled=True),
        lax.all_gather(third_gain, "grp", axis=0, tiled=True),
        lax.all_gather(third_bias, "grp", axis=0, tiled=True),
        lax.all_gather(expand_bias, "grp", axis=0, tiled=True),
        lax.all_gather(reduce_bias, "grp", axis=0, tiled=True),
    )
    gathered = (
        lax.all_gather(row_parts[0], "seq", axis=1, tiled=True),
        lax.all_gather(row_parts[1], "seq", axis=1, tiled=True),
        lax.all_gather(row_parts[2], "seq", axis=1, tiled=True),
        lax.all_gather(row_parts[3], "seq", axis=1, tiled=True),
        lax.all_gather(row_parts[4], "seq", axis=1, tiled=True),
        lax.all_gather(row_parts[5], "seq", axis=1, tiled=True),
        lax.all_gather(row_parts[6], "seq", axis=1, tiled=True),
        lax.all_gather(row_parts[7], "seq", axis=1, tiled=True),
        lax.all_gather(row_parts[8], "seq", axis=1, tiled=True),
        lax.all_gather(row_parts[9], "seq", axis=1, tiled=True),
    )
    w_query, w_key, w_value, w_mixer, x_query, x_key, x_value, x_mixer, w_expand, w_reduce = (
        gathered
    )
    vectors = [piece.astype(jnp.float32) for piece in row_parts[10:]]
    factor = 1.0 / math.sqrt(HEAD_DIM)
    seq_count = lax.axis_size("seq")
    span_rows = tokens.shape[1]
    query_pos = lax.axis_index("seq") * span_rows + jnp.arange(span_rows, dtype=jnp.int32)
    key_pos = jnp.arange(span_rows * seq_count, dtype=jnp.int32)
    self_mask = (key_pos[None, None, :] <= query_pos[None, :, None]) & (
        key_pos[None, None, :] < lengths[:, None, None]
    )
    frame_pos = jnp.arange(encoder_states.shape[1] * seq_count, dtype=jnp.int32)
    cross_mask = frame_pos[None, None, :] < frame_counts[:, None, None]
    layer_in = tokens.astype(jnp.float32)
    normed_one, norm_back_one = jax.vjp(norm_rows, layer_in, vectors[0], vectors[1])
    normed_one = normed_one.astype(jnp.bfloat16)
    query_low = ((linear(normed_one, w_query) + vectors[2]) * factor).astype(jnp.bfloat16)
    key_low = linear(normed_one, w_key).astype(jnp.bfloat16)
    value_low = (linear(normed_one, w_value) + vectors[3]).astype(jnp.bfloat16)
    key_all, value_all = (
        lax.all_gather(key_low, "seq", axis=1, tiled=True),
        lax.all_gather(value_low, "seq", axis=1, tiled=True),
    )
    self_out, self_logsum = attend(query_low, key_all, value_all, self_mask)
    after_self = layer_in + linear(self_out, w_mixer) + vectors[4]
    normed_two, norm_back_two = jax.vjp(norm_rows, after_self, vectors[5], vectors[6])
    normed_two = normed_two.astype(jnp.bfloat16)
    cross_query = ((linear(normed_two, x_query) + vectors[7]) * factor).astype(jnp.bfloat16)
    frames_all = lax.all_gather(encoder_states, "seq", axis=1, tiled=True)
    cross_keys_all = linear(frames_all, x_key).astype(jnp.bfloat16)
    cross_values_all = (linear(frames_all, x_value) + vectors[8]).astype(jnp.bfloat16)
    cross_out, cross_logsum = attend(cross_query, cross_keys_all, cross_values_all, cross_mask)
    after_cross = after_self + linear(cross_out, x_mixer) + vectors[9]
    normed_three, norm_back_three = jax.vjp(norm_rows, after_cross, vectors[10], vectors[11])
    normed_three = normed_three.astype(jnp.bfloat16)
    hidden = linear(normed_three, w_expand) + vectors[12]
    gated, gate_back = jax.vjp(smooth_gate, hidden)
    gated_low = gated.astype(jnp.bfloat16)
    result = after_cross + linear(gated_low, w_reduce) + vectors[13]
    layer_output = result.astype(jnp.bfloat16)
    present = (query_pos[None, :] < lengths[:, None]).astype(jnp.float32)
    corpus_index = jnp.arange(corpus_weights.shape[0], dtype=jnp.int32)
    corpus_scale = jnp.sum(
        jnp.where(corpus_ids[:, None] == corpus_index[None, :], corpus_weights[None, :], 0.0),
        axis=1,
    )
    grad_out = cotangent.astype(jnp.float32) * (present * corpus_scale[:, None])[:, :, None]
    reduce_low = grad_out.astype(jnp.bfloat16)
    slope_reduce_bias = row_total(reduce_low)
    slope_reduce = outer_sum(gated_low, reduce_low)
    grad_hidden = gate_back(linear_back(reduce_low, w_reduce))[0]
    hidden_low = grad_hidden.astype(jnp.bfloat16)
    slope_expand_bias = row_total(hidden_low)
    slope_expand = outer_sum(normed_three, hidden_low)
    grad_norm_in, slope_gain_three, slope_bias_three = norm_back_three(
        linear_back(hidden_low, w_expand)
    )
    grad_cross = grad_out + grad_norm_in
    cross_low = grad_cross.astype(jnp.bfloat16)
    slope_xmixer_bias = row_total(cross_low)
    slope_xmixer = outer_sum(cross_out, cross_low)
    grad_heard = linear_back(cross_low, x_mixer).astype(jnp.bfloat16)
    grad_cq, part_ck, part_cv = attend_back(
        grad_heard, cross_query, cross_keys_all, cross_values_all, cross_mask, cross_logsum
    )
    slope_xkey = outer_sum(frames_all, part_ck)
    slope_xvalue = outer_sum(frames_all, part_cv)
    slope_xvalue_bias = row_total(part_cv)
    low_cq = (grad_cq * factor).astype(jnp.bfloat16)
    slope_xquery_bias = row_total(low_cq)
    slope_xquery = outer_sum(normed_two, low_cq)
    grad_norm_two, slope_gain_two, slope_bias_two = norm_back_two(linear_back(low_cq, x_query))
    grad_self = grad_cross + grad_norm_two
    self_low = grad_self.astype(jnp.bfloat16)
    slope_mixer_bias = row_total(self_low)
    slope_mixer = outer_sum(self_out, self_low)
    grad_mixed = linear_back(self_low, w_mixer).astype(jnp.bfloat16)
    grad_q, part_k, part_v = attend_back(
        grad_mixed, query_low, key_all, value_all, self_mask, self_logsum
    )
    summed_k, summed_v = (
        lax.psum_scatter(
            part_k.astype(jnp.bfloat16), "seq", scatter_dimension=1, tiled=True
        ).astype(jnp.float32),
        lax.psum_scatter(
            part_v.astype(jnp.bfloat16), "seq", scatter_dimension=1, tiled=True
        ).astype(jnp.float32),
    )
    low_k = summed_k.astype(jnp.bfloat16)
    low_v = summed_v.astype(jnp.bfloat16)
    low_q = (grad_q * factor).astype(jnp.bfloat16)
    slope_query = outer_sum(normed_one, low_q)
    slope_query_bias = row_total(low_q)
    slope_key = outer_sum(normed_one, low_k)
    slope_value = outer_sum(normed_one, low_v)
    slope_value_bias = row_total(low_v)
    grad_normed = (
        linear_back(low_q, w_query) + linear_back(low_k, w_key) + linear_back(low_v, w_value)
    )
    grad_norm_one, slope_gain_one, slope_bias_one = norm_back_one(grad_normed)
    tokens_gradient = (grad_self + grad_norm_one).astype(jnp.bfloat16)
    owned = (
        lax.psum_scatter(slope_query, "grp", scatter_dimension=0, tiled=True),
        lax.psum_scatter(slope_key, "grp", scatter_dimension=0, tiled=True),
        lax.psum_scatter(slope_value, "grp", scatter_dimension=0, tiled=True),
        lax.psum_scatter(slope_mixer, "grp", scatter_dimension=0, tiled=True),
        lax.psum_scatter(slope_xquery, "grp", scatter_dimension=0, tiled=True),
        lax.psum_scatter(slope_xkey, "grp", scatter_dimension=0, tiled=True),
        lax.psum_scatter(slope_xvalue, "grp", scatter_dimension=0, tiled=True),
        lax.psum_scatter(slope_xmixer, "grp", scatter_dimension=0, tiled=True),
        lax.psum_scatter(slope_expand, "grp", scatter_dimension=0, tiled=True),
        lax.psum_scatter(slope_reduce, "grp", scatter_dimension=0, tiled=True),
        lax.psum_scatter(slope_gain_one, "grp", scatter_dimension=0, tiled=True),
        lax.psum_scatter(slope_bias_one, "grp", scatter_dimension=0, tiled=True),
        lax.psum_scatter(slope_query_bias, "grp", scatter_dimension=0, tiled=True),
        lax.psum_scatter(slope_value_bias, "grp", scatter_dimension=0, tiled=True),
        lax.psum_scatter(slope_mixer_bias, "grp", scatter_dimension=0, tiled=True),
        lax.psum_scatter(slope_gain_two, "grp", scatter_dimension=0, tiled=True),
        lax.psum_scatter(slope_bias_two, "grp", scatter_dimension=0, tiled=True),
        lax.psum_scatter(slope_xquery_bias, "grp", scatter_dimension=0, tiled=True),
        lax.psum_scatter(slope_xvalue_bias, "grp", scatter_dimension=0, tiled=True),
        lax.psum_scatter(slope_xmixer_bias, "grp", scatter_dimension=0, tiled=True),
        lax.psum_scatter(slope_gain_three, "grp", scatter_dimension=0, tiled=True),
        lax.psum_scatter(slope_bias_three, "grp", scatter_dimension=0, tiled=True),
        lax.psum_scatter(slope_expand_bias, "grp", scatter_dimension=0, tiled=True),
        lax.psum_scatter(slope_reduce_bias, "grp", scatter_dimension=0, tiled=True),
    )
    matrices = (
        lax.psum_scatter(
            owned[0].astype(jnp.bfloat16), "seq", scatter_dimension=1, tiled=True
        ).astype(jnp.float32),
        lax.psum_scatter(
            owned[1].astype(jnp.bfloat16), "seq", scatter_dimension=1, tiled=True
        ).astype(jnp.float32),
        lax.psum_scatter(
            owned[2].astype(jnp.bfloat16), "seq", scatter_dimension=1, tiled=True
        ).astype(jnp.float32),
        lax.psum_scatter(
            owned[3].astype(jnp.bfloat16), "seq", scatter_dimension=1, tiled=True
        ).astype(jnp.float32),
        lax.psum_scatter(
            owned[4].astype(jnp.bfloat16), "seq", scatter_dimension=1, tiled=True
        ).astype(jnp.float32),
        lax.psum_scatter(
            owned[5].astype(jnp.bfloat16), "seq", scatter_dimension=1, tiled=True
        ).astype(jnp.float32),
        lax.psum_scatter(
            owned[6].astype(jnp.bfloat16), "seq", scatter_dimension=1, tiled=True
        ).astype(jnp.float32),
        lax.psum_scatter(
            owned[7].astype(jnp.bfloat16), "seq", scatter_dimension=1, tiled=True
        ).astype(jnp.float32),
        lax.psum_scatter(
            owned[8].astype(jnp.bfloat16), "seq", scatter_dimension=1, tiled=True
        ).astype(jnp.float32),
        lax.psum_scatter(
            owned[9].astype(jnp.bfloat16), "seq", scatter_dimension=1, tiled=True
        ).astype(jnp.float32),
    )
    smaller = lax.psum(
        (
            owned[10],
            owned[11],
            owned[12],
            owned[13],
            owned[14],
            owned[15],
            owned[16],
            owned[17],
            owned[18],
            owned[19],
            owned[20],
            owned[21],
            owned[22],
            owned[23],
        ),
        "seq",
    )
    return (
        layer_output,
        tokens_gradient,
        smaller[0],
        smaller[1],
        matrices[0],
        smaller[2],
        matrices[1],
        matrices[2],
        smaller[3],
        matrices[3],
        smaller[4],
        smaller[5],
        smaller[6],
        matrices[4],
        smaller[7],
        matrices[5],
        matrices[6],
        smaller[8],
        matrices[7],
        smaller[9],
        smaller[10],
        smaller[11],
        matrices[8],
        smaller[12],
        matrices[9],
        smaller[13],
    )


MESH_ID = pl.DeviceIdType.MESH
NZ, NX, NY, NC = 4, 2, 2, 2
GROUPS = 8


def where_am_i():
    grp = lax.axis_index("grp")
    seq = lax.axis_index("seq")
    return grp // NX, lax.rem(grp, NX), seq // NC, lax.rem(seq, NC)


def device_at(z, x, y, c):
    return (z * NX + x, y * NC + c)


def lanes(start, size):
    return pl.ds(pl.multiple_of(start, 128), size)


def pieces_of(bank, group, y, c, x, z_from, z_to):
    heads, mixer, pairs, wide, tall = bank
    column = pl.ds(z_from, z_to - z_from)
    if group == 0:
        return [heads.at[column, x]]
    if group == 1:
        return [mixer.at[y, column, x, :, lanes(c * 256, 256)]]
    if group < 4:
        return [pairs.at[group - 2, y, column, x, :, lanes(c * 384, 384)]]
    if group < 6:
        start = (y * NC + c) * 768 + (group - 4) * 384
        return [wide.at[column, x, :, lanes(start, 384)]]
    return [
        tall.at[y, c, pl.ds((group - 6) * 96, 96), lanes((z * NX + x) * 384, 384)]
        for z in range(z_from, z_to)
    ]


def piece_at(bank, group, y, c, x, z):
    heads, mixer, pairs, wide, tall = bank
    if group == 0:
        return heads.at[z, x]
    if group == 1:
        return mixer.at[y, z, x, :, lanes(c * 256, 256)]
    if group < 4:
        return pairs.at[group - 2, y, z, x, :, lanes(c * 384, 384)]
    if group < 6:
        return wide.at[z, x, :, lanes((y * NC + c) * 768 + (group - 4) * 384, 384)]
    return tall.at[y, c, pl.ds((group - 6) * 96, 96), lanes((z * NX + x) * 384, 384)]


def own_piece(own, group):
    heads, mixer, pairs, wide, tall = own
    if group == 0:
        return heads
    if group == 1:
        return mixer
    if group < 4:
        return pairs.at[group - 2]
    if group < 6:
        return wide.at[:, pl.ds((group - 4) * 384, 384)]
    return tall.at[pl.ds((group - 6) * 96, 96), :]


class Mail:
    def __init__(self, send_sems, recv_sems):
        self.send_sems, self.recv_sems, self.count, self.sent = send_sems, recv_sems, 0, []

    def slots(self, number):
        first = self.count
        self.count += number
        return list(range(first, first + number))

    def post(self, source, target, slot, device):
        copy = pltpu.make_async_remote_copy(
            src_ref=source,
            dst_ref=target,
            send_sem=self.send_sems.at[slot],
            recv_sem=self.recv_sems.at[slot],
            device_id=device,
            device_id_type=MESH_ID,
        )
        copy.start()
        self.sent.append(copy)

    def arrive(self, target, slot, device):
        pltpu.make_async_remote_copy(
            src_ref=target,
            dst_ref=target,
            send_sem=self.send_sems.at[slot],
            recv_sem=self.recv_sems.at[slot],
            device_id=device,
            device_id_type=MESH_ID,
        ).wait_recv()

    def finish(self):
        for copy in self.sent:
            copy.wait_send()


def greet(z, x, y, c):
    barrier = pltpu.get_barrier_semaphore()
    friends = [device_at(lax.rem(z + k, NZ), x, y, c) for k in range(1, NZ)]
    friends += [device_at(lax.rem(z + k, NZ), 1 - x, y, c) for k in range(NZ)]
    friends += [device_at(z, x, 1 - y, c), device_at(z, x, y, 1 - c), device_at(z, x, 1 - y, 1 - c)]
    for friend in friends:
        pl.semaphore_signal(barrier, inc=1, device_id=friend, device_id_type=MESH_ID)
    pl.semaphore_wait(barrier, len(friends))


def parts_in(group, number):
    return number if group >= 6 else 1


def joined(first, second):
    return jnp.concatenate([first, second], axis=1)


def mixed(first, second, core):
    even = joined(joined(first[:, :128], joined(first[:, 128:], second[:, 128:])), second[:, :128])
    odd = joined(joined(first[:, 64:], joined(second[:, :64], first[:, :64])), second[:, 64:])
    return jnp.where(core == 0, even, odd).astype(jnp.bfloat16)


def packed_heads(query, key, value, core):
    nothing = jnp.zeros_like(value[:, :64])
    even = [query[:, :128], key[:, :128], value[:, :128], query[:, 128:], key[:, 128:], value[:, 128:], nothing]
    odd = [query[:, 64:], key[:, 64:], value[:, 64:], key[:, :64], query[:, :64], nothing, value[:, :64]]
    even, odd = jnp.concatenate(even, axis=1), jnp.concatenate(odd, axis=1)
    return jnp.where(core == 0, even, odd).astype(jnp.bfloat16)


def packed_mixer(mixer, core):
    nothing = jnp.zeros_like(mixer[:, :64])
    even = joined(mixer, nothing)
    odd = joined(mixer[:, 64:], joined(nothing, mixer[:, :64]))
    return jnp.where(core == 0, even, odd).astype(jnp.bfloat16)


def own_tiles(row, y, core):
    block = jnp.where(y == 0, row[:, :384], row[:, 384:])
    lane = lax.broadcasted_iota(jnp.int32, (1, 128), 1)
    mine = lax.shift_right_logical(lane, 6) == core
    return (
        jnp.where(core == 0, block[:, :128], block[:, 256:]),
        jnp.where(mine, block[:, 128:256], jnp.zeros((1, 128), jnp.float32)),
    )


def natural_row(pair, third, y, core):
    nothing = jnp.zeros_like(pair)
    first, last = jnp.where(core == 0, pair, nothing), jnp.where(core == 0, nothing, pair)
    block = jnp.concatenate([first, third, last], axis=1)
    empty = jnp.zeros_like(block)
    return jnp.concatenate([jnp.where(y == 0, block, empty), jnp.where(y == 0, empty, block)], axis=1)


ORDER = (0, 2, 1, 3, 4, 5, 6, 7)


def forward_kernel(
    frame_span, lengths, counts,
    query_in, key_in, value_in, mixer_in, xkey_in, xvalue_in, xquery_in, xmixer_in, wide_in, tall_in,
    vectors_in, wide_bias_in, frames_short, tokens_in,
    heads, mixer, pairs, wide, tall, frames, vec_out, wide_bias,
    a_to, rows_to, third_to, o_to, h1_to, c_to, p_self_to, ck_to, cv_to, cq_to, o2_to, h2_to, m_to, p_cross_to,
    tokens_got, small, heads_here, mixer_here, pairs_here, frames_here,
    a_all, head_rows, third, o, h1, c, p_self, ck, cv, cq, o2, h2, m, p_cross,
    o_send, o_got, scores, self_scores, self_bias, cross_bias, heads_in, mixer_in_v, pairs_in, frames_in, small_in,
    send_sems, recv_sems, local_sems, load_sems, save_sems,
):
    z, x, y, c_own = where_am_i()
    heads_in[...] = packed_heads(*[ref[...].astype(jnp.float32) for ref in (query_in, key_in, value_in)], c_own)
    mixer_in_v[...] = packed_mixer(mixer_in[...].astype(jnp.float32), c_own)
    for number, (first, second) in enumerate(((xkey_in, xvalue_in), (xquery_in, xmixer_in))):
        pairs_in[number] = mixed(first[...].astype(jnp.float32), second[...].astype(jnp.float32), c_own)
    small_in[...] = jnp.zeros((32, 128), jnp.bfloat16)
    small_in[0:13, 0:96] = vectors_in[...]
    small_in[16:19, :] = wide_bias_in[...]
    frames_in[:, 368:384] = jnp.zeros((2, 16, 768), jnp.bfloat16)
    frames_in[:, 0:frame_span] = frames_short[...]
    greet(z, x, y, c_own)
    mail = Mail(send_sems, recv_sems)
    own = (heads_in, mixer_in_v, pairs_in, wide_in, tall_in)
    bank = (heads, mixer, pairs, wide, tall)
    far_mate = device_at(z, x, 1 - y, 1 - c_own)
    x_mate, y_mate = device_at(z, 1 - x, y, c_own), device_at(z, x, 1 - y, c_own)
    c_mate = device_at(z, x, y, 1 - c_own)
    z_mates = [device_at(lax.rem(z + n, NZ), x, y, c_own) for n in range(1, NZ)]
    grp = z * NX + x
    seq = y * NC + c_own

    local = []

    def keep(source, target):
        copy = pltpu.make_async_copy(source, target, local_sems.at[len(local)])
        copy.start()
        local.append(copy)

    small_slots = mail.slots(2 * NZ - 1)
    small_to = z_mates + [device_at(lax.rem(z + n, NZ), 1 - x, y, c_own) for n in range(NZ)]
    token_slots = mail.slots(3)
    frame_slots = mail.slots(3)
    z_slots = [mail.slots(NZ - 1) for _ in range(GROUPS)]
    x_slots = [mail.slots(parts_in(g, 4)) for g in range(GROUPS)]
    y_slots = [mail.slots(parts_in(g, 4)) for g in range(GROUPS)]
    dy_slots = [mail.slots(parts_in(g, VIA_X)) for g in range(GROUPS)]
    dx_slots = [mail.slots(parts_in(g, 4 - VIA_X)) for g in range(GROUPS)]
    co_slots = [mail.slots(parts_in(g, 4)) for g in range(GROUPS)]
    cx_slots = [mail.slots(parts_in(g, 4)) for g in range(GROUPS)]
    cy_slots = [mail.slots(parts_in(g, 4)) for g in range(GROUPS)]
    cdy_slots = [mail.slots(parts_in(g, VIA_X)) for g in range(GROUPS)]
    cdx_slots = [mail.slots(parts_in(g, 4 - VIA_X)) for g in range(GROUPS)]

    def to_column(group):
        for n in range(1, NZ):
            mail.post(
                own_piece(own, group), piece_at(bank, group, y, c_own, x, z), z_slots[group][n - 1], z_mates[n - 1]
            )

    def post_all(group, slots, device, yy, cc, xx, z_from, z_to):
        for slot, ref in zip(slots, pieces_of(bank, group, yy, cc, xx, z_from, z_to)):
            mail.post(ref, ref, slot, device)

    def arrive_all(group, slots, device, yy, cc, xx, z_from, z_to):
        for slot, ref in zip(slots, pieces_of(bank, group, yy, cc, xx, z_from, z_to)):
            mail.arrive(ref, slot, device)

    def spread(group):
        for n in range(1, NZ):
            zz = lax.rem(z + NZ - n, NZ)
            mail.arrive(piece_at(bank, group, y, c_own, x, zz), z_slots[group][n - 1], z_mates[n - 1])
        local[group].wait()
        post_all(group, x_slots[group], x_mate, y, c_own, x, 0, 4)
        if group == 0:
            return
        post_all(group, y_slots[group], y_mate, y, c_own, x, 0, 4)
        post_all(group, co_slots[group], c_mate, y, c_own, x, 0, 4)

    def turn(group):
        if group == 0:
            arrive_all(group, x_slots[group], x_mate, y, c_own, 1 - x, 0, 4)
            return
        arrive_all(group, y_slots[group], y_mate, 1 - y, c_own, x, 0, 4)
        post_all(group, dx_slots[group], x_mate, 1 - y, c_own, x, VIA_X, 4)
        post_all(group, cy_slots[group], c_mate, 1 - y, c_own, x, 0, 4)
        arrive_all(group, x_slots[group], x_mate, y, c_own, 1 - x, 0, 4)
        post_all(group, dy_slots[group], y_mate, y, c_own, 1 - x, 0, VIA_X)
        post_all(group, cx_slots[group], c_mate, y, c_own, 1 - x, 0, 4)

    def share(group):
        if group == 0:
            return
        arrive_all(group, dy_slots[group], y_mate, 1 - y, c_own, 1 - x, 0, VIA_X)
        post_all(group, cdy_slots[group], c_mate, 1 - y, c_own, 1 - x, 0, VIA_X)
        arrive_all(group, dx_slots[group], x_mate, 1 - y, c_own, 1 - x, VIA_X, 4)
        post_all(group, cdx_slots[group], c_mate, 1 - y, c_own, 1 - x, VIA_X, 4)

    def complete(group):
        arrive_all(group, co_slots[group], c_mate, y, 1 - c_own, x, 0, 4)
        arrive_all(group, cx_slots[group], c_mate, y, 1 - c_own, 1 - x, 0, 4)
        arrive_all(group, cy_slots[group], c_mate, 1 - y, 1 - c_own, x, 0, 4)
        arrive_all(group, cdy_slots[group], c_mate, 1 - y, 1 - c_own, 1 - x, 0, VIA_X)
        arrive_all(group, cdx_slots[group], c_mate, 1 - y, 1 - c_own, 1 - x, VIA_X, 4)

    def frame_rows(number):
        return frames.at[:, number]

    loads = []

    def load(source, target):
        copy = pltpu.make_async_copy(source, target, load_sems.at[len(loads)])
        copy.start()
        loads.append(copy)
        return copy

    def load_pair(group):
        complete(group)
        return load(pairs.at[group - 2], pairs_here.at[group - 2])

    saves = []

    def save(source, target):
        copy = pltpu.make_async_copy(source, target, save_sems.at[len(saves)])
        copy.start()
        saves.append(copy)

    for group in range(GROUPS):
        keep(own_piece(own, group), piece_at(bank, group, y, c_own, x, z))
    keep(small_in, small.at[grp])
    keep(frames_in, frame_rows(seq))
    keep(tokens_in, tokens_got.at[seq])
    to_column(ORDER[0])
    for slot, device in zip(small_slots, small_to):
        mail.post(small_in, small.at[grp], slot, device)
    to_column(ORDER[1])
    mail.post(frames_in, frame_rows(seq), frame_slots[0], y_mate)
    mail.post(frames_in, frame_rows(seq), frame_slots[1], c_mate)
    mail.post(tokens_in, tokens_got.at[seq], token_slots[0], y_mate)
    mail.post(tokens_in, tokens_got.at[seq], token_slots[1], c_mate)
    to_column(ORDER[2])

    pending = []
    for step in range(GROUPS + 2):
        if step + 3 < GROUPS:
            pending.append((to_column, ORDER[step + 3]))
        if step < GROUPS:
            pending.append((spread, ORDER[step]))
        if 0 <= step - 1 < GROUPS:
            pending.append((turn, ORDER[step - 1]))
        if 0 <= step - 2 < GROUPS:
            pending.append((share, ORDER[step - 2]))

    def tick(number=1):
        while number > 0 and pending:
            action, group = pending.pop(0)
            action(group)
            if action is not to_column:
                number -= 1

    def until(action, group):
        while (action, group) in pending:
            tick()

    for n in range(1, NZ):
        zz = lax.rem(z + NZ - n, NZ)
        mail.arrive(small.at[zz * NX + x], small_slots[n - 1], z_mates[n - 1])
    for n in range(NZ):
        zz = lax.rem(z + NZ - n, NZ)
        mail.arrive(small.at[zz * NX + 1 - x], small_slots[NZ - 1 + n], x_mate)
    local[GROUPS].wait()
    vec_out[...] = jnp.concatenate([small[g, 0:16, 0:96].astype(jnp.float32) for g in range(8)], axis=1)
    for g in range(8):
        three = small[g, 16:24, :].astype(jnp.float32)
        for n in range(3):
            at = g * 384 + n * 128
            wide_bias[:, at:at + 128] = three[n:n + 1]

    o_slots = mail.slots(6)
    until(turn, 0)
    other = (1 - y) * NC + c_own
    mail.arrive(tokens_got.at[other], token_slots[0], y_mate)
    mail.post(tokens_got.at[other], tokens_got.at[other], token_slots[2], c_mate)
    heads_loaded = load(heads, heads_here)
    mail.arrive(frame_rows(other), frame_slots[0], y_mate)
    mail.post(frame_rows(other), frame_rows(other), frame_slots[2], c_mate)
    mail.arrive(tokens_got.at[y * NC + 1 - c_own], token_slots[1], c_mate)
    mail.arrive(tokens_got.at[(1 - y) * NC + 1 - c_own], token_slots[2], c_mate)
    for copy in local[GROUPS + 1:]:
        copy.wait()
    heads_loaded.wait()
    phase = self_forward(lengths, tokens_got, vec_out, heads_here, a_all, head_rows, third, p_self, o_send, self_scores, self_bias)
    mates = ((c_mate, y * NC + 1 - c_own), (y_mate, other), (far_mate, (1 - y) * NC + 1 - c_own))
    for number, t in enumerate(phase):
        if t is not None:
            for place, (mate, mate_seq) in enumerate(mates):
                mail.post(o_send.at[mate_seq, t], o_got.at[seq, t], o_slots[3 * t + place], mate)
            o_got[seq, t] = o_send[seq, t]
        if number % 2 == 1:
            tick()
    mail.arrive(frame_rows(y * NC + 1 - c_own), frame_slots[1], c_mate)
    mail.arrive(frame_rows((1 - y) * NC + 1 - c_own), frame_slots[2], c_mate)
    frames_loaded = load(frames, frames_here)
    for source, target in ((a_all, a_to), (head_rows, rows_to), (third, third_to), (p_self, p_self_to)):
        save(source, target)
    until(share, 2)
    kv_loaded = load_pair(2)
    frames_loaded.wait()
    kv_loaded.wait()
    for number, _ in enumerate(cross_keys(frames_here, vec_out, pairs_here.at[0], ck, cv)):
        if number % 2 == 1:
            tick()
    save(ck, ck_to)
    save(cv, cv_to)
    until(share, 1)
    complete(1)
    mixer_loaded = load(mixer, mixer_here)
    for t in range(2):
        for place, (mate, mate_seq) in enumerate(mates):
            mail.arrive(o_got.at[mate_seq, t], o_slots[3 * t + place], mate)
    mixer_loaded.wait()
    self_out(tokens_got, vec_out, mixer_here, o_got, o, h1, c)
    until(share, 3)
    third_loaded = load_pair(3)
    for source, target in ((o, o_to), (h1, h1_to), (c, c_to)):
        save(source, target)
    third_loaded.wait()
    phase = cross_forward(
        counts, frame_span, c, vec_out, pairs_here.at[1], ck, cv, h1, cq, o2, h2, m, p_cross, scores, cross_bias
    )
    for number, _ in enumerate(phase):
        if 1 <= number <= 12:
            t, pair = (number - 1) // 6, (number - 1) % 6
            save(p_cross.at[t, pair], p_cross_to.at[t, pair])
        if number % 2 == 1:
            tick()
    for source, target in ((cq, cq_to), (o2, o2_to), (h2, h2_to), (m, m_to)):
        save(source, target)
    tick(100)
    for group in (4, 5, 6, 7):
        complete(group)
    for copy in saves:
        copy.wait()
    mail.finish()


VIA_X = 2


def slots_needed():
    return (2 * NZ - 1) + 12 + sum(
        3 + parts_in(g, 4) * 5 + 2 * (parts_in(g, VIA_X) + parts_in(g, 4 - VIA_X)) for g in range(GROUPS)
    )


def run_forward(lengths, counts, matrices, vectors, wide_bias, frames, tokens):
    bf16, f32 = jnp.bfloat16, jnp.float32
    number = slots_needed()
    span = tokens.shape[1]
    anywhere = pl.BlockSpec(memory_space=pl.ANY)
    inside = pl.BlockSpec(memory_space=pltpu.VMEM)
    scalar = pl.BlockSpec(memory_space=pltpu.SMEM)
    rows = (2, span, 768)
    kept = [
        ((2, 4, span, 768), bf16), ((2, 512, 640), bf16), ((2, 512, 128), bf16), (rows, bf16), (rows, f32),
        (rows, bf16), ((2, 4, 3 * span, 512), bf16), ((2, 6, 1536, 128), bf16), ((2, 6, 1536, 128), bf16), (rows, bf16),
        (rows, bf16), (rows, f32), (rows, bf16), ((2, 6, 2 * span, 1536), bf16),
    ]
    frame_span = frames.shape[1]
    frames_shape = (2, NY * NC, 384, 768)
    return pl.pallas_call(
        lambda *refs: forward_kernel(frame_span, *refs),
        out_shape=(
            jax.ShapeDtypeStruct((NZ, NX, 96, 640), bf16),
            jax.ShapeDtypeStruct((NY, NZ, NX, 96, 512), bf16),
            jax.ShapeDtypeStruct((2, NY, NZ, NX, 96, 768), bf16),
            jax.ShapeDtypeStruct((NZ, NX, 96, 3072), bf16),
            jax.ShapeDtypeStruct((NY, NC, 192, 3072), bf16),
            jax.ShapeDtypeStruct(frames_shape, bf16),
            jax.ShapeDtypeStruct((16, 768), f32),
            jax.ShapeDtypeStruct((1, 3072), f32),
        ) + tuple(jax.ShapeDtypeStruct(shape, kind) for shape, kind in kept),
        in_specs=[scalar] * 2 + [inside] * 14,
        out_specs=(anywhere,) * 6 + (inside,) * 2 + (anywhere,) * len(kept),
        scratch_shapes=[
            pltpu.VMEM((4,) + tokens.shape, bf16),
            pltpu.VMEM((8, 32, 128), bf16),
            pltpu.VMEM((NZ, NX, 96, 640), bf16),
            pltpu.VMEM((NY, NZ, NX, 96, 512), bf16),
            pltpu.VMEM((2, NY, NZ, NX, 96, 768), bf16),
            pltpu.VMEM(frames_shape, bf16),
        ] + [pltpu.VMEM(shape, kind) for shape, kind in kept] + [
            pltpu.VMEM((4, 2, span, 256), bf16),
            pltpu.VMEM((4, 2, span, 256), bf16),
            pltpu.VMEM((2 * span, 1536), f32),
            pltpu.VMEM((3 * span, 512), f32),
            pltpu.VMEM((2, 4 * span, 512), f32),
            pltpu.VMEM((2, 1, 1536), f32),
            pltpu.VMEM((96, 640), bf16),
            pltpu.VMEM((96, 256), bf16),
            pltpu.VMEM((2, 96, 384), bf16),
            pltpu.VMEM((2, 384, 768), bf16),
            pltpu.VMEM((32, 128), bf16),
            pltpu.SemaphoreType.DMA((number,)),
            pltpu.SemaphoreType.DMA((number,)),
            pltpu.SemaphoreType.DMA((GROUPS + 3,)),
            pltpu.SemaphoreType.DMA((5,)),
            pltpu.SemaphoreType.DMA((26,)),
        ],
        compiler_params=pltpu.CompilerParams(
            collective_id=1, has_side_effects=True, vmem_limit_bytes=60 << 20
        ),
        name="gather_forward",
    )(lengths, counts, *matrices, vectors, wide_bias, frames, tokens)


def mm(left, right):
    return lax.dot_general(left, right, (((1,), (0,)), ((), ())), preferred_element_type=jnp.float32)


def mm_back(left, right):
    return lax.dot_general(left, right, (((1,), (1,)), ((), ())), preferred_element_type=jnp.float32)


def mm_rows(left, right):
    return lax.dot_general(left, right, (((0,), (0,)), ((), ())), preferred_element_type=jnp.float32)


def low_lanes(rows):
    return lax.broadcasted_iota(jnp.int32, (rows, 128), 1) < 64


def turned(tile):
    return pltpu.roll(tile, 64, 1)


def tile_of(values, number):
    return values[:, number * 128:(number + 1) * 128]


def split_first(near, far):
    low = low_lanes(near.shape[0])
    return [tile_of(near, 0), jnp.where(low, tile_of(near, 1), tile_of(far, 1)), tile_of(far, 0)]


def split_second(near, far):
    low = low_lanes(near.shape[0])
    return [tile_of(near, 1), turned(jnp.where(low, tile_of(far, 0), tile_of(near, 0))), tile_of(far, 1)]


def join_first(values):
    low = low_lanes(values.shape[0])
    middle = tile_of(values, 1)
    nothing = jnp.zeros_like(middle)
    near = jnp.concatenate([tile_of(values, 0), jnp.where(low, middle, nothing)], axis=1)
    far = jnp.concatenate([tile_of(values, 2), jnp.where(low, nothing, middle)], axis=1)
    return near.astype(jnp.bfloat16), far.astype(jnp.bfloat16)


def join_second(values):
    low = low_lanes(values.shape[0])
    middle = turned(tile_of(values, 1))
    nothing = jnp.zeros_like(middle)
    near = jnp.concatenate([jnp.where(low, nothing, middle), tile_of(values, 0)], axis=1)
    far = jnp.concatenate([jnp.where(low, middle, nothing), tile_of(values, 2)], axis=1)
    return near.astype(jnp.bfloat16), far.astype(jnp.bfloat16)


def join_both(first, second):
    low = low_lanes(first.shape[0])
    mine, other = tile_of(first, 1), turned(tile_of(second, 1))
    return jnp.concatenate(
        [
            tile_of(first, 0), jnp.where(low, mine, other), tile_of(second, 0),
            tile_of(first, 2), jnp.where(low, other, mine), tile_of(second, 2),
        ],
        axis=1,
    ).astype(jnp.bfloat16)


def block_of(pair, y, at):
    if len(pair.shape) == 3:
        return pair[y, :, at]
    return pair[y, :, :, :, at].reshape(768, -1)


def times_first(values, pair):
    tiles = []
    for y in range(2):
        tiles += split_first(mm(values, block_of(pair, y, slice(0, 256))), mm(values, block_of(pair, y, slice(384, 640))))
    return tiles


def times_second(values, pair):
    tiles = []
    for y in range(2):
        tiles += split_second(mm(values, block_of(pair, y, slice(128, 384))), mm(values, block_of(pair, y, slice(512, 768))))
    return tiles


def back_first(grads, pair):
    out = None
    for y in range(2):
        near, far = join_first(grads[:, y * 384:(y + 1) * 384])
        part = mm_back(near, block_of(pair, y, slice(0, 256))) + mm_back(far, block_of(pair, y, slice(384, 640)))
        out = part if out is None else out + part
    return out


def back_second(grads, pair):
    out = None
    for y in range(2):
        near, far = join_second(grads[:, y * 384:(y + 1) * 384])
        part = mm_back(near, block_of(pair, y, slice(128, 384))) + mm_back(far, block_of(pair, y, slice(512, 768)))
        out = part if out is None else out + part
    return out


def normed(values, gain, bias):
    return norm_rows(values, gain, bias).astype(jnp.bfloat16)


def normed_back(values, gain, grads):
    centre = values - jnp.mean(values, axis=-1, keepdims=True)
    scale = lax.rsqrt(jnp.mean(centre * centre, axis=-1, keepdims=True) + EPS)
    unit = centre * scale
    inner = grads * gain
    back = scale * (
        inner - jnp.mean(inner, axis=-1, keepdims=True) - unit * jnp.mean(inner * unit, axis=-1, keepdims=True)
    )
    return back, jnp.sum(grads * unit, axis=0, keepdims=True), jnp.sum(grads, axis=0, keepdims=True)


def column_sum(values):
    return jnp.sum(values.astype(jnp.float32), axis=0, keepdims=True)


def both_heads(both):
    low = low_lanes(both.shape[0])
    nothing = jnp.zeros_like(both)
    return jnp.concatenate([jnp.where(low, both, nothing), jnp.where(low, nothing, both)], axis=0)


def stacked(values, t, pair):
    return both_heads(values[t, :, pair * 128:(pair + 1) * 128])


def third_head(tile, core):
    lane = lax.broadcasted_iota(jnp.int32, tile.shape, 1)
    return jnp.where(lax.shift_right_logical(lane, 6) == core, tile, jnp.zeros_like(tile))


def unstacked(values):
    half = values.shape[0] // 2
    return jnp.where(low_lanes(half), values[:half], values[half:])


CHUNK = 16


def soften(scores, bias, chances, rows, width):
    def one(number, carry):
        first = pl.multiple_of(number * CHUNK, CHUNK)
        values = scores[pl.ds(first, CHUNK), 0:width] + bias(first)
        raised = jnp.exp(values - jnp.max(values, axis=1, keepdims=True))
        share = raised * (1.0 / jnp.sum(raised, axis=1, keepdims=True))
        chances[pl.ds(first, CHUNK), 0:width] = share.astype(jnp.bfloat16)
        return carry

    lax.fori_loop(0, rows // CHUNK, one, 0, unroll=2 if rows // CHUNK % 2 == 0 else 3)


def soften_back(chances, slopes, grads, rows, width):
    def one(number, carry):
        first = pl.multiple_of(number * CHUNK, CHUNK)
        share = chances[pl.ds(first, CHUNK), 0:width].astype(jnp.float32)
        slope = slopes[pl.ds(first, CHUNK), 0:width]
        inner = jnp.sum(share * slope, axis=1, keepdims=True)
        grads[pl.ds(first, CHUNK), 0:width] = (share * (slope - inner)).astype(jnp.bfloat16)
        return carry

    lax.fori_loop(0, rows // CHUNK, one, 0, unroll=2 if rows // CHUNK % 2 == 0 else 3)


def self_forward(lengths, tokens, vec, heads, a_out, rows_out, third_out, p_out, o_out, scores, bias):
    span = tokens.shape[2]
    z, x, y, core = where_am_i()
    factor = 1.0 / math.sqrt(HEAD_DIM)
    for s in range(4):
        for t in range(2):
            a_out[t, s] = normed(tokens[s, t].astype(jnp.float32), vec[0:1], vec[1:2])
    yield None
    lane = lax.broadcasted_iota(jnp.int32, (1, 128), 1)
    mine = lax.shift_right_logical(lane, 6) == core
    nothing = jnp.zeros((1, 128), jnp.float32)
    query_pair, query_third = own_tiles(vec[2:3], y, core)
    value_pair, value_third = own_tiles(vec[3:4], y, core)
    offset = jnp.concatenate([query_pair, nothing, value_pair, query_third, value_third], axis=1)
    ones = nothing + 1.0
    scale = jnp.concatenate([ones * factor, ones, ones, jnp.where(mine, ones * factor, ones), ones], axis=1)
    for t in range(2):
        row = lax.broadcasted_iota(jnp.int32, (4 * span, 512), 0)
        place = lax.broadcasted_iota(jnp.int32, (4 * span, 512), 1)
        bias[t] = jnp.where((place <= row) & (place < lengths[t]), 0.0, NEG)
        product = mm(a_out[t].reshape(4 * span, 768), heads[...].reshape(768, 640))
        product = (product + offset) * scale
        rows_out[t, 0:4 * span] = product.astype(jnp.bfloat16)
        rows_out[t, 4 * span:512] = jnp.zeros((512 - 4 * span, 640), jnp.bfloat16)
        third_out[t, 0:4 * span] = turned(product[:, 384:512]).astype(jnp.bfloat16)
        third_out[t, 4 * span:512] = jnp.zeros((512 - 4 * span, 128), jnp.bfloat16)
        yield None
    for t in range(2):
        for block in range(4):
            rows, width = slice(block * span, (block + 1) * span), 128 * (block + 1)
            scores[0:2 * span, 0:width] = mm_back(
                both_heads(rows_out[t, rows, 0:128]), rows_out[t, 0:width, 128:256]
            )
            scores[2 * span:3 * span, 0:width] = mm_back(
                third_head(rows_out[t, rows, 384:512], core), third_out[t, 0:width]
            )
            chances = p_out.at[t, block]
            soften(
                scores, lambda first: bias[t, pl.ds(block * span + lax.rem(first, span), CHUNK), 0:width], chances,
                3 * span, width,
            )
            blended = mm(chances[0:2 * span, 0:width], rows_out[t, 0:width, 256:384])
            o_out[block, t, :, 0:128] = unstacked(blended).astype(jnp.bfloat16)
            blended = mm(chances[2 * span:3 * span, 0:width], rows_out[t, 0:width, 512:640])
            o_out[block, t, :, 128:256] = blended.astype(jnp.bfloat16)
            yield t if block == 3 else None


def self_out(tokens, vec, mixer, o_got, o_out, h1_out, c_out):
    span = tokens.shape[2]
    seq = lax.axis_index("seq")
    low = low_lanes(span)
    for t in range(2):
        for y in range(2):
            even, odd = o_got[2 * y, t], o_got[2 * y + 1, t]
            tiles = [even[:, 0:128], jnp.where(low, even[:, 128:256], odd[:, 128:256]), odd[:, 0:128]]
            for number, tile in enumerate(tiles):
                at = slice(y * 384 + number * 128, y * 384 + (number + 1) * 128)
                o_out[t, :, at] = tile
    rows = o_out[...].reshape(2 * span, 768)
    low = low_lanes(2 * span)
    for y in range(2):
        product = mm(rows, mixer[y].reshape(768, 512))
        tiles = [product[:, 0:128], jnp.where(low, product[:, 128:256], product[:, 384:512]), product[:, 256:384]]
        for number, tile in enumerate(tiles):
            at = slice(y * 384 + number * 128, y * 384 + (number + 1) * 128)
            for t in range(2):
                h1_out[t, :, at] = (
                    tokens[seq, t, :, at].astype(jnp.float32) + tile[t * span:(t + 1) * span] + vec[4:5, at]
                )
    for t in range(2):
        c_out[t] = normed(h1_out[t], vec[5:6], vec[6:7])


def cross_keys(frames, vec, kv, ck_out, cv_out):
    for t in range(2):
        for s in range(4):
            block = frames[t, s]
            rows = slice(s * 384, (s + 1) * 384)
            for y in range(2):
                product = mm(block, block_of(kv, y, slice(0, 768)))
                near, far = product[:, 0:384], product[:, 384:768]
                keys = split_first(near[:, 0:256], far[:, 0:256])
                values = split_second(near[:, 128:384], far[:, 128:384])
                for place in range(3):
                    at = slice(y * 384 + place * 128, y * 384 + (place + 1) * 128)
                    ck_out[t, y * 3 + place, rows] = keys[place].astype(jnp.bfloat16)
                    cv_out[t, y * 3 + place, rows] = (values[place] + vec[8:9, at]).astype(jnp.bfloat16)
            yield


def cross_forward(counts, frame_span, c, vec, xqo, ck, cv, h1, cq_out, o2_out, h2_out, m_out, p_out, scores, bias):
    span = c.shape[1]
    factor = 1.0 / math.sqrt(HEAD_DIM)
    rows = c[...].reshape(2 * span, 768)
    for number, tile in enumerate(times_first(rows, xqo)):
        at = slice(number * 128, (number + 1) * 128)
        tile = ((tile + vec[7:8, at]) * factor).astype(jnp.bfloat16)
        for t in range(2):
            cq_out[t, :, at] = tile[t * span:(t + 1) * span]
    for t in range(2):
        for s in range(4):
            inside = lax.broadcasted_iota(jnp.int32, (1, 384), 1)
            good = (inside < frame_span) & (s * frame_span + inside < counts[t])
            bias[t, :, s * 384:(s + 1) * 384] = jnp.where(good, 0.0, NEG)
    yield
    for t in range(2):
        for pair in range(6):
            at = slice(pair * 128, (pair + 1) * 128)
            scores[...] = mm_back(stacked(cq_out, t, pair), ck[t, pair])
            chances = p_out.at[t, pair]
            soften(scores, lambda first: bias[t], chances, 2 * span, 1536)
            o2_out[t, :, at] = unstacked(mm(chances[...], cv[t, pair])).astype(jnp.bfloat16)
            yield
    out = o2_out[...].reshape(2 * span, 768)
    for number, tile in enumerate(times_second(out, xqo)):
        at = slice(number * 128, (number + 1) * 128)
        for t in range(2):
            h2_out[t, :, at] = h1[t, :, at] + tile[t * span:(t + 1) * span] + vec[9:10, at]
    for t in range(2):
        m_out[t] = normed(h2_out[t], vec[10:11], vec[11:12])
    yield


class Summing:
    def __init__(self, mail, place, mates, acc, diag_x, diag_y, x_in, y_in, z_in, total):
        self.mail, self.place, self.mates = mail, place, mates
        self.acc, self.diag_x, self.diag_y = acc, diag_x, diag_y
        self.x_in, self.y_in, self.z_in, self.total = x_in, y_in, z_in, total
        self.slots = [mail.slots(4 + NZ - 1) for _ in range(acc.shape[0])]

    def begin(self, n):
        z, x, y = self.place
        x_mate, y_mate, _ = self.mates
        self.mail.post(self.acc.at[n, 1 - y, pl.ds(0, 2), 1 - x], self.diag_x.at[n], self.slots[n][0], x_mate)
        self.mail.post(self.acc.at[n, 1 - y, pl.ds(2, 2), 1 - x], self.diag_y.at[n], self.slots[n][1], y_mate)

    def side(self, n):
        z, x, y = self.place
        x_mate, y_mate, _ = self.mates
        self.mail.arrive(self.diag_x.at[n], self.slots[n][0], x_mate)
        for k in range(2):
            self.acc[n, 1 - y, k, x] = self.acc[n, 1 - y, k, x] + self.diag_x[n, k]
        self.mail.post(self.acc.at[n, 1 - y, :, x], self.y_in.at[n], self.slots[n][2], y_mate)
        self.mail.arrive(self.diag_y.at[n], self.slots[n][1], y_mate)
        for k in range(2):
            self.acc[n, y, 2 + k, 1 - x] = self.acc[n, y, 2 + k, 1 - x] + self.diag_y[n, k]
        self.mail.post(self.acc.at[n, y, :, 1 - x], self.x_in.at[n], self.slots[n][3], x_mate)

    def column(self, n):
        z, x, y = self.place
        x_mate, y_mate, z_mates = self.mates
        self.mail.arrive(self.y_in.at[n], self.slots[n][2], y_mate)
        self.mail.arrive(self.x_in.at[n], self.slots[n][3], x_mate)
        for k in range(NZ):
            self.acc[n, y, k, x] = (
                self.acc[n, y, k, x].astype(jnp.float32)
                + self.x_in[n, k].astype(jnp.float32)
                + self.y_in[n, k].astype(jnp.float32)
            ).astype(jnp.bfloat16)
        for k in range(1, NZ):
            zz = lax.rem(z + k, NZ)
            self.mail.post(self.acc.at[n, y, zz, x], self.z_in.at[n, k - 1], self.slots[n][3 + k], z_mates[k - 1])

    def last(self, n):
        z, x, y = self.place
        _, _, z_mates = self.mates
        for k in range(1, NZ):
            self.mail.arrive(self.z_in.at[n, k - 1], self.slots[n][3 + k], z_mates[k - 1])
        self.total[n] = self.acc[n, y, z, x].astype(jnp.float32) + (
            self.z_in[n, 0].astype(jnp.float32) + self.z_in[n, 1].astype(jnp.float32)
        ) + self.z_in[n, 2].astype(jnp.float32)


def summing_scratch(n, width=384):
    piece = (96, width)
    shapes = [
        (n, NY, NZ, NX) + piece, (n, 2) + piece, (n, 2) + piece, (n, NZ) + piece, (n, NZ) + piece, (n, NZ - 1) + piece
    ]
    return [pltpu.VMEM(shape, jnp.bfloat16) for shape in shapes]


class Loads:
    def __init__(self, sems):
        self.sems, self.count = sems, 0

    def start(self, source, target):
        copy = pltpu.make_async_copy(source, target, self.sems.at[self.count])
        copy.start()
        self.count += 1
        return copy


def two(first, second):
    return jnp.concatenate([first, second], axis=0)


def feed_kernel(
    lengths, ids, weights, cotangent, vec, wide_bias, h2, m, o2, c, h1, cq,
    wide_far, tall_far, pairs_far, frames_far, ck_far, cv_far, p_far,
    y_out, dh1_out, total, acc_kv, acc_xqo, small_out, wide_small,
    acc, diag_x, diag_y, x_in, y_in, z_in,
    wide, tall, xqo, frames, keys_here, values_here, p_here,
    m_sib, g_own, g_sib, du_own, du_send, du_sib, dz_own, dz_send, dz_sib,
    o2_sib, c_sib, xb_own, xb_send, xb_sib, xa_own, xa_send, xa_sib, gkv, kv_in,
    dy, dh2, do, dq, scores, dscores, gate_slope,
    send_sems, recv_sems, load_sems, unit_sems,
):
    z, x, y, core = where_am_i()
    span = m.shape[1]
    seq = y * NC + core
    factor = 1.0 / math.sqrt(HEAD_DIM)
    low = low_lanes(2 * span)
    x_mate, y_mate, c_mate = device_at(z, 1 - x, y, core), device_at(z, x, 1 - y, core), device_at(z, x, y, 1 - core)
    z_mates = [device_at(lax.rem(z + n, NZ), x, y, core) for n in range(1, NZ)]
    loads = Loads(load_sems)
    order = [(yy, side) for yy in range(2) for side in range(2)]
    block_loads = []
    for yy, side in order:
        at = lanes((2 * yy + (core if side == 0 else 1 - core)) * 768, 768)
        block_loads.append((
            loads.start(wide_far.at[:, :, :, at], wide.at[:, :, :, at]),
            loads.start(tall_far.at[:, :, :, at], tall.at[:, :, :, at]),
        ))
    xqo_load = loads.start(pairs_far.at[1], xqo)
    frames_load = loads.start(frames_far, frames)
    units = [(pair, t) for pair in range(6) for t in range(2)]

    def unit_copies(n):
        pair, t = units[n]
        slot = n % 2
        return [
            pltpu.make_async_copy(ck_far.at[t, pair], keys_here.at[slot], unit_sems.at[slot, 0]),
            pltpu.make_async_copy(cv_far.at[t, pair], values_here.at[slot], unit_sems.at[slot, 1]),
            pltpu.make_async_copy(p_far.at[t, pair], p_here.at[slot], unit_sems.at[slot, 2]),
        ]

    for copy in unit_copies(0):
        copy.start()
    greet(z, x, y, core)
    mail = Mail(send_sems, recv_sems)
    sums = Summing(mail, (z, x, y), (x_mate, y_mate, z_mates), acc, diag_x, diag_y, x_in, y_in, z_in, total)
    swap = mail.slots(1 + 2 + 4 + 2 + 2 + 2 + 1)
    m_slot, dz_slots, g_slots, du_slots = swap[0], swap[1:3], swap[3:7], swap[7:9]
    xb_slots, xa_slots, kv_slot = swap[9:11], swap[11:13], swap[13]
    o2_slot, c_slot = mail.slots(2)
    mail.post(m, m_sib, m_slot, c_mate)
    mail.post(o2, o2_sib, o2_slot, c_mate)
    mail.post(c, c_sib, c_slot, c_mate)

    for t in range(2):
        weight = 0.0
        for corpus in range(weights.shape[0]):
            weight = weight + jnp.where(ids[t] == corpus, weights[corpus], 0.0)
        row = lax.broadcasted_iota(jnp.int32, (span, 1), 0) + seq * span
        scale = jnp.where(row < lengths[t], weight, 0.0)
        dy[t * span:(t + 1) * span] = cotangent[t].astype(jnp.float32) * scale
    dz = dy[...].astype(jnp.bfloat16)
    dz_wide = dz.astype(jnp.float32)
    small_out[...] = jnp.zeros_like(small_out)
    small_out[12:13] = column_sum(dz_wide)
    for yy in range(2):
        tiles = [dz_wide[:, yy * 384 + n * 128:yy * 384 + (n + 1) * 128] for n in range(3)]
        even = jnp.concatenate([tiles[0], tiles[1]], axis=1)
        last = turned(tiles[2])
        odd = jnp.concatenate([jnp.where(low, turned(tiles[1]), last), last], axis=1)
        dz_own[yy] = jnp.where(core == 0, even, odd).astype(jnp.bfloat16)
        dz_send[yy] = jnp.where(core == 0, odd, even).astype(jnp.bfloat16)
        mail.post(dz_send.at[yy], dz_sib.at[yy], dz_slots[yy], c_mate)
    rows = m[...].reshape(2 * span, 768)
    for number, (yy, side) in enumerate(order):
        at = lanes((2 * yy + (core if side == 0 else 1 - core)) * 768, 768)
        for copy in block_loads[number]:
            copy.wait()
        hidden = mm(rows, wide[:, :, :, at].reshape(768, 768)) + wide_bias[:, at]
        bell = 0.5 * (1.0 + lax.erf(hidden * 0.7071067811865476))
        g_own[:, at] = (hidden * bell).astype(jnp.bfloat16)
        mail.post(g_own.at[:, at], g_sib.at[:, at], g_slots[number], c_mate)
        gate_slope[:, at] = bell + hidden * (jnp.exp(-0.5 * hidden * hidden) * 0.3989422804014327)
    for number, (yy, side) in enumerate(order):
        at = lanes((2 * yy + (1 - core if side == 0 else core)) * 768, 768)
        mail.arrive(g_sib.at[:, at], g_slots[number], c_mate)
    for yy in range(2):
        mail.arrive(dz_sib.at[yy], dz_slots[yy], c_mate)
    for yy in range(2):
        slopes = two(dz_own[yy], dz_sib[yy])
        for zz in range(NZ):
            at = slice(zz * 768, (zz + 1) * 768)
            product = mm_rows(slopes, two(g_own[:, at], g_sib[:, at])).astype(jnp.bfloat16)
            for xx in range(NX):
                acc[2, yy, zz, xx] = product[0:96, xx * 384:(xx + 1) * 384]
                acc[3, yy, zz, xx] = product[96:192, xx * 384:(xx + 1) * 384]
    sums.begin(2)
    sums.begin(3)
    z_sum, dm_sum = None, None
    for number, (yy, side) in enumerate(order):
        at = lanes((2 * yy + (core if side == 0 else 1 - core)) * 768, 768)
        wide_here = wide[:, :, :, at].reshape(768, 768)
        tall_here = tall[:, :, :, at].reshape(768, 768)
        back = (mm(dz, tall_here) * gate_slope[:, at]).astype(jnp.bfloat16)
        if side == 0:
            du_own[yy] = back
        else:
            du_send[yy] = back
            mail.post(du_send.at[yy], du_sib.at[yy], du_slots[yy], c_mate)
        part = mm_back(g_own[:, at], tall_here)
        z_sum = part if z_sum is None else z_sum + part
        part = mm_back(back, wide_here)
        dm_sum = part if dm_sum is None else dm_sum + part
        wide_small[:, at] = column_sum(back)
    mail.arrive(m_sib, m_slot, c_mate)
    both_rows = two(rows, m_sib[...].reshape(2 * span, 768))
    for yy in range(2):
        mail.arrive(du_sib.at[yy], du_slots[yy], c_mate)
        product = mm_rows(both_rows, two(du_own[yy], du_sib[yy])).astype(jnp.bfloat16)
        acc[0, yy] = product[:, 0:384].reshape(NZ, NX, 96, 384)
        acc[1, yy] = product[:, 384:768].reshape(NZ, NX, 96, 384)
    sums.begin(0)
    sums.begin(1)
    h2_rows = h2[...].reshape(2 * span, 768)
    out = h2_rows + z_sum + vec[12:13]
    back, gain, offset = normed_back(h2_rows, vec[10:11], dm_sum)
    small_out[10:11] = gain
    small_out[11:12] = offset
    dh2[...] = dy[...] + back
    for t in range(2):
        y_out[t] = out[t * span:(t + 1) * span].astype(jnp.bfloat16)

    pending = []
    for step in range(6):
        for lag, action in ((0, sums.side), (1, sums.column), (2, sums.last)):
            if 0 <= step - lag < 4:
                pending.append((action, (2, 3, 0, 1)[step - lag]))

    def tick(number=1):
        for _ in range(number):
            if pending:
                action, group = pending.pop(0)
                action(group)

    low_wide = dh2[...].astype(jnp.bfloat16).astype(jnp.float32)
    small_out[9:10] = column_sum(low_wide)
    xqo_load.wait()
    for yy in range(2):
        near, far = join_second(low_wide[:, yy * 384:(yy + 1) * 384])
        xb_own[yy] = jnp.where(core == 0, near, far)
        xb_send[yy] = jnp.where(core == 0, far, near)
        mail.post(xb_send.at[yy], xb_sib.at[yy], xb_slots[yy], c_mate)
    heard = back_second(low_wide, xqo)
    small_out[8:9] = column_sum(heard.astype(jnp.bfloat16))
    for t in range(2):
        do[t] = heard[t * span:(t + 1) * span].astype(jnp.bfloat16)
    tick()
    frames_load.wait()
    total_kv = None
    for number, (pair, t) in enumerate(units):
        at = slice(pair * 128, (pair + 1) * 128)
        slot = number % 2
        if number + 1 < len(units):
            for copy in unit_copies(number + 1):
                copy.start()
        for copy in unit_copies(number):
            copy.wait()
        slopes, query = stacked(do, t, pair), stacked(cq, t, pair)
        scores[...] = mm_back(slopes, values_here[slot])
        chances = p_here.at[slot]
        soften_back(chances, scores, dscores, 2 * span, 1536)
        dq[t * span:(t + 1) * span, at] = unstacked(mm(dscores[...], keys_here[slot])) * factor
        turned_grads = two(mm_rows(query, dscores[...]), mm_rows(slopes, chances[...])).astype(jnp.bfloat16)
        part = mm(turned_grads, frames[t].reshape(1536, 768))
        total_kv = part if t == 0 else total_kv + part
        if t == 1:
            keys, values = total_kv[0:128].T, total_kv[128:256].T
            yy, place = pair // 3, pair % 3
            if place == 1:
                values = turned(values)
                half = low_lanes(768)
                gkv[0, yy, :, 128:256] = jnp.where(half, keys, values).astype(jnp.bfloat16)
                gkv[1, yy, :, 128:256] = jnp.where(half, values, keys).astype(jnp.bfloat16)
            else:
                gkv[place // 2, yy, :, 0:128] = keys.astype(jnp.bfloat16)
                gkv[place // 2, yy, :, 256:384] = values.astype(jnp.bfloat16)
        if number in (2, 4, 5, 6, 7, 8, 9, 10, 11):
            tick()
    mail.post(gkv.at[1 - core], kv_in, kv_slot, c_mate)
    low_q = dq[...].astype(jnp.bfloat16).astype(jnp.float32)
    small_out[7:8] = column_sum(low_q)
    for yy in range(2):
        near, far = join_first(low_q[:, yy * 384:(yy + 1) * 384])
        xa_own[yy] = jnp.where(core == 0, near, far)
        xa_send[yy] = jnp.where(core == 0, far, near)
        mail.post(xa_send.at[yy], xa_sib.at[yy], xa_slots[yy], c_mate)
    back, gain, offset = normed_back(h1[...].reshape(2 * span, 768), vec[5:6], back_first(low_q, xqo))
    small_out[5:6] = gain
    small_out[6:7] = offset
    for t in range(2):
        dh1_out[t] = dh2[t * span:(t + 1) * span] + back[t * span:(t + 1) * span]
    mail.arrive(o2_sib, o2_slot, c_mate)
    mail.arrive(c_sib, c_slot, c_mate)
    o2_both = two(o2[...].reshape(2 * span, 768), o2_sib[...].reshape(2 * span, 768))
    c_both = two(c[...].reshape(2 * span, 768), c_sib[...].reshape(2 * span, 768))
    for yy in range(2):
        mail.arrive(xb_sib.at[yy], xb_slots[yy], c_mate)
        mail.arrive(xa_sib.at[yy], xa_slots[yy], c_mate)
        second = mm_rows(o2_both, two(xb_own[yy], xb_sib[yy]))
        first = mm_rows(c_both, two(xa_own[yy], xa_sib[yy]))
        store_pair(acc_xqo.at[yy], first, second)
    mail.arrive(kv_in, kv_slot, c_mate)
    for yy in range(2):
        acc_kv[yy] = (gkv[core, yy] + kv_in[yy]).reshape(NZ, NX, 96, 384)
    tick(100)
    mail.finish()


def store_pair(out, first, second):
    shape = (NZ, NX, 96, 128)
    out[:, :, :, 0:128] = tile_of(first, 0).astype(jnp.bfloat16).reshape(shape)
    out[:, :, :, 128:256] = (tile_of(first, 1) + tile_of(second, 0)).astype(jnp.bfloat16).reshape(shape)
    out[:, :, :, 256:384] = tile_of(second, 1).astype(jnp.bfloat16).reshape(shape)


def run_feed(lengths, ids, weights, near, far):
    bf16, f32 = jnp.bfloat16, jnp.float32
    span = near[4].shape[1]
    rows, flat = (2, span, 768), 2 * span
    inside, anywhere = pl.BlockSpec(memory_space=pltpu.VMEM), pl.BlockSpec(memory_space=pl.ANY)
    scalar = pl.BlockSpec(memory_space=pltpu.SMEM)
    piece = (NY, NZ, NX, 96, 384)
    number = 4 * 7 + 16
    scratch = [
        ((NZ, NX, 96, 3072), bf16), ((NY, NC, 192, 3072), bf16), ((NY, NZ, NX, 96, 768), bf16), (far[3].shape, bf16),
        ((2, 1536, 128), bf16), ((2, 1536, 128), bf16), ((2, flat, 1536), bf16),
        (rows, bf16), ((flat, 3072), bf16), ((flat, 3072), bf16),
        ((2, flat, 768), bf16), ((2, flat, 768), bf16), ((2, flat, 768), bf16),
        ((2, flat, 256), bf16), ((2, flat, 256), bf16), ((2, flat, 256), bf16),
        (rows, bf16), (rows, bf16),
    ] + [((2, flat, 256), bf16)] * 6 + [
        ((2, 2, 768, 384), bf16), ((2, 768, 384), bf16),
        ((flat, 768), f32), ((flat, 768), f32), (rows, bf16), ((flat, 768), f32), ((flat, 1536), f32),
        ((flat, 1536), bf16), ((flat, 3072), f32),
    ]
    return pl.pallas_call(
        feed_kernel,
        out_shape=(
            jax.ShapeDtypeStruct(rows, bf16), jax.ShapeDtypeStruct(rows, f32),
            jax.ShapeDtypeStruct((4, 96, 384), f32),
            jax.ShapeDtypeStruct(piece, bf16), jax.ShapeDtypeStruct(piece, bf16),
            jax.ShapeDtypeStruct((16, 768), f32), jax.ShapeDtypeStruct((1, 3072), f32),
        ),
        in_specs=[scalar] * 3 + [inside] * len(near) + [anywhere] * len(far),
        out_specs=(inside,) * 7,
        scratch_shapes=summing_scratch(4) + [pltpu.VMEM(shape, kind) for shape, kind in scratch] + [
            pltpu.SemaphoreType.DMA((number,)),
            pltpu.SemaphoreType.DMA((number,)),
            pltpu.SemaphoreType.DMA((10,)),
            pltpu.SemaphoreType.DMA((2, 3)),
        ],
        compiler_params=pltpu.CompilerParams(
            collective_id=2, has_side_effects=True, vmem_limit_bytes=60 << 20
        ),
        name="feed_cross_back",
    )(lengths, ids, weights, *near, *far)


def last_kernel(
    tokens, dh1, o, vec, small_before, wide_small,
    heads_far, mixer_far, kv_far, xqo_far, a_far, rows_far, third_far, p_far,
    dx_out, total, total_o, total_q, small_total,
    acc, diag_x, diag_y, x_in, y_in, z_in,
    acc_o, diag_x_o, diag_y_o, x_in_o, y_in_o, z_in_o,
    acc_q, x_in_q, z_in_q,
    a, head_rows, third, p, heads, mixer, o_sib, ob_own, ob_send, ob_sib, do_send, do_got, kv_sum, dq_third, dheads,
    da_send, da_core, da_side, scores, dscores,
    small, pack, pack_in, pack_sum, pack_seq,
    send_sems, recv_sems, load_sems,
):
    z, x, y, core = where_am_i()
    span = o.shape[1]
    seq = y * NC + core
    grp = z * NX + x
    factor = 1.0 / math.sqrt(HEAD_DIM)
    x_mate, y_mate, c_mate = device_at(z, 1 - x, y, core), device_at(z, x, 1 - y, core), device_at(z, x, y, 1 - core)
    far_mate = device_at(z, x, 1 - y, 1 - core)
    z_mates = [device_at(lax.rem(z + n, NZ), x, y, core) for n in range(1, NZ)]
    loads = Loads(load_sems)
    mixer_load = loads.start(mixer_far, mixer)
    acc_loads = [loads.start(kv_far, acc.at[0]), loads.start(xqo_far, acc.at[1])]
    unit_loads = [loads.start(rows_far, head_rows), loads.start(third_far, third), loads.start(p_far, p)]
    heads_load = loads.start(heads_far, heads)
    a_load = loads.start(a_far, a)
    greet(z, x, y, core)
    mail = Mail(send_sems, recv_sems)
    mates3 = (x_mate, y_mate, z_mates)
    sums = Summing(mail, (z, x, y), mates3, acc, diag_x, diag_y, x_in, y_in, z_in, total)
    sums_o = Summing(mail, (z, x, y), mates3, acc_o, diag_x_o, diag_y_o, x_in_o, y_in_o, z_in_o, total_o)
    (o_slot,) = mail.slots(1)
    ob_slots, do_slots = mail.slots(2), mail.slots(6)
    core_slots, side_slots = mail.slots(4), mail.slots(2)
    xq_slots, zq_slots = mail.slots(2), mail.slots(6)
    pack_slots, seq_slots = mail.slots(2 * NZ - 1), mail.slots(2)
    mail.post(o, o_sib, o_slot, c_mate)
    small[...] = small_before[...]
    low_wide = dh1[...].reshape(2 * span, 768).astype(jnp.bfloat16).astype(jnp.float32)
    small[4:5] = column_sum(low_wide)
    heard = None
    mixer_load.wait()
    for yy in range(2):
        near, far = join_first(low_wide[:, yy * 384:(yy + 1) * 384])
        ob_own[yy] = jnp.where(core == 0, near, far)
        ob_send[yy] = jnp.where(core == 0, far, near)
        mail.post(ob_send.at[yy], ob_sib.at[yy], ob_slots[yy], c_mate)
        part = mm_back(jnp.concatenate([near, far], axis=1), mixer[yy].reshape(768, 512))
        heard = part if heard is None else heard + part
    for yy in range(2):
        near, far = join_first(heard[:, yy * 384:(yy + 1) * 384])
        for t in range(2):
            do_send[2 * yy, t] = near[t * span:(t + 1) * span]
            do_send[2 * yy + 1, t] = far[t * span:(t + 1) * span]
    mates = (
        (c_mate, y * NC + 1 - core), (y_mate, (1 - y) * NC + core), (far_mate, (1 - y) * NC + 1 - core)
    )
    for t in range(2):
        for place in (2, 1, 0):
            mate, mate_seq = mates[place]
            mail.post(do_send.at[mate_seq, t], do_got.at[seq, t], do_slots[3 * t + place], mate)
        do_got[seq, t] = do_send[seq, t]
    for copy in acc_loads:
        copy.wait()
    sums.begin(0)
    sums.begin(1)
    mail.arrive(o_sib, o_slot, c_mate)
    o_both = two(o[...].reshape(2 * span, 768), o_sib[...].reshape(2 * span, 768))
    for yy in range(2):
        mail.arrive(ob_sib.at[yy], ob_slots[yy], c_mate)
        product = mm_rows(o_both, two(ob_own[yy], ob_sib[yy])).astype(jnp.bfloat16)
        acc_o[0, yy] = product.reshape(NZ, NX, 96, 256)
    sums_o.begin(0)
    pending = [
        (sums.side, 0), (sums.side, 1), (sums_o.side, 0), (sums.column, 0), (sums.column, 1), (sums_o.column, 0),
        (sums.last, 0), (sums.last, 1), (sums_o.last, 0),
    ]

    def tick(number=1):
        for _ in range(number):
            if pending:
                action, group = pending.pop(0)
                action(group)

    def exchange_core(t):
        mail.post(da_send.at[y * NC + 1 - core, t], da_core.at[t, 0], core_slots[2 * t], c_mate)
        mail.post(da_send.at[(1 - y) * NC + 1 - core, t], da_core.at[t, 1], core_slots[2 * t + 1], c_mate)

    def exchange_side(t):
        mail.arrive(da_core.at[t, 1], core_slots[2 * t + 1], c_mate)
        across = (1 - y) * NC + core
        da_send[across, t] = da_send[across, t] + da_core[t, 1]
        mail.post(da_send.at[across, t], da_side.at[t], side_slots[t], y_mate)

    for copy in unit_loads:
        copy.wait()
    heads_load.wait()
    for t in range(2):
        for place, (mate, mate_seq) in enumerate(mates):
            mail.arrive(do_got.at[mate_seq, t], do_slots[3 * t + place], mate)
        for block in (3, 2, 1, 0):
            rows, width = slice(block * span, (block + 1) * span), 128 * (block + 1)
            slopes, slopes_third = both_heads(do_got[block, t, :, 0:128]), do_got[block, t, :, 128:256]
            query = both_heads(head_rows[t, rows, 0:128])
            query_third = third_head(head_rows[t, rows, 384:512], core)
            scores[0:2 * span, 0:width] = mm_back(slopes, head_rows[t, 0:width, 256:384])
            scores[2 * span:3 * span, 0:width] = mm_back(slopes_third, head_rows[t, 0:width, 512:640])
            chances = p.at[t, block]
            soften_back(chances, scores, dscores, 3 * span, width)
            pair_grads, third_grads = dscores[0:2 * span, 0:width], dscores[2 * span:3 * span, 0:width]
            dheads[t, rows, 0:128] = (
                unstacked(mm(pair_grads, head_rows[t, 0:width, 128:256])) * factor
            ).astype(jnp.bfloat16)
            dq_third[rows] = third_head(mm(third_grads, third[t, 0:width]) * factor, core)
            parts = (
                mm_rows(query, pair_grads), mm_rows(query_third, third_grads),
                mm_rows(slopes, chances[0:2 * span, 0:width]), mm_rows(slopes_third, chances[2 * span:3 * span, 0:width]),
            )
            for number, part in enumerate(parts):
                if block == 3:
                    kv_sum[number] = part
                else:
                    kv_sum[number, :, 0:width] += part
            if t == 1 and block == 3:
                exchange_side(0)
            elif (t, block) in ((0, 1), (0, 0), (1, 1), (1, 0)):
                tick()
        keys, keys_third, values, values_third = [kv_sum[number].T[0:4 * span] for number in range(4)]
        dheads[t, :, 128:256] = keys.astype(jnp.bfloat16)
        dheads[t, :, 256:384] = values.astype(jnp.bfloat16)
        dheads[t, :, 384:512] = (dq_third[...] + turned(keys_third)).astype(jnp.bfloat16)
        dheads[t, :, 512:640] = values_third.astype(jnp.bfloat16)
        if t == 1:
            a_load.wait()
            inputs = two(a[0].reshape(4 * span, 768), a[1].reshape(4 * span, 768))
            product = mm_rows(inputs, two(dheads[0], dheads[1])).astype(jnp.bfloat16)
            acc_q[...] = product.reshape(NZ, NX, 96, 640)
            for part, at in enumerate((slice(0, 384), slice(384, 640))):
                mail.post(acc_q.at[:, 1 - x, :, at], x_in_q.at[:, :, at], xq_slots[part], x_mate)
        back = mm_back(dheads[t], heads[...].reshape(768, 640)).astype(jnp.bfloat16)
        for s in range(4):
            da_send[s, t] = back[s * span:(s + 1) * span]
        exchange_core(t)
    tick(1)
    exchange_side(1)
    tick(1)
    sums_q = [column_sum(two(dheads[0, :, n * 128:(n + 1) * 128], dheads[1, :, n * 128:(n + 1) * 128])) for n in (0, 2, 3, 4)]
    small[2:3] = natural_row(sums_q[0], third_head(sums_q[2], core), y, core)
    small[3:4] = natural_row(sums_q[1], sums_q[3], y, core)
    for part, at in enumerate((slice(0, 384), slice(384, 640))):
        mail.arrive(x_in_q.at[:, :, at], xq_slots[part], x_mate)
        for k in range(NZ):
            acc_q[k, x, :, at] = acc_q[k, x, :, at] + x_in_q[k, :, at]
        for k in range(1, NZ):
            zz = lax.rem(z + k, NZ)
            mail.post(
                acc_q.at[zz, x, :, at], z_in_q.at[k - 1, :, at], zq_slots[3 * part + k - 1], z_mates[k - 1]
            )
    gain, offset = None, None
    for t in range(2):
        mail.arrive(da_core.at[t, 0], core_slots[2 * t], c_mate)
        mail.arrive(da_side.at[t], side_slots[t], y_mate)
        back = (
            da_send[seq, t].astype(jnp.float32) + da_core[t, 0].astype(jnp.float32) + da_side[t].astype(jnp.float32)
        )
        part, gain_part, offset_part = normed_back(tokens[t].astype(jnp.float32), vec[0:1], back)
        dx_out[t] = (dh1[t] + part).astype(jnp.bfloat16)
        gain = gain_part if t == 0 else gain + gain_part
        offset = offset_part if t == 0 else offset + offset_part
    small[0:1] = gain
    small[1:2] = offset
    for g in range(8):
        pack[g, 0:16, 0:96] = small[:, g * 96:(g + 1) * 96]
        pack[g, 0:16, 96:128] = jnp.zeros((16, 32), jnp.float32)
        for n in range(3):
            at = g * 384 + n * 128
            pack[g, 16 + n:17 + n, :] = wide_small[:, at:at + 128]
        pack[g, 19:24, :] = jnp.zeros((5, 128), jnp.float32)
    pack_to = [(lax.rem(z + n, NZ), x) for n in range(1, NZ)]
    pack_to += [(lax.rem(z + n, NZ), 1 - x) for n in range(NZ)]
    for number, (zz, xx) in enumerate(pack_to):
        mail.post(pack.at[zz * NX + xx], pack_in.at[number], pack_slots[number], device_at(zz, xx, y, core))
    tick(100)
    for number in range(2 * NZ - 1):
        mail.arrive(pack_in.at[number], pack_slots[number], x_mate)
    pack_sum[...] = (
        (pack[grp] + pack_in[0]) + (pack_in[1] + pack_in[2])
        + ((pack_in[3] + pack_in[4]) + (pack_in[5] + pack_in[6]))
    )
    mail.post(pack_sum, pack_seq.at[0], seq_slots[0], c_mate)
    mail.arrive(pack_seq.at[0], seq_slots[0], c_mate)
    pack_seq[1] = pack_sum[...] + pack_seq[0]
    mail.post(pack_seq.at[1], pack_seq.at[2], seq_slots[1], y_mate)
    for part, at in enumerate((slice(0, 384), slice(384, 640))):
        for k in range(1, NZ):
            mail.arrive(z_in_q.at[k - 1, :, at], zq_slots[3 * part + k - 1], z_mates[k - 1])
        total_q[:, at] = (acc_q[z, x, :, at].astype(jnp.float32) + z_in_q[0, :, at].astype(jnp.float32)) + (
            z_in_q[1, :, at].astype(jnp.float32) + z_in_q[2, :, at].astype(jnp.float32)
        )
    mail.arrive(pack_seq.at[2], seq_slots[1], y_mate)
    small_total[...] = pack_seq[1] + pack_seq[2]
    mail.finish()


def run_last(near, far):
    bf16, f32 = jnp.bfloat16, jnp.float32
    span = near[0].shape[1]
    rows, flat = (2, span, 768), 2 * span
    inside, anywhere = pl.BlockSpec(memory_space=pltpu.VMEM), pl.BlockSpec(memory_space=pl.ANY)
    number = 3 * 7 + 1 + 2 + 6 + 6 + 8 + 9
    scratch = [
        ((NZ, NX, 96, 640), bf16), ((NZ, 96, 640), bf16), ((NZ - 1, 96, 640), bf16),
    ] + [(ref.shape, bf16) for ref in far[4:]] + [
        ((NZ, NX, 96, 640), bf16), ((NY, NZ, NX, 96, 512), bf16), (rows, bf16),
        ((2, flat, 256), bf16), ((2, flat, 256), bf16), ((2, flat, 256), bf16),
        ((4, 2, span, 256), bf16), ((4, 2, span, 256), bf16), ((4, 128, 512), f32), ((4 * span, 128), f32),
        ((2, 4 * span, 640), bf16), ((4, 2, span, 768), bf16), ((2, 2, span, 768), bf16), ((2, span, 768), bf16),
        ((3 * span, 512), f32), ((3 * span, 512), bf16),
        ((16, 768), f32), ((8, 24, 128), f32), ((7, 24, 128), f32), ((24, 128), f32), ((3, 24, 128), f32),
    ]
    return pl.pallas_call(
        last_kernel,
        out_shape=(
            jax.ShapeDtypeStruct(rows, bf16), jax.ShapeDtypeStruct((2, 96, 384), f32),
            jax.ShapeDtypeStruct((1, 96, 256), f32), jax.ShapeDtypeStruct((96, 640), f32),
            jax.ShapeDtypeStruct((24, 128), f32),
        ),
        in_specs=[inside] * len(near) + [anywhere] * len(far),
        out_specs=(inside,) * 5,
        scratch_shapes=summing_scratch(2) + summing_scratch(1, 256) + [
            pltpu.VMEM(shape, kind) for shape, kind in scratch
        ] + [
            pltpu.SemaphoreType.DMA((number,)),
            pltpu.SemaphoreType.DMA((number,)),
            pltpu.SemaphoreType.DMA((8,)),
        ],
        compiler_params=pltpu.CompilerParams(
            collective_id=3, has_side_effects=True, vmem_limit_bytes=60 << 20
        ),
        name="self_back_sum",
    )(*near, *far)


def place_kernel(
    y, dx, total, total_o, total_q, total_ff, small,
    y_out, dx_out, query, key, value, mixer, xkey, xvalue, xquery, xmixer, wide, tall, *more,
):
    vectors, wide_bias = more[:13], more[13]
    core = lax.rem(lax.axis_index("seq"), NC)
    y_out[...] = y[...]
    dx_out[...] = dx[...]

    def put(out, even, odd):
        @pl.when(core == 0)
        def _():
            out[...] = jnp.concatenate(even, axis=1)

        @pl.when(core != 0)
        def _():
            out[...] = jnp.concatenate(odd, axis=1)

    heads = total_q[...]
    for out, pair, even, odd in ((query, 0, 384, 448), (key, 128, 448, 384), (value, 256, 512, 576)):
        whole = heads[:, pair:pair + 128]
        put(out, [whole, heads[:, even:even + 64]], [heads[:, odd:odd + 64], whole])
    piece = total_o[0]
    put(mixer, [piece[:, :192]], [piece[:, 192:], piece[:, :128]])
    for number, (first, second) in enumerate(((xkey, xvalue), (xquery, xmixer))):
        piece = total[number]
        put(first, [piece[:, :192]], [piece[:, 192:256], piece[:, :128]])
        put(second, [piece[:, 256:], piece[:, 192:256]], [piece[:, 128:192], piece[:, 256:]])
    wide[:, :384] = total_ff[0]
    wide[:, 384:] = total_ff[1]
    tall[:96] = total_ff[2]
    tall[96:] = total_ff[3]
    for number, out in enumerate(vectors):
        out[...] = small[number:number + 1, 0:96]
    for number in range(3):
        wide_bias[:, number * 128:(number + 1) * 128] = small[16 + number:17 + number]


def run_place(y, dx, *totals):
    f32 = jnp.float32
    inside = pl.BlockSpec(memory_space=pltpu.VMEM)
    like = jax.ShapeDtypeStruct(y.shape, y.dtype)
    return pl.pallas_call(
        place_kernel,
        out_shape=(like, like) + (jax.ShapeDtypeStruct((96, 192), f32),) * 8 + (
            jax.ShapeDtypeStruct((96, 768), f32), jax.ShapeDtypeStruct((192, 384), f32),
        ) + (jax.ShapeDtypeStruct((1, 96), f32),) * 13 + (jax.ShapeDtypeStruct((1, 384), f32),),
        in_specs=[inside] * 7,
        out_specs=(inside,) * 26,
        compiler_params=pltpu.CompilerParams(vmem_limit_bytes=60 << 20),
        name="place",
    )(y, dx, *totals)


def on_device_fast(*arguments):
    (
        tokens, encoder_states, lengths, frame_counts, corpus_ids, corpus_weights, cotangent,
        first_gain, first_bias, query_weight, query_bias, key_weight, value_weight, value_bias,
        output_weight, output_bias, second_gain, second_bias, cross_query_weight, cross_query_bias,
        cross_key_weight, cross_value_weight, cross_value_bias, cross_output_weight, cross_output_bias,
        third_gain, third_bias, expand_weight, expand_bias, reduce_weight, reduce_bias,
    ) = arguments
    bf16, f32 = jnp.bfloat16, jnp.float32
    small_vectors = (
        first_gain, first_bias, query_bias, value_bias, output_bias, second_gain, second_bias,
        cross_query_bias, cross_value_bias, cross_output_bias, third_gain, third_bias, reduce_bias, expand_bias,
    )
    matrices = (
        query_weight, key_weight, value_weight, output_weight, cross_key_weight, cross_value_weight,
        cross_query_weight, cross_output_weight, expand_weight, reduce_weight.T,
    )
    (
        heads_all, mixer_all, pairs_all, wide_all, tall_all, frames_all, vec, wide_bias,
        a_all, head_rows, third, o, h1, c, p_self, ck, cv, cq, o2, h2, m, p_cross,
    ) = run_forward(
        lengths, frame_counts, matrices, jnp.stack(small_vectors[:13]), expand_bias.reshape(3, 128), encoder_states, tokens
    )
    layer_output, dh1, total_ff, acc_kv, acc_xqo, small_before, wide_small = run_feed(
        lengths, corpus_ids, corpus_weights,
        [cotangent, vec, wide_bias, h2, m, o2, c, h1, cq],
        [wide_all, tall_all, pairs_all, frames_all, ck, cv, p_cross],
    )
    tokens_gradient, total, total_o, total_q, small_total = run_last(
        [tokens, dh1, o, vec, small_before, wide_small],
        [heads_all, mixer_all, acc_kv, acc_xqo, a_all, head_rows, third, p_self],
    )
    (
        layer_output, tokens_gradient, m_query, m_key, m_value, m_mixer, m_xkey, m_xvalue, m_xquery, m_xmixer,
        expand_grad, reduce_grad, *smaller,
    ) = run_place(layer_output, tokens_gradient, total, total_o, total_q, total_ff, small_total)
    reduce_grad = reduce_grad.T
    smaller = [row.reshape(-1) for row in smaller]
    expand_bias_grad = smaller[13]
    return (
        layer_output, tokens_gradient, smaller[0], smaller[1], m_query, smaller[2], m_key, m_value, smaller[3],
        m_mixer, smaller[4], smaller[5], smaller[6], m_xquery, smaller[7], m_xkey, m_xvalue, smaller[8],
        m_xmixer, smaller[9], smaller[10], smaller[11], expand_grad, expand_bias_grad, reduce_grad, smaller[12],
    )


def solution(mesh):
    placed = (
        P("grp", "seq", None),
        P("grp", "seq", None),
        P("grp"),
        P("grp"),
        P("grp"),
        P(),
        P("grp", "seq", None),
        P("grp"),
        P("grp"),
        P("grp", "seq"),
        P("grp"),
        P("grp", "seq"),
        P("grp", "seq"),
        P("grp"),
        P("grp", "seq"),
        P("grp"),
        P("grp"),
        P("grp"),
        P("grp", "seq"),
        P("grp"),
        P("grp", "seq"),
        P("grp", "seq"),
        P("grp"),
        P("grp", "seq"),
        P("grp"),
        P("grp"),
        P("grp"),
        P("grp", "seq"),
        P("grp"),
        P("grp", "seq"),
        P("grp"),
    )
    small_slice = mesh.shape["grp"] == NZ * NX and mesh.shape["seq"] == NY * NC
    return jax.shard_map(
        on_device_fast if small_slice else on_device_plain,
        mesh=mesh,
        in_specs=placed,
        out_specs=(
            P("grp", "seq", None),
            P("grp", "seq", None),
            P("grp"),
            P("grp"),
            P("grp", "seq"),
            P("grp"),
            P("grp", "seq"),
            P("grp", "seq"),
            P("grp"),
            P("grp", "seq"),
            P("grp"),
            P("grp"),
            P("grp"),
            P("grp", "seq"),
            P("grp"),
            P("grp", "seq"),
            P("grp", "seq"),
            P("grp"),
            P("grp", "seq"),
            P("grp"),
            P("grp"),
            P("grp"),
            P("grp", "seq"),
            P("grp"),
            P("grp", "seq"),
            P("grp"),
        ),
        check_vma=False,
    )
```

```python
import math

import jax
import jax.numpy as jnp
from jax import lax
from jax.experimental import pallas as pl
from jax.experimental.pallas import tpu as pltpu
from jax.sharding import PartitionSpec as P

HEADS = 12
HEAD_DIM = 64


NEG = -1e30
EPS = 1e-05


def norm_rows(values, scaling, offset):
    centre = values - jnp.mean(values, axis=-1, keepdims=True)
    spread = jnp.mean(centre * centre, axis=-1, keepdims=True)
    return centre * lax.rsqrt(spread + EPS) * scaling + offset


def smooth_gate(values):
    return 0.5 * values * (1.0 + lax.erf(values * 0.7071067811865476))


def linear(inputs, weight):
    return jnp.einsum("bri,ij->brj", inputs, weight, preferred_element_type=jnp.float32)


def linear_back(gradient, weight):
    return jnp.einsum("brj,ij->bri", gradient, weight, preferred_element_type=jnp.float32)


def outer_sum(inputs, gradient):
    return jnp.einsum("bri,brj->ij", inputs, gradient, preferred_element_type=jnp.float32)


def row_total(gradient):
    return jnp.sum(gradient.astype(jnp.float32), axis=(0, 1))


def split_heads(values):
    return values.reshape(values.shape[0], values.shape[1], HEADS, HEAD_DIM)


def scores_of(query, key_rows, allowed):
    scores = jnp.einsum(
        "bqhd,bkhd->bhqk",
        split_heads(query),
        split_heads(key_rows),
        preferred_element_type=jnp.float32,
    )
    return jnp.where(allowed[:, None], scores, NEG)


def attend(query, key_rows, values, allowed):
    scores = scores_of(query, key_rows, allowed)
    maximum = jnp.max(scores, axis=-1, keepdims=True)
    raised = jnp.exp(scores - maximum)
    summed = jnp.sum(raised, axis=-1, keepdims=True)
    chances = (raised / summed).astype(jnp.bfloat16)
    blended = jnp.einsum(
        "bhqk,bkhd->bqhd", chances, split_heads(values), preferred_element_type=jnp.float32
    )
    return (blended.reshape(query.shape).astype(jnp.bfloat16), maximum + jnp.log(summed))


def attend_back(grad_low, query, key_rows, values, allowed, logsum):
    scores = scores_of(query, key_rows, allowed)
    chances = jnp.exp(scores - logsum)
    grad_heads = split_heads(grad_low)
    grad_chance = jnp.einsum(
        "bqhd,bkhd->bhqk", grad_heads, split_heads(values), preferred_element_type=jnp.float32
    )
    offset = jnp.sum(chances * grad_chance, axis=-1, keepdims=True)
    grad_score = (chances * (grad_chance - offset)).astype(jnp.bfloat16)
    grad_query = jnp.einsum(
        "bhqk,bkhd->bqhd", grad_score, split_heads(key_rows), preferred_element_type=jnp.float32
    )
    grad_keys = jnp.einsum(
        "bhqk,bqhd->bkhd", grad_score, split_heads(query), preferred_element_type=jnp.float32
    )
    grad_values = jnp.einsum(
        "bhqk,bqhd->bkhd",
        chances.astype(jnp.bfloat16),
        grad_heads,
        preferred_element_type=jnp.float32,
    )
    return (
        grad_query.reshape(query.shape),
        grad_keys.reshape(key_rows.shape),
        grad_values.reshape(values.shape),
    )


def on_device_plain(
    tokens,
    encoder_states,
    lengths,
    frame_counts,
    corpus_ids,
    corpus_weights,
    cotangent,
    first_gain,
    first_bias,
    query_weight,
    query_bias,
    key_weight,
    value_weight,
    value_bias,
    output_weight,
    output_bias,
    second_gain,
    second_bias,
    cross_query_weight,
    cross_query_bias,
    cross_key_weight,
    cross_value_weight,
    cross_value_bias,
    cross_output_weight,
    cross_output_bias,
    third_gain,
    third_bias,
    expand_weight,
    expand_bias,
    reduce_weight,
    reduce_bias,
):
    row_parts = (
        lax.all_gather(query_weight, "grp", axis=0, tiled=True),
        lax.all_gather(key_weight, "grp", axis=0, tiled=True),
        lax.all_gather(value_weight, "grp", axis=0, tiled=True),
        lax.all_gather(output_weight, "grp", axis=0, tiled=True),
        lax.all_gather(cross_query_weight, "grp", axis=0, tiled=True),
        lax.all_gather(cross_key_weight, "grp", axis=0, tiled=True),
        lax.all_gather(cross_value_weight, "grp", axis=0, tiled=True),
        lax.all_gather(cross_output_weight, "grp", axis=0, tiled=True),
        lax.all_gather(expand_weight, "grp", axis=0, tiled=True),
        lax.all_gather(reduce_weight, "grp", axis=0, tiled=True),
        lax.all_gather(first_gain, "grp", axis=0, tiled=True),
        lax.all_gather(first_bias, "grp", axis=0, tiled=True),
        lax.all_gather(query_bias, "grp", axis=0, tiled=True),
        lax.all_gather(value_bias, "grp", axis=0, tiled=True),
        lax.all_gather(output_bias, "grp", axis=0, tiled=True),
        lax.all_gather(second_gain, "grp", axis=0, tiled=True),
        lax.all_gather(second_bias, "grp", axis=0, tiled=True),
        lax.all_gather(cross_query_bias, "grp", axis=0, tiled=True),
        lax.all_gather(cross_value_bias, "grp", axis=0, tiled=True),
        lax.all_gather(cross_output_bias, "grp", axis=0, tiled=True),
        lax.all_gather(third_gain, "grp", axis=0, tiled=True),
        lax.all_gather(third_bias, "grp", axis=0, tiled=True),
        lax.all_gather(expand_bias, "grp", axis=0, tiled=True),
        lax.all_gather(reduce_bias, "grp", axis=0, tiled=True),
    )
    gathered = (
        lax.all_gather(row_parts[0], "seq", axis=1, tiled=True),
        lax.all_gather(row_parts[1], "seq", axis=1, tiled=True),
        lax.all_gather(row_parts[2], "seq", axis=1, tiled=True),
        lax.all_gather(row_parts[3], "seq", axis=1, tiled=True),
        lax.all_gather(row_parts[4], "seq", axis=1, tiled=True),
        lax.all_gather(row_parts[5], "seq", axis=1, tiled=True),
        lax.all_gather(row_parts[6], "seq", axis=1, tiled=True),
        lax.all_gather(row_parts[7], "seq", axis=1, tiled=True),
        lax.all_gather(row_parts[8], "seq", axis=1, tiled=True),
        lax.all_gather(row_parts[9], "seq", axis=1, tiled=True),
    )
    w_query, w_key, w_value, w_mixer, x_query, x_key, x_value, x_mixer, w_expand, w_reduce = (
        gathered
    )
    vectors = [piece.astype(jnp.float32) for piece in row_parts[10:]]
    factor = 1.0 / math.sqrt(HEAD_DIM)
    seq_count = lax.axis_size("seq")
    span_rows = tokens.shape[1]
    query_pos = lax.axis_index("seq") * span_rows + jnp.arange(span_rows, dtype=jnp.int32)
    key_pos = jnp.arange(span_rows * seq_count, dtype=jnp.int32)
    self_mask = (key_pos[None, None, :] <= query_pos[None, :, None]) & (
        key_pos[None, None, :] < lengths[:, None, None]
    )
    frame_pos = jnp.arange(encoder_states.shape[1] * seq_count, dtype=jnp.int32)
    cross_mask = frame_pos[None, None, :] < frame_counts[:, None, None]
    layer_in = tokens.astype(jnp.float32)
    normed_one, norm_back_one = jax.vjp(norm_rows, layer_in, vectors[0], vectors[1])
    normed_one = normed_one.astype(jnp.bfloat16)
    query_low = ((linear(normed_one, w_query) + vectors[2]) * factor).astype(jnp.bfloat16)
    key_low = linear(normed_one, w_key).astype(jnp.bfloat16)
    value_low = (linear(normed_one, w_value) + vectors[3]).astype(jnp.bfloat16)
    key_all, value_all = (
        lax.all_gather(key_low, "seq", axis=1, tiled=True),
        lax.all_gather(value_low, "seq", axis=1, tiled=True),
    )
    self_out, self_logsum = attend(query_low, key_all, value_all, self_mask)
    after_self = layer_in + linear(self_out, w_mixer) + vectors[4]
    normed_two, norm_back_two = jax.vjp(norm_rows, after_self, vectors[5], vectors[6])
    normed_two = normed_two.astype(jnp.bfloat16)
    cross_query = ((linear(normed_two, x_query) + vectors[7]) * factor).astype(jnp.bfloat16)
    frames_all = lax.all_gather(encoder_states, "seq", axis=1, tiled=True)
    cross_keys_all = linear(frames_all, x_key).astype(jnp.bfloat16)
    cross_values_all = (linear(frames_all, x_value) + vectors[8]).astype(jnp.bfloat16)
    cross_out, cross_logsum = attend(cross_query, cross_keys_all, cross_values_all, cross_mask)
    after_cross = after_self + linear(cross_out, x_mixer) + vectors[9]
    normed_three, norm_back_three = jax.vjp(norm_rows, after_cross, vectors[10], vectors[11])
    normed_three = normed_three.astype(jnp.bfloat16)
    hidden = linear(normed_three, w_expand) + vectors[12]
    gated, gate_back = jax.vjp(smooth_gate, hidden)
    gated_low = gated.astype(jnp.bfloat16)
    result = after_cross + linear(gated_low, w_reduce) + vectors[13]
    layer_output = result.astype(jnp.bfloat16)
    present = (query_pos[None, :] < lengths[:, None]).astype(jnp.float32)
    corpus_index = jnp.arange(corpus_weights.shape[0], dtype=jnp.int32)
    corpus_scale = jnp.sum(
        jnp.where(corpus_ids[:, None] == corpus_index[None, :], corpus_weights[None, :], 0.0),
        axis=1,
    )
    grad_out = cotangent.astype(jnp.float32) * (present * corpus_scale[:, None])[:, :, None]
    reduce_low = grad_out.astype(jnp.bfloat16)
    slope_reduce_bias = row_total(reduce_low)
    slope_reduce = outer_sum(gated_low, reduce_low)
    grad_hidden = gate_back(linear_back(reduce_low, w_reduce))[0]
    hidden_low = grad_hidden.astype(jnp.bfloat16)
    slope_expand_bias = row_total(hidden_low)
    slope_expand = outer_sum(normed_three, hidden_low)
    grad_norm_in, slope_gain_three, slope_bias_three = norm_back_three(
        linear_back(hidden_low, w_expand)
    )
    grad_cross = grad_out + grad_norm_in
    cross_low = grad_cross.astype(jnp.bfloat16)
    slope_xmixer_bias = row_total(cross_low)
    slope_xmixer = outer_sum(cross_out, cross_low)
    grad_heard = linear_back(cross_low, x_mixer).astype(jnp.bfloat16)
    grad_cq, part_ck, part_cv = attend_back(
        grad_heard, cross_query, cross_keys_all, cross_values_all, cross_mask, cross_logsum
    )
    slope_xkey = outer_sum(frames_all, part_ck)
    slope_xvalue = outer_sum(frames_all, part_cv)
    slope_xvalue_bias = row_total(part_cv)
    low_cq = (grad_cq * factor).astype(jnp.bfloat16)
    slope_xquery_bias = row_total(low_cq)
    slope_xquery = outer_sum(normed_two, low_cq)
    grad_norm_two, slope_gain_two, slope_bias_two = norm_back_two(linear_back(low_cq, x_query))
    grad_self = grad_cross + grad_norm_two
    self_low = grad_self.astype(jnp.bfloat16)
    slope_mixer_bias = row_total(self_low)
    slope_mixer = outer_sum(self_out, self_low)
    grad_mixed = linear_back(self_low, w_mixer).astype(jnp.bfloat16)
    grad_q, part_k, part_v = attend_back(
        grad_mixed, query_low, key_all, value_all, self_mask, self_logsum
    )
    summed_k, summed_v = (
        lax.psum_scatter(
            part_k.astype(jnp.bfloat16), "seq", scatter_dimension=1, tiled=True
        ).astype(jnp.float32),
        lax.psum_scatter(
            part_v.astype(jnp.bfloat16), "seq", scatter_dimension=1, tiled=True
        ).astype(jnp.float32),
    )
    low_k = summed_k.astype(jnp.bfloat16)
    low_v = summed_v.astype(jnp.bfloat16)
    low_q = (grad_q * factor).astype(jnp.bfloat16)
    slope_query = outer_sum(normed_one, low_q)
    slope_query_bias = row_total(low_q)
    slope_key = outer_sum(normed_one, low_k)
    slope_value = outer_sum(normed_one, low_v)
    slope_value_bias = row_total(low_v)
    grad_normed = (
        linear_back(low_q, w_query) + linear_back(low_k, w_key) + linear_back(low_v, w_value)
    )
    grad_norm_one, slope_gain_one, slope_bias_one = norm_back_one(grad_normed)
    tokens_gradient = (grad_self + grad_norm_one).astype(jnp.bfloat16)
    owned = (
        lax.psum_scatter(slope_query, "grp", scatter_dimension=0, tiled=True),
        lax.psum_scatter(slope_key, "grp", scatter_dimension=0, tiled=True),
        lax.psum_scatter(slope_value, "grp", scatter_dimension=0, tiled=True),
        lax.psum_scatter(slope_mixer, "grp", scatter_dimension=0, tiled=True),
        lax.psum_scatter(slope_xquery, "grp", scatter_dimension=0, tiled=True),
        lax.psum_scatter(slope_xkey, "grp", scatter_dimension=0, tiled=True),
        lax.psum_scatter(slope_xvalue, "grp", scatter_dimension=0, tiled=True),
        lax.psum_scatter(slope_xmixer, "grp", scatter_dimension=0, tiled=True),
        lax.psum_scatter(slope_expand, "grp", scatter_dimension=0, tiled=True),
        lax.psum_scatter(slope_reduce, "grp", scatter_dimension=0, tiled=True),
        lax.psum_scatter(slope_gain_one, "grp", scatter_dimension=0, tiled=True),
        lax.psum_scatter(slope_bias_one, "grp", scatter_dimension=0, tiled=True),
        lax.psum_scatter(slope_query_bias, "grp", scatter_dimension=0, tiled=True),
        lax.psum_scatter(slope_value_bias, "grp", scatter_dimension=0, tiled=True),
        lax.psum_scatter(slope_mixer_bias, "grp", scatter_dimension=0, tiled=True),
        lax.psum_scatter(slope_gain_two, "grp", scatter_dimension=0, tiled=True),
        lax.psum_scatter(slope_bias_two, "grp", scatter_dimension=0, tiled=True),
        lax.psum_scatter(slope_xquery_bias, "grp", scatter_dimension=0, tiled=True),
        lax.psum_scatter(slope_xvalue_bias, "grp", scatter_dimension=0, tiled=True),
        lax.psum_scatter(slope_xmixer_bias, "grp", scatter_dimension=0, tiled=True),
        lax.psum_scatter(slope_gain_three, "grp", scatter_dimension=0, tiled=True),
        lax.psum_scatter(slope_bias_three, "grp", scatter_dimension=0, tiled=True),
        lax.psum_scatter(slope_expand_bias, "grp", scatter_dimension=0, tiled=True),
        lax.psum_scatter(slope_reduce_bias, "grp", scatter_dimension=0, tiled=True),
    )
    matrices = (
        lax.psum_scatter(
            owned[0].astype(jnp.bfloat16), "seq", scatter_dimension=1, tiled=True
        ).astype(jnp.float32),
        lax.psum_scatter(
            owned[1].astype(jnp.bfloat16), "seq", scatter_dimension=1, tiled=True
        ).astype(jnp.float32),
        lax.psum_scatter(
            owned[2].astype(jnp.bfloat16), "seq", scatter_dimension=1, tiled=True
        ).astype(jnp.float32),
        lax.psum_scatter(
            owned[3].astype(jnp.bfloat16), "seq", scatter_dimension=1, tiled=True
        ).astype(jnp.float32),
        lax.psum_scatter(
            owned[4].astype(jnp.bfloat16), "seq", scatter_dimension=1, tiled=True
        ).astype(jnp.float32),
        lax.psum_scatter(
            owned[5].astype(jnp.bfloat16), "seq", scatter_dimension=1, tiled=True
        ).astype(jnp.float32),
        lax.psum_scatter(
            owned[6].astype(jnp.bfloat16), "seq", scatter_dimension=1, tiled=True
        ).astype(jnp.float32),
        lax.psum_scatter(
            owned[7].astype(jnp.bfloat16), "seq", scatter_dimension=1, tiled=True
        ).astype(jnp.float32),
        lax.psum_scatter(
            owned[8].astype(jnp.bfloat16), "seq", scatter_dimension=1, tiled=True
        ).astype(jnp.float32),
        lax.psum_scatter(
            owned[9].astype(jnp.bfloat16), "seq", scatter_dimension=1, tiled=True
        ).astype(jnp.float32),
    )
    smaller = lax.psum(
        (
            owned[10],
            owned[11],
            owned[12],
            owned[13],
            owned[14],
            owned[15],
            owned[16],
            owned[17],
            owned[18],
            owned[19],
            owned[20],
            owned[21],
            owned[22],
            owned[23],
        ),
        "seq",
    )
    return (
        layer_output,
        tokens_gradient,
        smaller[0],
        smaller[1],
        matrices[0],
        smaller[2],
        matrices[1],
        matrices[2],
        smaller[3],
        matrices[3],
        smaller[4],
        smaller[5],
        smaller[6],
        matrices[4],
        smaller[7],
        matrices[5],
        matrices[6],
        smaller[8],
        matrices[7],
        smaller[9],
        smaller[10],
        smaller[11],
        matrices[8],
        smaller[12],
        matrices[9],
        smaller[13],
    )


MESH_ID = pl.DeviceIdType.MESH
NZ, NX, NY, NC = 4, 2, 2, 2
GROUPS = 8


def where_am_i():
    grp = lax.axis_index("grp")
    seq = lax.axis_index("seq")
    return grp // NX, lax.rem(grp, NX), seq // NC, lax.rem(seq, NC)


def device_at(z, x, y, c):
    return (z * NX + x, y * NC + c)


def lanes(start, size):
    return pl.ds(pl.multiple_of(start, 128), size)


def pieces_of(bank, group, y, c, x, z_from, z_to):
    heads, mixer, pairs, wide, tall = bank
    column = pl.ds(z_from, z_to - z_from)
    if group == 0:
        return [heads.at[column, x]]
    if group == 1:
        return [mixer.at[y, column, x, :, lanes(c * 256, 256)]]
    if group < 4:
        return [pairs.at[group - 2, y, column, x, :, lanes(c * 384, 384)]]
    if group < 6:
        start = (y * NC + c) * 768 + (group - 4) * 384
        return [wide.at[column, x, :, lanes(start, 384)]]
    return [
        tall.at[y, c, pl.ds((group - 6) * 96, 96), lanes((z * NX + x) * 384, 384)]
        for z in range(z_from, z_to)
    ]


def piece_at(bank, group, y, c, x, z):
    heads, mixer, pairs, wide, tall = bank
    if group == 0:
        return heads.at[z, x]
    if group == 1:
        return mixer.at[y, z, x, :, lanes(c * 256, 256)]
    if group < 4:
        return pairs.at[group - 2, y, z, x, :, lanes(c * 384, 384)]
    if group < 6:
        return wide.at[z, x, :, lanes((y * NC + c) * 768 + (group - 4) * 384, 384)]
    return tall.at[y, c, pl.ds((group - 6) * 96, 96), lanes((z * NX + x) * 384, 384)]


def own_piece(own, group):
    heads, mixer, pairs, wide, tall = own
    if group == 0:
        return heads
    if group == 1:
        return mixer
    if group < 4:
        return pairs.at[group - 2]
    if group < 6:
        return wide.at[:, pl.ds((group - 4) * 384, 384)]
    return tall.at[pl.ds((group - 6) * 96, 96), :]


class Mail:
    def __init__(self, send_sems, recv_sems):
        self.send_sems, self.recv_sems, self.count, self.sent = send_sems, recv_sems, 0, []

    def slots(self, number):
        first = self.count
        self.count += number
        return list(range(first, first + number))

    def post(self, source, target, slot, device):
        copy = pltpu.make_async_remote_copy(
            src_ref=source,
            dst_ref=target,
            send_sem=self.send_sems.at[slot],
            recv_sem=self.recv_sems.at[slot],
            device_id=device,
            device_id_type=MESH_ID,
        )
        copy.start()
        self.sent.append(copy)

    def arrive(self, target, slot, device):
        pltpu.make_async_remote_copy(
            src_ref=target,
            dst_ref=target,
            send_sem=self.send_sems.at[slot],
            recv_sem=self.recv_sems.at[slot],
            device_id=device,
            device_id_type=MESH_ID,
        ).wait_recv()

    def finish(self):
        for copy in self.sent:
            copy.wait_send()


def greet(z, x, y, c):
    barrier = pltpu.get_barrier_semaphore()
    friends = [device_at(lax.rem(z + k, NZ), x, y, c) for k in range(1, NZ)]
    friends += [device_at(lax.rem(z + k, NZ), 1 - x, y, c) for k in range(NZ)]
    friends += [device_at(z, x, 1 - y, c), device_at(z, x, y, 1 - c), device_at(z, x, 1 - y, 1 - c)]
    for friend in friends:
        pl.semaphore_signal(barrier, inc=1, device_id=friend, device_id_type=MESH_ID)
    pl.semaphore_wait(barrier, len(friends))


def parts_in(group, number):
    return number if group >= 6 else 1


def joined(first, second):
    return jnp.concatenate([first, second], axis=1)


def mixed(first, second, core):
    even = joined(joined(first[:, :128], joined(first[:, 128:], second[:, 128:])), second[:, :128])
    odd = joined(joined(first[:, 64:], joined(second[:, :64], first[:, :64])), second[:, 64:])
    return jnp.where(core == 0, even, odd).astype(jnp.bfloat16)


def packed_heads(query, key, value, core):
    nothing = jnp.zeros_like(value[:, :64])
    even = [query[:, :128], key[:, :128], value[:, :128], query[:, 128:], key[:, 128:], value[:, 128:], nothing]
    odd = [query[:, 64:], key[:, 64:], value[:, 64:], key[:, :64], query[:, :64], nothing, value[:, :64]]
    even, odd = jnp.concatenate(even, axis=1), jnp.concatenate(odd, axis=1)
    return jnp.where(core == 0, even, odd).astype(jnp.bfloat16)


def packed_mixer(mixer, core):
    nothing = jnp.zeros_like(mixer[:, :64])
    even = joined(mixer, nothing)
    odd = joined(mixer[:, 64:], joined(nothing, mixer[:, :64]))
    return jnp.where(core == 0, even, odd).astype(jnp.bfloat16)


def own_tiles(row, y, core):
    block = jnp.where(y == 0, row[:, :384], row[:, 384:])
    lane = lax.broadcasted_iota(jnp.int32, (1, 128), 1)
    mine = lax.shift_right_logical(lane, 6) == core
    return (
        jnp.where(core == 0, block[:, :128], block[:, 256:]),
        jnp.where(mine, block[:, 128:256], jnp.zeros((1, 128), jnp.float32)),
    )


def natural_row(pair, third, y, core):
    nothing = jnp.zeros_like(pair)
    first, last = jnp.where(core == 0, pair, nothing), jnp.where(core == 0, nothing, pair)
    block = jnp.concatenate([first, third, last], axis=1)
    empty = jnp.zeros_like(block)
    return jnp.concatenate([jnp.where(y == 0, block, empty), jnp.where(y == 0, empty, block)], axis=1)


ORDER = (0, 2, 1, 3, 4, 5, 6, 7)


def forward_kernel(
    frame_span, lengths, counts,
    query_in, key_in, value_in, mixer_in, xkey_in, xvalue_in, xquery_in, xmixer_in, wide_in, tall_in,
    vectors_in, wide_bias_in, frames_short, tokens_in,
    heads, mixer, pairs, wide, tall, frames, vec_out, wide_bias,
    a_to, rows_to, third_to, o_to, h1_to, c_to, p_self_to, ck_to, cv_to, cq_to, o2_to, h2_to, m_to, p_cross_to,
    tokens_got, small, heads_here, mixer_here, pairs_here, frames_here,
    a_all, head_rows, third, o, h1, c, p_self, ck, cv, cq, o2, h2, m, p_cross,
    o_send, o_got, scores, self_scores, self_bias, cross_bias, heads_in, mixer_in_v, pairs_in, frames_in, small_in,
    send_sems, recv_sems, local_sems, load_sems, save_sems,
):
    z, x, y, c_own = where_am_i()
    heads_in[...] = packed_heads(*[ref[...].astype(jnp.float32) for ref in (query_in, key_in, value_in)], c_own)
    mixer_in_v[...] = packed_mixer(mixer_in[...].astype(jnp.float32), c_own)
    for number, (first, second) in enumerate(((xkey_in, xvalue_in), (xquery_in, xmixer_in))):
        pairs_in[number] = mixed(first[...].astype(jnp.float32), second[...].astype(jnp.float32), c_own)
    small_in[...] = jnp.zeros((32, 128), jnp.bfloat16)
    small_in[0:13, 0:96] = vectors_in[...]
    small_in[16:19, :] = wide_bias_in[...]
    frames_in[:, 368:384] = jnp.zeros((2, 16, 768), jnp.bfloat16)
    frames_in[:, 0:frame_span] = frames_short[...]
    greet(z, x, y, c_own)
    mail = Mail(send_sems, recv_sems)
    own = (heads_in, mixer_in_v, pairs_in, wide_in, tall_in)
    bank = (heads, mixer, pairs, wide, tall)
    far_mate = device_at(z, x, 1 - y, 1 - c_own)
    x_mate, y_mate = device_at(z, 1 - x, y, c_own), device_at(z, x, 1 - y, c_own)
    c_mate = device_at(z, x, y, 1 - c_own)
    z_mates = [device_at(lax.rem(z + n, NZ), x, y, c_own) for n in range(1, NZ)]
    grp = z * NX + x
    seq = y * NC + c_own

    local = []

    def keep(source, target):
        copy = pltpu.make_async_copy(source, target, local_sems.at[len(local)])
        copy.start()
        local.append(copy)

    small_slots = mail.slots(2 * NZ - 1)
    small_to = z_mates + [device_at(lax.rem(z + n, NZ), 1 - x, y, c_own) for n in range(NZ)]
    token_slots = mail.slots(3)
    frame_slots = mail.slots(3)
    z_slots = [mail.slots(NZ - 1) for _ in range(GROUPS)]
    x_slots = [mail.slots(parts_in(g, 4)) for g in range(GROUPS)]
    y_slots = [mail.slots(parts_in(g, 4)) for g in range(GROUPS)]
    dy_slots = [mail.slots(parts_in(g, VIA_X)) for g in range(GROUPS)]
    dx_slots = [mail.slots(parts_in(g, 4 - VIA_X)) for g in range(GROUPS)]
    co_slots = [mail.slots(parts_in(g, 4)) for g in range(GROUPS)]
    cx_slots = [mail.slots(parts_in(g, 4)) for g in range(GROUPS)]
    cy_slots = [mail.slots(parts_in(g, 4)) for g in range(GROUPS)]
    cdy_slots = [mail.slots(parts_in(g, VIA_X)) for g in range(GROUPS)]
    cdx_slots = [mail.slots(parts_in(g, 4 - VIA_X)) for g in range(GROUPS)]

    def to_column(group):
        for n in range(1, NZ):
            mail.post(
                own_piece(own, group), piece_at(bank, group, y, c_own, x, z), z_slots[group][n - 1], z_mates[n - 1]
            )

    def post_all(group, slots, device, yy, cc, xx, z_from, z_to):
        for slot, ref in zip(slots, pieces_of(bank, group, yy, cc, xx, z_from, z_to)):
            mail.post(ref, ref, slot, device)

    def arrive_all(group, slots, device, yy, cc, xx, z_from, z_to):
        for slot, ref in zip(slots, pieces_of(bank, group, yy, cc, xx, z_from, z_to)):
            mail.arrive(ref, slot, device)

    def spread(group):
        for n in range(1, NZ):
            zz = lax.rem(z + NZ - n, NZ)
            mail.arrive(piece_at(bank, group, y, c_own, x, zz), z_slots[group][n - 1], z_mates[n - 1])
        local[group].wait()
        post_all(group, x_slots[group], x_mate, y, c_own, x, 0, 4)
        if group == 0:
            return
        post_all(group, y_slots[group], y_mate, y, c_own, x, 0, 4)
        post_all(group, co_slots[group], c_mate, y, c_own, x, 0, 4)

    def turn(group):
        if group == 0:
            arrive_all(group, x_slots[group], x_mate, y, c_own, 1 - x, 0, 4)
            return
        arrive_all(group, y_slots[group], y_mate, 1 - y, c_own, x, 0, 4)
        post_all(group, dx_slots[group], x_mate, 1 - y, c_own, x, VIA_X, 4)
        post_all(group, cy_slots[group], c_mate, 1 - y, c_own, x, 0, 4)
        arrive_all(group, x_slots[group], x_mate, y, c_own, 1 - x, 0, 4)
        post_all(group, dy_slots[group], y_mate, y, c_own, 1 - x, 0, VIA_X)
        post_all(group, cx_slots[group], c_mate, y, c_own, 1 - x, 0, 4)

    def share(group):
        if group == 0:
            return
        arrive_all(group, dy_slots[group], y_mate, 1 - y, c_own, 1 - x, 0, VIA_X)
        post_all(group, cdy_slots[group], c_mate, 1 - y, c_own, 1 - x, 0, VIA_X)
        arrive_all(group, dx_slots[group], x_mate, 1 - y, c_own, 1 - x, VIA_X, 4)
        post_all(group, cdx_slots[group], c_mate, 1 - y, c_own, 1 - x, VIA_X, 4)

    def complete(group):
        arrive_all(group, co_slots[group], c_mate, y, 1 - c_own, x, 0, 4)
        arrive_all(group, cx_slots[group], c_mate, y, 1 - c_own, 1 - x, 0, 4)
        arrive_all(group, cy_slots[group], c_mate, 1 - y, 1 - c_own, x, 0, 4)
        arrive_all(group, cdy_slots[group], c_mate, 1 - y, 1 - c_own, 1 - x, 0, VIA_X)
        arrive_all(group, cdx_slots[group], c_mate, 1 - y, 1 - c_own, 1 - x, VIA_X, 4)

    def frame_rows(number):
        return frames.at[:, number]

    loads = []

    def load(source, target):
        copy = pltpu.make_async_copy(source, target, load_sems.at[len(loads)])
        copy.start()
        loads.append(copy)
        return copy

    def load_pair(group):
        complete(group)
        return load(pairs.at[group - 2], pairs_here.at[group - 2])

    saves = []

    def save(source, target):
        copy = pltpu.make_async_copy(source, target, save_sems.at[len(saves)])
        copy.start()
        saves.append(copy)

    for group in range(GROUPS):
        keep(own_piece(own, group), piece_at(bank, group, y, c_own, x, z))
    keep(small_in, small.at[grp])
    keep(frames_in, frame_rows(seq))
    keep(tokens_in, tokens_got.at[seq])
    to_column(ORDER[0])
    for slot, device in zip(small_slots, small_to):
        mail.post(small_in, small.at[grp], slot, device)
    to_column(ORDER[1])
    mail.post(frames_in, frame_rows(seq), frame_slots[0], y_mate)
    mail.post(frames_in, frame_rows(seq), frame_slots[1], c_mate)
    mail.post(tokens_in, tokens_got.at[seq], token_slots[0], y_mate)
    mail.post(tokens_in, tokens_got.at[seq], token_slots[1], c_mate)
    to_column(ORDER[2])

    pending = []
    for step in range(GROUPS + 2):
        if step + 3 < GROUPS:
            pending.append((to_column, ORDER[step + 3]))
        if step < GROUPS:
            pending.append((spread, ORDER[step]))
        if 0 <= step - 1 < GROUPS:
            pending.append((turn, ORDER[step - 1]))
        if 0 <= step - 2 < GROUPS:
            pending.append((share, ORDER[step - 2]))

    def tick(number=1):
        while number > 0 and pending:
            action, group = pending.pop(0)
            action(group)
            if action is not to_column:
                number -= 1

    def until(action, group):
        while (action, group) in pending:
            tick()

    for n in range(1, NZ):
        zz = lax.rem(z + NZ - n, NZ)
        mail.arrive(small.at[zz * NX + x], small_slots[n - 1], z_mates[n - 1])
    for n in range(NZ):
        zz = lax.rem(z + NZ - n, NZ)
        mail.arrive(small.at[zz * NX + 1 - x], small_slots[NZ - 1 + n], x_mate)
    local[GROUPS].wait()
    vec_out[...] = jnp.concatenate([small[g, 0:16, 0:96].astype(jnp.float32) for g in range(8)], axis=1)
    for g in range(8):
        three = small[g, 16:24, :].astype(jnp.float32)
        for n in range(3):
            at = g * 384 + n * 128
            wide_bias[:, at:at + 128] = three[n:n + 1]

    o_slots = mail.slots(6)
    until(turn, 0)
    other = (1 - y) * NC + c_own
    mail.arrive(tokens_got.at[other], token_slots[0], y_mate)
    mail.post(tokens_got.at[other], tokens_got.at[other], token_slots[2], c_mate)
    heads_loaded = load(heads, heads_here)
    mail.arrive(frame_rows(other), frame_slots[0], y_mate)
    mail.post(frame_rows(other), frame_rows(other), frame_slots[2], c_mate)
    mail.arrive(tokens_got.at[y * NC + 1 - c_own], token_slots[1], c_mate)
    mail.arrive(tokens_got.at[(1 - y) * NC + 1 - c_own], token_slots[2], c_mate)
    for copy in local[GROUPS + 1:]:
        copy.wait()
    heads_loaded.wait()
    phase = self_forward(lengths, tokens_got, vec_out, heads_here, a_all, head_rows, third, p_self, o_send, self_scores, self_bias)
    mates = ((c_mate, y * NC + 1 - c_own), (y_mate, other), (far_mate, (1 - y) * NC + 1 - c_own))
    for number, t in enumerate(phase):
        if t is not None:
            for place, (mate, mate_seq) in enumerate(mates):
                mail.post(o_send.at[mate_seq, t], o_got.at[seq, t], o_slots[3 * t + place], mate)
            o_got[seq, t] = o_send[seq, t]
        if number % 2 == 1:
            tick()
    mail.arrive(frame_rows(y * NC + 1 - c_own), frame_slots[1], c_mate)
    mail.arrive(frame_rows((1 - y) * NC + 1 - c_own), frame_slots[2], c_mate)
    frames_loaded = load(frames, frames_here)
    for source, target in ((a_all, a_to), (head_rows, rows_to), (third, third_to), (p_self, p_self_to)):
        save(source, target)
    until(share, 2)
    kv_loaded = load_pair(2)
    frames_loaded.wait()
    kv_loaded.wait()
    for number, _ in enumerate(cross_keys(frames_here, vec_out, pairs_here.at[0], ck, cv)):
        if number % 2 == 1:
            tick()
    save(ck, ck_to)
    save(cv, cv_to)
    until(share, 1)
    complete(1)
    mixer_loaded = load(mixer, mixer_here)
    for t in range(2):
        for place, (mate, mate_seq) in enumerate(mates):
            mail.arrive(o_got.at[mate_seq, t], o_slots[3 * t + place], mate)
    mixer_loaded.wait()
    self_out(tokens_got, vec_out, mixer_here, o_got, o, h1, c)
    until(share, 3)
    third_loaded = load_pair(3)
    for source, target in ((o, o_to), (h1, h1_to), (c, c_to)):
        save(source, target)
    third_loaded.wait()
    phase = cross_forward(
        counts, frame_span, c, vec_out, pairs_here.at[1], ck, cv, h1, cq, o2, h2, m, p_cross, scores, cross_bias
    )
    for number, _ in enumerate(phase):
        if 1 <= number <= 12:
            t, pair = (number - 1) // 6, (number - 1) % 6
            save(p_cross.at[t, pair], p_cross_to.at[t, pair])
        if number % 2 == 1:
            tick()
    for source, target in ((cq, cq_to), (o2, o2_to), (h2, h2_to), (m, m_to)):
        save(source, target)
    tick(100)
    for group in (4, 5, 6, 7):
        complete(group)
    for copy in saves:
        copy.wait()
    mail.finish()


VIA_X = 2


def slots_needed():
    return (2 * NZ - 1) + 12 + sum(
        3 + parts_in(g, 4) * 5 + 2 * (parts_in(g, VIA_X) + parts_in(g, 4 - VIA_X)) for g in range(GROUPS)
    )


def run_forward(lengths, counts, matrices, vectors, wide_bias, frames, tokens):
    bf16, f32 = jnp.bfloat16, jnp.float32
    number = slots_needed()
    span = tokens.shape[1]
    anywhere = pl.BlockSpec(memory_space=pl.ANY)
    inside = pl.BlockSpec(memory_space=pltpu.VMEM)
    scalar = pl.BlockSpec(memory_space=pltpu.SMEM)
    rows = (2, span, 768)
    kept = [
        ((2, 4, span, 768), bf16), ((2, 512, 640), bf16), ((2, 512, 128), bf16), (rows, bf16), (rows, f32),
        (rows, bf16), ((2, 4, 3 * span, 512), bf16), ((2, 6, 1536, 128), bf16), ((2, 6, 1536, 128), bf16), (rows, bf16),
        (rows, bf16), (rows, f32), (rows, bf16), ((2, 6, 2 * span, 1536), bf16),
    ]
    frame_span = frames.shape[1]
    frames_shape = (2, NY * NC, 384, 768)
    return pl.pallas_call(
        lambda *refs: forward_kernel(frame_span, *refs),
        out_shape=(
            jax.ShapeDtypeStruct((NZ, NX, 96, 640), bf16),
            jax.ShapeDtypeStruct((NY, NZ, NX, 96, 512), bf16),
            jax.ShapeDtypeStruct((2, NY, NZ, NX, 96, 768), bf16),
            jax.ShapeDtypeStruct((NZ, NX, 96, 3072), bf16),
            jax.ShapeDtypeStruct((NY, NC, 192, 3072), bf16),
            jax.ShapeDtypeStruct(frames_shape, bf16),
            jax.ShapeDtypeStruct((16, 768), f32),
            jax.ShapeDtypeStruct((1, 3072), f32),
        ) + tuple(jax.ShapeDtypeStruct(shape, kind) for shape, kind in kept),
        in_specs=[scalar] * 2 + [inside] * 14,
        out_specs=(anywhere,) * 6 + (inside,) * 2 + (anywhere,) * len(kept),
        scratch_shapes=[
            pltpu.VMEM((4,) + tokens.shape, bf16),
            pltpu.VMEM((8, 32, 128), bf16),
            pltpu.VMEM((NZ, NX, 96, 640), bf16),
            pltpu.VMEM((NY, NZ, NX, 96, 512), bf16),
            pltpu.VMEM((2, NY, NZ, NX, 96, 768), bf16),
            pltpu.VMEM(frames_shape, bf16),
        ] + [pltpu.VMEM(shape, kind) for shape, kind in kept] + [
            pltpu.VMEM((4, 2, span, 256), bf16),
            pltpu.VMEM((4, 2, span, 256), bf16),
            pltpu.VMEM((2 * span, 1536), f32),
            pltpu.VMEM((3 * span, 512), f32),
            pltpu.VMEM((2, 4 * span, 512), f32),
            pltpu.VMEM((2, 1, 1536), f32),
            pltpu.VMEM((96, 640), bf16),
            pltpu.VMEM((96, 256), bf16),
            pltpu.VMEM((2, 96, 384), bf16),
            pltpu.VMEM((2, 384, 768), bf16),
            pltpu.VMEM((32, 128), bf16),
            pltpu.SemaphoreType.DMA((number,)),
            pltpu.SemaphoreType.DMA((number,)),
            pltpu.SemaphoreType.DMA((GROUPS + 3,)),
            pltpu.SemaphoreType.DMA((5,)),
            pltpu.SemaphoreType.DMA((26,)),
        ],
        compiler_params=pltpu.CompilerParams(
            collective_id=1, has_side_effects=True, vmem_limit_bytes=60 << 20
        ),
        name="gather_forward",
    )(lengths, counts, *matrices, vectors, wide_bias, frames, tokens)


def mm(left, right):
    return lax.dot_general(left, right, (((1,), (0,)), ((), ())), preferred_element_type=jnp.float32)


def mm_back(left, right):
    return lax.dot_general(left, right, (((1,), (1,)), ((), ())), preferred_element_type=jnp.float32)


def mm_rows(left, right):
    return lax.dot_general(left, right, (((0,), (0,)), ((), ())), preferred_element_type=jnp.float32)


def low_lanes(rows):
    return lax.broadcasted_iota(jnp.int32, (rows, 128), 1) < 64


def turned(tile):
    return pltpu.roll(tile, 64, 1)


def tile_of(values, number):
    return values[:, number * 128:(number + 1) * 128]


def split_first(near, far):
    low = low_lanes(near.shape[0])
    return [tile_of(near, 0), jnp.where(low, tile_of(near, 1), tile_of(far, 1)), tile_of(far, 0)]


def split_second(near, far):
    low = low_lanes(near.shape[0])
    return [tile_of(near, 1), turned(jnp.where(low, tile_of(far, 0), tile_of(near, 0))), tile_of(far, 1)]


def join_first(values):
    low = low_lanes(values.shape[0])
    middle = tile_of(values, 1)
    nothing = jnp.zeros_like(middle)
    near = jnp.concatenate([tile_of(values, 0), jnp.where(low, middle, nothing)], axis=1)
    far = jnp.concatenate([tile_of(values, 2), jnp.where(low, nothing, middle)], axis=1)
    return near.astype(jnp.bfloat16), far.astype(jnp.bfloat16)


def join_second(values):
    low = low_lanes(values.shape[0])
    middle = turned(tile_of(values, 1))
    nothing = jnp.zeros_like(middle)
    near = jnp.concatenate([jnp.where(low, nothing, middle), tile_of(values, 0)], axis=1)
    far = jnp.concatenate([jnp.where(low, middle, nothing), tile_of(values, 2)], axis=1)
    return near.astype(jnp.bfloat16), far.astype(jnp.bfloat16)


def join_both(first, second):
    low = low_lanes(first.shape[0])
    mine, other = tile_of(first, 1), turned(tile_of(second, 1))
    return jnp.concatenate(
        [
            tile_of(first, 0), jnp.where(low, mine, other), tile_of(second, 0),
            tile_of(first, 2), jnp.where(low, other, mine), tile_of(second, 2),
        ],
        axis=1,
    ).astype(jnp.bfloat16)


def block_of(pair, y, at):
    if len(pair.shape) == 3:
        return pair[y, :, at]
    return pair[y, :, :, :, at].reshape(768, -1)


def times_first(values, pair):
    tiles = []
    for y in range(2):
        tiles += split_first(mm(values, block_of(pair, y, slice(0, 256))), mm(values, block_of(pair, y, slice(384, 640))))
    return tiles


def times_second(values, pair):
    tiles = []
    for y in range(2):
        tiles += split_second(mm(values, block_of(pair, y, slice(128, 384))), mm(values, block_of(pair, y, slice(512, 768))))
    return tiles


def back_first(grads, pair):
    out = None
    for y in range(2):
        near, far = join_first(grads[:, y * 384:(y + 1) * 384])
        part = mm_back(near, block_of(pair, y, slice(0, 256))) + mm_back(far, block_of(pair, y, slice(384, 640)))
        out = part if out is None else out + part
    return out


def back_second(grads, pair):
    out = None
    for y in range(2):
        near, far = join_second(grads[:, y * 384:(y + 1) * 384])
        part = mm_back(near, block_of(pair, y, slice(128, 384))) + mm_back(far, block_of(pair, y, slice(512, 768)))
        out = part if out is None else out + part
    return out


def normed(values, gain, bias):
    return norm_rows(values, gain, bias).astype(jnp.bfloat16)


def normed_back(values, gain, grads):
    centre = values - jnp.mean(values, axis=-1, keepdims=True)
    scale = lax.rsqrt(jnp.mean(centre * centre, axis=-1, keepdims=True) + EPS)
    unit = centre * scale
    inner = grads * gain
    back = scale * (
        inner - jnp.mean(inner, axis=-1, keepdims=True) - unit * jnp.mean(inner * unit, axis=-1, keepdims=True)
    )
    return back, jnp.sum(grads * unit, axis=0, keepdims=True), jnp.sum(grads, axis=0, keepdims=True)


def column_sum(values):
    return jnp.sum(values.astype(jnp.float32), axis=0, keepdims=True)


def both_heads(both):
    low = low_lanes(both.shape[0])
    nothing = jnp.zeros_like(both)
    return jnp.concatenate([jnp.where(low, both, nothing), jnp.where(low, nothing, both)], axis=0)


def stacked(values, t, pair):
    return both_heads(values[t, :, pair * 128:(pair + 1) * 128])


def third_head(tile, core):
    lane = lax.broadcasted_iota(jnp.int32, tile.shape, 1)
    return jnp.where(lax.shift_right_logical(lane, 6) == core, tile, jnp.zeros_like(tile))


def unstacked(values):
    half = values.shape[0] // 2
    return jnp.where(low_lanes(half), values[:half], values[half:])


CHUNK = 16


def soften(scores, bias, chances, rows, width):
    def one(number, carry):
        first = pl.multiple_of(number * CHUNK, CHUNK)
        values = scores[pl.ds(first, CHUNK), 0:width] + bias(first)
        raised = jnp.exp(values - jnp.max(values, axis=1, keepdims=True))
        share = raised * (1.0 / jnp.sum(raised, axis=1, keepdims=True))
        chances[pl.ds(first, CHUNK), 0:width] = share.astype(jnp.bfloat16)
        return carry

    lax.fori_loop(0, rows // CHUNK, one, 0, unroll=7)


def soften_back(chances, slopes, grads, rows, width):
    def one(number, carry):
        first = pl.multiple_of(number * CHUNK, CHUNK)
        share = chances[pl.ds(first, CHUNK), 0:width].astype(jnp.float32)
        slope = slopes[pl.ds(first, CHUNK), 0:width]
        inner = jnp.sum(share * slope, axis=1, keepdims=True)
        grads[pl.ds(first, CHUNK), 0:width] = (share * (slope - inner)).astype(jnp.bfloat16)
        return carry

    lax.fori_loop(0, rows // CHUNK, one, 0, unroll=7)


def self_forward(lengths, tokens, vec, heads, a_out, rows_out, third_out, p_out, o_out, scores, bias):
    span = tokens.shape[2]
    z, x, y, core = where_am_i()
    factor = 1.0 / math.sqrt(HEAD_DIM)
    for s in range(4):
        for t in range(2):
            a_out[t, s] = normed(tokens[s, t].astype(jnp.float32), vec[0:1], vec[1:2])
    yield None
    lane = lax.broadcasted_iota(jnp.int32, (1, 128), 1)
    mine = lax.shift_right_logical(lane, 6) == core
    nothing = jnp.zeros((1, 128), jnp.float32)
    query_pair, query_third = own_tiles(vec[2:3], y, core)
    value_pair, value_third = own_tiles(vec[3:4], y, core)
    offset = jnp.concatenate([query_pair, nothing, value_pair, query_third, value_third], axis=1)
    ones = nothing + 1.0
    scale = jnp.concatenate([ones * factor, ones, ones, jnp.where(mine, ones * factor, ones), ones], axis=1)
    for t in range(2):
        row = lax.broadcasted_iota(jnp.int32, (4 * span, 512), 0)
        place = lax.broadcasted_iota(jnp.int32, (4 * span, 512), 1)
        bias[t] = jnp.where((place <= row) & (place < lengths[t]), 0.0, NEG)
        product = mm(a_out[t].reshape(4 * span, 768), heads[...].reshape(768, 640))
        product = (product + offset) * scale
        rows_out[t, 0:4 * span] = product.astype(jnp.bfloat16)
        rows_out[t, 4 * span:512] = jnp.zeros((512 - 4 * span, 640), jnp.bfloat16)
        third_out[t, 0:4 * span] = turned(product[:, 384:512]).astype(jnp.bfloat16)
        third_out[t, 4 * span:512] = jnp.zeros((512 - 4 * span, 128), jnp.bfloat16)
        yield None
    for t in range(2):
        for block in range(4):
            rows, width = slice(block * span, (block + 1) * span), 128 * (block + 1)
            scores[0:2 * span, 0:width] = mm_back(
                both_heads(rows_out[t, rows, 0:128]), rows_out[t, 0:width, 128:256]
            )
            scores[2 * span:3 * span, 0:width] = mm_back(
                third_head(rows_out[t, rows, 384:512], core), third_out[t, 0:width]
            )
            chances = p_out.at[t, block]
            soften(
                scores, lambda first: bias[t, pl.ds(block * span + lax.rem(first, span), CHUNK), 0:width], chances,
                3 * span, width,
            )
            blended = mm(chances[0:2 * span, 0:width], rows_out[t, 0:width, 256:384])
            o_out[block, t, :, 0:128] = unstacked(blended).astype(jnp.bfloat16)
            blended = mm(chances[2 * span:3 * span, 0:width], rows_out[t, 0:width, 512:640])
            o_out[block, t, :, 128:256] = blended.astype(jnp.bfloat16)
            yield t if block == 3 else None


def self_out(tokens, vec, mixer, o_got, o_out, h1_out, c_out):
    span = tokens.shape[2]
    seq = lax.axis_index("seq")
    low = low_lanes(span)
    for t in range(2):
        for y in range(2):
            even, odd = o_got[2 * y, t], o_got[2 * y + 1, t]
            tiles = [even[:, 0:128], jnp.where(low, even[:, 128:256], odd[:, 128:256]), odd[:, 0:128]]
            for number, tile in enumerate(tiles):
                at = slice(y * 384 + number * 128, y * 384 + (number + 1) * 128)
                o_out[t, :, at] = tile
    rows = o_out[...].reshape(2 * span, 768)
    low = low_lanes(2 * span)
    for y in range(2):
        product = mm(rows, mixer[y].reshape(768, 512))
        tiles = [product[:, 0:128], jnp.where(low, product[:, 128:256], product[:, 384:512]), product[:, 256:384]]
        for number, tile in enumerate(tiles):
            at = slice(y * 384 + number * 128, y * 384 + (number + 1) * 128)
            for t in range(2):
                h1_out[t, :, at] = (
                    tokens[seq, t, :, at].astype(jnp.float32) + tile[t * span:(t + 1) * span] + vec[4:5, at]
                )
    for t in range(2):
        c_out[t] = normed(h1_out[t], vec[5:6], vec[6:7])


def cross_keys(frames, vec, kv, ck_out, cv_out):
    for t in range(2):
        for s in range(4):
            block = frames[t, s]
            rows = slice(s * 384, (s + 1) * 384)
            for y in range(2):
                product = mm(block, block_of(kv, y, slice(0, 768)))
                near, far = product[:, 0:384], product[:, 384:768]
                keys = split_first(near[:, 0:256], far[:, 0:256])
                values = split_second(near[:, 128:384], far[:, 128:384])
                for place in range(3):
                    at = slice(y * 384 + place * 128, y * 384 + (place + 1) * 128)
                    ck_out[t, y * 3 + place, rows] = keys[place].astype(jnp.bfloat16)
                    cv_out[t, y * 3 + place, rows] = (values[place] + vec[8:9, at]).astype(jnp.bfloat16)
            yield


def cross_forward(counts, frame_span, c, vec, xqo, ck, cv, h1, cq_out, o2_out, h2_out, m_out, p_out, scores, bias):
    span = c.shape[1]
    factor = 1.0 / math.sqrt(HEAD_DIM)
    rows = c[...].reshape(2 * span, 768)
    for number, tile in enumerate(times_first(rows, xqo)):
        at = slice(number * 128, (number + 1) * 128)
        tile = ((tile + vec[7:8, at]) * factor).astype(jnp.bfloat16)
        for t in range(2):
            cq_out[t, :, at] = tile[t * span:(t + 1) * span]
    for t in range(2):
        for s in range(4):
            inside = lax.broadcasted_iota(jnp.int32, (1, 384), 1)
            good = (inside < frame_span) & (s * frame_span + inside < counts[t])
            bias[t, :, s * 384:(s + 1) * 384] = jnp.where(good, 0.0, NEG)
    yield
    for t in range(2):
        for pair in range(6):
            at = slice(pair * 128, (pair + 1) * 128)
            scores[...] = mm_back(stacked(cq_out, t, pair), ck[t, pair])
            chances = p_out.at[t, pair]
            soften(scores, lambda first: bias[t], chances, 2 * span, 1536)
            o2_out[t, :, at] = unstacked(mm(chances[...], cv[t, pair])).astype(jnp.bfloat16)
            yield
    out = o2_out[...].reshape(2 * span, 768)
    for number, tile in enumerate(times_second(out, xqo)):
        at = slice(number * 128, (number + 1) * 128)
        for t in range(2):
            h2_out[t, :, at] = h1[t, :, at] + tile[t * span:(t + 1) * span] + vec[9:10, at]
    for t in range(2):
        m_out[t] = normed(h2_out[t], vec[10:11], vec[11:12])
    yield


class Summing:
    def __init__(self, mail, place, mates, acc, diag_x, diag_y, x_in, y_in, z_in, total):
        self.mail, self.place, self.mates = mail, place, mates
        self.acc, self.diag_x, self.diag_y = acc, diag_x, diag_y
        self.x_in, self.y_in, self.z_in, self.total = x_in, y_in, z_in, total
        self.slots = [mail.slots(4 + NZ - 1) for _ in range(acc.shape[0])]

    def begin(self, n):
        z, x, y = self.place
        x_mate, y_mate, _ = self.mates
        self.mail.post(self.acc.at[n, 1 - y, pl.ds(0, 2), 1 - x], self.diag_x.at[n], self.slots[n][0], x_mate)
        self.mail.post(self.acc.at[n, 1 - y, pl.ds(2, 2), 1 - x], self.diag_y.at[n], self.slots[n][1], y_mate)

    def side(self, n):
        z, x, y = self.place
        x_mate, y_mate, _ = self.mates
        self.mail.arrive(self.diag_x.at[n], self.slots[n][0], x_mate)
        for k in range(2):
            self.acc[n, 1 - y, k, x] = self.acc[n, 1 - y, k, x] + self.diag_x[n, k]
        self.mail.post(self.acc.at[n, 1 - y, :, x], self.y_in.at[n], self.slots[n][2], y_mate)
        self.mail.arrive(self.diag_y.at[n], self.slots[n][1], y_mate)
        for k in range(2):
            self.acc[n, y, 2 + k, 1 - x] = self.acc[n, y, 2 + k, 1 - x] + self.diag_y[n, k]
        self.mail.post(self.acc.at[n, y, :, 1 - x], self.x_in.at[n], self.slots[n][3], x_mate)

    def column(self, n):
        z, x, y = self.place
        x_mate, y_mate, z_mates = self.mates
        self.mail.arrive(self.y_in.at[n], self.slots[n][2], y_mate)
        self.mail.arrive(self.x_in.at[n], self.slots[n][3], x_mate)
        for k in range(NZ):
            self.acc[n, y, k, x] = (
                self.acc[n, y, k, x].astype(jnp.float32)
                + self.x_in[n, k].astype(jnp.float32)
                + self.y_in[n, k].astype(jnp.float32)
            ).astype(jnp.bfloat16)
        for k in range(1, NZ):
            zz = lax.rem(z + k, NZ)
            self.mail.post(self.acc.at[n, y, zz, x], self.z_in.at[n, k - 1], self.slots[n][3 + k], z_mates[k - 1])

    def last(self, n):
        z, x, y = self.place
        _, _, z_mates = self.mates
        for k in range(1, NZ):
            self.mail.arrive(self.z_in.at[n, k - 1], self.slots[n][3 + k], z_mates[k - 1])
        self.total[n] = self.acc[n, y, z, x].astype(jnp.float32) + (
            self.z_in[n, 0].astype(jnp.float32) + self.z_in[n, 1].astype(jnp.float32)
        ) + self.z_in[n, 2].astype(jnp.float32)


def summing_scratch(n, width=384):
    piece = (96, width)
    shapes = [
        (n, NY, NZ, NX) + piece, (n, 2) + piece, (n, 2) + piece, (n, NZ) + piece, (n, NZ) + piece, (n, NZ - 1) + piece
    ]
    return [pltpu.VMEM(shape, jnp.bfloat16) for shape in shapes]


class Loads:
    def __init__(self, sems):
        self.sems, self.count = sems, 0

    def start(self, source, target):
        copy = pltpu.make_async_copy(source, target, self.sems.at[self.count])
        copy.start()
        self.count += 1
        return copy


def two(first, second):
    return jnp.concatenate([first, second], axis=0)


def feed_kernel(
    lengths, ids, weights, cotangent, vec, wide_bias, h2, m, o2, c, h1, cq,
    wide_far, tall_far, pairs_far, frames_far, ck_far, cv_far, p_far,
    y_out, dh1_out, total, acc_kv, acc_xqo, small_out, wide_small,
    acc, diag_x, diag_y, x_in, y_in, z_in,
    wide, tall, xqo, frames, keys_here, values_here, p_here,
    m_sib, g_own, g_sib, du_own, du_send, du_sib, dz_own, dz_send, dz_sib,
    o2_sib, c_sib, xb_own, xb_send, xb_sib, xa_own, xa_send, xa_sib, gkv, kv_in,
    dy, dh2, do, dq, scores, dscores, gate_slope,
    send_sems, recv_sems, load_sems, unit_sems,
):
    z, x, y, core = where_am_i()
    span = m.shape[1]
    seq = y * NC + core
    factor = 1.0 / math.sqrt(HEAD_DIM)
    low = low_lanes(2 * span)
    x_mate, y_mate, c_mate = device_at(z, 1 - x, y, core), device_at(z, x, 1 - y, core), device_at(z, x, y, 1 - core)
    z_mates = [device_at(lax.rem(z + n, NZ), x, y, core) for n in range(1, NZ)]
    loads = Loads(load_sems)
    order = [(yy, side) for yy in range(2) for side in range(2)]
    block_loads = []
    for yy, side in order:
        at = lanes((2 * yy + (core if side == 0 else 1 - core)) * 768, 768)
        block_loads.append((
            loads.start(wide_far.at[:, :, :, at], wide.at[:, :, :, at]),
            loads.start(tall_far.at[:, :, :, at], tall.at[:, :, :, at]),
        ))
    xqo_load = loads.start(pairs_far.at[1], xqo)
    frames_load = loads.start(frames_far, frames)
    units = [(pair, t) for pair in range(6) for t in range(2)]

    def unit_copies(n):
        pair, t = units[n]
        slot = n % 2
        return [
            pltpu.make_async_copy(ck_far.at[t, pair], keys_here.at[slot], unit_sems.at[slot, 0]),
            pltpu.make_async_copy(cv_far.at[t, pair], values_here.at[slot], unit_sems.at[slot, 1]),
            pltpu.make_async_copy(p_far.at[t, pair], p_here.at[slot], unit_sems.at[slot, 2]),
        ]

    for copy in unit_copies(0):
        copy.start()
    greet(z, x, y, core)
    mail = Mail(send_sems, recv_sems)
    sums = Summing(mail, (z, x, y), (x_mate, y_mate, z_mates), acc, diag_x, diag_y, x_in, y_in, z_in, total)
    swap = mail.slots(1 + 2 + 4 + 2 + 2 + 2 + 1)
    m_slot, dz_slots, g_slots, du_slots = swap[0], swap[1:3], swap[3:7], swap[7:9]
    xb_slots, xa_slots, kv_slot = swap[9:11], swap[11:13], swap[13]
    o2_slot, c_slot = mail.slots(2)
    mail.post(m, m_sib, m_slot, c_mate)
    mail.post(o2, o2_sib, o2_slot, c_mate)
    mail.post(c, c_sib, c_slot, c_mate)

    for t in range(2):
        weight = 0.0
        for corpus in range(weights.shape[0]):
            weight = weight + jnp.where(ids[t] == corpus, weights[corpus], 0.0)
        row = lax.broadcasted_iota(jnp.int32, (span, 1), 0) + seq * span
        scale = jnp.where(row < lengths[t], weight, 0.0)
        dy[t * span:(t + 1) * span] = cotangent[t].astype(jnp.float32) * scale
    dz = dy[...].astype(jnp.bfloat16)
    dz_wide = dz.astype(jnp.float32)
    small_out[...] = jnp.zeros_like(small_out)
    small_out[12:13] = column_sum(dz_wide)
    for yy in range(2):
        tiles = [dz_wide[:, yy * 384 + n * 128:yy * 384 + (n + 1) * 128] for n in range(3)]
        even = jnp.concatenate([tiles[0], tiles[1]], axis=1)
        last = turned(tiles[2])
        odd = jnp.concatenate([jnp.where(low, turned(tiles[1]), last), last], axis=1)
        dz_own[yy] = jnp.where(core == 0, even, odd).astype(jnp.bfloat16)
        dz_send[yy] = jnp.where(core == 0, odd, even).astype(jnp.bfloat16)
        mail.post(dz_send.at[yy], dz_sib.at[yy], dz_slots[yy], c_mate)
    rows = m[...].reshape(2 * span, 768)
    for number, (yy, side) in enumerate(order):
        at = lanes((2 * yy + (core if side == 0 else 1 - core)) * 768, 768)
        for copy in block_loads[number]:
            copy.wait()
        hidden = mm(rows, wide[:, :, :, at].reshape(768, 768)) + wide_bias[:, at]
        bell = 0.5 * (1.0 + lax.erf(hidden * 0.7071067811865476))
        g_own[:, at] = (hidden * bell).astype(jnp.bfloat16)
        mail.post(g_own.at[:, at], g_sib.at[:, at], g_slots[number], c_mate)
        gate_slope[:, at] = bell + hidden * (jnp.exp(-0.5 * hidden * hidden) * 0.3989422804014327)
    for number, (yy, side) in enumerate(order):
        at = lanes((2 * yy + (1 - core if side == 0 else core)) * 768, 768)
        mail.arrive(g_sib.at[:, at], g_slots[number], c_mate)
    for yy in range(2):
        mail.arrive(dz_sib.at[yy], dz_slots[yy], c_mate)
    for yy in range(2):
        slopes = two(dz_own[yy], dz_sib[yy])
        for zz in range(NZ):
            at = slice(zz * 768, (zz + 1) * 768)
            product = mm_rows(slopes, two(g_own[:, at], g_sib[:, at])).astype(jnp.bfloat16)
            for xx in range(NX):
                acc[2, yy, zz, xx] = product[0:96, xx * 384:(xx + 1) * 384]
                acc[3, yy, zz, xx] = product[96:192, xx * 384:(xx + 1) * 384]
    sums.begin(2)
    sums.begin(3)
    z_sum, dm_sum = None, None
    for number, (yy, side) in enumerate(order):
        at = lanes((2 * yy + (core if side == 0 else 1 - core)) * 768, 768)
        wide_here = wide[:, :, :, at].reshape(768, 768)
        tall_here = tall[:, :, :, at].reshape(768, 768)
        back = (mm(dz, tall_here) * gate_slope[:, at]).astype(jnp.bfloat16)
        if side == 0:
            du_own[yy] = back
        else:
            du_send[yy] = back
            mail.post(du_send.at[yy], du_sib.at[yy], du_slots[yy], c_mate)
        part = mm_back(g_own[:, at], tall_here)
        z_sum = part if z_sum is None else z_sum + part
        part = mm_back(back, wide_here)
        dm_sum = part if dm_sum is None else dm_sum + part
        wide_small[:, at] = column_sum(back)
    mail.arrive(m_sib, m_slot, c_mate)
    both_rows = two(rows, m_sib[...].reshape(2 * span, 768))
    for yy in range(2):
        mail.arrive(du_sib.at[yy], du_slots[yy], c_mate)
        product = mm_rows(both_rows, two(du_own[yy], du_sib[yy])).astype(jnp.bfloat16)
        acc[0, yy] = product[:, 0:384].reshape(NZ, NX, 96, 384)
        acc[1, yy] = product[:, 384:768].reshape(NZ, NX, 96, 384)
    sums.begin(0)
    sums.begin(1)
    h2_rows = h2[...].reshape(2 * span, 768)
    out = h2_rows + z_sum + vec[12:13]
    back, gain, offset = normed_back(h2_rows, vec[10:11], dm_sum)
    small_out[10:11] = gain
    small_out[11:12] = offset
    dh2[...] = dy[...] + back
    for t in range(2):
        y_out[t] = out[t * span:(t + 1) * span].astype(jnp.bfloat16)

    pending = []
    for step in range(6):
        for lag, action in ((0, sums.side), (1, sums.column), (2, sums.last)):
            if 0 <= step - lag < 4:
                pending.append((action, (2, 3, 0, 1)[step - lag]))

    def tick(number=1):
        for _ in range(number):
            if pending:
                action, group = pending.pop(0)
                action(group)

    low_wide = dh2[...].astype(jnp.bfloat16).astype(jnp.float32)
    small_out[9:10] = column_sum(low_wide)
    xqo_load.wait()
    for yy in range(2):
        near, far = join_second(low_wide[:, yy * 384:(yy + 1) * 384])
        xb_own[yy] = jnp.where(core == 0, near, far)
        xb_send[yy] = jnp.where(core == 0, far, near)
        mail.post(xb_send.at[yy], xb_sib.at[yy], xb_slots[yy], c_mate)
    heard = back_second(low_wide, xqo)
    small_out[8:9] = column_sum(heard.astype(jnp.bfloat16))
    for t in range(2):
        do[t] = heard[t * span:(t + 1) * span].astype(jnp.bfloat16)
    tick()
    frames_load.wait()
    total_kv = None
    for number, (pair, t) in enumerate(units):
        at = slice(pair * 128, (pair + 1) * 128)
        slot = number % 2
        if number + 1 < len(units):
            for copy in unit_copies(number + 1):
                copy.start()
        for copy in unit_copies(number):
            copy.wait()
        slopes, query = stacked(do, t, pair), stacked(cq, t, pair)
        scores[...] = mm_back(slopes, values_here[slot])
        chances = p_here.at[slot]
        soften_back(chances, scores, dscores, 2 * span, 1536)
        dq[t * span:(t + 1) * span, at] = unstacked(mm(dscores[...], keys_here[slot])) * factor
        turned_grads = two(mm_rows(query, dscores[...]), mm_rows(slopes, chances[...])).astype(jnp.bfloat16)
        part = mm(turned_grads, frames[t].reshape(1536, 768))
        total_kv = part if t == 0 else total_kv + part
        if t == 1:
            keys, values = total_kv[0:128].T, total_kv[128:256].T
            yy, place = pair // 3, pair % 3
            if place == 1:
                values = turned(values)
                half = low_lanes(768)
                gkv[0, yy, :, 128:256] = jnp.where(half, keys, values).astype(jnp.bfloat16)
                gkv[1, yy, :, 128:256] = jnp.where(half, values, keys).astype(jnp.bfloat16)
            else:
                gkv[place // 2, yy, :, 0:128] = keys.astype(jnp.bfloat16)
                gkv[place // 2, yy, :, 256:384] = values.astype(jnp.bfloat16)
        if number in (2, 4, 5, 6, 7, 8, 9, 10, 11):
            tick()
    mail.post(gkv.at[1 - core], kv_in, kv_slot, c_mate)
    low_q = dq[...].astype(jnp.bfloat16).astype(jnp.float32)
    small_out[7:8] = column_sum(low_q)
    for yy in range(2):
        near, far = join_first(low_q[:, yy * 384:(yy + 1) * 384])
        xa_own[yy] = jnp.where(core == 0, near, far)
        xa_send[yy] = jnp.where(core == 0, far, near)
        mail.post(xa_send.at[yy], xa_sib.at[yy], xa_slots[yy], c_mate)
    back, gain, offset = normed_back(h1[...].reshape(2 * span, 768), vec[5:6], back_first(low_q, xqo))
    small_out[5:6] = gain
    small_out[6:7] = offset
    for t in range(2):
        dh1_out[t] = dh2[t * span:(t + 1) * span] + back[t * span:(t + 1) * span]
    mail.arrive(o2_sib, o2_slot, c_mate)
    mail.arrive(c_sib, c_slot, c_mate)
    o2_both = two(o2[...].reshape(2 * span, 768), o2_sib[...].reshape(2 * span, 768))
    c_both = two(c[...].reshape(2 * span, 768), c_sib[...].reshape(2 * span, 768))
    for yy in range(2):
        mail.arrive(xb_sib.at[yy], xb_slots[yy], c_mate)
        mail.arrive(xa_sib.at[yy], xa_slots[yy], c_mate)
        second = mm_rows(o2_both, two(xb_own[yy], xb_sib[yy]))
        first = mm_rows(c_both, two(xa_own[yy], xa_sib[yy]))
        store_pair(acc_xqo.at[yy], first, second)
    mail.arrive(kv_in, kv_slot, c_mate)
    for yy in range(2):
        acc_kv[yy] = (gkv[core, yy] + kv_in[yy]).reshape(NZ, NX, 96, 384)
    tick(100)
    mail.finish()


def store_pair(out, first, second):
    shape = (NZ, NX, 96, 128)
    out[:, :, :, 0:128] = tile_of(first, 0).astype(jnp.bfloat16).reshape(shape)
    out[:, :, :, 128:256] = (tile_of(first, 1) + tile_of(second, 0)).astype(jnp.bfloat16).reshape(shape)
    out[:, :, :, 256:384] = tile_of(second, 1).astype(jnp.bfloat16).reshape(shape)


def run_feed(lengths, ids, weights, near, far):
    bf16, f32 = jnp.bfloat16, jnp.float32
    span = near[4].shape[1]
    rows, flat = (2, span, 768), 2 * span
    inside, anywhere = pl.BlockSpec(memory_space=pltpu.VMEM), pl.BlockSpec(memory_space=pl.ANY)
    scalar = pl.BlockSpec(memory_space=pltpu.SMEM)
    piece = (NY, NZ, NX, 96, 384)
    number = 4 * 7 + 16
    scratch = [
        ((NZ, NX, 96, 3072), bf16), ((NY, NC, 192, 3072), bf16), ((NY, NZ, NX, 96, 768), bf16), (far[3].shape, bf16),
        ((2, 1536, 128), bf16), ((2, 1536, 128), bf16), ((2, flat, 1536), bf16),
        (rows, bf16), ((flat, 3072), bf16), ((flat, 3072), bf16),
        ((2, flat, 768), bf16), ((2, flat, 768), bf16), ((2, flat, 768), bf16),
        ((2, flat, 256), bf16), ((2, flat, 256), bf16), ((2, flat, 256), bf16),
        (rows, bf16), (rows, bf16),
    ] + [((2, flat, 256), bf16)] * 6 + [
        ((2, 2, 768, 384), bf16), ((2, 768, 384), bf16),
        ((flat, 768), f32), ((flat, 768), f32), (rows, bf16), ((flat, 768), f32), ((flat, 1536), f32),
        ((flat, 1536), bf16), ((flat, 3072), f32),
    ]
    return pl.pallas_call(
        feed_kernel,
        out_shape=(
            jax.ShapeDtypeStruct(rows, bf16), jax.ShapeDtypeStruct(rows, f32),
            jax.ShapeDtypeStruct((4, 96, 384), f32),
            jax.ShapeDtypeStruct(piece, bf16), jax.ShapeDtypeStruct(piece, bf16),
            jax.ShapeDtypeStruct((16, 768), f32), jax.ShapeDtypeStruct((1, 3072), f32),
        ),
        in_specs=[scalar] * 3 + [inside] * len(near) + [anywhere] * len(far),
        out_specs=(inside,) * 7,
        scratch_shapes=summing_scratch(4) + [pltpu.VMEM(shape, kind) for shape, kind in scratch] + [
            pltpu.SemaphoreType.DMA((number,)),
            pltpu.SemaphoreType.DMA((number,)),
            pltpu.SemaphoreType.DMA((10,)),
            pltpu.SemaphoreType.DMA((2, 3)),
        ],
        compiler_params=pltpu.CompilerParams(
            collective_id=2, has_side_effects=True, vmem_limit_bytes=60 << 20
        ),
        name="feed_cross_back",
    )(lengths, ids, weights, *near, *far)


def last_kernel(
    tokens, dh1, o, vec, small_before, wide_small,
    heads_far, mixer_far, kv_far, xqo_far, a_far, rows_far, third_far, p_far,
    dx_out, total, total_o, total_q, small_total,
    acc, diag_x, diag_y, x_in, y_in, z_in,
    acc_o, diag_x_o, diag_y_o, x_in_o, y_in_o, z_in_o,
    acc_q, x_in_q, z_in_q,
    a, head_rows, third, p, heads, mixer, o_sib, ob_own, ob_send, ob_sib, do_send, do_got, kv_sum, dq_third, dheads,
    da_send, da_core, da_side, scores, dscores,
    small, pack, pack_in, pack_sum, pack_seq,
    send_sems, recv_sems, load_sems,
):
    z, x, y, core = where_am_i()
    span = o.shape[1]
    seq = y * NC + core
    grp = z * NX + x
    factor = 1.0 / math.sqrt(HEAD_DIM)
    x_mate, y_mate, c_mate = device_at(z, 1 - x, y, core), device_at(z, x, 1 - y, core), device_at(z, x, y, 1 - core)
    far_mate = device_at(z, x, 1 - y, 1 - core)
    z_mates = [device_at(lax.rem(z + n, NZ), x, y, core) for n in range(1, NZ)]
    loads = Loads(load_sems)
    mixer_load = loads.start(mixer_far, mixer)
    acc_loads = [loads.start(kv_far, acc.at[0]), loads.start(xqo_far, acc.at[1])]
    unit_loads = [loads.start(rows_far, head_rows), loads.start(third_far, third), loads.start(p_far, p)]
    heads_load = loads.start(heads_far, heads)
    a_load = loads.start(a_far, a)
    greet(z, x, y, core)
    mail = Mail(send_sems, recv_sems)
    mates3 = (x_mate, y_mate, z_mates)
    sums = Summing(mail, (z, x, y), mates3, acc, diag_x, diag_y, x_in, y_in, z_in, total)
    sums_o = Summing(mail, (z, x, y), mates3, acc_o, diag_x_o, diag_y_o, x_in_o, y_in_o, z_in_o, total_o)
    (o_slot,) = mail.slots(1)
    ob_slots, do_slots = mail.slots(2), mail.slots(6)
    core_slots, side_slots = mail.slots(4), mail.slots(2)
    xq_slots, zq_slots = mail.slots(2), mail.slots(6)
    pack_slots, seq_slots = mail.slots(2 * NZ - 1), mail.slots(2)
    mail.post(o, o_sib, o_slot, c_mate)
    small[...] = small_before[...]
    low_wide = dh1[...].reshape(2 * span, 768).astype(jnp.bfloat16).astype(jnp.float32)
    small[4:5] = column_sum(low_wide)
    heard = None
    mixer_load.wait()
    for yy in range(2):
        near, far = join_first(low_wide[:, yy * 384:(yy + 1) * 384])
        ob_own[yy] = jnp.where(core == 0, near, far)
        ob_send[yy] = jnp.where(core == 0, far, near)
        mail.post(ob_send.at[yy], ob_sib.at[yy], ob_slots[yy], c_mate)
        part = mm_back(jnp.concatenate([near, far], axis=1), mixer[yy].reshape(768, 512))
        heard = part if heard is None else heard + part
    for yy in range(2):
        near, far = join_first(heard[:, yy * 384:(yy + 1) * 384])
        for t in range(2):
            do_send[2 * yy, t] = near[t * span:(t + 1) * span]
            do_send[2 * yy + 1, t] = far[t * span:(t + 1) * span]
    mates = (
        (c_mate, y * NC + 1 - core), (y_mate, (1 - y) * NC + core), (far_mate, (1 - y) * NC + 1 - core)
    )
    for t in range(2):
        for place in (2, 1, 0):
            mate, mate_seq = mates[place]
            mail.post(do_send.at[mate_seq, t], do_got.at[seq, t], do_slots[3 * t + place], mate)
        do_got[seq, t] = do_send[seq, t]
    for copy in acc_loads:
        copy.wait()
    sums.begin(0)
    sums.begin(1)
    mail.arrive(o_sib, o_slot, c_mate)
    o_both = two(o[...].reshape(2 * span, 768), o_sib[...].reshape(2 * span, 768))
    for yy in range(2):
        mail.arrive(ob_sib.at[yy], ob_slots[yy], c_mate)
        product = mm_rows(o_both, two(ob_own[yy], ob_sib[yy])).astype(jnp.bfloat16)
        acc_o[0, yy] = product.reshape(NZ, NX, 96, 256)
    sums_o.begin(0)
    pending = [
        (sums.side, 0), (sums.side, 1), (sums_o.side, 0), (sums.column, 0), (sums.column, 1), (sums_o.column, 0),
        (sums.last, 0), (sums.last, 1), (sums_o.last, 0),
    ]

    def tick(number=1):
        for _ in range(number):
            if pending:
                action, group = pending.pop(0)
                action(group)

    def exchange_core(t):
        mail.post(da_send.at[y * NC + 1 - core, t], da_core.at[t, 0], core_slots[2 * t], c_mate)
        mail.post(da_send.at[(1 - y) * NC + 1 - core, t], da_core.at[t, 1], core_slots[2 * t + 1], c_mate)

    def exchange_side(t):
        mail.arrive(da_core.at[t, 1], core_slots[2 * t + 1], c_mate)
        across = (1 - y) * NC + core
        da_send[across, t] = da_send[across, t] + da_core[t, 1]
        mail.post(da_send.at[across, t], da_side.at[t], side_slots[t], y_mate)

    for copy in unit_loads:
        copy.wait()
    heads_load.wait()
    for t in range(2):
        for place, (mate, mate_seq) in enumerate(mates):
            mail.arrive(do_got.at[mate_seq, t], do_slots[3 * t + place], mate)
        for block in (3, 2, 1, 0):
            rows, width = slice(block * span, (block + 1) * span), 128 * (block + 1)
            slopes, slopes_third = both_heads(do_got[block, t, :, 0:128]), do_got[block, t, :, 128:256]
            query = both_heads(head_rows[t, rows, 0:128])
            query_third = third_head(head_rows[t, rows, 384:512], core)
            scores[0:2 * span, 0:width] = mm_back(slopes, head_rows[t, 0:width, 256:384])
            scores[2 * span:3 * span, 0:width] = mm_back(slopes_third, head_rows[t, 0:width, 512:640])
            chances = p.at[t, block]
            soften_back(chances, scores, dscores, 3 * span, width)
            pair_grads, third_grads = dscores[0:2 * span, 0:width], dscores[2 * span:3 * span, 0:width]
            dheads[t, rows, 0:128] = (
                unstacked(mm(pair_grads, head_rows[t, 0:width, 128:256])) * factor
            ).astype(jnp.bfloat16)
            dq_third[rows] = third_head(mm(third_grads, third[t, 0:width]) * factor, core)
            parts = (
                mm_rows(query, pair_grads), mm_rows(query_third, third_grads),
                mm_rows(slopes, chances[0:2 * span, 0:width]), mm_rows(slopes_third, chances[2 * span:3 * span, 0:width]),
            )
            for number, part in enumerate(parts):
                if block == 3:
                    kv_sum[number] = part
                else:
                    kv_sum[number, :, 0:width] += part
            if t == 1 and block == 3:
                exchange_side(0)
            elif (t, block) in ((0, 1), (0, 0), (1, 1), (1, 0)):
                tick()
        keys, keys_third, values, values_third = [kv_sum[number].T[0:4 * span] for number in range(4)]
        dheads[t, :, 128:256] = keys.astype(jnp.bfloat16)
        dheads[t, :, 256:384] = values.astype(jnp.bfloat16)
        dheads[t, :, 384:512] = (dq_third[...] + turned(keys_third)).astype(jnp.bfloat16)
        dheads[t, :, 512:640] = values_third.astype(jnp.bfloat16)
        if t == 1:
            a_load.wait()
            inputs = two(a[0].reshape(4 * span, 768), a[1].reshape(4 * span, 768))
            product = mm_rows(inputs, two(dheads[0], dheads[1])).astype(jnp.bfloat16)
            acc_q[...] = product.reshape(NZ, NX, 96, 640)
            for part, at in enumerate((slice(0, 384), slice(384, 640))):
                mail.post(acc_q.at[:, 1 - x, :, at], x_in_q.at[:, :, at], xq_slots[part], x_mate)
        back = mm_back(dheads[t], heads[...].reshape(768, 640)).astype(jnp.bfloat16)
        for s in range(4):
            da_send[s, t] = back[s * span:(s + 1) * span]
        exchange_core(t)
    tick(1)
    exchange_side(1)
    tick(1)
    sums_q = [column_sum(two(dheads[0, :, n * 128:(n + 1) * 128], dheads[1, :, n * 128:(n + 1) * 128])) for n in (0, 2, 3, 4)]
    small[2:3] = natural_row(sums_q[0], third_head(sums_q[2], core), y, core)
    small[3:4] = natural_row(sums_q[1], sums_q[3], y, core)
    for part, at in enumerate((slice(0, 384), slice(384, 640))):
        mail.arrive(x_in_q.at[:, :, at], xq_slots[part], x_mate)
        for k in range(NZ):
            acc_q[k, x, :, at] = acc_q[k, x, :, at] + x_in_q[k, :, at]
        for k in range(1, NZ):
            zz = lax.rem(z + k, NZ)
            mail.post(
                acc_q.at[zz, x, :, at], z_in_q.at[k - 1, :, at], zq_slots[3 * part + k - 1], z_mates[k - 1]
            )
    gain, offset = None, None
    for t in range(2):
        mail.arrive(da_core.at[t, 0], core_slots[2 * t], c_mate)
        mail.arrive(da_side.at[t], side_slots[t], y_mate)
        back = (
            da_send[seq, t].astype(jnp.float32) + da_core[t, 0].astype(jnp.float32) + da_side[t].astype(jnp.float32)
        )
        part, gain_part, offset_part = normed_back(tokens[t].astype(jnp.float32), vec[0:1], back)
        dx_out[t] = (dh1[t] + part).astype(jnp.bfloat16)
        gain = gain_part if t == 0 else gain + gain_part
        offset = offset_part if t == 0 else offset + offset_part
    small[0:1] = gain
    small[1:2] = offset
    for g in range(8):
        pack[g, 0:16, 0:96] = small[:, g * 96:(g + 1) * 96]
        pack[g, 0:16, 96:128] = jnp.zeros((16, 32), jnp.float32)
        for n in range(3):
            at = g * 384 + n * 128
            pack[g, 16 + n:17 + n, :] = wide_small[:, at:at + 128]
        pack[g, 19:24, :] = jnp.zeros((5, 128), jnp.float32)
    pack_to = [(lax.rem(z + n, NZ), x) for n in range(1, NZ)]
    pack_to += [(lax.rem(z + n, NZ), 1 - x) for n in range(NZ)]
    for number, (zz, xx) in enumerate(pack_to):
        mail.post(pack.at[zz * NX + xx], pack_in.at[number], pack_slots[number], device_at(zz, xx, y, core))
    tick(100)
    for number in range(2 * NZ - 1):
        mail.arrive(pack_in.at[number], pack_slots[number], x_mate)
    pack_sum[...] = (
        (pack[grp] + pack_in[0]) + (pack_in[1] + pack_in[2])
        + ((pack_in[3] + pack_in[4]) + (pack_in[5] + pack_in[6]))
    )
    mail.post(pack_sum, pack_seq.at[0], seq_slots[0], c_mate)
    mail.arrive(pack_seq.at[0], seq_slots[0], c_mate)
    pack_seq[1] = pack_sum[...] + pack_seq[0]
    mail.post(pack_seq.at[1], pack_seq.at[2], seq_slots[1], y_mate)
    for part, at in enumerate((slice(0, 384), slice(384, 640))):
        for k in range(1, NZ):
            mail.arrive(z_in_q.at[k - 1, :, at], zq_slots[3 * part + k - 1], z_mates[k - 1])
        total_q[:, at] = (acc_q[z, x, :, at].astype(jnp.float32) + z_in_q[0, :, at].astype(jnp.float32)) + (
            z_in_q[1, :, at].astype(jnp.float32) + z_in_q[2, :, at].astype(jnp.float32)
        )
    mail.arrive(pack_seq.at[2], seq_slots[1], y_mate)
    small_total[...] = pack_seq[1] + pack_seq[2]
    mail.finish()


def run_last(near, far):
    bf16, f32 = jnp.bfloat16, jnp.float32
    span = near[0].shape[1]
    rows, flat = (2, span, 768), 2 * span
    inside, anywhere = pl.BlockSpec(memory_space=pltpu.VMEM), pl.BlockSpec(memory_space=pl.ANY)
    number = 3 * 7 + 1 + 2 + 6 + 6 + 8 + 9
    scratch = [
        ((NZ, NX, 96, 640), bf16), ((NZ, 96, 640), bf16), ((NZ - 1, 96, 640), bf16),
    ] + [(ref.shape, bf16) for ref in far[4:]] + [
        ((NZ, NX, 96, 640), bf16), ((NY, NZ, NX, 96, 512), bf16), (rows, bf16),
        ((2, flat, 256), bf16), ((2, flat, 256), bf16), ((2, flat, 256), bf16),
        ((4, 2, span, 256), bf16), ((4, 2, span, 256), bf16), ((4, 128, 512), f32), ((4 * span, 128), f32),
        ((2, 4 * span, 640), bf16), ((4, 2, span, 768), bf16), ((2, 2, span, 768), bf16), ((2, span, 768), bf16),
        ((3 * span, 512), f32), ((3 * span, 512), bf16),
        ((16, 768), f32), ((8, 24, 128), f32), ((7, 24, 128), f32), ((24, 128), f32), ((3, 24, 128), f32),
    ]
    return pl.pallas_call(
        last_kernel,
        out_shape=(
            jax.ShapeDtypeStruct(rows, bf16), jax.ShapeDtypeStruct((2, 96, 384), f32),
            jax.ShapeDtypeStruct((1, 96, 256), f32), jax.ShapeDtypeStruct((96, 640), f32),
            jax.ShapeDtypeStruct((24, 128), f32),
        ),
        in_specs=[inside] * len(near) + [anywhere] * len(far),
        out_specs=(inside,) * 5,
        scratch_shapes=summing_scratch(2) + summing_scratch(1, 256) + [
            pltpu.VMEM(shape, kind) for shape, kind in scratch
        ] + [
            pltpu.SemaphoreType.DMA((number,)),
            pltpu.SemaphoreType.DMA((number,)),
            pltpu.SemaphoreType.DMA((8,)),
        ],
        compiler_params=pltpu.CompilerParams(
            collective_id=3, has_side_effects=True, vmem_limit_bytes=60 << 20
        ),
        name="self_back_sum",
    )(*near, *far)


def place_kernel(
    y, dx, total, total_o, total_q, total_ff, small,
    y_out, dx_out, query, key, value, mixer, xkey, xvalue, xquery, xmixer, wide, tall, *more,
):
    vectors, wide_bias = more[:13], more[13]
    core = lax.rem(lax.axis_index("seq"), NC)
    y_out[...] = y[...]
    dx_out[...] = dx[...]

    def put(out, even, odd):
        @pl.when(core == 0)
        def _():
            out[...] = jnp.concatenate(even, axis=1)

        @pl.when(core != 0)
        def _():
            out[...] = jnp.concatenate(odd, axis=1)

    heads = total_q[...]
    for out, pair, even, odd in ((query, 0, 384, 448), (key, 128, 448, 384), (value, 256, 512, 576)):
        whole = heads[:, pair:pair + 128]
        put(out, [whole, heads[:, even:even + 64]], [heads[:, odd:odd + 64], whole])
    piece = total_o[0]
    put(mixer, [piece[:, :192]], [piece[:, 192:], piece[:, :128]])
    for number, (first, second) in enumerate(((xkey, xvalue), (xquery, xmixer))):
        piece = total[number]
        put(first, [piece[:, :192]], [piece[:, 192:256], piece[:, :128]])
        put(second, [piece[:, 256:], piece[:, 192:256]], [piece[:, 128:192], piece[:, 256:]])
    wide[:, :384] = total_ff[0]
    wide[:, 384:] = total_ff[1]
    tall[:96] = total_ff[2]
    tall[96:] = total_ff[3]
    for number, out in enumerate(vectors):
        out[...] = small[number:number + 1, 0:96]
    for number in range(3):
        wide_bias[:, number * 128:(number + 1) * 128] = small[16 + number:17 + number]


def run_place(y, dx, *totals):
    f32 = jnp.float32
    inside = pl.BlockSpec(memory_space=pltpu.VMEM)
    like = jax.ShapeDtypeStruct(y.shape, y.dtype)
    return pl.pallas_call(
        place_kernel,
        out_shape=(like, like) + (jax.ShapeDtypeStruct((96, 192), f32),) * 8 + (
            jax.ShapeDtypeStruct((96, 768), f32), jax.ShapeDtypeStruct((192, 384), f32),
        ) + (jax.ShapeDtypeStruct((1, 96), f32),) * 13 + (jax.ShapeDtypeStruct((1, 384), f32),),
        in_specs=[inside] * 7,
        out_specs=(inside,) * 26,
        compiler_params=pltpu.CompilerParams(vmem_limit_bytes=60 << 20),
        name="place",
    )(y, dx, *totals)


def on_device_fast(*arguments):
    (
        tokens, encoder_states, lengths, frame_counts, corpus_ids, corpus_weights, cotangent,
        first_gain, first_bias, query_weight, query_bias, key_weight, value_weight, value_bias,
        output_weight, output_bias, second_gain, second_bias, cross_query_weight, cross_query_bias,
        cross_key_weight, cross_value_weight, cross_value_bias, cross_output_weight, cross_output_bias,
        third_gain, third_bias, expand_weight, expand_bias, reduce_weight, reduce_bias,
    ) = arguments
    bf16, f32 = jnp.bfloat16, jnp.float32
    small_vectors = (
        first_gain, first_bias, query_bias, value_bias, output_bias, second_gain, second_bias,
        cross_query_bias, cross_value_bias, cross_output_bias, third_gain, third_bias, reduce_bias, expand_bias,
    )
    matrices = (
        query_weight, key_weight, value_weight, output_weight, cross_key_weight, cross_value_weight,
        cross_query_weight, cross_output_weight, expand_weight, reduce_weight.T,
    )
    (
        heads_all, mixer_all, pairs_all, wide_all, tall_all, frames_all, vec, wide_bias,
        a_all, head_rows, third, o, h1, c, p_self, ck, cv, cq, o2, h2, m, p_cross,
    ) = run_forward(
        lengths, frame_counts, matrices, jnp.stack(small_vectors[:13]), expand_bias.reshape(3, 128), encoder_states, tokens
    )
    layer_output, dh1, total_ff, acc_kv, acc_xqo, small_before, wide_small = run_feed(
        lengths, corpus_ids, corpus_weights,
        [cotangent, vec, wide_bias, h2, m, o2, c, h1, cq],
        [wide_all, tall_all, pairs_all, frames_all, ck, cv, p_cross],
    )
    tokens_gradient, total, total_o, total_q, small_total = run_last(
        [tokens, dh1, o, vec, small_before, wide_small],
        [heads_all, mixer_all, acc_kv, acc_xqo, a_all, head_rows, third, p_self],
    )
    (
        layer_output, tokens_gradient, m_query, m_key, m_value, m_mixer, m_xkey, m_xvalue, m_xquery, m_xmixer,
        expand_grad, reduce_grad, *smaller,
    ) = run_place(layer_output, tokens_gradient, total, total_o, total_q, total_ff, small_total)
    reduce_grad = reduce_grad.T
    smaller = [row.reshape(-1) for row in smaller]
    expand_bias_grad = smaller[13]
    return (
        layer_output, tokens_gradient, smaller[0], smaller[1], m_query, smaller[2], m_key, m_value, smaller[3],
        m_mixer, smaller[4], smaller[5], smaller[6], m_xquery, smaller[7], m_xkey, m_xvalue, smaller[8],
        m_xmixer, smaller[9], smaller[10], smaller[11], expand_grad, expand_bias_grad, reduce_grad, smaller[12],
    )


def solution(mesh):
    placed = (
        P("grp", "seq", None),
        P("grp", "seq", None),
        P("grp"),
        P("grp"),
        P("grp"),
        P(),
        P("grp", "seq", None),
        P("grp"),
        P("grp"),
        P("grp", "seq"),
        P("grp"),
        P("grp", "seq"),
        P("grp", "seq"),
        P("grp"),
        P("grp", "seq"),
        P("grp"),
        P("grp"),
        P("grp"),
        P("grp", "seq"),
        P("grp"),
        P("grp", "seq"),
        P("grp", "seq"),
        P("grp"),
        P("grp", "seq"),
        P("grp"),
        P("grp"),
        P("grp"),
        P("grp", "seq"),
        P("grp"),
        P("grp", "seq"),
        P("grp"),
    )
    small_slice = mesh.shape["grp"] == NZ * NX and mesh.shape["seq"] == NY * NC
    return jax.shard_map(
        on_device_fast if small_slice else on_device_plain,
        mesh=mesh,
        in_specs=placed,
        out_specs=(
            P("grp", "seq", None),
            P("grp", "seq", None),
            P("grp"),
            P("grp"),
            P("grp", "seq"),
            P("grp"),
            P("grp", "seq"),
            P("grp", "seq"),
            P("grp"),
            P("grp", "seq"),
            P("grp"),
            P("grp"),
            P("grp"),
            P("grp", "seq"),
            P("grp"),
            P("grp", "seq"),
            P("grp", "seq"),
            P("grp"),
            P("grp", "seq"),
            P("grp"),
            P("grp"),
            P("grp"),
            P("grp", "seq"),
            P("grp"),
            P("grp", "seq"),
            P("grp"),
        ),
        check_vma=False,
    )
```
